32 devices in a mesh: fsdp: 2 (over y), ctx: 4 (over z), tp: 4 (over x, core).
Axes of the slice: x: 2, y: 2, z: 4, core: 2. Of those that a mesh axis runs over, the one named last changes fastest.
Arguments:
- inputs: bfloat16 [4, 2048, 768], P('fsdp', 'ctx'), may hold values from -6 to 6
- positions: int32 [4, 2048], P('fsdp'), may hold values from 0 to 2047, as said below
- query_key_value_weight: bfloat16 [768, 3, 768], P('fsdp', None, 'tp'), may hold values from -0.21875 to 0.21875
- query_key_value_bias: float32 [3, 768], P(None, 'tp'), may hold values from -3 to 3
- attention_output_weight: bfloat16 [768, 768], P('tp', 'fsdp'), may hold values from -1.75 to 1.75
- attention_output_bias: float32 [768], replicated, may hold values from -3 to 3
- up_projection_weight: bfloat16 [768, 3072], P('fsdp', 'tp'), may hold values from -0.21875 to 0.21875
- up_projection_bias: float32 [3072], P('tp'), may hold values from -3 to 3
- down_projection_weight: bfloat16 [3072, 768], P('tp', 'fsdp'), may hold values from -0.109375 to 0.109375
- down_projection_bias: float32 [768], replicated, may hold values from -3 to 3
- first_scale: float32 [768], replicated, may hold values from 0.5 to 1.5
- first_shift: float32 [768], replicated, may hold values from -1.8 to 1.8
- second_scale: float32 [768], replicated, may hold values from 0.5 to 1.5
- second_shift: float32 [768], replicated, may hold values from -1.8 to 1.8
- cotangent: bfloat16 [4, 2048, 768], P('fsdp', 'ctx'), may hold values from -6 to 6
Outputs:
- block_out: float32 [4, 2048, 768], P('fsdp', 'ctx')
- inputs_grad: float32 [4, 2048, 768], P('fsdp', 'ctx')
- mix_weight_grad: float32 [768, 3, 768], P('fsdp', None, 'tp')
- mix_bias_grad: float32 [3, 768], P(None, 'tp')
- out_weight_grad: float32 [768, 768], P('tp', 'fsdp')
- out_bias_grad: float32 [768], replicated
- up_weight_grad: float32 [768, 3072], P('fsdp', 'tp')
- up_bias_grad: float32 [3072], P('tp')
- down_weight_grad: float32 [3072, 768], P('tp', 'fsdp')
- down_bias_grad: float32 [768], replicated
- first_scale_grad: float32 [768], replicated
- first_shift_grad: float32 [768], replicated
- second_scale_grad: float32 [768], replicated
- second_shift_grad: float32 [768], replicated
The draws below stay inside these ranges and needn't reach their ends.
Inputs may be any that keep to these rules, and one draw needn't show every extreme that they name: `positions`: each row is a permutation of the ids 0 to 2047 made of runs of 64 ids that rise by one, each run starting at a multiple of 64.
All inputs are finite; a program needn't handle non-finite values.
Results may differ from the reference program's by a relative error of at most 0.0089.
Values may be sent and summed in bfloat16 or wider, within the bound.
No kernel may reach another device: no remote copies, remote signals or barrier semaphores. Data moves between devices by JAX's collectives and lax.ppermute only.
A program may use at most 128 MiB of HBM per device.

```python
import jax
import jax.numpy as jnp
from jax import lax

D = 768
HEADS = 12
HEAD = 64
ROT = 16
FF = 3072
LEN = 2048
PIECE = 64
SEQS = 4


def draw_positions(key, part):
    key = jax.random.fold_in(key, 7)
    run_count = LEN // PIECE
    seq_keys = jax.random.split(key, SEQS)
    orders = jax.vmap(lambda one_key: jax.random.permutation(one_key, run_count))(seq_keys)
    spots = orders[:, :, None] * PIECE + jnp.arange(PIECE)[None, None, :]
    return spots.reshape(SEQS, LEN).astype(jnp.int32)


def steps_of(stream_key, dims, shards, least, high):
    def one(axis_at, parts):
        draws = jax.random.uniform(jax.random.fold_in(jax.random.fold_in(stream_key, 6), axis_at), (parts,), jnp.float32, least / len(shards), high / len(shards))
        return jnp.repeat(jnp.exp(draws), dims[axis_at] // parts).reshape((-1,) + (1,) * (len(dims) - axis_at - 1))

    loudness = one(*shards[0])
    for cut in shards[1:]:
        loudness = loudness * one(*cut)
    return loudness


def normal_values(stream_key, shape, deviation, reach, cuts=(), held_as=jnp.bfloat16):
    entries = deviation * jax.random.normal(stream_key, shape, jnp.float32)
    if cuts:
        entries = entries * steps_of(stream_key, shape, cuts, -0.22, 0.18)
    return jnp.clip(entries, -reach, reach).astype(held_as)


def setup_inputs(seed: int = 0) -> dict:
    streams_of = jax.random.split(jax.random.key(seed), 16)
    inputs = normal_values(streams_of[0], (SEQS, LEN, D), 1.0, 6.0, ((0, 2), (1, 4)))
    positions = draw_positions(jax.random.fold_in(streams_of[15], 71), 0)
    query_key_value_weight = normal_values(streams_of[2], (D, 3, HEADS * HEAD), D ** -0.5, 0.21875, ((0, 2), (2, 4)))
    query_key_value_bias = normal_values(streams_of[3], (3, HEADS * HEAD), 0.5, 3.0, ((1, 4),), jnp.float32)
    attention_output_weight = normal_values(streams_of[4], (HEADS * HEAD, D), (D // 64) ** -0.5, 1.75, ((0, 4), (1, 2)))
    attention_output_bias = normal_values(streams_of[5], (D,), 0.5, 3.0, (), jnp.float32)
    up_projection_weight = normal_values(streams_of[6], (D, FF), D ** -0.5, 0.21875, ((0, 2), (1, 4)))
    up_projection_bias = normal_values(streams_of[7], (FF,), 0.5, 3.0, ((0, 4),), jnp.float32)
    down_projection_weight = normal_values(streams_of[8], (FF, D), FF ** -0.5, 0.109375, ((0, 4), (1, 2)))
    down_projection_bias = normal_values(streams_of[9], (D,), 0.5, 3.0, (), jnp.float32)
    first_scale = jnp.clip(1.0 + 0.1 * jax.random.normal(streams_of[10], (D,), jnp.float32), 0.5, 1.5)
    first_shift = normal_values(streams_of[11], (D,), 0.3, 1.8, (), jnp.float32)
    second_scale = jnp.clip(1.0 + 0.1 * jax.random.normal(streams_of[12], (D,), jnp.float32), 0.5, 1.5)
    second_shift = normal_values(streams_of[13], (D,), 0.3, 1.8, (), jnp.float32)
    cotangent = normal_values(streams_of[14], (SEQS, LEN, D), 1.0, 6.0, ((0, 2), (1, 4)))
    return {"inputs": inputs, "positions": positions, "query_key_value_weight": query_key_value_weight, "query_key_value_bias": query_key_value_bias, "attention_output_weight": attention_output_weight, "attention_output_bias": attention_output_bias, "up_projection_weight": up_projection_weight, "up_projection_bias": up_projection_bias, "down_projection_weight": down_projection_weight, "down_projection_bias": down_projection_bias, "first_scale": first_scale, "first_shift": first_shift, "second_scale": second_scale, "second_shift": second_shift, "cotangent": cotangent}


@jax.custom_vjp
def low(v):
    return lax.optimization_barrier(v.astype(jnp.bfloat16)).astype(jnp.float32)

@jax.custom_vjp
def reduced_backward(v):
    return v

def low_keep(v):
    return (low(v), None)

def low_pass(kept, grad):
    return (grad,)

def back_keep(v):
    return (v, None)

def back_low(kept, grad):
    return (low(grad),)
low.defvjp(low_keep, low_pass)
reduced_backward.defvjp(back_keep, back_low)

def layer_norm(values, scales, offsets):
    average = lax.optimization_barrier(jnp.mean(values, axis=-1, keepdims=True))
    centred = values - average
    spread = lax.optimization_barrier(jnp.mean(centred * centred, axis=-1, keepdims=True))
    return centred * lax.rsqrt(spread + 1e-05) * scales + offsets

def rotate(values, places):
    halfway = ROT // 2
    inverse = 10000.0 ** (-2.0 * jnp.arange(halfway, dtype=jnp.float32) / ROT)
    angles = places.astype(jnp.float32)[..., None] * inverse
    cosine = jnp.cos(angles)[..., None, :]
    sine_part = jnp.sin(angles)[..., None, :]
    leading = values[..., :halfway]
    trailing = values[..., halfway:ROT]
    return jnp.concatenate([leading * cosine - trailing * sine_part, trailing * cosine + leading * sine_part, values[..., ROT:]], axis=-1)

def exact_gelu(values):
    return jax.nn.gelu(values, approximate=False)

def forward(inputs, query_key_value_weight, query_key_value_bias, attention_output_weight, attention_output_bias, up_projection_weight, up_projection_bias, down_projection_weight, down_projection_bias, first_scale, first_shift, second_scale, second_shift, positions):
    highest_precision = lax.Precision.HIGHEST
    seq_count, length, width = inputs.shape
    first_reduced = low(layer_norm(inputs, first_scale, first_shift))
    second_reduced = low(layer_norm(inputs, second_scale, second_shift))
    query_key_value_output = reduced_backward(jnp.einsum('egq,qbi->egbi', first_reduced, query_key_value_weight, precision=highest_precision) + query_key_value_bias)
    pieces = query_key_value_output.reshape(seq_count, length, 3, HEADS, HEAD)
    queries = low(rotate(pieces[:, :, 0], positions))
    keys = low(rotate(pieces[:, :, 1], positions))
    values = low(pieces[:, :, 2])
    factor = HEAD ** (-0.5)

    def attend(blocks_in):
        query_part, key_part, value_part, places = blocks_in
        products = reduced_backward(jnp.einsum('qhe,khe->hqk', query_part, key_part, precision=highest_precision))
        allowed = places[None, :] <= places[:, None]
        scores = jnp.where(allowed[None], products * factor, -1e+30)
        highest_score = lax.optimization_barrier(jnp.max(scores, axis=-1, keepdims=True))
        weights = jnp.exp(scores - highest_score)
        probabilities = weights / lax.optimization_barrier(jnp.sum(weights, axis=-1, keepdims=True))
        result = jnp.einsum('hqk,khe->qhe', low(probabilities), value_part, precision=highest_precision)
        return reduced_backward(low(result))
    attention_result = lax.map(jax.checkpoint(attend), (queries, keys, values, positions))
    attention_result = attention_result.reshape(seq_count, length, HEADS * HEAD)
    attention_branch = jnp.einsum('oaw,wn->oan', attention_result, attention_output_weight, precision=highest_precision) + attention_output_bias
    up_preactivation = reduced_backward(jnp.einsum('iwe,eb->iwb', second_reduced, up_projection_weight, precision=highest_precision) + up_projection_bias)
    hidden_activation = low(exact_gelu(up_preactivation))
    feedforward_branch = jnp.einsum('itr,ro->ito', hidden_activation, down_projection_weight, precision=highest_precision) + down_projection_bias
    return inputs + attention_branch + feedforward_branch

def reference(inputs, positions, query_key_value_weight, query_key_value_bias, attention_output_weight, attention_output_bias, up_projection_weight, up_projection_bias, down_projection_weight, down_projection_bias, first_scale, first_shift, second_scale, second_shift, cotangent):
    floats = (inputs.astype(jnp.float32), query_key_value_weight.astype(jnp.float32), query_key_value_bias.astype(jnp.float32), attention_output_weight.astype(jnp.float32), attention_output_bias.astype(jnp.float32), up_projection_weight.astype(jnp.float32), up_projection_bias.astype(jnp.float32), down_projection_weight.astype(jnp.float32), down_projection_bias.astype(jnp.float32), first_scale.astype(jnp.float32), first_shift.astype(jnp.float32), second_scale.astype(jnp.float32), second_shift.astype(jnp.float32))

    def closed(*params):
        return forward(*params, positions)
    block_out, pullback = jax.vjp(closed, *floats)
    grads = pullback(cotangent.astype(jnp.float32))
    return (block_out, grads[0], grads[1], grads[2], grads[3], grads[4], grads[5], grads[6], grads[7], grads[8], grads[9], grads[10], grads[11], grads[12])
```

```python
import functools

import jax
import jax.numpy as jnp
from jax import lax
from jax.experimental import pallas as pl
from jax.experimental.pallas import tpu as pltpu
from jax.sharding import PartitionSpec as P

HEAD = 64
ROT = 16
HALF = ROT // 2
EPS = 1e-5
NEG = -1e30
F32 = jnp.float32
BF16 = jnp.bfloat16
MIB = 1024 * 1024


def mm(a, b, ca=1, cb=0):
    return lax.dot_general(a, b, (((ca,), (cb,)), ((), ())), preferred_element_type=F32)


def params(mib):
    return pltpu.CompilerParams(vmem_limit_bytes=mib * MIB)


def xhat_of(x):
    width = x.shape[-1]
    centred = x - jnp.sum(x, axis=-1, keepdims=True) * (1.0 / width)
    spread = jnp.sum(centred * centred, axis=-1, keepdims=True) * (1.0 / width)
    inv = lax.rsqrt(spread + EPS)
    return centred * inv, inv


def prep_kernel(own, *refs):
    if own:
        (x_ref, cos_ref, sin_ref, w_ref, b_ref, s1_ref, b1_ref, s2_ref, b2_ref,
         n1_ref, k_ref, v_ref, q_ref, n2_ref) = refs
    else:
        x_ref, cos_ref, sin_ref, w_ref, b_ref, s1_ref, b1_ref, n1_ref, k_ref, v_ref = refs
    xhat, _ = xhat_of(x_ref[...].astype(F32))
    n1 = (xhat * s1_ref[...] + b1_ref[...]).astype(BF16)
    n1_ref[...] = n1
    if own:
        n2_ref[...] = (xhat * s2_ref[...] + b2_ref[...]).astype(BF16)
    mixed = mm(w_ref[...], n1, 1, 1) + b_ref[...]
    cosine, sine = cos_ref[...], sin_ref[...]
    wide = k_ref.shape[0]

    def rotated(ref, base, factor):
        for h in range(0, wide, HEAD):
            a = mixed[base + h : base + h + HALF]
            b = mixed[base + h + HALF : base + h + ROT]
            turned = jnp.concatenate([a * cosine - b * sine, b * cosine + a * sine], axis=0)
            ref[h : h + ROT, :] = turned.astype(BF16) * factor
            ref[h + ROT : h + HEAD, :] = (
                mixed[base + h + ROT : base + h + HEAD].astype(BF16) * factor
            )

    at = 0
    if own:
        rotated(q_ref, 0, BF16(HEAD**-0.5))
        at = wide
    rotated(k_ref, at, BF16(1.0))
    v_ref[...] = mixed[at + wide : at + 2 * wide].astype(BF16)


def prep(own, x, cosine, sine, wt, bias, norm_params):
    rows, width = x.shape
    tall = wt.shape[0]
    wide = tall // 3 if own else tall // 2
    step = 256
    row = pl.BlockSpec((step, width), lambda i: (i, 0))
    trig = pl.BlockSpec((HALF, step), lambda i: (0, i))
    col = pl.BlockSpec((wide, step), lambda i: (0, i))
    vec = pl.BlockSpec((1, width), lambda i: (0, 0))
    out_specs = [row, col, col] + ([col, row] if own else [])
    low_rows = jax.ShapeDtypeStruct((rows, width), BF16)
    low_cols = jax.ShapeDtypeStruct((wide, rows), BF16)
    out_shape = [low_rows, low_cols, low_cols] + ([low_cols, low_rows] if own else [])
    return pl.pallas_call(
        functools.partial(prep_kernel, own),
        grid=(rows // step,),
        in_specs=[row, trig, trig, pl.BlockSpec((tall, width), lambda i: (0, 0)),
                  pl.BlockSpec((tall, 1), lambda i: (0, 0))] + [vec] * len(norm_params),
        out_specs=out_specs,
        out_shape=out_shape,
        compiler_params=params(24),
        cost_estimate=pl.CostEstimate(
            flops=2 * rows * width * tall, bytes_accessed=rows * width * 8, transcendentals=0
        ),
    )(x, cosine, sine, wt, bias, *norm_params)


def attention_kernel(chunk, q_ref, do_ref, ko_ref, kx_ref, vo_ref, vx_ref, kpos_ref, qpos_ref,
                     qcos_ref, qsin_ref, kcos_ref, ksin_ref, o_ref, dq_ref, dk_ref, dv_ref,
                     kn, vn, kt, vt, dk, dv, es, dps):
    i = pl.program_id(1)
    half = ko_ref.shape[1]
    length = 2 * half
    steps = length // chunk

    @pl.when(i == 0)
    def _():
        kt[:, :half] = ko_ref[...]
        kt[:, half:] = kx_ref[...]
        vt[:, :half] = vo_ref[...]
        vt[:, half:] = vx_ref[...]
        kn[:half, :] = ko_ref[...].T
        kn[half:, :] = kx_ref[...].T
        vn[:half, :] = vo_ref[...].T
        vn[half:, :] = vx_ref[...].T
        dk[...] = jnp.zeros_like(dk)
        dv[...] = jnp.zeros_like(dv)

    qt = q_ref[...]
    dot = do_ref[...]
    qn = qt.T
    don = dot.T
    qpos = qpos_ref[...]
    lanes = qt.shape[1]
    fold = (chunk // 8, 8, lanes)

    top = jnp.full((8, lanes), NEG, F32)
    for j in range(steps):
        here = slice(j * chunk, (j + 1) * chunk)
        s = mm(kn[here, :], qt)
        s = jnp.where(kpos_ref[here, :] <= qpos, s, NEG)
        es[here, :] = s
        top = jnp.maximum(top, jnp.max(s.reshape(fold), axis=0))
    top = jnp.max(top, axis=0, keepdims=True)

    total = jnp.zeros((8, lanes), F32)
    inner = jnp.zeros((8, lanes), F32)
    for j in range(steps):
        here = slice(j * chunk, (j + 1) * chunk)
        e = jnp.exp(es[here, :] - top)
        dp = mm(vn[here, :], dot)
        es[here, :] = e
        dps[here, :] = dp
        total = total + jnp.sum(e.reshape(fold), axis=0)
        inner = inner + jnp.sum((e * dp).reshape(fold), axis=0)
    share = 1.0 / jnp.sum(total, axis=0, keepdims=True)
    inner = jnp.sum(inner, axis=0, keepdims=True) * share

    ot = jnp.zeros((HEAD, lanes), F32)
    dqt = jnp.zeros((HEAD, lanes), F32)
    for j in range(steps):
        here = slice(j * chunk, (j + 1) * chunk)
        p = es[here, :] * share
        ds = (p * (dps[here, :] - inner)).astype(BF16)
        p = p.astype(BF16)
        dv[here, :] += mm(p, don)
        dk[here, :] += mm(ds, qn)
        ot = ot + mm(vt[:, here], p)
        dqt = dqt + mm(kt[:, here], ds)
    o_ref[...] = ot.astype(BF16)

    def unrotated(ref, grad, cosine, sine):
        a, b = grad[:HALF], grad[HALF:ROT]
        ref[:ROT, :] = jnp.concatenate(
            [a * cosine + b * sine, b * cosine - a * sine], axis=0
        ).astype(BF16)
        ref[ROT:, :] = grad[ROT:].astype(BF16)

    unrotated(dq_ref, dqt * (HEAD**-0.5), qcos_ref[...], qsin_ref[...])

    @pl.when(i == pl.num_programs(1) - 1)
    def _():
        unrotated(dk_ref, dk[...].T, kcos_ref[...], ksin_ref[...])
        dv_ref[...] = dv[...].T.astype(BF16)


def attention(qt, dot, ko, kx, vo, vx, kpos, qpos, qcos, qsin, kcos, ksin):
    wide, rows = qt.shape
    half = ko.shape[1]
    length = 2 * half
    lanes, chunk = 256, 256
    heads = wide // HEAD
    q_spec = pl.BlockSpec((HEAD, lanes), lambda h, i: (h, i))
    k_spec = pl.BlockSpec((HEAD, half), lambda h, i: (h, 0))
    whole = pl.BlockSpec((HEAD, length), lambda h, i: (h, 0))
    trig_q = pl.BlockSpec((HALF, lanes), lambda h, i: (0, i))
    trig_k = pl.BlockSpec((HALF, length), lambda h, i: (0, 0))
    return pl.pallas_call(
        functools.partial(attention_kernel, chunk),
        grid=(heads, rows // lanes),
        in_specs=[q_spec, q_spec, k_spec, k_spec, k_spec, k_spec,
                  pl.BlockSpec((length, 1), lambda h, i: (0, 0)),
                  pl.BlockSpec((1, lanes), lambda h, i: (0, i)),
                  trig_q, trig_q, trig_k, trig_k],
        out_specs=[q_spec, q_spec, whole, whole],
        out_shape=[jax.ShapeDtypeStruct((wide, rows), BF16)] * 2
        + [jax.ShapeDtypeStruct((wide, length), BF16)] * 2,
        scratch_shapes=[
            pltpu.VMEM((length, HEAD), BF16),
            pltpu.VMEM((length, HEAD), BF16),
            pltpu.VMEM((HEAD, length), BF16),
            pltpu.VMEM((HEAD, length), BF16),
            pltpu.VMEM((length, HEAD), F32),
            pltpu.VMEM((length, HEAD), F32),
            pltpu.VMEM((length, lanes), F32),
            pltpu.VMEM((length, lanes), F32),
        ],
        compiler_params=params(32),
        cost_estimate=pl.CostEstimate(
            flops=40 * rows * length * wide, bytes_accessed=16 * wide * length,
            transcendentals=heads * rows * length,
        ),
    )(qt, dot, ko, kx, vo, vx, kpos, qpos, qcos, qsin, kcos, ksin)


def forward_kernel(n2_ref, g_ref, x_ref, up_ref, bias_ref, down_ref, s2_ref,
                   ff_ref, a_ref, up_part, down_part, small_ref):
    i = pl.program_id(0)

    @pl.when(i == 0)
    def _():
        up_part[...] = jnp.zeros_like(up_part)
        down_part[...] = jnp.zeros_like(down_part)
        small_ref[...] = jnp.zeros_like(small_ref)

    n2, g = n2_ref[...], g_ref[...]
    up = mm(n2, up_ref[...]) + bias_ref[...]
    cdf = 0.5 + 0.5 * lax.erf(up * (0.5**0.5))
    act = (up * cdf).astype(BF16)
    slope = cdf + up * (jnp.exp(up * up * -0.5) * 0.3989422804014327)
    up_grad_f = mm(g, down_ref[...], 1, 1) * slope
    up_grad = up_grad_f.astype(BF16)
    ff_ref[...] = mm(act, down_ref[...])
    second = mm(up_grad, up_ref[...], 1, 1)
    up_part[...] += mm(n2, up_grad, 0, 0)
    down_part[...] += mm(act, g, 0, 0)
    xhat, _ = xhat_of(x_ref[...].astype(F32))
    a_ref[...] = second * s2_ref[...]
    small_ref[0:1, :] += jnp.sum(up_grad.astype(F32), axis=0, keepdims=True)
    small_ref[1:2, :] += jnp.sum(g.astype(F32), axis=0, keepdims=True)
    small_ref[2:3, :] += jnp.sum(second * xhat, axis=0, keepdims=True)
    small_ref[3:4, :] += jnp.sum(second, axis=0, keepdims=True)


def feed_forward(n2, g, x, up, bias, down, scale):
    rows, width = x.shape
    hidden = up.shape[1]
    step = 256
    row = pl.BlockSpec((step, width), lambda i: (i, 0))

    def fixed(*shape):
        return pl.BlockSpec(shape, lambda i: (0, 0))

    return pl.pallas_call(
        forward_kernel,
        grid=(rows // step,),
        in_specs=[row, row, row, fixed(width, hidden), fixed(1, hidden), fixed(hidden, width),
                  fixed(1, width)],
        out_specs=[row, row, fixed(width, hidden), fixed(hidden, width), fixed(8, width)],
        out_shape=[jax.ShapeDtypeStruct((rows, width), F32)] * 2
        + [jax.ShapeDtypeStruct((width, hidden), F32), jax.ShapeDtypeStruct((hidden, width), F32),
           jax.ShapeDtypeStruct((8, width), F32)],
        compiler_params=params(40),
        cost_estimate=pl.CostEstimate(
            flops=12 * rows * width * hidden, bytes_accessed=16 * MIB, transcendentals=0
        ),
    )(n2, g, x, up, bias, down, scale)


def back_kernel(own, *refs):
    if own:
        (dq_ref, dk_ref, dv_ref, n1_ref, x_ref, w_ref, s1_ref, a2_ref,
         a_ref, part_ref, small_ref, bias_ref) = refs
        grads = [dq_ref[...], dk_ref[...], dv_ref[...]]
    else:
        (dk_ref, dv_ref, n1_ref, x_ref, w_ref, s1_ref, a_ref, part_ref, small_ref, bias_ref) = refs
        grads = [dk_ref[...], dv_ref[...]]

    @pl.when(pl.program_id(0) == 0)
    def _():
        part_ref[...] = jnp.zeros_like(part_ref)
        small_ref[...] = jnp.zeros_like(small_ref)
        bias_ref[...] = jnp.zeros_like(bias_ref)

    grad = jnp.concatenate(grads, axis=0)
    part_ref[...] += mm(grad, n1_ref[...])
    bias_ref[...] += jnp.sum(grad.astype(F32), axis=1, keepdims=True)
    first = mm(grad, w_ref[...], 0, 0)
    xhat, _ = xhat_of(x_ref[...].astype(F32))
    a = first * s1_ref[...]
    if own:
        a = a + a2_ref[...]
    a_ref[...] = a.astype(BF16)
    small_ref[0:1, :] += jnp.sum(first * xhat, axis=0, keepdims=True)
    small_ref[1:2, :] += jnp.sum(first, axis=0, keepdims=True)


def back(own, grads, offset, n1, x, wt, scale, extra):
    rows, width = x.shape
    tall = wt.shape[0]
    step = 256
    wide = tall // len(grads)
    row = pl.BlockSpec((step, width), lambda i: (i, 0))
    shift = offset // step
    cols = [pl.BlockSpec((wide, step), lambda i: (0, i))] * (len(grads) - 2)
    cols += [pl.BlockSpec((wide, step), lambda i: (0, i + shift))] * 2

    def fixed(*shape):
        return pl.BlockSpec(shape, lambda i: (0, 0))

    return pl.pallas_call(
        functools.partial(back_kernel, own),
        grid=(rows // step,),
        in_specs=cols + [row, row, fixed(tall, width), fixed(1, width)] + [row] * len(extra),
        out_specs=[row, fixed(tall, width), fixed(8, width), fixed(tall, 1)],
        out_shape=[jax.ShapeDtypeStruct((rows, width), BF16),
                   jax.ShapeDtypeStruct((tall, width), F32),
                   jax.ShapeDtypeStruct((8, width), F32),
                   jax.ShapeDtypeStruct((tall, 1), F32)],
        compiler_params=params(24),
        cost_estimate=pl.CostEstimate(
            flops=4 * rows * width * tall, bytes_accessed=8 * MIB, transcendentals=0
        ),
    )(*grads, n1, x, wt, scale, *extra)


def swap(v, axis, size, distance):
    return lax.ppermute(v, axis, [(i, i ^ distance) for i in range(size)])


def by_xor(pieces, index):
    low, high = (index & 1) == 1, (index & 2) == 2
    a, b, c, d = pieces
    a, b, c, d = (jnp.where(low, b, a), jnp.where(low, a, b),
                  jnp.where(low, d, c), jnp.where(low, c, d))
    return (jnp.where(high, c, a), jnp.where(high, d, b),
            jnp.where(high, a, c), jnp.where(high, b, d))


def gather_rows(shard, axis_name, size, mine, dim):
    if size != 2:
        return lax.all_gather(shard, axis_name, axis=dim, tiled=True)
    other = swap(shard, axis_name, 2, 1)
    first = mine == 0
    return jnp.concatenate(
        [jnp.where(first, shard, other), jnp.where(first, other, shard)], axis=dim
    )


def scatter_rows(part, axis_name, size, mine, dim):
    if size != 2:
        return lax.psum_scatter(
            part.astype(BF16), axis_name, scatter_dimension=dim, tiled=True
        ).astype(F32)
    width = part.shape[dim] // 2
    send = lax.dynamic_slice_in_dim(part, (1 - mine) * width, width, dim).astype(BF16)
    keep = lax.dynamic_slice_in_dim(part, mine * width, width, dim)
    return keep + swap(send, axis_name, 2, 1).astype(F32)


def sum_over_four(v, axis_name, mine):
    rows = v.shape[0] // 4
    low = v.astype(BF16)

    def part(j):
        return lax.dynamic_slice_in_dim(low, (mine ^ j) * rows, rows, 0)

    total = lax.dynamic_slice_in_dim(v, mine * rows, rows, 0)
    for j in (3, 2, 1):
        total = total + swap(part(j), axis_name, 4, j).astype(F32)
    total = total.astype(BF16)
    pieces = [total] + [swap(total, axis_name, 4, j) for j in (1, 2, 3)]
    return jnp.concatenate(by_xor(pieces, mine), axis=0).astype(F32)


def butterfly(v, axis_name, size):
    distance = 1
    while distance < size:
        v = v + swap(v, axis_name, size, distance)
        distance *= 2
    return v


def shards(
    sizes,
    inputs,
    positions,
    query_key_value_weight,
    query_key_value_bias,
    attention_output_weight,
    attention_output_bias,
    up_projection_weight,
    up_projection_bias,
    down_projection_weight,
    down_projection_bias,
    first_scale,
    first_shift,
    second_scale,
    second_shift,
    cotangent,
):
    fsdp = sizes["fsdp"]
    seq_count, block, width = inputs.shape
    assert seq_count == 2 and sizes["ctx"] == 4 and sizes["tp"] == 4
    length = positions.shape[1]
    local = query_key_value_weight.shape[2]
    quarter = block // 4
    f = lax.axis_index("fsdp")
    c = lax.axis_index("ctx")
    t = lax.axis_index("tp")
    s = c // 2

    mix_shard = query_key_value_weight.transpose(1, 2, 0).reshape(3 * local, -1)
    wt = gather_rows(mix_shard, "fsdp", fsdp, f, 1)
    wo = gather_rows(attention_output_weight, "fsdp", fsdp, f, 1)
    wup = gather_rows(up_projection_weight, "fsdp", fsdp, f, 0)
    wdown = gather_rows(down_projection_weight, "fsdp", fsdp, f, 1)

    def quarters(v, seq):
        one = lax.dynamic_index_in_dim(v, seq, 0, keepdims=False)
        return [
            lax.dynamic_slice_in_dim(one, (t ^ j) * quarter, quarter, 0) for j in (0, 2, 1, 3)
        ]

    def over_tp(v):
        v = jnp.concatenate([v, swap(v, "tp", 4, 2)], axis=-2)
        return jnp.concatenate([v, swap(v, "tp", 4, 1)], axis=-2)

    x_mine = quarters(inputs, s)
    x_theirs = quarters(inputs, 1 - s)[0]
    g_mine = quarters(cotangent, s)
    g_theirs = quarters(cotangent, 1 - s)[0]
    x_far = over_tp(swap(x_theirs, "ctx", 4, 2))
    x_near = over_tp(swap(x_mine[0], "ctx", 4, 1))
    x_cross = over_tp(swap(x_theirs, "ctx", 4, 3))
    g_far = over_tp(swap(g_theirs, "ctx", 4, 2))
    x_own = jnp.concatenate(x_mine + [x_far], axis=0)
    x_other = jnp.concatenate([x_near, x_cross], axis=0)
    g_own = jnp.concatenate(g_mine + [g_far], axis=0)

    places = lax.dynamic_index_in_dim(positions, s, 0, keepdims=False)
    places = places.reshape(2, 2, 2, 2, quarter)
    for axis, bit in ((0, c >> 1), (1, c & 1), (2, t >> 1), (3, t & 1)):
        places = jnp.where(bit == 1, jnp.flip(places, axis), places)
    places = places.transpose(1, 0, 3, 2, 4).reshape(length)
    inverse = 10000.0 ** (-2.0 * jnp.arange(HALF, dtype=F32) / ROT)
    angles = inverse[:, None] * places.astype(F32)[None, :]
    cosine, sine = jnp.cos(angles), jnp.sin(angles)
    own_rows = 2 * block

    s1, b1 = first_scale.reshape(1, width), first_shift.reshape(1, width)
    s2, b2 = second_scale.reshape(1, width), second_shift.reshape(1, width)
    mix_bias = query_key_value_bias.reshape(3 * local, 1)
    n1_own, k_own, v_own, qt, n2 = prep(
        True, x_own, cosine[:, :own_rows], sine[:, :own_rows], wt, mix_bias, (s1, b1, s2, b2)
    )
    n1_other, k_other, v_other = prep(
        False, x_other, cosine[:, own_rows:], sine[:, own_rows:], wt[local:], mix_bias[local:],
        (s1, b1),
    )
    dot = mm(wo, g_own, 1, 1).astype(BF16)

    ff, a2, up_part, down_part, small_ff = feed_forward(
        n2, g_own, x_own, wup, up_projection_bias.reshape(1, -1), wdown, s2
    )

    ot, dqt, dkt, dvt = attention(
        qt, dot, k_own, k_other, v_own, v_other, places.reshape(length, 1),
        places[:own_rows].reshape(1, own_rows), cosine[:, :own_rows], sine[:, :own_rows],
        cosine, sine,
    )
    branches = (mm(ot, wo, 0, 0) + ff).astype(BF16)
    out_part = mm(ot, g_own)

    a_other, part_other, small_other, bias_other = back(
        False, (dkt, dvt), own_rows, n1_other, x_other, wt[local:], s1, ()
    )
    a_own, part_own, small_own, bias_own = back(
        True, (dqt, dkt, dvt), 0, n1_own, x_own, wt, s1, (a2,)
    )

    def scatter_tp(v):
        v = v.reshape(-1, 2, 2 * quarter, width)
        kept = v[:, 0].astype(F32) + swap(v[:, 1], "tp", 4, 1).astype(F32)
        kept = kept.reshape(-1, 2, quarter, width)
        return kept[:, 0] + swap(kept[:, 1].astype(BF16), "tp", 4, 2).astype(F32)

    def gather_tp(v):
        v = v.astype(BF16)
        x_side = swap(v, "tp", 4, 2)
        pair = jnp.stack([v, x_side])
        core_side = swap(pair, "tp", 4, 1)
        pieces = (v, core_side[0], x_side, core_side[1])
        return jnp.concatenate(by_xor(pieces, t), axis=1)

    def by_sequence(mine, theirs):
        return jnp.stack([jnp.where(s == 0, mine, theirs), jnp.where(s == 0, theirs, mine)])

    branch_sums = scatter_tp(branches)
    theirs = swap(branch_sums[1].astype(BF16), "ctx", 4, 2).astype(F32)
    full = gather_tp(by_sequence(branch_sums[0], theirs))
    block_out = (
        inputs.astype(F32) + full.astype(F32) + (attention_output_bias + down_projection_bias)
    )

    other_sums = scatter_tp(a_other)
    own_sums = scatter_tp(a_own)
    crossed = swap(other_sums[1].astype(BF16), "ctx", 4, 3).astype(F32)
    far = swap(own_sums[1].astype(BF16), "ctx", 4, 2).astype(F32)
    near = swap(other_sums[0].astype(BF16), "ctx", 4, 1).astype(F32)
    a = by_sequence(own_sums[0] + near, far + crossed)
    x_quarter = by_sequence(x_mine[0], x_theirs).astype(F32)
    xhat, inv = xhat_of(x_quarter)
    norm_grad = inv * (
        a
        - jnp.mean(a, axis=-1, keepdims=True)
        - xhat * jnp.mean(a * xhat, axis=-1, keepdims=True)
    )
    inputs_grad = cotangent.astype(F32) + gather_tp(norm_grad).astype(F32)

    def owned(part, dim):
        return sum_over_four(scatter_rows(part, "fsdp", fsdp, f, dim), "ctx", c)

    up_total = owned(up_part, 0)
    down_total = owned(down_part, 1)
    out_total = owned(out_part, 1)
    mix_part = part_own + jnp.concatenate([jnp.zeros((local, width), F32), part_other], axis=0)
    mix_total = owned(mix_part, 1).reshape(3, local, -1).transpose(2, 0, 1)

    mix_bias_grad = bias_own + jnp.concatenate([jnp.zeros((local, 1), F32), bias_other], axis=0)
    mix_bias_grad = jnp.pad(mix_bias_grad.reshape(1, -1), ((0, 0), (0, width - 3 * local)))
    small = jnp.concatenate(
        [small_own[0:2] + small_other[0:2], small_ff[2:4], small_ff[0:2], mix_bias_grad,
         jnp.zeros((1, width), F32)], axis=0
    )
    small = butterfly(small, "fsdp", fsdp)
    small = butterfly(small, "ctx", 4)
    norm_small = butterfly(small[0:4], "tp", 4)
    bias_total = small[5]
    return (
        block_out,
        inputs_grad,
        mix_total,
        small[6, : 3 * local].reshape(3, local),
        out_total,
        bias_total,
        up_total,
        small[4],
        down_total,
        bias_total,
        norm_small[0],
        norm_small[1],
        norm_small[2],
        norm_small[3],
    )


def solution(mesh):
    in_specs = (
        P("fsdp", "ctx", None),
        P("fsdp", None),
        P("fsdp", None, "tp"),
        P(None, "tp"),
        P("tp", "fsdp"),
        P(),
        P("fsdp", "tp"),
        P("tp"),
        P("tp", "fsdp"),
        P(),
        P(),
        P(),
        P(),
        P(),
        P("fsdp", "ctx", None),
    )
    out_specs = (
        P("fsdp", "ctx", None),
        P("fsdp", "ctx", None),
        P("fsdp", None, "tp"),
        P(None, "tp"),
        P("tp", "fsdp"),
        P(),
        P("fsdp", "tp"),
        P("tp"),
        P("tp", "fsdp"),
        P(),
        P(),
        P(),
        P(),
        P(),
    )
    body = functools.partial(shards, dict(mesh.shape))
    return jax.shard_map(body, mesh=mesh, in_specs=in_specs, out_specs=out_specs, check_vma=False)
```

```python
import functools

import jax
import jax.numpy as jnp
from jax import lax
from jax.experimental import pallas as pl
from jax.experimental.pallas import tpu as pltpu
from jax.sharding import PartitionSpec as P

HEAD = 64
ROT = 16
HALF = ROT // 2
EPS = 1e-5
NEG = -1e30
STEP = 256
F32 = jnp.float32
BF16 = jnp.bfloat16
MIB = 1024 * 1024


def mm(a, b, ca=1, cb=0):
    return lax.dot_general(a, b, (((ca,), (cb,)), ((), ())), preferred_element_type=F32)


def params(mib):
    return pltpu.CompilerParams(vmem_limit_bytes=mib * MIB)


def cost(flops, moved, exps=0):
    return pl.CostEstimate(flops=int(flops), bytes_accessed=int(moved), transcendentals=int(exps))


def xhat_of(x):
    width = x.shape[-1]
    centred = x - jnp.sum(x, axis=-1, keepdims=True) * (1.0 / width)
    spread = jnp.sum(centred * centred, axis=-1, keepdims=True) * (1.0 / width)
    inv = lax.rsqrt(spread + EPS)
    return centred * inv, inv


def row_of(ref):
    return ref[...].reshape(1, -1)


def shape(*dims):
    return jax.ShapeDtypeStruct(dims, F32)


def low_shape(*dims):
    return jax.ShapeDtypeStruct(dims, BF16)


def norm_own_kernel(at, xa, xb, ga, gb, fz, fx, fc, ta, tb, s1, b1, s2, b2,
                    n1_ref, n2_ref, xhat_ref, g_ref, trig_ref, x):
    i = pl.program_id(0)
    q = xa.shape[1]

    @pl.when(i < 2)
    def _():
        x[:q, :] = xa[0]
        x[q:, :] = xb[0]
        g_ref[:q, :] = ga[0]
        g_ref[q:, :] = gb[0]

    @pl.when(i == 2)
    def _():
        x[:q, :] = fz[0]
        x[q:, :] = fx[0]
        g_ref[:q, :] = fz[1]
        g_ref[q:, :] = fx[1]

    @pl.when(i == 3)
    def _():
        x[:q, :] = fc[0, 0]
        x[q:, :] = fc[1, 0]
        g_ref[:q, :] = fc[0, 1]
        g_ref[q:, :] = fc[1, 1]

    trig_ref[:, :q] = ta[0]
    trig_ref[:, q:] = tb[0]
    xhat, _ = xhat_of(x[...].astype(F32))
    xhat_ref[...] = xhat.astype(BF16)
    n1_ref[...] = (xhat * row_of(s1) + row_of(b1)).astype(BF16)
    n2_ref[...] = (xhat * row_of(s2) + row_of(b2)).astype(BF16)


def norm_other_kernel(at, nz, nx, nc, ta, tb, s1, b1, n1_ref, xhat_ref, trig_ref, x):
    i = pl.program_id(0)
    q = nz.shape[1]
    b = i // 2

    @pl.when(i % 2 == 0)
    def _():
        x[:q, :] = nz[b]
        x[q:, :] = nx[b]

    @pl.when(i % 2 == 1)
    def _():
        x[:q, :] = nc[0, b]
        x[q:, :] = nc[1, b]

    trig_ref[:, :q] = ta[0]
    trig_ref[:, q:] = tb[0]
    xhat, _ = xhat_of(x[...].astype(F32))
    xhat_ref[...] = xhat.astype(BF16)
    n1_ref[...] = (xhat * row_of(s1) + row_of(b1)).astype(BF16)


def norms(at, own, arrays, trig, vectors):
    width = vectors[0].shape[0]
    rows, q = 4 * STEP, STEP // 2
    tall = trig.shape[1]
    first = 0 if own else 1

    def pick(high):
        def place(i, at):
            block = at[1] ^ (first + 2 * (i // 2))
            return (at[0], 0, block * 4 + (at[2] ^ (i % 2 + high)))

        return pl.BlockSpec((1, tall, q), place)

    def piece(high):
        return pl.BlockSpec(
            (1, q, width), lambda i, at: (at[0], at[2] ^ (jnp.minimum(i, 1) + high), 0)
        )

    def whole(v):
        return pl.BlockSpec(v.shape, lambda i, at: (0,) * v.ndim)

    row = pl.BlockSpec((STEP, width), lambda i, at: (i, 0))
    out_trig = pl.BlockSpec((tall, STEP), lambda i, at: (0, i))
    if own:
        x, g, received = arrays[0], arrays[1], arrays[2:]
        specs = [piece(0), piece(2), piece(0), piece(2)]
        operands = [x, x, g, g]
        kernel, count = norm_own_kernel, 4
    else:
        received, specs, operands = arrays, [], []
        kernel, count = norm_other_kernel, 2
    specs += [whole(v) for v in received] + [pick(0), pick(2)] + [whole(v) for v in vectors]
    operands += [*received, trig, trig, *vectors]
    return pl.pallas_call(
        kernel,
        grid_spec=pltpu.PrefetchScalarGridSpec(
            num_scalar_prefetch=1,
            grid=(rows // STEP,),
            in_specs=specs,
            out_specs=[row] * count + [out_trig],
            scratch_shapes=[pltpu.VMEM((STEP, width), BF16)],
        ),
        out_shape=[low_shape(rows, width)] * count + [shape(tall, rows)],
        compiler_params=params(24),
        cost_estimate=cost(0, 6 * rows * width),
    )(at, *operands)


def project_kernel(n1o, n1x, to, tx, g_ref, w_ref, b_ref, k_ref, v_ref, q_ref, do_ref, bias):
    i = pl.program_id(0)
    wide = k_ref.shape[0]

    @pl.when(i == 0)
    def _():
        for j in range(3):
            line = jnp.broadcast_to(b_ref[j : j + 1, :], (8, wide))
            bias[j * wide : (j + 1) * wide, :] = line.T[:, 0:1]

    def rotated(ref, mixed, trig, factor):
        cosine, sine = trig[:HALF], trig[HALF:ROT]
        for h in range(0, wide, HEAD):
            a, b = mixed[h : h + HALF], mixed[h + HALF : h + ROT]
            turned = jnp.concatenate([a * cosine - b * sine, b * cosine + a * sine], axis=0)
            ref[h : h + ROT, :] = turned.astype(BF16) * factor
            ref[h + ROT : h + HEAD, :] = mixed[h + ROT : h + HEAD].astype(BF16) * factor

    def keys_values(mixed, trig):
        rotated(k_ref, mixed[:wide], trig, BF16(1.0))
        v_ref[...] = mixed[wide:].astype(BF16)

    @pl.when(i < 4)
    def _():
        trig = to[...]
        mixed = mm(w_ref[: 3 * wide, :], n1o[...], 1, 1) + bias[...]
        rotated(q_ref, mixed[:wide], trig, BF16(HEAD**-0.5))
        keys_values(mixed[wide:], trig)
        do_ref[...] = mm(w_ref[3 * wide :, :], g_ref[...], 1, 1).astype(BF16)

    @pl.when(i >= 4)
    def _():
        mixed = mm(w_ref[wide : 3 * wide, :], n1x[...], 1, 1) + bias[wide:, :]
        keys_values(mixed, tx[...])


def project(n1_own, n1_other, trig_own, trig_other, g, weights, bias):
    rows, width = n1_own.shape
    wide = bias.shape[1]
    tall = trig_own.shape[0]

    def own(i):
        return jnp.minimum(i, 3)

    def other(i):
        return jnp.maximum(i - 4, 0)

    col = pl.BlockSpec((wide, STEP), lambda i: (0, i))
    own_col = pl.BlockSpec((wide, STEP), lambda i: (0, own(i)))
    return pl.pallas_call(
        project_kernel,
        grid=(8,),
        in_specs=[
            pl.BlockSpec((STEP, width), lambda i: (own(i), 0)),
            pl.BlockSpec((STEP, width), lambda i: (other(i), 0)),
            pl.BlockSpec((tall, STEP), lambda i: (0, own(i))),
            pl.BlockSpec((tall, STEP), lambda i: (0, other(i))),
            pl.BlockSpec((STEP, width), lambda i: (own(i), 0)),
            pl.BlockSpec((4 * wide, width), lambda i: (0, 0)),
            pl.BlockSpec((3, wide), lambda i: (0, 0)),
        ],
        out_specs=[col, col, own_col, own_col],
        out_shape=[low_shape(wide, 2 * rows)] * 2 + [low_shape(wide, rows)] * 2,
        scratch_shapes=[pltpu.VMEM((3 * wide, 1), F32)],
        compiler_params=params(24),
        cost_estimate=cost(12 * rows * width * wide, 12 * rows * width),
    )(n1_own, n1_other, trig_own, trig_other, g, weights, bias)


def attention_kernel(after, q_ref, do_ref, k_ref, v_ref, tq_ref, to_ref, tx_ref,
                     o_ref, dq_ref, dk_ref, dv_ref, kn, vn, kp, dk, dv, es, dps):
    i = pl.program_id(0)
    length = k_ref.shape[1]
    half = length // 2
    chunk = STEP
    steps = length // chunk

    @pl.when(i == 0)
    def _():
        kn[...] = k_ref[...].T
        vn[...] = v_ref[...].T
        kp[:half, :] = to_ref[ROT:, :].T[:, 0:1]
        kp[half:, :] = tx_ref[ROT:, :].T[:, 0:1]
        dk[...] = jnp.zeros_like(dk)
        dv[...] = jnp.zeros_like(dv)

    qt = q_ref[...]
    dot = do_ref[...]
    qn = qt.T
    don = dot.T
    qpos = tq_ref[ROT : ROT + 1, :]
    lanes = qt.shape[1]
    fold = (chunk // 8, 8, lanes)

    top = jnp.full((8, lanes), NEG, F32)
    for j in range(steps):
        here = slice(j * chunk, (j + 1) * chunk)
        s = mm(kn[here, :], qt)
        s = jnp.where(kp[here, :] <= qpos, s, NEG)
        es[here, :] = s
        top = jnp.maximum(top, jnp.max(s.reshape(fold), axis=0))
    top = jnp.max(top, axis=0, keepdims=True)

    total = jnp.zeros((8, lanes), F32)
    inner = jnp.zeros((8, lanes), F32)
    for j in range(steps):
        here = slice(j * chunk, (j + 1) * chunk)
        e = jnp.exp(es[here, :] - top)
        dp = mm(vn[here, :], dot)
        es[here, :] = e
        dps[here, :] = dp
        total = total + jnp.sum(e.reshape(fold), axis=0)
        inner = inner + jnp.sum((e * dp).reshape(fold), axis=0)
    share = 1.0 / jnp.sum(total, axis=0, keepdims=True)
    inner = jnp.sum(inner, axis=0, keepdims=True) * share

    ot = jnp.zeros((HEAD, lanes), F32)
    dqt = jnp.zeros((HEAD, lanes), F32)
    for j in range(steps):
        here = slice(j * chunk, (j + 1) * chunk)
        p = es[here, :] * share
        ds = (p * (dps[here, :] - inner)).astype(BF16)
        p = p.astype(BF16)
        dv[here, :] += mm(p, don)
        dk[here, :] += mm(ds, qn)
        ot = ot + mm(v_ref[:, here], p)
        dqt = dqt + mm(k_ref[:, here], ds)
    o_ref[...] = ot.astype(BF16)

    def unrotated(grad, trig):
        cosine, sine = trig[:HALF], trig[HALF:ROT]
        a, b = grad[:HALF], grad[HALF:ROT]
        turned = jnp.concatenate([a * cosine + b * sine, b * cosine - a * sine], axis=0)
        return turned.astype(BF16), grad[ROT:].astype(BF16)

    dq_ref[:ROT, :], dq_ref[ROT:, :] = unrotated(dqt * (HEAD**-0.5), tq_ref[...])

    @pl.when(i == pl.num_programs(0) - 1)
    def _():
        grad = dk[...].T
        dk_ref[:ROT, :half], dk_ref[ROT:, :half] = unrotated(grad[:, :half], to_ref[...])
        dk_ref[:ROT, half:], dk_ref[ROT:, half:] = unrotated(grad[:, half:], tx_ref[...])
        dv_ref[...] = dv[...].T.astype(BF16)


def attention(h, after, qt, dot, kt, vt, trig_own, trig_other):
    rows, length = qt.shape[1], kt.shape[1]
    lanes = STEP
    tall = trig_own.shape[0]
    q_spec = pl.BlockSpec((HEAD, lanes), lambda i: (h, i))
    k_spec = pl.BlockSpec((HEAD, length), lambda i: (h, 0))
    trig_spec = pl.BlockSpec((tall, rows), lambda i: (0, 0))
    return pl.pallas_call(
        attention_kernel,
        grid=(rows // lanes,),
        in_specs=[pl.BlockSpec(memory_space=pl.ANY), q_spec, q_spec, k_spec, k_spec,
                  pl.BlockSpec((tall, lanes), lambda i: (0, i)), trig_spec, trig_spec],
        out_specs=[pl.BlockSpec((HEAD, lanes), lambda i: (0, i))] * 2
        + [pl.BlockSpec((HEAD, length), lambda i: (0, 0))] * 2,
        out_shape=[low_shape(HEAD, rows)] * 2 + [low_shape(HEAD, length)] * 2,
        scratch_shapes=[
            pltpu.VMEM((length, HEAD), BF16),
            pltpu.VMEM((length, HEAD), BF16),
            pltpu.VMEM((length, 1), F32),
            pltpu.VMEM((length, HEAD), F32),
            pltpu.VMEM((length, HEAD), F32),
            pltpu.VMEM((length, lanes), F32),
            pltpu.VMEM((length, lanes), F32),
        ],
        compiler_params=params(32),
        cost_estimate=cost(40 * rows * length * HEAD, 16 * HEAD * length, rows * length),
    )(after, qt, dot, kt, vt, trig_own, trig_own, trig_other)


def forward_kernel(split, at, n2_ref, g_ref, xhat_ref, up_ref, bias_ref, down_ref, s2_ref,
                   ff_ref, a_ref, small_ref, first_ref, second_ref, *scratch):
    i = pl.program_id(0)
    up_part, down_part = scratch if split else (first_ref, second_ref)

    @pl.when(i == 0)
    def _():
        up_part[...] = jnp.zeros_like(up_part)
        down_part[...] = jnp.zeros_like(down_part)
        small_ref[...] = jnp.zeros_like(small_ref)

    n2, g = n2_ref[...], g_ref[...]
    up = mm(n2, up_ref[...]) + row_of(bias_ref)
    cdf = 0.5 + 0.5 * lax.erf(up * (0.5**0.5))
    act = (up * cdf).astype(BF16)
    slope = cdf + up * (jnp.exp(up * up * -0.5) * 0.3989422804014327)
    up_grad = (mm(g, down_ref[...], 1, 1) * slope).astype(BF16)
    ff_ref[...] = mm(act, down_ref[...]).astype(BF16)
    second = mm(up_grad, up_ref[...], 1, 1)
    up_part[...] += mm(n2, up_grad, 0, 0)
    down_part[...] += mm(act, g, 0, 0)
    a_ref[...] = (second * row_of(s2_ref)).astype(BF16)
    small_ref[0:1, :] += jnp.sum(up_grad.astype(F32), axis=0, keepdims=True)
    small_ref[1:2, :] += jnp.sum(g.astype(F32), axis=0, keepdims=True)
    small_ref[2:3, :] += jnp.sum(second * xhat_ref[...].astype(F32), axis=0, keepdims=True)
    small_ref[3:4, :] += jnp.sum(second, axis=0, keepdims=True)

    if split:
        half = up_part.shape[0] // 2

        @pl.when(i == pl.num_programs(0) - 1)
        def _():
            for ref, f in ((first_ref, at[3]), (second_ref, 1 - at[3])):
                piece = pl.ds(pl.multiple_of(f * half, 128), half)
                ref[:half, :] = up_part[piece, :].astype(ref.dtype)
                ref[half:, :half] = down_part[:half, piece].astype(ref.dtype)
                ref[half:, half:] = down_part[half:, piece].astype(ref.dtype)


def feed_forward(split, at, n2, g, xhat, up, bias, down, scale):
    rows, width = n2.shape
    hidden = up.shape[1]
    row = pl.BlockSpec((STEP, width), lambda i, at: (i, 0))

    def whole(*dims):
        return pl.BlockSpec(dims, lambda i, at: (0,) * len(dims))

    if split:
        assert width == hidden
        parts = [shape(width, hidden), low_shape(width, hidden)]
    else:
        parts = [shape(width, hidden), shape(hidden, width)]
    return pl.pallas_call(
        functools.partial(forward_kernel, split),
        grid_spec=pltpu.PrefetchScalarGridSpec(
            num_scalar_prefetch=1,
            grid=(rows // STEP,),
            in_specs=[row, row, row, whole(width, hidden), whole(hidden), whole(hidden, width),
                      whole(width)],
            out_specs=[row, row, whole(8, width)] + [whole(*p.shape) for p in parts],
            scratch_shapes=[pltpu.VMEM((width, hidden), F32), pltpu.VMEM((hidden, width), F32)]
            if split
            else [],
        ),
        out_shape=[low_shape(rows, width)] * 2 + [shape(8, width)] + parts,
        compiler_params=params(40),
        cost_estimate=cost(12 * rows * width * hidden, 16 * MIB, 2 * rows * hidden),
    )(at, n2, g, xhat, up, bias, down, scale)


def back_kernel(split, heads, at, *refs):
    o, dq, dk, dv = (refs[j * heads : (j + 1) * heads] for j in range(4))
    (n1o, n1x, xho, xhx, g_ref, ff_ref, a2_ref, w_ref, s1_ref, small_ff,
     keep_ref, send_ref, first_ref, second_ref, mix, out, small) = refs[4 * heads :]
    i = pl.program_id(0)
    wide = heads * HEAD

    @pl.when(i == 0)
    def _():
        mix[...] = jnp.zeros_like(mix)
        out[...] = jnp.zeros_like(out)
        small[...] = jnp.zeros_like(small)

    def emit(v):
        @pl.when(i % 2 == 0)
        def _():
            keep_ref[0] = v.astype(BF16)

        @pl.when(i % 2 == 1)
        def _():
            send_ref[0] = v.astype(BF16)

    @pl.when(i < 4)
    def _():
        ot = jnp.concatenate([r[...] for r in o], axis=0)
        emit(mm(ot, w_ref[3 * wide :, :], 0, 0) + ff_ref[...].astype(F32))
        out[...] += mm(ot, g_ref[...])

    def through(grad, low, n1, xhat, extra):
        rows = slice(low, 3 * wide)
        first = mm(grad, w_ref[rows, :], 0, 0)
        a = first * row_of(s1_ref)
        emit(a if extra is None else a + extra)
        mix[rows, :] += mm(grad, n1)
        small[0:1, :] += jnp.sum(first * xhat.astype(F32), axis=0, keepdims=True)
        small[1:2, :] += jnp.sum(first, axis=0, keepdims=True)
        ones = jnp.ones((8, grad.shape[1]), BF16)
        small[6:7, low : 3 * wide] += mm(ones, grad, 1, 1)[0:1]

    @pl.when((i >= 4) & (i < 8))
    def _():
        grad = jnp.concatenate([r[...] for r in (*dq, *dk, *dv)], axis=0)
        through(grad, 0, n1o[...], xho[...], a2_ref[...].astype(F32))

    @pl.when(i >= 8)
    def _():
        grad = jnp.concatenate([r[...] for r in (*dk, *dv)], axis=0)
        through(grad, wide, n1x[...], xhx[...], None)

    @pl.when(i == 11)
    def _():
        small[2:4, :] = small_ff[2:4, :]
        small[4:6, :] = small_ff[0:2, :]
        if split:
            half = mix.shape[1] // 2
            vectors = small[...].astype(BF16)
            for ref, f in ((first_ref, at[3]), (second_ref, 1 - at[3])):
                piece = pl.ds(pl.multiple_of(f * half, 128), half)
                ref[: 3 * wide, :] = mix[:, piece].astype(ref.dtype)
                ref[3 * wide : 4 * wide, :] = out[:, piece].astype(ref.dtype)
                both = jnp.concatenate([vectors[:, :half], vectors[:, half:]], axis=0)
                ref[4 * wide : 4 * wide + 16, :] = both.astype(ref.dtype)
                ref[4 * wide + 16 :, :] = jnp.zeros((48, half), ref.dtype)
        else:
            first_ref[: 3 * wide, :] = mix[...]
            first_ref[3 * wide :, :] = out[...]
            second_ref[...] = small[...]


def back(split, at, o, dq, dk, dv, n1_own, n1_other, xhat_own, xhat_other, g, ff, a2, weights,
         scale, small_ff):
    rows, width = g.shape
    heads = len(o)
    wide = heads * HEAD

    def branch(i, at):
        return jnp.minimum(i, 3)

    def own(i, at):
        return jnp.clip(i - 4, 0, 3)

    def other(i, at):
        return jnp.maximum(i - 8, 0)

    def key(i, at):
        return jnp.maximum(i - 4, 0)

    def row(of):
        return pl.BlockSpec((STEP, width), lambda i, at: (of(i, at), 0))

    def col(of):
        return [pl.BlockSpec((HEAD, STEP), lambda i, at: (0, of(i, at)))] * heads

    def whole(*dims):
        return pl.BlockSpec(dims, lambda i, at: (0,) * len(dims))

    def slot(i, at):
        b = jnp.maximum(i - 4, 0) // 2
        return (jnp.where(i < 4, 4 * (1 - i // 2), jnp.where(b == 0, 5, b)), 0, 0)

    half = width // 2
    if split:
        parts = [shape(4 * wide + 64, half), low_shape(4 * wide + 64, half)]
    else:
        parts = [shape(4 * wide, width), shape(8, width)]
    slots = pl.BlockSpec((1, STEP, width), slot)
    return pl.pallas_call(
        functools.partial(back_kernel, split, heads),
        grid_spec=pltpu.PrefetchScalarGridSpec(
            num_scalar_prefetch=1,
            grid=(12,),
            in_specs=col(branch) + col(own) + col(key) + col(key)
            + [row(own), row(other), row(own), row(other), row(branch), row(branch), row(own),
               whole(4 * wide, width), whole(width), whole(8, width)],
            out_specs=[slots, slots] + [whole(*p.shape) for p in parts],
            scratch_shapes=[pltpu.VMEM((3 * wide, width), F32), pltpu.VMEM((wide, width), F32),
                            pltpu.VMEM((8, width), F32)],
        ),
        out_shape=[low_shape(6, STEP, width)] * 2 + parts,
        compiler_params=params(32),
        cost_estimate=cost(28 * rows * width * wide, 20 * MIB),
    )(at, *o, *dq, *dk, *dv, n1_own, n1_other, xhat_own, xhat_other, g, ff, a2, weights, scale,
      small_ff)


def finish_kernel(at, pair, core, x_ref, g_ref, bias_a, bias_b, out_ref, grad_ref):
    j = at[2] ^ pl.program_id(1)

    def write(part):
        bias = row_of(bias_a) + row_of(bias_b)
        out_ref[0] = x_ref[0].astype(F32) + part[0, 0, 0].astype(F32) + bias
        grad_ref[0] = g_ref[0].astype(F32) + part[0, 1, 0].astype(F32)

    @pl.when(j % 2 == 0)
    def _():
        write(pair)

    @pl.when(j % 2 == 1)
    def _():
        write(core)


def finish(at, pair, core, x, g, bias_a, bias_b):
    seqs, block, width = x.shape
    q = block // 4

    def place(i, j, at):
        return (i, j, 0)

    piece = pl.BlockSpec(
        (1, 2, 1, q, width), lambda i, j, at: ((at[2] ^ j) // 2, 0, at[0] ^ i, 0, 0)
    )
    rows = pl.BlockSpec((1, q, width), place)
    vec = pl.BlockSpec((width,), lambda i, j, at: (0,))
    return pl.pallas_call(
        finish_kernel,
        grid_spec=pltpu.PrefetchScalarGridSpec(
            num_scalar_prefetch=1,
            grid=(seqs, 4),
            in_specs=[piece, piece, rows, rows, vec, vec],
            out_specs=[rows, rows],
        ),
        out_shape=[shape(seqs, block, width)] * 2,
        compiler_params=params(24),
        cost_estimate=cost(0, 16 * seqs * block * width),
    )(at, pair, core, x, g, bias_a, bias_b)


def swap(v, axis, size, distance):
    return lax.ppermute(v, axis, [(i, i ^ distance) for i in range(size)])


def by_xor(pieces, index):
    low, high = (index & 1) == 1, (index & 2) == 2
    a, b, c, d = pieces
    a, b, c, d = (jnp.where(low, b, a), jnp.where(low, a, b),
                  jnp.where(low, d, c), jnp.where(low, c, d))
    return (jnp.where(high, c, a), jnp.where(high, d, b),
            jnp.where(high, a, c), jnp.where(high, b, d))


def gather_halves(shard, size, mine, dim):
    if size != 2:
        return lax.all_gather(shard, "fsdp", axis=dim, tiled=True)
    other = swap(shard, "fsdp", 2, 1)
    first = mine == 0
    return jnp.concatenate(
        [jnp.where(first, shard, other), jnp.where(first, other, shard)], axis=dim
    )


def scatter_any(part, dim):
    return lax.psum_scatter(
        part.astype(BF16), "fsdp", scatter_dimension=dim, tiled=True
    ).astype(F32)


def sum_over_ctx(v, c):
    low, high = c % 2, c // 2
    rows = v.shape[0] // 2
    keep = lax.dynamic_slice_in_dim(v, low * rows, rows, 0)
    send = lax.dynamic_slice_in_dim(v, (1 - low) * rows, rows, 0).astype(BF16)
    v = keep + swap(send, "ctx", 4, 1).astype(F32)
    rows = rows // 2
    keep = lax.dynamic_slice_in_dim(v, high * rows, rows, 0)
    send = lax.dynamic_slice_in_dim(v, (1 - high) * rows, rows, 0).astype(BF16)
    v = (keep + swap(send, "ctx", 4, 2).astype(F32)).astype(BF16)
    pair = jnp.stack([v, swap(v, "ctx", 4, 2)])
    others = swap(pair, "ctx", 4, 1)
    return by_xor([pair[0], pair[1], others[0], others[1]], 2 * low + high)


def butterfly(v, axis_name, size):
    distance = 1
    while distance < size:
        v = v + swap(v, axis_name, size, distance)
        distance *= 2
    return v


def shards(
    sizes,
    inputs,
    positions,
    query_key_value_weight,
    query_key_value_bias,
    attention_output_weight,
    attention_output_bias,
    up_projection_weight,
    up_projection_bias,
    down_projection_weight,
    down_projection_bias,
    first_scale,
    first_shift,
    second_scale,
    second_shift,
    cotangent,
):
    fsdp = sizes["fsdp"]
    split = fsdp == 2
    seq_count, block, width = inputs.shape
    assert seq_count == 2 and sizes["ctx"] == 4 and sizes["tp"] == 4 and block == 2 * STEP
    length = positions.shape[1]
    local = query_key_value_weight.shape[2]
    heads = local // HEAD
    hidden = up_projection_weight.shape[1]
    quarter = block // 4
    f = lax.axis_index("fsdp")
    c = lax.axis_index("ctx")
    t = lax.axis_index("tp")
    s = c // 2
    at = jnp.stack([s, c, t, f]).astype(jnp.int32)

    def my_quarter(v, seq):
        return lax.dynamic_slice(v, (seq, t * quarter, 0), (1, quarter, width))

    x_mine, x_theirs = my_quarter(inputs, s), my_quarter(inputs, 1 - s)
    g_theirs = my_quarter(cotangent, 1 - s)
    far_z = swap(jnp.concatenate([x_theirs, g_theirs], axis=0), "ctx", 4, 2)
    cross = swap(x_theirs, "ctx", 4, 3)
    near = swap(x_mine, "ctx", 4, 1)

    def over_tp(v):
        v_x = swap(v, "tp", 4, 2)
        return v, v_x, swap(jnp.stack([v, v_x]), "tp", 4, 1)

    far = over_tp(far_z)
    others = over_tp(jnp.concatenate([near, cross], axis=0))

    wup = gather_halves(up_projection_weight, fsdp, f, 0)
    wdown = gather_halves(down_projection_weight, fsdp, f, 1)
    mix_shard = query_key_value_weight.transpose(1, 2, 0).reshape(3 * local, -1)
    weights = gather_halves(
        jnp.concatenate([mix_shard, attention_output_weight], axis=0), fsdp, f, 1
    )

    inverse = 10000.0 ** (-2.0 * jnp.arange(HALF, dtype=F32) / ROT)
    places = positions.astype(F32)[:, None, :]
    angles = inverse[None, :, None] * places
    trig = jnp.concatenate(
        [jnp.cos(angles), jnp.sin(angles), jnp.broadcast_to(places, angles.shape)], axis=1
    )

    n1_own, n2, xhat_own, g, trig_own = norms(
        at, True, (inputs, cotangent, *far), trig,
        (first_scale, first_shift, second_scale, second_shift),
    )
    ff, a2, small_ff, ff_first, ff_second = feed_forward(
        split, at, n2, g, xhat_own, wup, up_projection_bias, wdown, second_scale
    )
    n1_other, xhat_other, trig_other = norms(
        at, False, others, trig, (first_scale, first_shift)
    )
    kt, vt, qt, dot = project(
        n1_own, n1_other, trig_own, trig_other, g, weights, query_key_value_bias
    )
    per_head = []
    after = small_ff
    for h in range(heads):
        per_head.append(attention(h, after, qt, dot, kt, vt, trig_own, trig_other))
        after = per_head[-1][0]
    o, dq, dk, dv = zip(*per_head)
    keep, send, late_first, late_second = back(
        split, at, o, dq, dk, dv, n1_own, n1_other, xhat_own, xhat_other, g, ff, a2, weights,
        first_scale, small_ff,
    )

    half_sums = keep.astype(F32) + swap(send, "tp", 4, 1).astype(F32)
    half_sums = half_sums.reshape(6, 2, quarter, width)

    def over_x(v):
        return v[:, 0] + swap(v[:, 1].astype(BF16), "tp", 4, 2).astype(F32)

    travel = over_x(half_sums[0:4]).astype(BF16)
    far_back = swap(travel[0:2], "ctx", 4, 2).astype(F32)
    near_back = swap(travel[2], "ctx", 4, 1).astype(F32)
    cross_back = swap(travel[3], "ctx", 4, 3).astype(F32)
    stay = over_x(half_sums[4:6])
    branches = jnp.stack([stay[0], far_back[0]])
    a = jnp.stack([stay[1] + near_back, far_back[1] + cross_back])
    xhat, inv = xhat_of(jnp.concatenate([x_mine, x_theirs], axis=0).astype(F32))
    norm_grad = inv * (
        a
        - jnp.mean(a, axis=-1, keepdims=True)
        - xhat * jnp.mean(a * xhat, axis=-1, keepdims=True)
    )
    ours = jnp.stack([branches, norm_grad]).astype(BF16)
    pair = jnp.stack([ours, swap(ours, "tp", 4, 2)])
    core = swap(pair, "tp", 4, 1)
    block_out, inputs_grad = finish(
        at, pair, core, inputs, cotangent, attention_output_bias, down_projection_bias
    )

    if split:
        q = sum_over_ctx(ff_first + swap(ff_second, "fsdp", 2, 1).astype(F32), c)
        up_total = jnp.concatenate(q[:2], axis=0).astype(F32)
        down_total = jnp.concatenate(q[2:], axis=0).astype(F32)
        down_total = jnp.concatenate(
            [down_total[:, : width // 2], down_total[:, width // 2 :]], axis=0
        )
        q = sum_over_ctx(late_first + swap(late_second, "fsdp", 2, 1).astype(F32), c)
        late = jnp.concatenate(q, axis=0).astype(F32)
        small = jnp.concatenate([late[4 * local : 4 * local + 8], late[4 * local + 8 :][:8]], axis=1)
    else:
        q = sum_over_ctx(scatter_any(ff_first, 0), c)
        up_total = jnp.concatenate(q, axis=0).astype(F32)
        q = sum_over_ctx(scatter_any(ff_second, 1), c)
        down_total = jnp.concatenate(q, axis=0).astype(F32)
        q = sum_over_ctx(scatter_any(late_first, 1), c)
        late = jnp.concatenate(q, axis=0).astype(F32)
        small = butterfly(butterfly(late_second, "fsdp", fsdp), "ctx", 4)
    mix_total = late[: 3 * local].reshape(3, local, -1).transpose(2, 0, 1)
    out_total = late[3 * local : 4 * local]
    norm_small = butterfly(small, "tp", 4)
    bias_total = norm_small[5] * 0.25
    return (
        block_out,
        inputs_grad,
        mix_total,
        small[6, : 3 * local].reshape(3, local),
        out_total,
        bias_total,
        up_total,
        small[4, :hidden],
        down_total,
        bias_total,
        norm_small[0],
        norm_small[1],
        norm_small[2],
        norm_small[3],
    )


def solution(mesh):
    in_specs = (
        P("fsdp", "ctx", None),
        P("fsdp", None),
        P("fsdp", None, "tp"),
        P(None, "tp"),
        P("tp", "fsdp"),
        P(),
        P("fsdp", "tp"),
        P("tp"),
        P("tp", "fsdp"),
        P(),
        P(),
        P(),
        P(),
        P(),
        P("fsdp", "ctx", None),
    )
    out_specs = (
        P("fsdp", "ctx", None),
        P("fsdp", "ctx", None),
        P("fsdp", None, "tp"),
        P(None, "tp"),
        P("tp", "fsdp"),
        P(),
        P("fsdp", "tp"),
        P("tp"),
        P("tp", "fsdp"),
        P(),
        P(),
        P(),
        P(),
        P(),
    )
    body = functools.partial(shards, dict(mesh.shape))
    return jax.shard_map(body, mesh=mesh, in_specs=in_specs, out_specs=out_specs, check_vma=False)
```

```python
import functools

import jax
import jax.numpy as jnp
from jax import lax
from jax.experimental import pallas as pl
from jax.experimental.pallas import tpu as pltpu
from jax.sharding import PartitionSpec as P

HEAD = 64
ROT = 16
HALF = ROT // 2
EPS = 1e-5
NEG = -1e30
STEP = 256
F32 = jnp.float32
BF16 = jnp.bfloat16
MIB = 1024 * 1024


def mm(a, b, ca=1, cb=0):
    return lax.dot_general(a, b, (((ca,), (cb,)), ((), ())), preferred_element_type=F32)


def params(mib):
    return pltpu.CompilerParams(vmem_limit_bytes=mib * MIB)


def cost(flops, moved, exps=0):
    return pl.CostEstimate(flops=int(flops), bytes_accessed=int(moved), transcendentals=int(exps))


def xhat_of(x):
    width = x.shape[-1]
    centred = x - jnp.sum(x, axis=-1, keepdims=True) * (1.0 / width)
    spread = jnp.sum(centred * centred, axis=-1, keepdims=True) * (1.0 / width)
    inv = lax.rsqrt(spread + EPS)
    return centred * inv, inv


def row_of(ref):
    return ref[...].reshape(1, -1)


def shape(*dims):
    return jax.ShapeDtypeStruct(dims, F32)


def low_shape(*dims):
    return jax.ShapeDtypeStruct(dims, BF16)


def norm_own_kernel(at, xa, xb, ga, gb, fz, fx, fc, ta, tb, s1, b1, s2, b2,
                    n1_ref, n2_ref, xhat_ref, g_ref, trig_ref, x):
    i = pl.program_id(0)
    q = xa.shape[1]

    @pl.when(i < 2)
    def _():
        x[:q, :] = xa[0]
        x[q:, :] = xb[0]
        g_ref[:q, :] = ga[0]
        g_ref[q:, :] = gb[0]

    @pl.when(i == 2)
    def _():
        x[:q, :] = fz[0]
        x[q:, :] = fx[0]
        g_ref[:q, :] = fz[1]
        g_ref[q:, :] = fx[1]

    @pl.when(i == 3)
    def _():
        x[:q, :] = fc[0, 0]
        x[q:, :] = fc[1, 0]
        g_ref[:q, :] = fc[0, 1]
        g_ref[q:, :] = fc[1, 1]

    trig_ref[:, :q] = ta[0]
    trig_ref[:, q:] = tb[0]
    xhat, _ = xhat_of(x[...].astype(F32))
    xhat_ref[...] = xhat.astype(BF16)
    n1_ref[...] = (xhat * row_of(s1) + row_of(b1)).astype(BF16)
    n2_ref[...] = (xhat * row_of(s2) + row_of(b2)).astype(BF16)


def norm_other_kernel(at, nz, nx, nc, ta, tb, s1, b1, n1_ref, xhat_ref, trig_ref, x):
    i = pl.program_id(0)
    q = nz.shape[1]
    b = i // 2

    @pl.when(i % 2 == 0)
    def _():
        x[:q, :] = nz[b]
        x[q:, :] = nx[b]

    @pl.when(i % 2 == 1)
    def _():
        x[:q, :] = nc[0, b]
        x[q:, :] = nc[1, b]

    trig_ref[:, :q] = ta[0]
    trig_ref[:, q:] = tb[0]
    xhat, _ = xhat_of(x[...].astype(F32))
    xhat_ref[...] = xhat.astype(BF16)
    n1_ref[...] = (xhat * row_of(s1) + row_of(b1)).astype(BF16)


def norms(at, own, arrays, trig, vectors):
    width = vectors[0].shape[0]
    rows, q = 4 * STEP, STEP // 2
    tall = trig.shape[1]
    first = 0 if own else 1

    def pick(high):
        def place(i, at):
            block = at[1] ^ (first + 2 * (i // 2))
            return (at[0], 0, block * 4 + (at[2] ^ (i % 2 + high)))

        return pl.BlockSpec((1, tall, q), place)

    def piece(high):
        return pl.BlockSpec(
            (1, q, width), lambda i, at: (at[0], at[2] ^ (jnp.minimum(i, 1) + high), 0)
        )

    def whole(v):
        return pl.BlockSpec(v.shape, lambda i, at: (0,) * v.ndim)

    row = pl.BlockSpec((STEP, width), lambda i, at: (i, 0))
    out_trig = pl.BlockSpec((tall, STEP), lambda i, at: (0, i))
    if own:
        x, g, received = arrays[0], arrays[1], arrays[2:]
        specs = [piece(0), piece(2), piece(0), piece(2)]
        operands = [x, x, g, g]
        kernel, count = norm_own_kernel, 4
    else:
        received, specs, operands = arrays, [], []
        kernel, count = norm_other_kernel, 2
    specs += [whole(v) for v in received] + [pick(0), pick(2)] + [whole(v) for v in vectors]
    operands += [*received, trig, trig, *vectors]
    return pl.pallas_call(
        kernel,
        grid_spec=pltpu.PrefetchScalarGridSpec(
            num_scalar_prefetch=1,
            grid=(rows // STEP,),
            in_specs=specs,
            out_specs=[row] * count + [out_trig],
            scratch_shapes=[pltpu.VMEM((STEP, width), BF16)],
        ),
        out_shape=[low_shape(rows, width)] * count + [shape(tall, rows)],
        compiler_params=params(24),
        cost_estimate=cost(0, 6 * rows * width),
    )(at, *operands)


def project_kernel(n1o, n1x, to, tx, g_ref, w_ref, b_ref, k_ref, v_ref, q_ref, do_ref, bias):
    i = pl.program_id(0)
    wide = k_ref.shape[0]

    @pl.when(i == 0)
    def _():
        for j in range(3):
            line = jnp.broadcast_to(b_ref[j : j + 1, :], (8, wide))
            bias[j * wide : (j + 1) * wide, :] = line.T[:, 0:1]

    def rotated(ref, mixed, trig, factor):
        cosine, sine = trig[:HALF], trig[HALF:ROT]
        for h in range(0, wide, HEAD):
            a, b = mixed[h : h + HALF], mixed[h + HALF : h + ROT]
            turned = jnp.concatenate([a * cosine - b * sine, b * cosine + a * sine], axis=0)
            ref[h : h + ROT, :] = turned.astype(BF16) * factor
            ref[h + ROT : h + HEAD, :] = mixed[h + ROT : h + HEAD].astype(BF16) * factor

    def keys_values(mixed, trig):
        rotated(k_ref, mixed[:wide], trig, BF16(1.0))
        v_ref[...] = mixed[wide:].astype(BF16)

    @pl.when(i < 4)
    def _():
        trig = to[...]
        mixed = mm(w_ref[: 3 * wide, :], n1o[...], 1, 1) + bias[...]
        rotated(q_ref, mixed[:wide], trig, BF16(HEAD**-0.5))
        keys_values(mixed[wide:], trig)
        do_ref[...] = mm(w_ref[3 * wide :, :], g_ref[...], 1, 1).astype(BF16)

    @pl.when(i >= 4)
    def _():
        mixed = mm(w_ref[wide : 3 * wide, :], n1x[...], 1, 1) + bias[wide:, :]
        keys_values(mixed, tx[...])


def project(n1_own, n1_other, trig_own, trig_other, g, weights, bias):
    rows, width = n1_own.shape
    wide = bias.shape[1]
    tall = trig_own.shape[0]

    def own(i):
        return jnp.minimum(i, 3)

    def other(i):
        return jnp.maximum(i - 4, 0)

    col = pl.BlockSpec((wide, STEP), lambda i: (0, i))
    own_col = pl.BlockSpec((wide, STEP), lambda i: (0, own(i)))
    return pl.pallas_call(
        project_kernel,
        grid=(8,),
        in_specs=[
            pl.BlockSpec((STEP, width), lambda i: (own(i), 0)),
            pl.BlockSpec((STEP, width), lambda i: (other(i), 0)),
            pl.BlockSpec((tall, STEP), lambda i: (0, own(i))),
            pl.BlockSpec((tall, STEP), lambda i: (0, other(i))),
            pl.BlockSpec((STEP, width), lambda i: (own(i), 0)),
            pl.BlockSpec((4 * wide, width), lambda i: (0, 0)),
            pl.BlockSpec((3, wide), lambda i: (0, 0)),
        ],
        out_specs=[col, col, own_col, own_col],
        out_shape=[low_shape(wide, 2 * rows)] * 2 + [low_shape(wide, rows)] * 2,
        scratch_shapes=[pltpu.VMEM((3 * wide, 1), F32)],
        compiler_params=params(24),
        cost_estimate=cost(12 * rows * width * wide, 12 * rows * width),
    )(n1_own, n1_other, trig_own, trig_other, g, weights, bias)


def attention_kernel(after, q_ref, do_ref, k_ref, v_ref, tq_ref, to_ref, tx_ref,
                     o_ref, dq_ref, dk_ref, dv_ref, kn, vn, kp, dk, dv, es, dps):
    i = pl.program_id(0)
    length = k_ref.shape[1]
    half = length // 2
    chunk = STEP
    steps = length // chunk

    @pl.when(i == 0)
    def _():
        kn[...] = k_ref[...].T
        vn[...] = v_ref[...].T
        kp[:half, :] = to_ref[ROT:, :].T[:, 0:1]
        kp[half:, :] = tx_ref[ROT:, :].T[:, 0:1]
        dk[...] = jnp.zeros_like(dk)
        dv[...] = jnp.zeros_like(dv)

    qt = q_ref[...]
    dot = do_ref[...]
    qn = qt.T
    don = dot.T
    qpos = tq_ref[ROT : ROT + 1, :]
    lanes = qt.shape[1]
    fold = (chunk // 8, 8, lanes)

    top = jnp.full((8, lanes), NEG, F32)
    for j in range(steps):
        here = slice(j * chunk, (j + 1) * chunk)
        s = mm(kn[here, :], qt)
        s = jnp.where(kp[here, :] <= qpos, s, NEG)
        es[here, :] = s
        top = jnp.maximum(top, jnp.max(s.reshape(fold), axis=0))
    top = jnp.max(top, axis=0, keepdims=True)

    total = jnp.zeros((8, lanes), F32)
    inner = jnp.zeros((8, lanes), F32)
    for j in range(steps):
        here = slice(j * chunk, (j + 1) * chunk)
        e = jnp.exp(es[here, :] - top)
        dp = mm(vn[here, :], dot)
        es[here, :] = e
        dps[here, :] = dp
        total = total + jnp.sum(e.reshape(fold), axis=0)
        inner = inner + jnp.sum((e * dp).reshape(fold), axis=0)
    share = 1.0 / jnp.sum(total, axis=0, keepdims=True)
    inner = jnp.sum(inner, axis=0, keepdims=True) * share

    ot = jnp.zeros((HEAD, lanes), F32)
    dqt = jnp.zeros((HEAD, lanes), F32)
    for j in range(steps):
        here = slice(j * chunk, (j + 1) * chunk)
        p = es[here, :] * share
        ds = (p * (dps[here, :] - inner)).astype(BF16)
        p = p.astype(BF16)
        dv[here, :] += mm(p, don)
        dk[here, :] += mm(ds, qn)
        ot = ot + mm(v_ref[:, here], p)
        dqt = dqt + mm(k_ref[:, here], ds)
    o_ref[...] = ot.astype(BF16)

    def unrotated(grad, trig):
        cosine, sine = trig[:HALF], trig[HALF:ROT]
        a, b = grad[:HALF], grad[HALF:ROT]
        turned = jnp.concatenate([a * cosine + b * sine, b * cosine - a * sine], axis=0)
        return turned.astype(BF16), grad[ROT:].astype(BF16)

    dq_ref[:ROT, :], dq_ref[ROT:, :] = unrotated(dqt * (HEAD**-0.5), tq_ref[...])

    @pl.when(i == pl.num_programs(0) - 1)
    def _():
        grad = dk[...].T
        dk_ref[:ROT, :half], dk_ref[ROT:, :half] = unrotated(grad[:, :half], to_ref[...])
        dk_ref[:ROT, half:], dk_ref[ROT:, half:] = unrotated(grad[:, half:], tx_ref[...])
        dv_ref[...] = dv[...].T.astype(BF16)


def attention(h, after, qt, dot, kt, vt, trig_own, trig_other):
    rows, length = qt.shape[1], kt.shape[1]
    lanes = STEP
    tall = trig_own.shape[0]
    q_spec = pl.BlockSpec((HEAD, lanes), lambda i: (h, i))
    k_spec = pl.BlockSpec((HEAD, length), lambda i: (h, 0))
    trig_spec = pl.BlockSpec((tall, rows), lambda i: (0, 0))
    return pl.pallas_call(
        attention_kernel,
        grid=(rows // lanes,),
        in_specs=[pl.BlockSpec(memory_space=pl.ANY), q_spec, q_spec, k_spec, k_spec,
                  pl.BlockSpec((tall, lanes), lambda i: (0, i)), trig_spec, trig_spec],
        out_specs=[pl.BlockSpec((HEAD, lanes), lambda i: (0, i))] * 2
        + [pl.BlockSpec((HEAD, length), lambda i: (0, 0))] * 2,
        out_shape=[low_shape(HEAD, rows)] * 2 + [low_shape(HEAD, length)] * 2,
        scratch_shapes=[
            pltpu.VMEM((length, HEAD), BF16),
            pltpu.VMEM((length, HEAD), BF16),
            pltpu.VMEM((length, 1), F32),
            pltpu.VMEM((length, HEAD), F32),
            pltpu.VMEM((length, HEAD), F32),
            pltpu.VMEM((length, lanes), F32),
            pltpu.VMEM((length, lanes), F32),
        ],
        compiler_params=params(32),
        cost_estimate=cost(40 * rows * length * HEAD, 16 * HEAD * length, rows * length),
    )(after, qt, dot, kt, vt, trig_own, trig_own, trig_other)


def forward_kernel(split, at, n2_ref, g_ref, xhat_ref, up_ref, bias_ref, down_ref, s2_ref,
                   ff_ref, a_ref, small_ref, first_ref, second_ref, *scratch):
    i = pl.program_id(0)
    up_part, down_part = scratch if split else (first_ref, second_ref)

    @pl.when(i == 0)
    def _():
        up_part[...] = jnp.zeros_like(up_part)
        down_part[...] = jnp.zeros_like(down_part)
        small_ref[...] = jnp.zeros_like(small_ref)

    n2, g = n2_ref[...], g_ref[...]
    up = mm(n2, up_ref[...]) + row_of(bias_ref)
    cdf = 0.5 + 0.5 * lax.erf(up * (0.5**0.5))
    act = (up * cdf).astype(BF16)
    slope = cdf + up * (jnp.exp(up * up * -0.5) * 0.3989422804014327)
    up_grad = (mm(g, down_ref[...], 1, 1) * slope).astype(BF16)
    ff_ref[...] = mm(act, down_ref[...]).astype(BF16)
    second = mm(up_grad, up_ref[...], 1, 1)
    up_part[...] += mm(n2, up_grad, 0, 0)
    down_part[...] += mm(act, g, 0, 0)
    a_ref[...] = (second * row_of(s2_ref)).astype(BF16)
    small_ref[0:1, :] += jnp.sum(up_grad.astype(F32), axis=0, keepdims=True)
    small_ref[1:2, :] += jnp.sum(g.astype(F32), axis=0, keepdims=True)
    small_ref[2:3, :] += jnp.sum(second * xhat_ref[...].astype(F32), axis=0, keepdims=True)
    small_ref[3:4, :] += jnp.sum(second, axis=0, keepdims=True)

    if split:
        half = up_part.shape[0] // 2

        @pl.when(i == pl.num_programs(0) - 1)
        def _():
            for ref, f in ((first_ref, at[3]), (second_ref, 1 - at[3])):
                piece = pl.ds(pl.multiple_of(f * half, 128), half)
                ref[:half, :] = up_part[piece, :].astype(ref.dtype)
                ref[half:, :half] = down_part[:half, piece].astype(ref.dtype)
                ref[half:, half:] = down_part[half:, piece].astype(ref.dtype)


def feed_forward(split, at, n2, g, xhat, up, bias, down, scale):
    rows, width = n2.shape
    hidden = up.shape[1]
    row = pl.BlockSpec((STEP, width), lambda i, at: (i, 0))

    def whole(*dims):
        return pl.BlockSpec(dims, lambda i, at: (0,) * len(dims))

    if split:
        assert width == hidden
        parts = [shape(width, hidden), low_shape(width, hidden)]
    else:
        parts = [shape(width, hidden), shape(hidden, width)]
    return pl.pallas_call(
        functools.partial(forward_kernel, split),
        grid_spec=pltpu.PrefetchScalarGridSpec(
            num_scalar_prefetch=1,
            grid=(rows // STEP,),
            in_specs=[row, row, row, whole(width, hidden), whole(hidden), whole(hidden, width),
                      whole(width)],
            out_specs=[row, row, whole(8, width)] + [whole(*p.shape) for p in parts],
            scratch_shapes=[pltpu.VMEM((width, hidden), F32), pltpu.VMEM((hidden, width), F32)]
            if split
            else [],
        ),
        out_shape=[low_shape(rows, width)] * 2 + [shape(8, width)] + parts,
        compiler_params=params(40),
        cost_estimate=cost(12 * rows * width * hidden, 16 * MIB, 2 * rows * hidden),
    )(at, n2, g, xhat, up, bias, down, scale)


def emit(keep_ref, send_ref, v):
    i = pl.program_id(0)

    @pl.when(i % 2 == 0)
    def _():
        keep_ref[0] = v.astype(BF16)

    @pl.when(i % 2 == 1)
    def _():
        send_ref[0] = v.astype(BF16)


def branch_kernel(heads, *refs):
    o = refs[:heads]
    g_ref, ff_ref, w_ref, keep_ref, send_ref, out = refs[heads:]
    wide = heads * HEAD

    @pl.when(pl.program_id(0) == 0)
    def _():
        out[...] = jnp.zeros_like(out)

    ot = jnp.concatenate([r[...] for r in o], axis=0)
    emit(keep_ref, send_ref, mm(ot, w_ref[...], 0, 0) + ff_ref[...].astype(F32))
    out[...] += mm(ot, g_ref[...])


def branch(o, g, ff, weights):
    rows, width = g.shape
    heads = len(o)
    wide = heads * HEAD
    row = pl.BlockSpec((STEP, width), lambda i: (i, 0))
    slots = pl.BlockSpec((1, STEP, width), lambda i: (i // 2, 0, 0))
    return pl.pallas_call(
        functools.partial(branch_kernel, heads),
        grid=(rows // STEP,),
        in_specs=[pl.BlockSpec((HEAD, STEP), lambda i: (0, i))] * heads
        + [row, row, pl.BlockSpec((wide, width), lambda i: (3, 0))],
        out_specs=[slots, slots, pl.BlockSpec((wide, width), lambda i: (0, 0))],
        out_shape=[low_shape(2, STEP, width)] * 2 + [shape(wide, width)],
        compiler_params=params(24),
        cost_estimate=cost(4 * rows * width * wide, 8 * MIB),
    )(*o, g, ff, weights)


def back_kernel(own, split, heads, at, *refs):
    count = 3 if own else 2
    grads, refs = refs[: count * heads], refs[count * heads :]
    n1_ref, xhat_ref, w_ref, s1_ref, *refs = refs
    if own:
        (a2_ref, small_ff, small_other, mix_other, out_part, after,
         keep_ref, send_ref, first_ref, second_ref, mix, small) = refs
    else:
        keep_ref, send_ref, mix, small = refs
    i = pl.program_id(0)
    wide = heads * HEAD
    tall = mix.shape[0]

    @pl.when(i == 0)
    def _():
        if own:
            mix[:wide, :] = jnp.zeros((wide, mix.shape[1]), F32)
            mix[wide:, :] = mix_other[...]
            small[...] = small_other[...]
        else:
            mix[...] = jnp.zeros_like(mix)
            small[...] = jnp.zeros_like(small)

    grad = jnp.concatenate([r[...] for r in grads], axis=0)
    first = mm(grad, w_ref[3 * wide - tall : 3 * wide, :], 0, 0)
    a = first * row_of(s1_ref)
    emit(keep_ref, send_ref, a + a2_ref[...].astype(F32) if own else a)
    mix[...] += mm(grad, n1_ref[...])
    small[0:1, :] += jnp.sum(first * xhat_ref[...].astype(F32), axis=0, keepdims=True)
    small[1:2, :] += jnp.sum(first, axis=0, keepdims=True)
    ones = jnp.ones((8, grad.shape[1]), BF16)
    small[6:7, 3 * wide - tall : 3 * wide] += mm(ones, grad, 1, 1)[0:1]

    if own:
        @pl.when(i == pl.num_programs(0) - 1)
        def _():
            small[2:4, :] = small_ff[2:4, :]
            small[4:6, :] = small_ff[0:2, :]
            if split:
                half = mix.shape[1] // 2
                vectors = small[...].astype(BF16)
                for ref, f in ((first_ref, at[3]), (second_ref, 1 - at[3])):
                    piece = pl.ds(pl.multiple_of(f * half, 128), half)
                    ref[: 3 * wide, :] = mix[:, piece].astype(ref.dtype)
                    ref[3 * wide : 4 * wide, :] = out_part[:, piece].astype(ref.dtype)
                    both = jnp.concatenate([vectors[:, :half], vectors[:, half:]], axis=0)
                    ref[4 * wide : 4 * wide + 16, :] = both.astype(ref.dtype)
                    ref[4 * wide + 16 :, :] = jnp.zeros((48, half), ref.dtype)
            else:
                first_ref[: 3 * wide, :] = mix[...]
                first_ref[3 * wide :, :] = out_part[...]
                second_ref[...] = small[...]


def back(own, split, at, grads, n1, xhat, weights, scale, extra):
    rows, width = n1.shape
    heads = len(grads[0])
    wide = heads * HEAD
    tall = 3 * wide if own else 2 * wide
    offset = 0 if own else rows // STEP
    row = pl.BlockSpec((STEP, width), lambda i, at: (i, 0))
    col = pl.BlockSpec((HEAD, STEP), lambda i, at: (0, i + offset))
    slots = pl.BlockSpec((1, STEP, width), lambda i, at: (i // 2, 0, 0))

    def whole(*dims):
        return pl.BlockSpec(dims, lambda i, at: (0,) * len(dims))

    half = width // 2
    specs = [col] * (len(grads) * heads) + [row, row, whole(4 * wide, width), whole(width)]
    if not own:
        parts = [shape(tall, width), shape(8, width)]
        scratch = []
    else:
        specs += [row, whole(8, width), whole(8, width), whole(2 * wide, width),
                  whole(wide, width), pl.BlockSpec(memory_space=pl.ANY)]
        scratch = [pltpu.VMEM((tall, width), F32), pltpu.VMEM((8, width), F32)]
        if split:
            parts = [shape(4 * wide + 64, half), low_shape(4 * wide + 64, half)]
        else:
            parts = [shape(4 * wide, width), shape(8, width)]
    return pl.pallas_call(
        functools.partial(back_kernel, own, split, heads),
        grid_spec=pltpu.PrefetchScalarGridSpec(
            num_scalar_prefetch=1,
            grid=(rows // STEP,),
            in_specs=specs,
            out_specs=[slots, slots] + [whole(*p.shape) for p in parts],
            scratch_shapes=scratch,
        ),
        out_shape=[low_shape(2, STEP, width)] * 2 + parts,
        compiler_params=params(32),
        cost_estimate=cost(4 * rows * width * tall, 10 * MIB),
    )(at, *[v for vs in grads for v in vs], n1, xhat, weights, scale, *extra)


def swap(v, axis, size, distance):
    return lax.ppermute(v, axis, [(i, i ^ distance) for i in range(size)])


def by_xor(pieces, index):
    low, high = (index & 1) == 1, (index & 2) == 2
    a, b, c, d = pieces
    a, b, c, d = (jnp.where(low, b, a), jnp.where(low, a, b),
                  jnp.where(low, d, c), jnp.where(low, c, d))
    return (jnp.where(high, c, a), jnp.where(high, d, b),
            jnp.where(high, a, c), jnp.where(high, b, d))


def tie(v, *earlier):
    return lax.optimization_barrier((v, *earlier))[0]


def gather_halves(shard, size, mine, dim, *earlier):
    if size != 2:
        return lax.all_gather(shard, "fsdp", axis=dim, tiled=True)
    other = swap(shard, "fsdp", 2, 1)
    if earlier:
        other = tie(other, *earlier)
    first = mine == 0
    return jnp.concatenate(
        [jnp.where(first, shard, other), jnp.where(first, other, shard)], axis=dim
    )


def scatter_any(part, dim):
    return lax.psum_scatter(
        part.astype(BF16), "fsdp", scatter_dimension=dim, tiled=True
    ).astype(F32)


def halve(v, distance, bit):
    rows = v.shape[0] // 2
    keep = lax.dynamic_slice_in_dim(v, bit * rows, rows, 0)
    send = lax.dynamic_slice_in_dim(v, (1 - bit) * rows, rows, 0).astype(BF16)
    return keep + swap(send, "ctx", 4, distance).astype(F32)


def double(v, c):
    v = v.astype(BF16)
    pair = jnp.stack([v, swap(v, "ctx", 4, 2)])
    others = swap(pair, "ctx", 4, 1)
    return by_xor([pair[0], pair[1], others[0], others[1]], 2 * (c % 2) + c // 2)


def sum_over_ctx(v, c):
    return double(halve(halve(v, 1, c % 2), 2, c // 2), c)


def butterfly(v, axis_name, size):
    distance = 1
    while distance < size:
        v = v + swap(v, axis_name, size, distance)
        distance *= 2
    return v


def shards(
    sizes,
    inputs,
    positions,
    query_key_value_weight,
    query_key_value_bias,
    attention_output_weight,
    attention_output_bias,
    up_projection_weight,
    up_projection_bias,
    down_projection_weight,
    down_projection_bias,
    first_scale,
    first_shift,
    second_scale,
    second_shift,
    cotangent,
):
    fsdp = sizes["fsdp"]
    split = fsdp == 2
    seq_count, block, width = inputs.shape
    assert seq_count == 2 and sizes["ctx"] == 4 and sizes["tp"] == 4 and block == 2 * STEP
    length = positions.shape[1]
    local = query_key_value_weight.shape[2]
    heads = local // HEAD
    hidden = up_projection_weight.shape[1]
    quarter = block // 4
    f = lax.axis_index("fsdp")
    c = lax.axis_index("ctx")
    t = lax.axis_index("tp")
    s = c // 2
    at = jnp.stack([s, c, t, f]).astype(jnp.int32)

    def my_quarter(v, seq):
        return lax.dynamic_slice(v, (seq, t * quarter, 0), (1, quarter, width))

    x_mine, x_theirs = my_quarter(inputs, s), my_quarter(inputs, 1 - s)
    g_theirs = my_quarter(cotangent, 1 - s)
    far_z = swap(jnp.concatenate([x_theirs, g_theirs], axis=0), "ctx", 4, 2)
    cross = swap(x_theirs, "ctx", 4, 3)
    near = swap(x_mine, "ctx", 4, 1)

    def over_tp(v):
        v_x = swap(v, "tp", 4, 2)
        return v, v_x, swap(jnp.stack([v, v_x]), "tp", 4, 1)

    far = over_tp(far_z)
    others = over_tp(jnp.concatenate([near, cross], axis=0))

    wup = gather_halves(up_projection_weight, fsdp, f, 0)
    wdown = gather_halves(down_projection_weight, fsdp, f, 1)
    mix_shard = query_key_value_weight.transpose(1, 2, 0).reshape(3 * local, -1)
    mix_out_shard = jnp.concatenate([mix_shard, attention_output_weight], axis=0)

    inverse = 10000.0 ** (-2.0 * jnp.arange(HALF, dtype=F32) / ROT)
    places = positions.astype(F32)[:, None, :]
    angles = inverse[None, :, None] * places
    trig = jnp.concatenate(
        [jnp.cos(angles), jnp.sin(angles), jnp.broadcast_to(places, angles.shape)], axis=1
    )

    n1_own, n2, xhat_own, g, trig_own = norms(
        at, True, (inputs, cotangent, *far), trig,
        (first_scale, first_shift, second_scale, second_shift),
    )
    ff, a2, small_ff, ff_first, ff_second = feed_forward(
        split, at, n2, g, xhat_own, wup, up_projection_bias, wdown, second_scale
    )
    weights = gather_halves(mix_out_shard, fsdp, f, 1, small_ff)
    n1_other, xhat_other, trig_other = norms(
        at, False, (others[0], others[1], tie(others[2], small_ff)), trig,
        (first_scale, first_shift),
    )
    kt, vt, qt, dot = project(
        n1_own, n1_other, trig_own, trig_other, g, weights, query_key_value_bias
    )
    if split:
        ff_rest = ff_first + swap(ff_second, "fsdp", 2, 1).astype(F32)
    else:
        ff_rest = small_ff
    per_head = []
    for h in range(heads):
        after = ff_rest if h == heads - 1 else small_ff
        per_head.append(attention(h, after, qt, dot, kt, vt, trig_own, trig_other))
    o, dq, dk, dv = zip(*per_head)
    keep_b, send_b, out_part = branch(o, g, ff, weights)
    if split:
        ff_half = halve(ff_rest, 1, c % 2)
    else:
        ff_half = small_ff
    keep_o, send_o, mix_other, small_other = back(
        False, split, at, (dk, dv), n1_other, xhat_other, weights, first_scale, ()
    )
    keep_w, send_w, late_first, late_second = back(
        True, split, at, (dq, dk, dv), n1_own, xhat_own, weights, first_scale,
        (a2, small_ff, small_other, mix_other, out_part, ff_half),
    )

    def scatter_tp(keep, send):
        v = keep.astype(F32) + swap(send, "tp", 4, 1).astype(F32)
        v = v.reshape(2, 2, quarter, width)
        return v[:, 0] + swap(v[:, 1].astype(BF16), "tp", 4, 2).astype(F32)

    def over_ctx(v, distance):
        return swap(v.astype(BF16), "ctx", 4, distance).astype(F32)

    def gather_tp(mine, theirs):
        ours = jnp.stack([mine, theirs]).astype(BF16)
        pair = jnp.stack([ours, swap(ours, "tp", 4, 2)])
        core = swap(pair, "tp", 4, 1)
        pieces = by_xor((pair[0], core[0], pair[1], core[1]), t)
        pieces = jnp.concatenate(pieces, axis=1)
        return jnp.stack([jnp.where(s == 0, pieces[0], pieces[1]),
                          jnp.where(s == 0, pieces[1], pieces[0])]).astype(F32)

    sums_b = scatter_tp(keep_b, send_b)
    block_out = gather_tp(sums_b[0], over_ctx(sums_b[1], 2))
    block_out = (
        inputs.astype(F32) + block_out + (attention_output_bias + down_projection_bias)
    )

    sums_o = scatter_tp(keep_o, send_o)
    sums_w = scatter_tp(keep_w, send_w)
    a = jnp.stack([
        sums_w[0] + over_ctx(sums_o[0], 1),
        over_ctx(sums_w[1], 2) + over_ctx(sums_o[1], 3),
    ])
    xhat, inv = xhat_of(jnp.concatenate([x_mine, x_theirs], axis=0).astype(F32))
    norm_grad = inv * (
        a
        - jnp.mean(a, axis=-1, keepdims=True)
        - xhat * jnp.mean(a * xhat, axis=-1, keepdims=True)
    )
    inputs_grad = cotangent.astype(F32) + gather_tp(norm_grad[0], norm_grad[1])

    if split:
        q = double(halve(ff_half, 2, c // 2), c)
        up_total = jnp.concatenate(q[:2], axis=0).astype(F32)
        down_total = jnp.concatenate(q[2:], axis=0).astype(F32)
        down_total = jnp.concatenate(
            [down_total[:, : width // 2], down_total[:, width // 2 :]], axis=0
        )
        late = late_first + swap(late_second, "fsdp", 2, 1).astype(F32)
        late = jnp.concatenate(sum_over_ctx(late, c), axis=0).astype(F32)
        small = jnp.concatenate([late[4 * local : 4 * local + 8], late[4 * local + 8 :][:8]], axis=1)
    else:
        q = sum_over_ctx(scatter_any(ff_first, 0), c)
        up_total = jnp.concatenate(q, axis=0).astype(F32)
        q = sum_over_ctx(scatter_any(ff_second, 1), c)
        down_total = jnp.concatenate(q, axis=0).astype(F32)
        q = sum_over_ctx(scatter_any(late_first, 1), c)
        late = jnp.concatenate(q, axis=0).astype(F32)
        small = butterfly(butterfly(late_second, "fsdp", fsdp), "ctx", 4)
    mix_total = late[: 3 * local].reshape(3, local, -1).transpose(2, 0, 1)
    out_total = late[3 * local : 4 * local]
    norm_small = butterfly(small, "tp", 4)
    bias_total = norm_small[5] * 0.25
    return (
        block_out,
        inputs_grad,
        mix_total,
        small[6, : 3 * local].reshape(3, local),
        out_total,
        bias_total,
        up_total,
        small[4, :hidden],
        down_total,
        bias_total,
        norm_small[0],
        norm_small[1],
        norm_small[2],
        norm_small[3],
    )


def solution(mesh):
    in_specs = (
        P("fsdp", "ctx", None),
        P("fsdp", None),
        P("fsdp", None, "tp"),
        P(None, "tp"),
        P("tp", "fsdp"),
        P(),
        P("fsdp", "tp"),
        P("tp"),
        P("tp", "fsdp"),
        P(),
        P(),
        P(),
        P(),
        P(),
        P("fsdp", "ctx", None),
    )
    out_specs = (
        P("fsdp", "ctx", None),
        P("fsdp", "ctx", None),
        P("fsdp", None, "tp"),
        P(None, "tp"),
        P("tp", "fsdp"),
        P(),
        P("fsdp", "tp"),
        P("tp"),
        P("tp", "fsdp"),
        P(),
        P(),
        P(),
        P(),
        P(),
    )
    body = functools.partial(shards, dict(mesh.shape))
    return jax.shard_map(body, mesh=mesh, in_specs=in_specs, out_specs=out_specs, check_vma=False)
```

```python
import functools

import jax
import jax.numpy as jnp
from jax import lax
from jax.experimental import pallas as pl
from jax.experimental.pallas import tpu as pltpu
from jax.sharding import PartitionSpec as P

HEAD = 64
ROT = 16
HALF = ROT // 2
EPS = 1e-5
NEG = -1e30
STEP = 256
F32 = jnp.float32
BF16 = jnp.bfloat16
MIB = 1024 * 1024


def mm(a, b, ca=1, cb=0):
    return lax.dot_general(a, b, (((ca,), (cb,)), ((), ())), preferred_element_type=F32)


def params(mib):
    return pltpu.CompilerParams(vmem_limit_bytes=mib * MIB)


def cost(flops, moved, exps=0):
    return pl.CostEstimate(flops=int(flops), bytes_accessed=int(moved), transcendentals=int(exps))


def xhat_of(x):
    width = x.shape[-1]
    centred = x - jnp.sum(x, axis=-1, keepdims=True) * (1.0 / width)
    spread = jnp.sum(centred * centred, axis=-1, keepdims=True) * (1.0 / width)
    inv = lax.rsqrt(spread + EPS)
    return centred * inv, inv


def row_of(ref):
    return ref[...].reshape(1, -1)


def shape(*dims):
    return jax.ShapeDtypeStruct(dims, F32)


def low_shape(*dims):
    return jax.ShapeDtypeStruct(dims, BF16)


def two_quarters(width, seq_of):
    def piece(high):
        return pl.BlockSpec(
            (1, STEP // 2, width), lambda i, at: (seq_of(i, at), at[2] ^ (i % 2 + high), 0)
        )

    return [piece(0), piece(2)]


def project_kernel(at, xa, xb, ga, gb, fz, fx, fc, nz, nx, nc, ta, tb, w_ref, b_ref, s1, b1,
                   n1_ref, xhat_ref, g_ref, trig_ref, k_ref, v_ref, q_ref, do_ref, x, bias):
    i = pl.program_id(0)
    wide = k_ref.shape[0]
    q = STEP // 2
    b = jnp.maximum(i // 2 - 2, 0)

    @pl.when(i == 0)
    def _():
        for j in range(3):
            line = jnp.broadcast_to(b_ref[j : j + 1, :], (8, wide))
            bias[j * wide : (j + 1) * wide, :] = line.T[:, 0:1]

    @pl.when(i < 2)
    def _():
        x[:q, :] = xa[0]
        x[q:, :] = xb[0]
        g_ref[:q, :] = ga[0]
        g_ref[q:, :] = gb[0]

    @pl.when(i == 2)
    def _():
        x[:q, :] = fz[0]
        x[q:, :] = fx[0]
        g_ref[:q, :] = fz[1]
        g_ref[q:, :] = fx[1]

    @pl.when(i == 3)
    def _():
        x[:q, :] = fc[0, 0]
        x[q:, :] = fc[1, 0]
        g_ref[:q, :] = fc[0, 1]
        g_ref[q:, :] = fc[1, 1]

    @pl.when((i >= 4) & (i % 2 == 0))
    def _():
        x[:q, :] = nz[b]
        x[q:, :] = nx[b]

    @pl.when((i >= 4) & (i % 2 == 1))
    def _():
        x[:q, :] = nc[0, b]
        x[q:, :] = nc[1, b]

    trig_ref[:, :q] = ta[0]
    trig_ref[:, q:] = tb[0]
    trig = trig_ref[...]
    cosine, sine = trig[:HALF], trig[HALF:ROT]
    xhat, _ = xhat_of(x[...].astype(F32))
    xhat_ref[...] = xhat.astype(BF16)
    n1 = (xhat * row_of(s1) + row_of(b1)).astype(BF16)
    n1_ref[...] = n1

    def rotated(ref, mixed, factor):
        for h in range(0, wide, HEAD):
            a, b = mixed[h : h + HALF], mixed[h + HALF : h + ROT]
            turned = jnp.concatenate([a * cosine - b * sine, b * cosine + a * sine], axis=0)
            ref[h : h + ROT, :] = turned.astype(BF16) * factor
            ref[h + ROT : h + HEAD, :] = mixed[h + ROT : h + HEAD].astype(BF16) * factor

    mixed = mm(w_ref[wide : 3 * wide, :], n1, 1, 1) + bias[wide:, :]
    rotated(k_ref, mixed[:wide], BF16(1.0))
    v_ref[...] = mixed[wide:].astype(BF16)

    @pl.when(i < 4)
    def _():
        rotated(q_ref, mm(w_ref[:wide, :], n1, 1, 1) + bias[:wide, :], BF16(HEAD**-0.5))
        do_ref[...] = mm(w_ref[3 * wide :, :], g_ref[...], 1, 1).astype(BF16)


def project(at, x, g, far, others, trig, weights, bias, scale, offset):
    width = x.shape[2]
    rows = 8 * STEP
    wide = bias.shape[1]
    tall = trig.shape[1]

    def pick(high):
        def place(i, at):
            b = i // 2
            block = at[1] ^ (b % 2 * 2 + b // 2)
            return (at[0], 0, block * 4 + (at[2] ^ (i % 2 + high)))

        return pl.BlockSpec((1, tall, STEP // 2), place)

    def whole(v):
        return pl.BlockSpec(v.shape, lambda i, at: (0,) * v.ndim)

    def piece(high):
        return pl.BlockSpec(
            (1, STEP // 2, width), lambda i, at: (at[0], at[2] ^ (jnp.minimum(i, 1) + high), 0)
        )

    pieces = [piece(0), piece(2)]
    row = pl.BlockSpec((STEP, width), lambda i, at: (i, 0))
    own_row = pl.BlockSpec((STEP, width), lambda i, at: (jnp.minimum(i, 3), 0))
    col = pl.BlockSpec((wide, STEP), lambda i, at: (0, i))
    own_col = pl.BlockSpec((wide, STEP), lambda i, at: (0, jnp.minimum(i, 3)))
    received = (*far, *others)
    fixed = (weights, bias, scale, offset)
    return pl.pallas_call(
        project_kernel,
        grid_spec=pltpu.PrefetchScalarGridSpec(
            num_scalar_prefetch=1,
            grid=(8,),
            in_specs=pieces * 2 + [whole(v) for v in received] + [pick(0), pick(2)]
            + [whole(v) for v in fixed],
            out_specs=[row, row, own_row, pl.BlockSpec((tall, STEP), lambda i, at: (0, i)),
                       col, col, own_col, own_col],
            scratch_shapes=[pltpu.VMEM((STEP, width), BF16), pltpu.VMEM((3 * wide, 1), F32)],
        ),
        out_shape=[low_shape(rows, width)] * 2
        + [low_shape(rows // 2, width), shape(tall, rows)]
        + [low_shape(wide, rows)] * 2 + [low_shape(wide, rows // 2)] * 2,
        compiler_params=params(32),
        cost_estimate=cost(6 * rows * width * wide, 8 * rows * width),
    )(at, x, x, g, g, *received, trig, trig, *fixed)


def attention_kernel(count, *refs):
    (q_ref, do_ref, k_ref, v_ref, tq_ref, tk_ref,
     o_ref, dq_ref, dk_ref, dv_ref, kn, vn, kp, dk, dv, es, dps) = refs[count:]
    i = pl.program_id(0)
    length = k_ref.shape[1]
    chunk = STEP
    steps = length // chunk

    @pl.when(i == 0)
    def _():
        kn[...] = k_ref[...].T
        vn[...] = v_ref[...].T
        kp[...] = tk_ref[ROT:, :].T[:, 0:1]
        dk[...] = jnp.zeros_like(dk)
        dv[...] = jnp.zeros_like(dv)

    qt = q_ref[...]
    dot = do_ref[...]
    qn = qt.T
    don = dot.T
    qpos = tq_ref[ROT : ROT + 1, :]
    lanes = qt.shape[1]
    fold = (chunk // 8, 8, lanes)

    top = jnp.full((8, lanes), NEG, F32)
    for j in range(steps):
        here = slice(j * chunk, (j + 1) * chunk)
        s = mm(kn[here, :], qt)
        s = jnp.where(kp[here, :] <= qpos, s, NEG)
        es[here, :] = s
        top = jnp.maximum(top, jnp.max(s.reshape(fold), axis=0))
    top = jnp.max(top, axis=0, keepdims=True)

    total = jnp.zeros((8, lanes), F32)
    inner = jnp.zeros((8, lanes), F32)
    for j in range(steps):
        here = slice(j * chunk, (j + 1) * chunk)
        e = jnp.exp(es[here, :] - top)
        dp = mm(vn[here, :], dot)
        es[here, :] = e
        dps[here, :] = dp
        total = total + jnp.sum(e.reshape(fold), axis=0)
        inner = inner + jnp.sum((e * dp).reshape(fold), axis=0)
    share = 1.0 / jnp.sum(total, axis=0, keepdims=True)
    inner = jnp.sum(inner, axis=0, keepdims=True) * share

    ot = jnp.zeros((HEAD, lanes), F32)
    dqt = jnp.zeros((HEAD, lanes), F32)
    for j in range(steps):
        here = slice(j * chunk, (j + 1) * chunk)
        p = es[here, :] * share
        ds = (p * (dps[here, :] - inner)).astype(BF16)
        p = p.astype(BF16)
        dv[here, :] += mm(p, don)
        dk[here, :] += mm(ds, qn)
        ot = ot + mm(v_ref[:, here], p)
        dqt = dqt + mm(k_ref[:, here], ds)
    o_ref[...] = ot.astype(BF16)

    def unrotated(grad, trig):
        cosine, sine = trig[:HALF], trig[HALF:ROT]
        a, b = grad[:HALF], grad[HALF:ROT]
        turned = jnp.concatenate([a * cosine + b * sine, b * cosine - a * sine], axis=0)
        return turned.astype(BF16), grad[ROT:].astype(BF16)

    dq_ref[:ROT, :], dq_ref[ROT:, :] = unrotated(dqt * (HEAD**-0.5), tq_ref[...])

    @pl.when(i == pl.num_programs(0) - 1)
    def _():
        dk_ref[:ROT, :], dk_ref[ROT:, :] = unrotated(dk[...].T, tk_ref[...])
        dv_ref[...] = dv[...].T.astype(BF16)


def attention(h, after, qt, dot, kt, vt, trig):
    rows, length = qt.shape[1], kt.shape[1]
    lanes = STEP
    tall = trig.shape[0]
    q_spec = pl.BlockSpec((HEAD, lanes), lambda i: (h, i))
    k_spec = pl.BlockSpec((HEAD, length), lambda i: (h, 0))
    return pl.pallas_call(
        functools.partial(attention_kernel, len(after)),
        grid=(rows // lanes,),
        in_specs=[pl.BlockSpec(memory_space=pl.ANY)] * len(after)
        + [q_spec, q_spec, k_spec, k_spec, pl.BlockSpec((tall, lanes), lambda i: (0, i)),
           pl.BlockSpec((tall, length), lambda i: (0, 0))],
        out_specs=[pl.BlockSpec((HEAD, lanes), lambda i: (0, i))] * 2
        + [pl.BlockSpec((HEAD, length), lambda i: (0, 0))] * 2,
        out_shape=[low_shape(HEAD, rows)] * 2 + [low_shape(HEAD, length)] * 2,
        scratch_shapes=[
            pltpu.VMEM((length, HEAD), BF16),
            pltpu.VMEM((length, HEAD), BF16),
            pltpu.VMEM((length, 1), F32),
            pltpu.VMEM((length, HEAD), F32),
            pltpu.VMEM((length, HEAD), F32),
            pltpu.VMEM((length, lanes), F32),
            pltpu.VMEM((length, lanes), F32),
        ],
        compiler_params=params(32),
        cost_estimate=cost(40 * rows * length * HEAD, 16 * HEAD * length, rows * length),
    )(*after, qt, dot, kt, vt, trig, trig)


def forward_kernel(split, at, xa, xb, ga, gb, up_ref, bias_ref, down_ref, s2_ref, b2_ref,
                   ff_ref, a_ref, keep_ref, send_ref, small_ref, first_ref, second_ref, *scratch):
    i = pl.program_id(0)
    up_part, down_part = scratch if split else (first_ref, second_ref)

    @pl.when(i == 0)
    def _():
        up_part[...] = jnp.zeros_like(up_part)
        down_part[...] = jnp.zeros_like(down_part)
        small_ref[...] = jnp.zeros_like(small_ref)

    xhat, _ = xhat_of(jnp.concatenate([xa[0], xb[0]], axis=0).astype(F32))
    g = jnp.concatenate([ga[0], gb[0]], axis=0)
    scale = row_of(s2_ref)
    n2 = (xhat * scale + row_of(b2_ref)).astype(BF16)
    up = mm(n2, up_ref[...]) + row_of(bias_ref)
    cdf = 0.5 + 0.5 * lax.erf(up * (0.5**0.5))
    act = (up * cdf).astype(BF16)
    slope = cdf + up * (jnp.exp(up * up * -0.5) * 0.3989422804014327)
    up_grad = (mm(g, down_ref[...], 1, 1) * slope).astype(BF16)
    ff = mm(act, down_ref[...]).astype(BF16)
    second = mm(up_grad, up_ref[...], 1, 1)
    a = (second * scale).astype(BF16)

    @pl.when(i < 2)
    def _():
        ff_ref[...] = ff
        a_ref[...] = a

    @pl.when(i == 2)
    def _():
        keep_ref[0] = ff
        keep_ref[1] = a

    @pl.when(i == 3)
    def _():
        send_ref[0] = ff
        send_ref[1] = a

    up_part[...] += mm(n2, up_grad, 0, 0)
    down_part[...] += mm(act, g, 0, 0)
    small_ref[0:1, :] += jnp.sum(up_grad.astype(F32), axis=0, keepdims=True)
    small_ref[1:2, :] += jnp.sum(g.astype(F32), axis=0, keepdims=True)
    small_ref[2:3, :] += jnp.sum(second * xhat, axis=0, keepdims=True)
    small_ref[3:4, :] += jnp.sum(second, axis=0, keepdims=True)

    if split:
        half = up_part.shape[0] // 2

        @pl.when(i == pl.num_programs(0) - 1)
        def _():
            for ref, f in ((first_ref, at[3]), (second_ref, 1 - at[3])):
                piece = pl.ds(pl.multiple_of(f * half, 128), half)
                ref[:half, :] = up_part[piece, :].astype(ref.dtype)
                ref[half:, :half] = down_part[:half, piece].astype(ref.dtype)
                ref[half:, half:] = down_part[half:, piece].astype(ref.dtype)


def feed_forward(split, at, x, g, up, bias, down, scale, offset):
    width = x.shape[2]
    hidden = up.shape[1]
    pieces = two_quarters(width, lambda i, at: at[0] ^ (i // 2))
    own_row = pl.BlockSpec((STEP, width), lambda i, at: (jnp.minimum(i, 1), 0))

    def whole(*dims):
        return pl.BlockSpec(dims, lambda i, at: (0,) * len(dims))

    if split:
        assert width == hidden
        parts = [shape(width, hidden), low_shape(width, hidden)]
    else:
        parts = [shape(width, hidden), shape(hidden, width)]
    slots = whole(2, STEP, width)
    return pl.pallas_call(
        functools.partial(forward_kernel, split),
        grid_spec=pltpu.PrefetchScalarGridSpec(
            num_scalar_prefetch=1,
            grid=(4,),
            in_specs=pieces * 2 + [whole(width, hidden), whole(hidden), whole(hidden, width),
                                   whole(width), whole(width)],
            out_specs=[own_row, own_row, slots, slots, whole(8, width)]
            + [whole(*p.shape) for p in parts],
            scratch_shapes=[pltpu.VMEM((width, hidden), F32), pltpu.VMEM((hidden, width), F32)]
            if split
            else [],
        ),
        out_shape=[low_shape(2 * STEP, width)] * 2 + [low_shape(2, STEP, width)] * 2
        + [shape(8, width)] + parts,
        compiler_params=params(40),
        cost_estimate=cost(48 * STEP * width * hidden, 16 * MIB, 8 * STEP * hidden),
    )(at, x, x, g, g, up, bias, down, scale, offset)


def emit(keep_ref, send_ref, v, own_ref=None):
    i = pl.program_id(0)
    if own_ref is not None:
        v = jnp.where(i < 2, v + own_ref[...].astype(F32), v)

    @pl.when(i % 2 == 0)
    def _():
        keep_ref[0] = v.astype(BF16)

    @pl.when(i % 2 == 1)
    def _():
        send_ref[0] = v.astype(BF16)


def branch_kernel(heads, *refs):
    o = refs[:heads]
    g_ref, ff_ref, w_ref, keep_ref, send_ref, out = refs[heads:]
    wide = heads * HEAD

    @pl.when(pl.program_id(0) == 0)
    def _():
        out[...] = jnp.zeros_like(out)

    ot = jnp.concatenate([r[...] for r in o], axis=0)
    emit(keep_ref, send_ref, mm(ot, w_ref[...], 0, 0), ff_ref)
    out[...] += mm(ot, g_ref[...])


def branch(o, g, ff, weights):
    rows, width = g.shape
    heads = len(o)
    wide = heads * HEAD
    row = pl.BlockSpec((STEP, width), lambda i: (i, 0))
    slots = pl.BlockSpec((1, STEP, width), lambda i: (i // 2, 0, 0))
    return pl.pallas_call(
        functools.partial(branch_kernel, heads),
        grid=(rows // STEP,),
        in_specs=[pl.BlockSpec((HEAD, STEP), lambda i: (0, i))] * heads
        + [row, pl.BlockSpec((STEP, width), lambda i: (jnp.minimum(i, 1), 0)),
           pl.BlockSpec((wide, width), lambda i: (3, 0))],
        out_specs=[slots, slots, pl.BlockSpec((wide, width), lambda i: (0, 0))],
        out_shape=[low_shape(2, STEP, width)] * 2 + [shape(wide, width)],
        compiler_params=params(24),
        cost_estimate=cost(4 * rows * width * wide, 8 * MIB),
    )(*o, g, ff, weights)


def back_kernel(own, split, heads, at, *refs):
    count = 3 if own else 2
    grads, refs = refs[: count * heads], refs[count * heads :]
    n1_ref, xhat_ref, w_ref, s1_ref, *refs = refs
    if own:
        (a2_ref, small_ff, small_other, mix_other, out_part, after,
         keep_ref, send_ref, first_ref, second_ref, mix, small) = refs
    else:
        keep_ref, send_ref, mix, small = refs
    i = pl.program_id(0)
    wide = heads * HEAD
    tall = mix.shape[0]

    @pl.when(i == 0)
    def _():
        if own:
            mix[:wide, :] = jnp.zeros((wide, mix.shape[1]), F32)
            mix[wide:, :] = mix_other[...]
            small[...] = small_other[...]
        else:
            mix[...] = jnp.zeros_like(mix)
            small[...] = jnp.zeros_like(small)

    grad = jnp.concatenate([r[...] for r in grads], axis=0)
    first = mm(grad, w_ref[3 * wide - tall : 3 * wide, :], 0, 0)
    a = first * row_of(s1_ref)
    emit(keep_ref, send_ref, a, a2_ref if own else None)
    mix[...] += mm(grad, n1_ref[...])
    small[0:1, :] += jnp.sum(first * xhat_ref[...].astype(F32), axis=0, keepdims=True)
    small[1:2, :] += jnp.sum(first, axis=0, keepdims=True)
    ones = jnp.ones((8, grad.shape[1]), BF16)
    small[6:7, 3 * wide - tall : 3 * wide] += mm(ones, grad, 1, 1)[0:1]

    if own:
        @pl.when(i == pl.num_programs(0) - 1)
        def _():
            small[2:4, :] = small_ff[2:4, :]
            small[4:6, :] = small_ff[0:2, :]
            if split:
                half = mix.shape[1] // 2
                vectors = small[...].astype(BF16)
                for ref, f in ((first_ref, at[3]), (second_ref, 1 - at[3])):
                    piece = pl.ds(pl.multiple_of(f * half, 128), half)
                    ref[: 3 * wide, :] = mix[:, piece].astype(ref.dtype)
                    ref[3 * wide : 4 * wide, :] = out_part[:, piece].astype(ref.dtype)
                    both = jnp.concatenate([vectors[:, :half], vectors[:, half:]], axis=0)
                    ref[4 * wide : 4 * wide + 16, :] = both.astype(ref.dtype)
                    ref[4 * wide + 16 :, :] = jnp.zeros((48, half), ref.dtype)
            else:
                first_ref[: 3 * wide, :] = mix[...]
                first_ref[3 * wide :, :] = out_part[...]
                second_ref[...] = small[...]


def back(own, split, at, grads, n1, xhat, weights, scale, extra):
    rows, width = n1.shape[0] // 2, n1.shape[1]
    heads = len(grads[0])
    wide = heads * HEAD
    tall = 3 * wide if own else 2 * wide
    offset = 0 if own else rows // STEP
    row = pl.BlockSpec((STEP, width), lambda i, at: (i + offset, 0))
    col = pl.BlockSpec((HEAD, STEP), lambda i, at: (0, i + offset))
    slots = pl.BlockSpec((1, STEP, width), lambda i, at: (i // 2, 0, 0))

    def whole(*dims):
        return pl.BlockSpec(dims, lambda i, at: (0,) * len(dims))

    half = width // 2
    specs = [col] * (len(grads) * heads) + [row, row, whole(4 * wide, width), whole(width)]
    if not own:
        parts = [shape(tall, width), shape(8, width)]
        scratch = []
    else:
        specs += [pl.BlockSpec((STEP, width), lambda i, at: (jnp.minimum(i, 1), 0)),
                  whole(8, width), whole(8, width), whole(2 * wide, width),
                  whole(wide, width), pl.BlockSpec(memory_space=pl.ANY)]
        scratch = [pltpu.VMEM((tall, width), F32), pltpu.VMEM((8, width), F32)]
        if split:
            parts = [shape(4 * wide + 64, half), low_shape(4 * wide + 64, half)]
        else:
            parts = [shape(4 * wide, width), shape(8, width)]
    return pl.pallas_call(
        functools.partial(back_kernel, own, split, heads),
        grid_spec=pltpu.PrefetchScalarGridSpec(
            num_scalar_prefetch=1,
            grid=(rows // STEP,),
            in_specs=specs,
            out_specs=[slots, slots] + [whole(*p.shape) for p in parts],
            scratch_shapes=scratch,
        ),
        out_shape=[low_shape(2, STEP, width)] * 2 + parts,
        compiler_params=params(32),
        cost_estimate=cost(4 * rows * width * tall, 10 * MIB),
    )(at, *[v for vs in grads for v in vs], n1, xhat, weights, scale, *extra)


def swap(v, axis, size, distance):
    return lax.ppermute(v, axis, [(i, i ^ distance) for i in range(size)])


def by_xor(pieces, index):
    low, high = (index & 1) == 1, (index & 2) == 2
    a, b, c, d = pieces
    a, b, c, d = (jnp.where(low, b, a), jnp.where(low, a, b),
                  jnp.where(low, d, c), jnp.where(low, c, d))
    return (jnp.where(high, c, a), jnp.where(high, d, b),
            jnp.where(high, a, c), jnp.where(high, b, d))


def tie(v, *earlier):
    return lax.optimization_barrier((v, *earlier))[0]


def gather_halves(shard, size, mine, dim, *earlier):
    if size != 2:
        return lax.all_gather(shard, "fsdp", axis=dim, tiled=True)
    other = swap(shard, "fsdp", 2, 1)
    if earlier:
        other = tie(other, *earlier)
    first = mine == 0
    return jnp.concatenate(
        [jnp.where(first, shard, other), jnp.where(first, other, shard)], axis=dim
    )


def scatter_any(part, dim):
    return lax.psum_scatter(
        part.astype(BF16), "fsdp", scatter_dimension=dim, tiled=True
    ).astype(F32)


def halve(v, distance, bit):
    rows = v.shape[0] // 2
    keep = lax.dynamic_slice_in_dim(v, bit * rows, rows, 0)
    send = lax.dynamic_slice_in_dim(v, (1 - bit) * rows, rows, 0).astype(BF16)
    return keep + swap(send, "ctx", 4, distance).astype(F32)


def double(v, c):
    v = v.astype(BF16)
    pair = jnp.stack([v, swap(v, "ctx", 4, 2)])
    others = swap(pair, "ctx", 4, 1)
    return by_xor([pair[0], pair[1], others[0], others[1]], 2 * (c % 2) + c // 2)


def sum_over_ctx(v, c):
    return double(halve(halve(v, 1, c % 2), 2, c // 2), c)


def butterfly(v, axis_name, size):
    distance = 1
    while distance < size:
        v = v + swap(v, axis_name, size, distance)
        distance *= 2
    return v


def shards(
    sizes,
    inputs,
    positions,
    query_key_value_weight,
    query_key_value_bias,
    attention_output_weight,
    attention_output_bias,
    up_projection_weight,
    up_projection_bias,
    down_projection_weight,
    down_projection_bias,
    first_scale,
    first_shift,
    second_scale,
    second_shift,
    cotangent,
):
    fsdp = sizes["fsdp"]
    split = fsdp == 2
    seq_count, block, width = inputs.shape
    assert seq_count == 2 and sizes["ctx"] == 4 and sizes["tp"] == 4 and block == 2 * STEP
    length = positions.shape[1]
    local = query_key_value_weight.shape[2]
    heads = local // HEAD
    hidden = up_projection_weight.shape[1]
    quarter = block // 4
    f = lax.axis_index("fsdp")
    c = lax.axis_index("ctx")
    t = lax.axis_index("tp")
    s = c // 2
    at = jnp.stack([s, c, t, f]).astype(jnp.int32)

    def my_quarter(v, seq):
        return lax.dynamic_slice(v, (seq, t * quarter, 0), (1, quarter, width))

    x_mine, x_theirs = my_quarter(inputs, s), my_quarter(inputs, 1 - s)
    g_theirs = my_quarter(cotangent, 1 - s)
    far_z = swap(jnp.concatenate([x_theirs, g_theirs], axis=0), "ctx", 4, 2)
    cross = swap(tie(x_theirs, far_z), "ctx", 4, 3)
    near = swap(tie(x_mine, far_z), "ctx", 4, 1)

    def over_tp(v):
        v_x = swap(v, "tp", 4, 2)
        return v, v_x, swap(jnp.stack([v, v_x]), "tp", 4, 1)

    far = over_tp(far_z)
    others = over_tp(jnp.concatenate([near, cross], axis=0))

    wup = gather_halves(up_projection_weight, fsdp, f, 0)
    wdown = gather_halves(down_projection_weight, fsdp, f, 1)
    mix_shard = query_key_value_weight.transpose(1, 2, 0).reshape(3 * local, -1)
    mix_out_shard = jnp.concatenate([mix_shard, attention_output_weight], axis=0)

    inverse = 10000.0 ** (-2.0 * jnp.arange(HALF, dtype=F32) / ROT)
    places = positions.astype(F32)[:, None, :]
    angles = inverse[None, :, None] * places
    trig = jnp.concatenate(
        [jnp.cos(angles), jnp.sin(angles), jnp.broadcast_to(places, angles.shape)], axis=1
    )

    ff, a2, keep_e, send_e, small_ff, ff_first, ff_second = feed_forward(
        split, at, inputs, cotangent, wup, up_projection_bias, wdown, second_scale, second_shift
    )

    weights = gather_halves(mix_out_shard, fsdp, f, 1, small_ff)
    n1, xhat_all, g, trig, kt, vt, qt, dot = project(
        at, inputs, cotangent, (far[0], far[1], tie(far[2], small_ff)),
        (others[0], others[1], tie(others[2], small_ff)), trig, weights, query_key_value_bias,
        first_scale, first_shift,
    )
    def over_core(keep, send, *earlier):
        v = keep.astype(F32) + tie(swap(send, "tp", 4, 1), *earlier).astype(F32)
        return v.reshape(2, 2, quarter, width)

    def over_x(v, *earlier):
        return v[:, 0] + tie(swap(v[:, 1].astype(BF16), "tp", 4, 2), *earlier).astype(F32)

    def scatter_tp(keep, send):
        return over_x(over_core(keep, send))

    per_head = []
    for h in range(heads):
        after = ()
        if h == 1:
            early = over_core(keep_e, send_e, per_head[0][0])
            after = (early,)
        if h == heads - 1:
            early = over_x(early, per_head[h - 1][0])
            ff_rest = small_ff
            if split:
                ff_rest = tie(swap(ff_second, "fsdp", 2, 1), per_head[h - 1][0])
                ff_rest = ff_first + ff_rest.astype(F32)
            after = (early, ff_rest)
        per_head.append(attention(h, after, qt, dot, kt, vt, trig))
    o, dq, dk, dv = zip(*per_head)
    keep_b, send_b, out_part = branch(o, g, ff, weights)
    if split:
        ff_half = halve(ff_rest, 1, c % 2)
    else:
        ff_half = small_ff
    keep_o, send_o, mix_other, small_other = back(
        False, split, at, (dk, dv), n1, xhat_all, weights, first_scale, ()
    )
    keep_w, send_w, late_first, late_second = back(
        True, split, at, (dq, dk, dv), n1, xhat_all, weights, first_scale,
        (a2, small_ff, small_other, mix_other, out_part, ff_half),
    )

    def over_ctx(v, distance):
        return swap(v.astype(BF16), "ctx", 4, distance).astype(F32)

    def gather_tp(mine, theirs):
        ours = jnp.stack([mine, theirs]).astype(BF16)
        pair = jnp.stack([ours, swap(ours, "tp", 4, 2)])
        core = swap(pair, "tp", 4, 1)
        pieces = by_xor((pair[0], core[0], pair[1], core[1]), t)
        pieces = jnp.concatenate(pieces, axis=1)
        return jnp.stack([jnp.where(s == 0, pieces[0], pieces[1]),
                          jnp.where(s == 0, pieces[1], pieces[0])]).astype(F32)

    sums_b = scatter_tp(keep_b, send_b)
    block_out = gather_tp(sums_b[0], over_ctx(sums_b[1], 2) + early[0])
    block_out = (
        inputs.astype(F32) + block_out + (attention_output_bias + down_projection_bias)
    )

    sums_o = scatter_tp(keep_o, send_o)
    sums_w = scatter_tp(keep_w, send_w)
    a = jnp.stack([
        sums_w[0] + over_ctx(sums_o[0], 1),
        over_ctx(sums_w[1], 2) + over_ctx(sums_o[1], 3) + early[1],
    ])
    xhat, inv = xhat_of(jnp.concatenate([x_mine, x_theirs], axis=0).astype(F32))
    norm_grad = inv * (
        a
        - jnp.mean(a, axis=-1, keepdims=True)
        - xhat * jnp.mean(a * xhat, axis=-1, keepdims=True)
    )
    inputs_grad = cotangent.astype(F32) + gather_tp(norm_grad[0], norm_grad[1])

    if split:
        q = double(halve(ff_half, 2, c // 2), c)
        up_total = jnp.concatenate(q[:2], axis=0).astype(F32)
        down_total = jnp.concatenate(q[2:], axis=0).astype(F32)
        down_total = jnp.concatenate(
            [down_total[:, : width // 2], down_total[:, width // 2 :]], axis=0
        )
        late = late_first + tie(swap(late_second, "fsdp", 2, 1), sums_w).astype(F32)
        late = jnp.concatenate(sum_over_ctx(late, c), axis=0).astype(F32)
        small = jnp.concatenate([late[4 * local : 4 * local + 8], late[4 * local + 8 :][:8]], axis=1)
    else:
        q = sum_over_ctx(scatter_any(ff_first, 0), c)
        up_total = jnp.concatenate(q, axis=0).astype(F32)
        q = sum_over_ctx(scatter_any(ff_second, 1), c)
        down_total = jnp.concatenate(q, axis=0).astype(F32)
        q = sum_over_ctx(scatter_any(late_first, 1), c)
        late = jnp.concatenate(q, axis=0).astype(F32)
        small = butterfly(butterfly(late_second, "fsdp", fsdp), "ctx", 4)
    mix_total = late[: 3 * local].reshape(3, local, -1).transpose(2, 0, 1)
    out_total = late[3 * local : 4 * local]
    norm_small = butterfly(small, "tp", 4)
    bias_total = norm_small[5] * 0.25
    return (
        block_out,
        inputs_grad,
        mix_total,
        small[6, : 3 * local].reshape(3, local),
        out_total,
        bias_total,
        up_total,
        small[4, :hidden],
        down_total,
        bias_total,
        norm_small[0],
        norm_small[1],
        norm_small[2],
        norm_small[3],
    )


def solution(mesh):
    in_specs = (
        P("fsdp", "ctx", None),
        P("fsdp", None),
        P("fsdp", None, "tp"),
        P(None, "tp"),
        P("tp", "fsdp"),
        P(),
        P("fsdp", "tp"),
        P("tp"),
        P("tp", "fsdp"),
        P(),
        P(),
        P(),
        P(),
        P(),
        P("fsdp", "ctx", None),
    )
    out_specs = (
        P("fsdp", "ctx", None),
        P("fsdp", "ctx", None),
        P("fsdp", None, "tp"),
        P(None, "tp"),
        P("tp", "fsdp"),
        P(),
        P("fsdp", "tp"),
        P("tp"),
        P("tp", "fsdp"),
        P(),
        P(),
        P(),
        P(),
        P(),
    )
    body = functools.partial(shards, dict(mesh.shape))
    return jax.shard_map(body, mesh=mesh, in_specs=in_specs, out_specs=out_specs, check_vma=False)
```

```python
import functools

import jax
import jax.numpy as jnp
from jax import lax
from jax.experimental import pallas as pl
from jax.experimental.pallas import tpu as pltpu
from jax.sharding import PartitionSpec as P

HEAD = 64
ROT = 16
HALF = ROT // 2
EPS = 1e-5
NEG = -1e30
STEP = 256
F32 = jnp.float32
BF16 = jnp.bfloat16
MIB = 1024 * 1024


def mm(a, b, ca=1, cb=0):
    return lax.dot_general(a, b, (((ca,), (cb,)), ((), ())), preferred_element_type=F32)


def params(mib):
    return pltpu.CompilerParams(vmem_limit_bytes=mib * MIB)


def cost(flops, moved, exps=0):
    return pl.CostEstimate(flops=int(flops), bytes_accessed=int(moved), transcendentals=int(exps))


def xhat_of(x):
    width = x.shape[-1]
    centred = x - jnp.sum(x, axis=-1, keepdims=True) * (1.0 / width)
    spread = jnp.sum(centred * centred, axis=-1, keepdims=True) * (1.0 / width)
    inv = lax.rsqrt(spread + EPS)
    return centred * inv, inv


def row_of(ref):
    return ref[...].reshape(1, -1)


def shape(*dims):
    return jax.ShapeDtypeStruct(dims, F32)


def low_shape(*dims):
    return jax.ShapeDtypeStruct(dims, BF16)


def two_quarters(width, seq_of):
    def piece(high):
        return pl.BlockSpec(
            (1, STEP // 2, width), lambda i, at: (seq_of(i, at), at[2] ^ (i % 2 + high), 0)
        )

    return [piece(0), piece(2)]


def project_kernel(at, xa, xb, ga, gb, fz, fx, fc, nz, nx, nc, ta, tb, w_ref, b_ref, s1, b1,
                   n1_ref, xhat_ref, g_ref, trig_ref, k_ref, v_ref, q_ref, do_ref, x, bias):
    i = pl.program_id(0)
    wide = k_ref.shape[0]
    q = STEP // 2
    b = jnp.maximum(i // 2 - 2, 0)

    @pl.when(i == 0)
    def _():
        for j in range(3):
            line = jnp.broadcast_to(b_ref[j : j + 1, :], (8, wide))
            bias[j * wide : (j + 1) * wide, :] = line.T[:, 0:1]

    @pl.when(i < 2)
    def _():
        x[:q, :] = xa[0]
        x[q:, :] = xb[0]
        g_ref[:q, :] = ga[0]
        g_ref[q:, :] = gb[0]

    @pl.when(i == 2)
    def _():
        x[:q, :] = fz[0]
        x[q:, :] = fx[0]
        g_ref[:q, :] = fz[1]
        g_ref[q:, :] = fx[1]

    @pl.when(i == 3)
    def _():
        x[:q, :] = fc[0, 0]
        x[q:, :] = fc[1, 0]
        g_ref[:q, :] = fc[0, 1]
        g_ref[q:, :] = fc[1, 1]

    @pl.when((i >= 4) & (i % 2 == 0))
    def _():
        x[:q, :] = nz[b]
        x[q:, :] = nx[b]

    @pl.when((i >= 4) & (i % 2 == 1))
    def _():
        x[:q, :] = nc[0, b]
        x[q:, :] = nc[1, b]

    trig_ref[:, :q] = ta[0]
    trig_ref[:, q:] = tb[0]
    trig = trig_ref[...]
    cosine, sine = trig[:HALF], trig[HALF:ROT]
    xhat, _ = xhat_of(x[...].astype(F32))
    xhat_ref[...] = xhat.astype(BF16)
    n1 = (xhat * row_of(s1) + row_of(b1)).astype(BF16)
    n1_ref[...] = n1

    def rotated(ref, mixed, factor):
        for h in range(0, wide, HEAD):
            a, b = mixed[h : h + HALF], mixed[h + HALF : h + ROT]
            turned = jnp.concatenate([a * cosine - b * sine, b * cosine + a * sine], axis=0)
            ref[h : h + ROT, :] = turned.astype(BF16) * factor
            ref[h + ROT : h + HEAD, :] = mixed[h + ROT : h + HEAD].astype(BF16) * factor

    mixed = mm(w_ref[wide : 3 * wide, :], n1, 1, 1) + bias[wide:, :]
    rotated(k_ref, mixed[:wide], BF16(1.0))
    v_ref[...] = mixed[wide:].astype(BF16)

    @pl.when(i < 4)
    def _():
        rotated(q_ref, mm(w_ref[:wide, :], n1, 1, 1) + bias[:wide, :], BF16(HEAD**-0.5))
        do_ref[...] = mm(w_ref[3 * wide :, :], g_ref[...], 1, 1).astype(BF16)


def project(at, x, g, far, others, trig, weights, bias, scale, offset):
    width = x.shape[2]
    rows = 8 * STEP
    wide = bias.shape[1]
    tall = trig.shape[1]

    def pick(high):
        def place(i, at):
            b = i // 2
            block = at[1] ^ (b % 2 * 2 + b // 2)
            return (at[0], 0, block * 4 + (at[2] ^ (i % 2 + high)))

        return pl.BlockSpec((1, tall, STEP // 2), place)

    def whole(v):
        return pl.BlockSpec(v.shape, lambda i, at: (0,) * v.ndim)

    def piece(high):
        return pl.BlockSpec(
            (1, STEP // 2, width), lambda i, at: (at[0], at[2] ^ (jnp.minimum(i, 1) + high), 0)
        )

    pieces = [piece(0), piece(2)]
    row = pl.BlockSpec((STEP, width), lambda i, at: (i, 0))
    own_row = pl.BlockSpec((STEP, width), lambda i, at: (jnp.minimum(i, 3), 0))
    col = pl.BlockSpec((wide, STEP), lambda i, at: (0, i))
    own_col = pl.BlockSpec((wide, STEP), lambda i, at: (0, jnp.minimum(i, 3)))
    received = (*far, *others)
    fixed = (weights, bias, scale, offset)
    return pl.pallas_call(
        project_kernel,
        grid_spec=pltpu.PrefetchScalarGridSpec(
            num_scalar_prefetch=1,
            grid=(8,),
            in_specs=pieces * 2 + [whole(v) for v in received] + [pick(0), pick(2)]
            + [whole(v) for v in fixed],
            out_specs=[row, row, own_row, pl.BlockSpec((tall, STEP), lambda i, at: (0, i)),
                       col, col, own_col, own_col],
            scratch_shapes=[pltpu.VMEM((STEP, width), BF16), pltpu.VMEM((3 * wide, 1), F32)],
        ),
        out_shape=[low_shape(rows, width)] * 2
        + [low_shape(rows // 2, width), shape(tall, rows)]
        + [low_shape(wide, rows)] * 2 + [low_shape(wide, rows // 2)] * 2,
        compiler_params=params(56),
        cost_estimate=cost(6 * rows * width * wide, 8 * rows * width),
    )(at, x, x, g, g, *received, trig, trig, *fixed)


def attention_kernel(count, *refs):
    (q_ref, do_ref, k_ref, v_ref, tq_ref, tk_ref,
     o_ref, dq_ref, dk_ref, dv_ref, kn, vn, kp, dk, dv, es, dps) = refs[count:]
    i = pl.program_id(0)
    length = k_ref.shape[1]
    chunk = STEP
    steps = length // chunk

    @pl.when(i == 0)
    def _():
        kn[...] = k_ref[...].T
        vn[...] = v_ref[...].T
        kp[...] = tk_ref[ROT:, :].T[:, 0:1]
        dk[...] = jnp.zeros_like(dk)
        dv[...] = jnp.zeros_like(dv)

    qt = q_ref[...]
    dot = do_ref[...]
    qn = qt.T
    don = dot.T
    qpos = tq_ref[ROT : ROT + 1, :]
    lanes = qt.shape[1]
    fold = (chunk // 8, 8, lanes)

    top = jnp.full((8, lanes), NEG, F32)
    for j in range(steps):
        here = slice(j * chunk, (j + 1) * chunk)
        s = mm(kn[here, :], qt)
        s = jnp.where(kp[here, :] <= qpos, s, NEG)
        es[here, :] = s
        top = jnp.maximum(top, jnp.max(s.reshape(fold), axis=0))
    top = jnp.max(top, axis=0, keepdims=True)

    total = jnp.zeros((8, lanes), F32)
    inner = jnp.zeros((8, lanes), F32)
    for j in range(steps):
        here = slice(j * chunk, (j + 1) * chunk)
        e = jnp.exp(es[here, :] - top)
        dp = mm(vn[here, :], dot)
        es[here, :] = e
        dps[here, :] = dp
        total = total + jnp.sum(e.reshape(fold), axis=0)
        inner = inner + jnp.sum((e * dp).reshape(fold), axis=0)
    share = 1.0 / jnp.sum(total, axis=0, keepdims=True)
    inner = jnp.sum(inner, axis=0, keepdims=True) * share

    ot = jnp.zeros((HEAD, lanes), F32)
    dqt = jnp.zeros((HEAD, lanes), F32)
    for j in range(steps):
        here = slice(j * chunk, (j + 1) * chunk)
        p = es[here, :] * share
        ds = (p * (dps[here, :] - inner)).astype(BF16)
        p = p.astype(BF16)
        dv[here, :] += mm(p, don)
        dk[here, :] += mm(ds, qn)
        ot = ot + mm(v_ref[:, here], p)
        dqt = dqt + mm(k_ref[:, here], ds)
    o_ref[...] = ot.astype(BF16)

    def unrotated(grad, trig):
        cosine, sine = trig[:HALF], trig[HALF:ROT]
        a, b = grad[:HALF], grad[HALF:ROT]
        turned = jnp.concatenate([a * cosine + b * sine, b * cosine - a * sine], axis=0)
        return turned.astype(BF16), grad[ROT:].astype(BF16)

    dq_ref[:ROT, :], dq_ref[ROT:, :] = unrotated(dqt * (HEAD**-0.5), tq_ref[...])

    @pl.when(i == pl.num_programs(0) - 1)
    def _():
        dk_ref[:ROT, :], dk_ref[ROT:, :] = unrotated(dk[...].T, tk_ref[...])
        dv_ref[...] = dv[...].T.astype(BF16)


def attention(h, after, qt, dot, kt, vt, trig):
    rows, length = qt.shape[1], kt.shape[1]
    lanes = STEP
    tall = trig.shape[0]
    q_spec = pl.BlockSpec((HEAD, lanes), lambda i: (h, i))
    k_spec = pl.BlockSpec((HEAD, length), lambda i: (h, 0))
    return pl.pallas_call(
        functools.partial(attention_kernel, len(after)),
        grid=(rows // lanes,),
        in_specs=[pl.BlockSpec(memory_space=pl.ANY)] * len(after)
        + [q_spec, q_spec, k_spec, k_spec, pl.BlockSpec((tall, lanes), lambda i: (0, i)),
           pl.BlockSpec((tall, length), lambda i: (0, 0))],
        out_specs=[pl.BlockSpec((HEAD, lanes), lambda i: (0, i))] * 2
        + [pl.BlockSpec((HEAD, length), lambda i: (0, 0))] * 2,
        out_shape=[low_shape(HEAD, rows)] * 2 + [low_shape(HEAD, length)] * 2,
        scratch_shapes=[
            pltpu.VMEM((length, HEAD), BF16),
            pltpu.VMEM((length, HEAD), BF16),
            pltpu.VMEM((length, 1), F32),
            pltpu.VMEM((length, HEAD), F32),
            pltpu.VMEM((length, HEAD), F32),
            pltpu.VMEM((length, lanes), F32),
            pltpu.VMEM((length, lanes), F32),
        ],
        compiler_params=params(56),
        cost_estimate=cost(40 * rows * length * HEAD, 16 * HEAD * length, rows * length),
    )(*after, qt, dot, kt, vt, trig, trig)


def forward_kernel(split, at, xa, xb, ga, gb, up_ref, bias_ref, down_ref, s2_ref, b2_ref,
                   ff_ref, a_ref, keep_ref, send_ref, small_ref, first_ref, second_ref, *scratch):
    i = pl.program_id(0)
    up_part, down_part = scratch if split else (first_ref, second_ref)

    @pl.when(i == 0)
    def _():
        up_part[...] = jnp.zeros_like(up_part)
        down_part[...] = jnp.zeros_like(down_part)
        small_ref[...] = jnp.zeros_like(small_ref)

    xhat, _ = xhat_of(jnp.concatenate([xa[0], xb[0]], axis=0).astype(F32))
    g = jnp.concatenate([ga[0], gb[0]], axis=0)
    scale = row_of(s2_ref)
    n2 = (xhat * scale + row_of(b2_ref)).astype(BF16)
    up = mm(n2, up_ref[...]) + row_of(bias_ref)
    cdf = 0.5 + 0.5 * lax.erf(up * (0.5**0.5))
    act = (up * cdf).astype(BF16)
    slope = cdf + up * (jnp.exp(up * up * -0.5) * 0.3989422804014327)
    up_grad = (mm(g, down_ref[...], 1, 1) * slope).astype(BF16)
    ff = mm(act, down_ref[...]).astype(BF16)
    second = mm(up_grad, up_ref[...], 1, 1)
    a = (second * scale).astype(BF16)

    @pl.when(i < 2)
    def _():
        ff_ref[...] = ff
        a_ref[...] = a

    @pl.when(i == 2)
    def _():
        keep_ref[0] = ff
        keep_ref[1] = a

    @pl.when(i == 3)
    def _():
        send_ref[0] = ff
        send_ref[1] = a

    up_part[...] += mm(n2, up_grad, 0, 0)
    down_part[...] += mm(act, g, 0, 0)
    small_ref[0:1, :] += jnp.sum(up_grad.astype(F32), axis=0, keepdims=True)
    small_ref[1:2, :] += jnp.sum(g.astype(F32), axis=0, keepdims=True)
    small_ref[2:3, :] += jnp.sum(second * xhat, axis=0, keepdims=True)
    small_ref[3:4, :] += jnp.sum(second, axis=0, keepdims=True)

    if split:
        half = up_part.shape[0] // 2

        @pl.when(i == pl.num_programs(0) - 1)
        def _():
            for ref, f in ((first_ref, at[3]), (second_ref, 1 - at[3])):
                piece = pl.ds(pl.multiple_of(f * half, 128), half)
                ref[:half, :] = up_part[piece, :].astype(ref.dtype)
                ref[half:, :half] = down_part[:half, piece].astype(ref.dtype)
                ref[half:, half:] = down_part[half:, piece].astype(ref.dtype)


def feed_forward(split, at, x, g, up, bias, down, scale, offset):
    width = x.shape[2]
    hidden = up.shape[1]
    pieces = two_quarters(width, lambda i, at: at[0] ^ (i // 2))
    own_row = pl.BlockSpec((STEP, width), lambda i, at: (jnp.minimum(i, 1), 0))

    def whole(*dims):
        return pl.BlockSpec(dims, lambda i, at: (0,) * len(dims))

    if split:
        assert width == hidden
        parts = [shape(width, hidden), low_shape(width, hidden)]
    else:
        parts = [shape(width, hidden), shape(hidden, width)]
    slots = whole(2, STEP, width)
    return pl.pallas_call(
        functools.partial(forward_kernel, split),
        grid_spec=pltpu.PrefetchScalarGridSpec(
            num_scalar_prefetch=1,
            grid=(4,),
            in_specs=pieces * 2 + [whole(width, hidden), whole(hidden), whole(hidden, width),
                                   whole(width), whole(width)],
            out_specs=[own_row, own_row, slots, slots, whole(8, width)]
            + [whole(*p.shape) for p in parts],
            scratch_shapes=[pltpu.VMEM((width, hidden), F32), pltpu.VMEM((hidden, width), F32)]
            if split
            else [],
        ),
        out_shape=[low_shape(2 * STEP, width)] * 2 + [low_shape(2, STEP, width)] * 2
        + [shape(8, width)] + parts,
        compiler_params=params(56),
        cost_estimate=cost(48 * STEP * width * hidden, 16 * MIB, 8 * STEP * hidden),
    )(at, x, x, g, g, up, bias, down, scale, offset)


def emit(keep_ref, send_ref, v, own_ref=None):
    i = pl.program_id(0)
    if own_ref is not None:
        v = jnp.where(i < 2, v + own_ref[...].astype(F32), v)

    @pl.when(i % 2 == 0)
    def _():
        keep_ref[0] = v.astype(BF16)

    @pl.when(i % 2 == 1)
    def _():
        send_ref[0] = v.astype(BF16)


def branch_kernel(heads, *refs):
    o = refs[:heads]
    g_ref, ff_ref, w_ref, keep_ref, send_ref, out = refs[heads:]
    wide = heads * HEAD

    @pl.when(pl.program_id(0) == 0)
    def _():
        out[...] = jnp.zeros_like(out)

    ot = jnp.concatenate([r[...] for r in o], axis=0)
    emit(keep_ref, send_ref, mm(ot, w_ref[...], 0, 0), ff_ref)
    out[...] += mm(ot, g_ref[...])


def branch(o, g, ff, weights):
    rows, width = g.shape
    heads = len(o)
    wide = heads * HEAD
    row = pl.BlockSpec((STEP, width), lambda i: (i, 0))
    slots = pl.BlockSpec((1, STEP, width), lambda i: (i // 2, 0, 0))
    return pl.pallas_call(
        functools.partial(branch_kernel, heads),
        grid=(rows // STEP,),
        in_specs=[pl.BlockSpec((HEAD, STEP), lambda i: (0, i))] * heads
        + [row, pl.BlockSpec((STEP, width), lambda i: (jnp.minimum(i, 1), 0)),
           pl.BlockSpec((wide, width), lambda i: (3, 0))],
        out_specs=[slots, slots, pl.BlockSpec((wide, width), lambda i: (0, 0))],
        out_shape=[low_shape(2, STEP, width)] * 2 + [shape(wide, width)],
        compiler_params=params(56),
        cost_estimate=cost(4 * rows * width * wide, 8 * MIB),
    )(*o, g, ff, weights)


def back_kernel(own, split, heads, at, *refs):
    count = 3 if own else 2
    grads, refs = refs[: count * heads], refs[count * heads :]
    n1_ref, xhat_ref, w_ref, s1_ref, *refs = refs
    if own:
        (a2_ref, small_ff, small_other, mix_other, out_part,
         keep_ref, send_ref, first_ref, second_ref, mix, small) = refs
    else:
        keep_ref, send_ref, mix, small = refs
    i = pl.program_id(0)
    wide = heads * HEAD
    tall = mix.shape[0]

    @pl.when(i == 0)
    def _():
        if own:
            mix[:wide, :] = jnp.zeros((wide, mix.shape[1]), F32)
            mix[wide:, :] = mix_other[...]
            small[...] = small_other[...]
        else:
            mix[...] = jnp.zeros_like(mix)
            small[...] = jnp.zeros_like(small)

    grad = jnp.concatenate([r[...] for r in grads], axis=0)
    first = mm(grad, w_ref[3 * wide - tall : 3 * wide, :], 0, 0)
    a = first * row_of(s1_ref)
    emit(keep_ref, send_ref, a, a2_ref if own else None)
    mix[...] += mm(grad, n1_ref[...])
    small[0:1, :] += jnp.sum(first * xhat_ref[...].astype(F32), axis=0, keepdims=True)
    small[1:2, :] += jnp.sum(first, axis=0, keepdims=True)
    ones = jnp.ones((8, grad.shape[1]), BF16)
    small[6:7, 3 * wide - tall : 3 * wide] += mm(ones, grad, 1, 1)[0:1]

    if own:
        @pl.when(i == pl.num_programs(0) - 1)
        def _():
            small[2:4, :] = small_ff[2:4, :]
            small[4:6, :] = small_ff[0:2, :]
            if split:
                half = mix.shape[1] // 2
                vectors = small[...].astype(BF16)
                for ref, f in ((first_ref, at[3]), (second_ref, 1 - at[3])):
                    piece = pl.ds(pl.multiple_of(f * half, 128), half)
                    ref[: 3 * wide, :] = mix[:, piece].astype(ref.dtype)
                    ref[3 * wide : 4 * wide, :] = out_part[:, piece].astype(ref.dtype)
                    both = jnp.concatenate([vectors[:, :half], vectors[:, half:]], axis=0)
                    ref[4 * wide : 4 * wide + 16, :] = both.astype(ref.dtype)
                    ref[4 * wide + 16 :, :] = jnp.zeros((48, half), ref.dtype)
            else:
                first_ref[: 3 * wide, :] = mix[...]
                first_ref[3 * wide :, :] = out_part[...]
                second_ref[...] = small[...]


def back(own, split, at, grads, n1, xhat, weights, scale, extra):
    rows, width = n1.shape[0] // 2, n1.shape[1]
    heads = len(grads[0])
    wide = heads * HEAD
    tall = 3 * wide if own else 2 * wide
    offset = 0 if own else rows // STEP
    row = pl.BlockSpec((STEP, width), lambda i, at: (i + offset, 0))
    col = pl.BlockSpec((HEAD, STEP), lambda i, at: (0, i + offset))
    slots = pl.BlockSpec((1, STEP, width), lambda i, at: (i // 2, 0, 0))

    def whole(*dims):
        return pl.BlockSpec(dims, lambda i, at: (0,) * len(dims))

    half = width // 2
    specs = [col] * (len(grads) * heads) + [row, row, whole(4 * wide, width), whole(width)]
    if not own:
        parts = [shape(tall, width), shape(8, width)]
        scratch = []
    else:
        specs += [pl.BlockSpec((STEP, width), lambda i, at: (jnp.minimum(i, 1), 0)),
                  whole(8, width), whole(8, width), whole(2 * wide, width),
                  whole(wide, width)]
        scratch = [pltpu.VMEM((tall, width), F32), pltpu.VMEM((8, width), F32)]
        if split:
            parts = [shape(4 * wide + 64, half), low_shape(4 * wide + 64, half)]
        else:
            parts = [shape(4 * wide, width), shape(8, width)]
    return pl.pallas_call(
        functools.partial(back_kernel, own, split, heads),
        grid_spec=pltpu.PrefetchScalarGridSpec(
            num_scalar_prefetch=1,
            grid=(rows // STEP,),
            in_specs=specs,
            out_specs=[slots, slots] + [whole(*p.shape) for p in parts],
            scratch_shapes=scratch,
        ),
        out_shape=[low_shape(2, STEP, width)] * 2 + parts,
        compiler_params=params(56),
        cost_estimate=cost(4 * rows * width * tall, 10 * MIB),
    )(at, *[v for vs in grads for v in vs], n1, xhat, weights, scale, *extra)


def swap(v, axis, size, distance):
    return lax.ppermute(v, axis, [(i, i ^ distance) for i in range(size)])


def by_xor(pieces, index):
    low, high = (index & 1) == 1, (index & 2) == 2
    a, b, c, d = pieces
    a, b, c, d = (jnp.where(low, b, a), jnp.where(low, a, b),
                  jnp.where(low, d, c), jnp.where(low, c, d))
    return (jnp.where(high, c, a), jnp.where(high, d, b),
            jnp.where(high, a, c), jnp.where(high, b, d))


def tie(v, *earlier):
    return lax.optimization_barrier((v, *earlier))[0]


def gather_halves(shard, size, mine, dim, *earlier):
    if size != 2:
        return lax.all_gather(shard, "fsdp", axis=dim, tiled=True)
    other = swap(shard, "fsdp", 2, 1)
    if earlier:
        other = tie(other, *earlier)
    first = mine == 0
    return jnp.concatenate(
        [jnp.where(first, shard, other), jnp.where(first, other, shard)], axis=dim
    )


def scatter_any(part, dim):
    return lax.psum_scatter(
        part.astype(BF16), "fsdp", scatter_dimension=dim, tiled=True
    ).astype(F32)


def quarter_sum(v, c, *earlier):
    rows = v.shape[0] // 4
    mine = 2 * (c % 2) + c // 2

    def part(j):
        return lax.dynamic_slice_in_dim(v, (mine ^ j) * rows, rows, 0)

    total = part(0)
    for distance, j in ((3, 3), (2, 1), (1, 2)):
        sent = swap(part(j).astype(BF16), "ctx", 4, distance)
        total = total + tie(sent, *earlier).astype(F32)
    return total


def double(v, c, first=(), second=()):
    v = v.astype(BF16)
    pair = jnp.stack([v, tie(swap(v, "ctx", 4, 2), *first)])
    others = tie(swap(pair, "ctx", 4, 1), *second)
    return by_xor([pair[0], pair[1], others[0], others[1]], 2 * (c % 2) + c // 2)


def sum_over_ctx(v, c):
    return double(quarter_sum(v, c), c)


def butterfly(v, axis_name, size):
    distance = 1
    while distance < size:
        v = v + swap(v, axis_name, size, distance)
        distance *= 2
    return v


def shards(
    sizes,
    inputs,
    positions,
    query_key_value_weight,
    query_key_value_bias,
    attention_output_weight,
    attention_output_bias,
    up_projection_weight,
    up_projection_bias,
    down_projection_weight,
    down_projection_bias,
    first_scale,
    first_shift,
    second_scale,
    second_shift,
    cotangent,
):
    fsdp = sizes["fsdp"]
    split = fsdp == 2
    seq_count, block, width = inputs.shape
    assert seq_count == 2 and sizes["ctx"] == 4 and sizes["tp"] == 4 and block == 2 * STEP
    length = positions.shape[1]
    local = query_key_value_weight.shape[2]
    heads = local // HEAD
    hidden = up_projection_weight.shape[1]
    quarter = block // 4
    f = lax.axis_index("fsdp")
    c = lax.axis_index("ctx")
    t = lax.axis_index("tp")
    s = c // 2
    at = jnp.stack([s, c, t, f]).astype(jnp.int32)

    def my_quarter(v, seq):
        return lax.dynamic_slice(v, (seq, t * quarter, 0), (1, quarter, width))

    x_mine, x_theirs = my_quarter(inputs, s), my_quarter(inputs, 1 - s)
    g_theirs = my_quarter(cotangent, 1 - s)
    far_z = swap(jnp.concatenate([x_theirs, g_theirs], axis=0), "ctx", 4, 2)
    cross = swap(x_theirs, "ctx", 4, 3)
    near = swap(x_mine, "ctx", 4, 1)

    others_z = jnp.concatenate([near, cross], axis=0)
    others_x = swap(others_z, "tp", 4, 2)
    far_x = swap(far_z, "tp", 4, 2)

    wup = gather_halves(up_projection_weight, fsdp, f, 0)
    wdown = gather_halves(down_projection_weight, fsdp, f, 1)
    mix_shard = query_key_value_weight.transpose(1, 2, 0).reshape(3 * local, -1)
    mix_out_shard = jnp.concatenate([mix_shard, attention_output_weight], axis=0)

    inverse = 10000.0 ** (-2.0 * jnp.arange(HALF, dtype=F32) / ROT)
    places = positions.astype(F32)[:, None, :]
    angles = inverse[None, :, None] * places
    trig = jnp.concatenate(
        [jnp.cos(angles), jnp.sin(angles), jnp.broadcast_to(places, angles.shape)], axis=1
    )

    ff, a2, keep_e, send_e, small_ff, ff_first, ff_second = feed_forward(
        split, at, inputs, cotangent, wup, up_projection_bias, wdown, second_scale, second_shift
    )

    def over_tp(v_z, v_x):
        v_x = tie(v_x, small_ff)
        return v_z, v_x, swap(jnp.stack([v_z, v_x]), "tp", 4, 1)

    weights = gather_halves(mix_out_shard, fsdp, f, 1, small_ff)
    n1, xhat_all, g, trig, kt, vt, qt, dot = project(
        at, inputs, cotangent, over_tp(far_z, far_x), over_tp(others_z, others_x), trig, weights,
        query_key_value_bias, first_scale, first_shift,
    )
    def over_core(keep, send, *earlier):
        v = keep.astype(F32) + tie(swap(send, "tp", 4, 1), *earlier).astype(F32)
        return v.reshape(2, 2, quarter, width)

    def over_x(v, *earlier):
        return v[:, 0] + tie(swap(v[:, 1].astype(BF16), "tp", 4, 2), *earlier).astype(F32)

    per_head = []
    for h in range(heads):
        after = ()
        if h == 1:
            early = over_core(keep_e, send_e, per_head[0][0])
            ff_rest = small_ff
            if split:
                ff_rest = tie(swap(ff_second, "fsdp", 2, 1), per_head[0][0])
                ff_rest = ff_first + ff_rest.astype(F32)
            after = (early, ff_rest)
        if h == heads - 1:
            early = over_x(early, per_head[h - 1][0])
            after = (early,)
        per_head.append(attention(h, after, qt, dot, kt, vt, trig))
    o, dq, dk, dv = zip(*per_head)
    ff_quarter = quarter_sum(ff_rest, c, o[-1]) if split else small_ff
    keep_o, send_o, mix_other, small_other = back(
        False, split, at, (dk, dv), n1, xhat_all, weights, first_scale, ()
    )
    keep_b, send_b, out_part = branch(o, g, tie(ff, keep_o), weights)
    keep_w, send_w, late_first, late_second = back(
        True, split, at, (dq, dk, dv), n1, xhat_all, weights, tie(first_scale, ff_quarter),
        (a2, small_ff, small_other, mix_other, out_part),
    )
    half_o = over_core(keep_o, send_o)
    half_b = over_core(keep_b, send_b)
    half_w = over_core(keep_w, send_w)

    def over_ctx(v, distance):
        return swap(v.astype(BF16), "ctx", 4, distance).astype(F32)

    def gather_tp(mine, theirs):
        ours = jnp.stack([mine, theirs]).astype(BF16)
        pair = jnp.stack([ours, swap(ours, "tp", 4, 2)])
        core = swap(pair, "tp", 4, 1)
        pieces = by_xor((pair[0], core[0], pair[1], core[1]), t)
        pieces = jnp.concatenate(pieces, axis=1)
        return jnp.stack([jnp.where(s == 0, pieces[0], pieces[1]),
                          jnp.where(s == 0, pieces[1], pieces[0])]).astype(F32)

    sums_b = over_x(half_b)
    block_out = gather_tp(sums_b[0], over_ctx(sums_b[1], 2) + early[0])
    block_out = (
        inputs.astype(F32) + block_out + (attention_output_bias + down_projection_bias)
    )

    sums_o = over_x(half_o)
    sums_w = over_x(half_w)
    a = jnp.stack([
        sums_w[0] + over_ctx(sums_o[0], 1),
        over_ctx(sums_w[1], 2) + over_ctx(sums_o[1], 3) + early[1],
    ])
    xhat, inv = xhat_of(jnp.concatenate([x_mine, x_theirs], axis=0).astype(F32))
    norm_grad = inv * (
        a
        - jnp.mean(a, axis=-1, keepdims=True)
        - xhat * jnp.mean(a * xhat, axis=-1, keepdims=True)
    )
    inputs_grad = cotangent.astype(F32) + gather_tp(norm_grad[0], norm_grad[1])

    if split:
        q = double(ff_quarter, c, (sums_w,), (norm_grad,))
        up_total = jnp.concatenate(q[:2], axis=0).astype(F32)
        down_total = jnp.concatenate(q[2:], axis=0).astype(F32)
        down_total = jnp.concatenate(
            [down_total[:, : width // 2], down_total[:, width // 2 :]], axis=0
        )
        late = late_first + tie(swap(late_second, "fsdp", 2, 1), sums_o).astype(F32)
        late = double(quarter_sum(late, c, sums_w), c)
        late = jnp.concatenate(late, axis=0).astype(F32)
        small = jnp.concatenate([late[4 * local : 4 * local + 8], late[4 * local + 8 :][:8]], axis=1)
    else:
        q = sum_over_ctx(scatter_any(ff_first, 0), c)
        up_total = jnp.concatenate(q, axis=0).astype(F32)
        q = sum_over_ctx(scatter_any(ff_second, 1), c)
        down_total = jnp.concatenate(q, axis=0).astype(F32)
        q = sum_over_ctx(scatter_any(late_first, 1), c)
        late = jnp.concatenate(q, axis=0).astype(F32)
        small = butterfly(butterfly(late_second, "fsdp", fsdp), "ctx", 4)
    mix_total = late[: 3 * local].reshape(3, local, -1).transpose(2, 0, 1)
    out_total = late[3 * local : 4 * local]
    norm_small = butterfly(small, "tp", 4)
    bias_total = norm_small[5] * 0.25
    return (
        block_out,
        inputs_grad,
        mix_total,
        small[6, : 3 * local].reshape(3, local),
        out_total,
        bias_total,
        up_total,
        small[4, :hidden],
        down_total,
        bias_total,
        norm_small[0],
        norm_small[1],
        norm_small[2],
        norm_small[3],
    )


def solution(mesh):
    in_specs = (
        P("fsdp", "ctx", None),
        P("fsdp", None),
        P("fsdp", None, "tp"),
        P(None, "tp"),
        P("tp", "fsdp"),
        P(),
        P("fsdp", "tp"),
        P("tp"),
        P("tp", "fsdp"),
        P(),
        P(),
        P(),
        P(),
        P(),
        P("fsdp", "ctx", None),
    )
    out_specs = (
        P("fsdp", "ctx", None),
        P("fsdp", "ctx", None),
        P("fsdp", None, "tp"),
        P(None, "tp"),
        P("tp", "fsdp"),
        P(),
        P("fsdp", "tp"),
        P("tp"),
        P("tp", "fsdp"),
        P(),
        P(),
        P(),
        P(),
        P(),
    )
    body = functools.partial(shards, dict(mesh.shape))
    return jax.shard_map(body, mesh=mesh, in_specs=in_specs, out_specs=out_specs, check_vma=False)
```

```python
import functools

import jax
import jax.numpy as jnp
from jax import lax
from jax.experimental import pallas as pl
from jax.experimental.pallas import tpu as pltpu
from jax.sharding import PartitionSpec as P

HEAD = 64
ROT = 16
HALF = ROT // 2
EPS = 1e-5
NEG = -1e30
STEP = 256
F32 = jnp.float32
BF16 = jnp.bfloat16
MIB = 1024 * 1024


def mm(a, b, ca=1, cb=0):
    return lax.dot_general(a, b, (((ca,), (cb,)), ((), ())), preferred_element_type=F32)


def params(mib):
    return pltpu.CompilerParams(vmem_limit_bytes=mib * MIB)


def cost(flops, moved, exps=0):
    return pl.CostEstimate(flops=int(flops), bytes_accessed=int(moved), transcendentals=int(exps))


def xhat_of(x):
    width = x.shape[-1]
    centred = x - jnp.sum(x, axis=-1, keepdims=True) * (1.0 / width)
    spread = jnp.sum(centred * centred, axis=-1, keepdims=True) * (1.0 / width)
    inv = lax.rsqrt(spread + EPS)
    return centred * inv, inv


def row_of(ref):
    return ref[...].reshape(1, -1)


def shape(*dims):
    return jax.ShapeDtypeStruct(dims, F32)


def low_shape(*dims):
    return jax.ShapeDtypeStruct(dims, BF16)


def two_quarters(width, seq_of):
    def piece(high):
        return pl.BlockSpec(
            (1, STEP // 2, width), lambda i, at: (seq_of(i, at), at[2] ^ (i % 2 + high), 0)
        )

    return [piece(0), piece(2)]


def project_kernel(at, xa, xb, ga, gb, fz, fx, fc, nz, nx, nc, ta, tb, w_ref, b_ref, s1, b1,
                   n1_ref, xhat_ref, g_ref, trig_ref, k_ref, v_ref, q_ref, do_ref, x, bias):
    i = pl.program_id(0)
    wide = k_ref.shape[0]
    q = STEP // 2
    b = jnp.maximum(i // 2 - 2, 0)

    @pl.when(i == 0)
    def _():
        for j in range(3):
            line = jnp.broadcast_to(b_ref[j : j + 1, :], (8, wide))
            bias[j * wide : (j + 1) * wide, :] = line.T[:, 0:1]

    @pl.when(i < 2)
    def _():
        x[:q, :] = xa[0]
        x[q:, :] = xb[0]
        g_ref[:q, :] = ga[0]
        g_ref[q:, :] = gb[0]

    @pl.when(i == 2)
    def _():
        x[:q, :] = fz[0]
        x[q:, :] = fx[0]
        g_ref[:q, :] = fz[1]
        g_ref[q:, :] = fx[1]

    @pl.when(i == 3)
    def _():
        x[:q, :] = fc[0, 0]
        x[q:, :] = fc[1, 0]
        g_ref[:q, :] = fc[0, 1]
        g_ref[q:, :] = fc[1, 1]

    @pl.when((i >= 4) & (i % 2 == 0))
    def _():
        x[:q, :] = nz[b]
        x[q:, :] = nx[b]

    @pl.when((i >= 4) & (i % 2 == 1))
    def _():
        x[:q, :] = nc[0, b]
        x[q:, :] = nc[1, b]

    trig_ref[:, :q] = ta[0]
    trig_ref[:, q:] = tb[0]
    trig = trig_ref[...]
    cosine, sine = trig[:HALF], trig[HALF:ROT]
    xhat, _ = xhat_of(x[...].astype(F32))
    xhat_ref[...] = xhat.astype(BF16)
    n1 = (xhat * row_of(s1) + row_of(b1)).astype(BF16)
    n1_ref[...] = n1

    def rotated(ref, mixed, factor):
        for h in range(0, wide, HEAD):
            a, b = mixed[h : h + HALF], mixed[h + HALF : h + ROT]
            turned = jnp.concatenate([a * cosine - b * sine, b * cosine + a * sine], axis=0)
            ref[h : h + ROT, :] = turned.astype(BF16) * factor
            ref[h + ROT : h + HEAD, :] = mixed[h + ROT : h + HEAD].astype(BF16) * factor

    mixed = mm(w_ref[wide : 3 * wide, :], n1, 1, 1) + bias[wide:, :]
    rotated(k_ref, mixed[:wide], BF16(1.0))
    v_ref[...] = mixed[wide:].astype(BF16)

    @pl.when(i < 4)
    def _():
        rotated(q_ref, mm(w_ref[:wide, :], n1, 1, 1) + bias[:wide, :], BF16(HEAD**-0.5))
        do_ref[...] = mm(w_ref[3 * wide :, :], g_ref[...], 1, 1).astype(BF16)


def project(at, x, g, far, others, trig, weights, bias, scale, offset):
    width = x.shape[2]
    rows = 8 * STEP
    wide = bias.shape[1]
    tall = trig.shape[1]

    def pick(high):
        def place(i, at):
            b = i // 2
            block = at[1] ^ (b % 2 * 2 + b // 2)
            return (at[0], 0, block * 4 + (at[2] ^ (i % 2 + high)))

        return pl.BlockSpec((1, tall, STEP // 2), place)

    def whole(v):
        return pl.BlockSpec(v.shape, lambda i, at: (0,) * v.ndim)

    def piece(high):
        return pl.BlockSpec(
            (1, STEP // 2, width), lambda i, at: (at[0], at[2] ^ (jnp.minimum(i, 1) + high), 0)
        )

    pieces = [piece(0), piece(2)]
    row = pl.BlockSpec((STEP, width), lambda i, at: (i, 0))
    own_row = pl.BlockSpec((STEP, width), lambda i, at: (jnp.minimum(i, 3), 0))
    col = pl.BlockSpec((wide, STEP), lambda i, at: (0, i))
    own_col = pl.BlockSpec((wide, STEP), lambda i, at: (0, jnp.minimum(i, 3)))
    received = (*far, *others)
    fixed = (weights, bias, scale, offset)
    return pl.pallas_call(
        project_kernel,
        grid_spec=pltpu.PrefetchScalarGridSpec(
            num_scalar_prefetch=1,
            grid=(8,),
            in_specs=pieces * 2 + [whole(v) for v in received] + [pick(0), pick(2)]
            + [whole(v) for v in fixed],
            out_specs=[row, row, own_row, pl.BlockSpec((tall, STEP), lambda i, at: (0, i)),
                       col, col, own_col, own_col],
            scratch_shapes=[pltpu.VMEM((STEP, width), BF16), pltpu.VMEM((3 * wide, 1), F32)],
        ),
        out_shape=[low_shape(rows, width)] * 2
        + [low_shape(rows // 2, width), shape(tall, rows)]
        + [low_shape(wide, rows)] * 2 + [low_shape(wide, rows // 2)] * 2,
        compiler_params=params(20),
        cost_estimate=cost(6 * rows * width * wide, 8 * rows * width),
    )(at, x, x, g, g, *received, trig, trig, *fixed)


def attention_kernel(count, *refs):
    (q_ref, do_ref, k_ref, v_ref, tq_ref, tk_ref,
     o_ref, dq_ref, dk_ref, dv_ref, kn, vn, kp, dk, dv, es, dps) = refs[count:]
    i = pl.program_id(0)
    length = k_ref.shape[1]
    chunk = STEP
    steps = length // chunk

    @pl.when(i == 0)
    def _():
        kn[...] = k_ref[...].T
        vn[...] = v_ref[...].T
        kp[...] = tk_ref[ROT:, :].T[:, 0:1]
        dk[...] = jnp.zeros_like(dk)
        dv[...] = jnp.zeros_like(dv)

    qt = q_ref[...]
    dot = do_ref[...]
    qn = qt.T
    don = dot.T
    qpos = tq_ref[ROT : ROT + 1, :]
    lanes = qt.shape[1]
    fold = (chunk // 8, 8, lanes)

    top = jnp.full((8, lanes), NEG, F32)
    for j in range(steps):
        here = slice(j * chunk, (j + 1) * chunk)
        s = mm(kn[here, :], qt)
        s = jnp.where(kp[here, :] <= qpos, s, NEG)
        es[here, :] = s
        top = jnp.maximum(top, jnp.max(s.reshape(fold), axis=0))
    top = jnp.max(top, axis=0, keepdims=True)

    total = jnp.zeros((8, lanes), F32)
    inner = jnp.zeros((8, lanes), F32)
    for j in range(steps):
        here = slice(j * chunk, (j + 1) * chunk)
        e = jnp.exp(es[here, :] - top)
        dp = mm(vn[here, :], dot)
        es[here, :] = e
        dps[here, :] = dp
        total = total + jnp.sum(e.reshape(fold), axis=0)
        inner = inner + jnp.sum((e * dp).reshape(fold), axis=0)
    share = 1.0 / jnp.sum(total, axis=0, keepdims=True)
    inner = jnp.sum(inner, axis=0, keepdims=True) * share

    ot = jnp.zeros((HEAD, lanes), F32)
    dqt = jnp.zeros((HEAD, lanes), F32)
    for j in range(steps):
        here = slice(j * chunk, (j + 1) * chunk)
        p = es[here, :] * share
        ds = (p * (dps[here, :] - inner)).astype(BF16)
        p = p.astype(BF16)
        dv[here, :] += mm(p, don)
        dk[here, :] += mm(ds, qn)
        ot = ot + mm(v_ref[:, here], p)
        dqt = dqt + mm(k_ref[:, here], ds)
    o_ref[...] = ot.astype(BF16)

    def unrotated(grad, trig):
        cosine, sine = trig[:HALF], trig[HALF:ROT]
        a, b = grad[:HALF], grad[HALF:ROT]
        turned = jnp.concatenate([a * cosine + b * sine, b * cosine - a * sine], axis=0)
        return turned.astype(BF16), grad[ROT:].astype(BF16)

    dq_ref[:ROT, :], dq_ref[ROT:, :] = unrotated(dqt * (HEAD**-0.5), tq_ref[...])

    @pl.when(i == pl.num_programs(0) - 1)
    def _():
        dk_ref[:ROT, :], dk_ref[ROT:, :] = unrotated(dk[...].T, tk_ref[...])
        dv_ref[...] = dv[...].T.astype(BF16)


def attention(h, after, qt, dot, kt, vt, trig):
    rows, length = qt.shape[1], kt.shape[1]
    lanes = STEP
    tall = trig.shape[0]
    q_spec = pl.BlockSpec((HEAD, lanes), lambda i: (h, i))
    k_spec = pl.BlockSpec((HEAD, length), lambda i: (h, 0))
    return pl.pallas_call(
        functools.partial(attention_kernel, len(after)),
        grid=(rows // lanes,),
        in_specs=[pl.BlockSpec(memory_space=pl.ANY)] * len(after)
        + [q_spec, q_spec, k_spec, k_spec, pl.BlockSpec((tall, lanes), lambda i: (0, i)),
           pl.BlockSpec((tall, length), lambda i: (0, 0))],
        out_specs=[pl.BlockSpec((HEAD, lanes), lambda i: (0, i))] * 2
        + [pl.BlockSpec((HEAD, length), lambda i: (0, 0))] * 2,
        out_shape=[low_shape(HEAD, rows)] * 2 + [low_shape(HEAD, length)] * 2,
        scratch_shapes=[
            pltpu.VMEM((length, HEAD), BF16),
            pltpu.VMEM((length, HEAD), BF16),
            pltpu.VMEM((length, 1), F32),
            pltpu.VMEM((length, HEAD), F32),
            pltpu.VMEM((length, HEAD), F32),
            pltpu.VMEM((length, lanes), F32),
            pltpu.VMEM((length, lanes), F32),
        ],
        compiler_params=params(16),
        cost_estimate=cost(40 * rows * length * HEAD, 16 * HEAD * length, rows * length),
    )(*after, qt, dot, kt, vt, trig, trig)


def forward_kernel(split, at, xa, xb, ga, gb, up_ref, bias_ref, down_ref, s2_ref, b2_ref,
                   ff_ref, a_ref, keep_ref, send_ref, small_ref, first_ref, second_ref, *scratch):
    i = pl.program_id(0)
    up_part, down_part = scratch if split else (first_ref, second_ref)

    @pl.when(i == 0)
    def _():
        up_part[...] = jnp.zeros_like(up_part)
        down_part[...] = jnp.zeros_like(down_part)
        small_ref[...] = jnp.zeros_like(small_ref)

    xhat, _ = xhat_of(jnp.concatenate([xa[0], xb[0]], axis=0).astype(F32))
    g = jnp.concatenate([ga[0], gb[0]], axis=0)
    scale = row_of(s2_ref)
    n2 = (xhat * scale + row_of(b2_ref)).astype(BF16)
    up = mm(n2, up_ref[...]) + row_of(bias_ref)
    cdf = 0.5 + 0.5 * lax.erf(up * (0.5**0.5))
    act = (up * cdf).astype(BF16)
    slope = cdf + up * (jnp.exp(up * up * -0.5) * 0.3989422804014327)
    up_grad = (mm(g, down_ref[...], 1, 1) * slope).astype(BF16)
    ff = mm(act, down_ref[...]).astype(BF16)
    second = mm(up_grad, up_ref[...], 1, 1)
    a = (second * scale).astype(BF16)

    @pl.when(i < 2)
    def _():
        ff_ref[...] = ff
        a_ref[...] = a

    @pl.when(i == 2)
    def _():
        keep_ref[0] = ff
        keep_ref[1] = a

    @pl.when(i == 3)
    def _():
        send_ref[0] = ff
        send_ref[1] = a

    up_part[...] += mm(n2, up_grad, 0, 0)
    down_part[...] += mm(act, g, 0, 0)
    small_ref[0:1, :] += jnp.sum(up_grad.astype(F32), axis=0, keepdims=True)
    small_ref[1:2, :] += jnp.sum(g.astype(F32), axis=0, keepdims=True)
    small_ref[2:3, :] += jnp.sum(second * xhat, axis=0, keepdims=True)
    small_ref[3:4, :] += jnp.sum(second, axis=0, keepdims=True)

    if split:
        half = up_part.shape[0] // 2

        @pl.when(i == pl.num_programs(0) - 1)
        def _():
            for ref, f in ((first_ref, at[3]), (second_ref, 1 - at[3])):
                piece = pl.ds(pl.multiple_of(f * half, 128), half)
                ref[:half, :] = up_part[piece, :].astype(ref.dtype)
                ref[half:, :half] = down_part[:half, piece].astype(ref.dtype)
                ref[half:, half:] = down_part[half:, piece].astype(ref.dtype)


def feed_forward(split, at, x, g, up, bias, down, scale, offset):
    width = x.shape[2]
    hidden = up.shape[1]
    pieces = two_quarters(width, lambda i, at: at[0] ^ (i // 2))
    own_row = pl.BlockSpec((STEP, width), lambda i, at: (jnp.minimum(i, 1), 0))

    def whole(*dims):
        return pl.BlockSpec(dims, lambda i, at: (0,) * len(dims))

    if split:
        assert width == hidden
        parts = [shape(width, hidden), low_shape(width, hidden)]
    else:
        parts = [shape(width, hidden), shape(hidden, width)]
    slots = whole(2, STEP, width)
    return pl.pallas_call(
        functools.partial(forward_kernel, split),
        grid_spec=pltpu.PrefetchScalarGridSpec(
            num_scalar_prefetch=1,
            grid=(4,),
            in_specs=pieces * 2 + [whole(width, hidden), whole(hidden), whole(hidden, width),
                                   whole(width), whole(width)],
            out_specs=[own_row, own_row, slots, slots, whole(8, width)]
            + [whole(*p.shape) for p in parts],
            scratch_shapes=[pltpu.VMEM((width, hidden), F32), pltpu.VMEM((hidden, width), F32)]
            if split
            else [],
        ),
        out_shape=[low_shape(2 * STEP, width)] * 2 + [low_shape(2, STEP, width)] * 2
        + [shape(8, width)] + parts,
        compiler_params=params(28),
        cost_estimate=cost(48 * STEP * width * hidden, 16 * MIB, 8 * STEP * hidden),
    )(at, x, x, g, g, up, bias, down, scale, offset)


def emit(keep_ref, send_ref, v, own_ref=None):
    i = pl.program_id(0)
    if own_ref is not None:
        v = jnp.where(i < 2, v + own_ref[...].astype(F32), v)

    @pl.when(i % 2 == 0)
    def _():
        keep_ref[0] = v.astype(BF16)

    @pl.when(i % 2 == 1)
    def _():
        send_ref[0] = v.astype(BF16)


def branch_kernel(heads, *refs):
    o = refs[:heads]
    g_ref, ff_ref, w_ref, keep_ref, send_ref, out = refs[heads:]
    wide = heads * HEAD

    @pl.when(pl.program_id(0) == 0)
    def _():
        out[...] = jnp.zeros_like(out)

    ot = jnp.concatenate([r[...] for r in o], axis=0)
    emit(keep_ref, send_ref, mm(ot, w_ref[...], 0, 0), ff_ref)
    out[...] += mm(ot, g_ref[...])


def branch(o, g, ff, weights):
    rows, width = g.shape
    heads = len(o)
    wide = heads * HEAD
    row = pl.BlockSpec((STEP, width), lambda i: (i, 0))
    slots = pl.BlockSpec((1, STEP, width), lambda i: (i // 2, 0, 0))
    return pl.pallas_call(
        functools.partial(branch_kernel, heads),
        grid=(rows // STEP,),
        in_specs=[pl.BlockSpec((HEAD, STEP), lambda i: (0, i))] * heads
        + [row, pl.BlockSpec((STEP, width), lambda i: (jnp.minimum(i, 1), 0)),
           pl.BlockSpec((wide, width), lambda i: (3, 0))],
        out_specs=[slots, slots, pl.BlockSpec((wide, width), lambda i: (0, 0))],
        out_shape=[low_shape(2, STEP, width)] * 2 + [shape(wide, width)],
        compiler_params=params(12),
        cost_estimate=cost(4 * rows * width * wide, 8 * MIB),
    )(*o, g, ff, weights)


def back_kernel(own, split, heads, at, *refs):
    count = 3 if own else 2
    grads, refs = refs[: count * heads], refs[count * heads :]
    n1_ref, xhat_ref, w_ref, s1_ref, *refs = refs
    if own:
        (a2_ref, small_ff, small_other, mix_other, out_part,
         keep_ref, send_ref, first_ref, second_ref, mix, small) = refs
    else:
        keep_ref, send_ref, mix, small = refs
    i = pl.program_id(0)
    wide = heads * HEAD
    tall = mix.shape[0]

    @pl.when(i == 0)
    def _():
        if own:
            mix[:wide, :] = jnp.zeros((wide, mix.shape[1]), F32)
            mix[wide:, :] = mix_other[...]
            small[...] = small_other[...]
        else:
            mix[...] = jnp.zeros_like(mix)
            small[...] = jnp.zeros_like(small)

    grad = jnp.concatenate([r[...] for r in grads], axis=0)
    first = mm(grad, w_ref[3 * wide - tall : 3 * wide, :], 0, 0)
    a = first * row_of(s1_ref)
    emit(keep_ref, send_ref, a, a2_ref if own else None)
    mix[...] += mm(grad, n1_ref[...])
    small[0:1, :] += jnp.sum(first * xhat_ref[...].astype(F32), axis=0, keepdims=True)
    small[1:2, :] += jnp.sum(first, axis=0, keepdims=True)
    ones = jnp.ones((8, grad.shape[1]), BF16)
    small[6:7, 3 * wide - tall : 3 * wide] += mm(ones, grad, 1, 1)[0:1]

    if own:
        @pl.when(i == pl.num_programs(0) - 1)
        def _():
            small[2:4, :] = small_ff[2:4, :]
            small[4:6, :] = small_ff[0:2, :]
            if split:
                half = mix.shape[1] // 2
                vectors = small[...].astype(BF16)
                for ref, f in ((first_ref, at[3]), (second_ref, 1 - at[3])):
                    piece = pl.ds(pl.multiple_of(f * half, 128), half)
                    ref[: 3 * wide, :] = mix[:, piece].astype(ref.dtype)
                    ref[3 * wide : 4 * wide, :] = out_part[:, piece].astype(ref.dtype)
                    both = jnp.concatenate([vectors[:, :half], vectors[:, half:]], axis=0)
                    ref[4 * wide : 4 * wide + 16, :] = both.astype(ref.dtype)
                    ref[4 * wide + 16 :, :] = jnp.zeros((48, half), ref.dtype)
            else:
                first_ref[: 3 * wide, :] = mix[...]
                first_ref[3 * wide :, :] = out_part[...]
                second_ref[...] = small[...]


def back(own, split, at, grads, n1, xhat, weights, scale, extra):
    rows, width = n1.shape[0] // 2, n1.shape[1]
    heads = len(grads[0])
    wide = heads * HEAD
    tall = 3 * wide if own else 2 * wide
    offset = 0 if own else rows // STEP
    row = pl.BlockSpec((STEP, width), lambda i, at: (i + offset, 0))
    col = pl.BlockSpec((HEAD, STEP), lambda i, at: (0, i + offset))
    slots = pl.BlockSpec((1, STEP, width), lambda i, at: (i // 2, 0, 0))

    def whole(*dims):
        return pl.BlockSpec(dims, lambda i, at: (0,) * len(dims))

    half = width // 2
    specs = [col] * (len(grads) * heads) + [row, row, whole(4 * wide, width), whole(width)]
    if not own:
        parts = [shape(tall, width), shape(8, width)]
        scratch = []
    else:
        specs += [pl.BlockSpec((STEP, width), lambda i, at: (jnp.minimum(i, 1), 0)),
                  whole(8, width), whole(8, width), whole(2 * wide, width),
                  whole(wide, width)]
        scratch = [pltpu.VMEM((tall, width), F32), pltpu.VMEM((8, width), F32)]
        if split:
            parts = [shape(4 * wide + 64, half), low_shape(4 * wide + 64, half)]
        else:
            parts = [shape(4 * wide, width), shape(8, width)]
    return pl.pallas_call(
        functools.partial(back_kernel, own, split, heads),
        grid_spec=pltpu.PrefetchScalarGridSpec(
            num_scalar_prefetch=1,
            grid=(rows // STEP,),
            in_specs=specs,
            out_specs=[slots, slots] + [whole(*p.shape) for p in parts],
            scratch_shapes=scratch,
        ),
        out_shape=[low_shape(2, STEP, width)] * 2 + parts,
        compiler_params=params(20),
        cost_estimate=cost(4 * rows * width * tall, 10 * MIB),
    )(at, *[v for vs in grads for v in vs], n1, xhat, weights, scale, *extra)


def swap(v, axis, size, distance):
    return lax.ppermute(v, axis, [(i, i ^ distance) for i in range(size)])


def by_xor(pieces, index):
    low, high = (index & 1) == 1, (index & 2) == 2
    a, b, c, d = pieces
    a, b, c, d = (jnp.where(low, b, a), jnp.where(low, a, b),
                  jnp.where(low, d, c), jnp.where(low, c, d))
    return (jnp.where(high, c, a), jnp.where(high, d, b),
            jnp.where(high, a, c), jnp.where(high, b, d))


def tie(v, *earlier):
    return lax.optimization_barrier((v, *earlier))[0]


def gather_halves(shard, size, mine, dim, *earlier):
    if size != 2:
        return lax.all_gather(shard, "fsdp", axis=dim, tiled=True)
    other = swap(shard, "fsdp", 2, 1)
    if earlier:
        other = tie(other, *earlier)
    first = mine == 0
    return jnp.concatenate(
        [jnp.where(first, shard, other), jnp.where(first, other, shard)], axis=dim
    )


def scatter_any(part, dim):
    return lax.psum_scatter(
        part.astype(BF16), "fsdp", scatter_dimension=dim, tiled=True
    ).astype(F32)


def quarter_sum(v, c, *earlier):
    rows = v.shape[0] // 4
    mine = 2 * (c % 2) + c // 2

    def part(j):
        return lax.dynamic_slice_in_dim(v, (mine ^ j) * rows, rows, 0)

    total = part(0)
    for distance, j in ((3, 3), (2, 1), (1, 2)):
        sent = swap(part(j).astype(BF16), "ctx", 4, distance)
        total = total + tie(sent, *earlier).astype(F32)
    return total


def pair_up(v, *earlier):
    v = v.astype(BF16)
    return jnp.stack([v, tie(swap(v, "ctx", 4, 2), *earlier)])


def double(pair, c, *earlier):
    others = tie(swap(pair, "ctx", 4, 1), *earlier)
    return by_xor([pair[0], pair[1], others[0], others[1]], 2 * (c % 2) + c // 2)


def sum_over_ctx(v, c):
    return double(pair_up(quarter_sum(v, c)), c)


def butterfly(v, axis_name, size):
    distance = 1
    while distance < size:
        v = v + swap(v, axis_name, size, distance)
        distance *= 2
    return v


def shards(
    sizes,
    inputs,
    positions,
    query_key_value_weight,
    query_key_value_bias,
    attention_output_weight,
    attention_output_bias,
    up_projection_weight,
    up_projection_bias,
    down_projection_weight,
    down_projection_bias,
    first_scale,
    first_shift,
    second_scale,
    second_shift,
    cotangent,
):
    fsdp = sizes["fsdp"]
    split = fsdp == 2
    seq_count, block, width = inputs.shape
    assert seq_count == 2 and sizes["ctx"] == 4 and sizes["tp"] == 4 and block == 2 * STEP
    length = positions.shape[1]
    local = query_key_value_weight.shape[2]
    heads = local // HEAD
    hidden = up_projection_weight.shape[1]
    quarter = block // 4
    f = lax.axis_index("fsdp")
    c = lax.axis_index("ctx")
    t = lax.axis_index("tp")
    s = c // 2
    at = jnp.stack([s, c, t, f]).astype(jnp.int32)

    def my_quarter(v, seq):
        return lax.dynamic_slice(v, (seq, t * quarter, 0), (1, quarter, width))

    x_mine, x_theirs = my_quarter(inputs, s), my_quarter(inputs, 1 - s)
    g_theirs = my_quarter(cotangent, 1 - s)
    far_z = swap(jnp.concatenate([x_theirs, g_theirs], axis=0), "ctx", 4, 2)
    cross = swap(x_theirs, "ctx", 4, 3)
    near = swap(x_mine, "ctx", 4, 1)

    others_z = jnp.concatenate([near, cross], axis=0)
    others_x = swap(others_z, "tp", 4, 2)
    far_x = swap(far_z, "tp", 4, 2)

    wup = gather_halves(up_projection_weight, fsdp, f, 0)
    wdown = gather_halves(down_projection_weight, fsdp, f, 1)
    mix_shard = query_key_value_weight.transpose(1, 2, 0).reshape(3 * local, -1)
    mix_out_shard = jnp.concatenate([mix_shard, attention_output_weight], axis=0)

    inverse = 10000.0 ** (-2.0 * jnp.arange(HALF, dtype=F32) / ROT)
    places = positions.astype(F32)[:, None, :]
    angles = inverse[None, :, None] * places
    trig = jnp.concatenate(
        [jnp.cos(angles), jnp.sin(angles), jnp.broadcast_to(places, angles.shape)], axis=1
    )

    ff, a2, keep_e, send_e, small_ff, ff_first, ff_second = feed_forward(
        split, at, inputs, cotangent, wup, up_projection_bias, wdown, second_scale, second_shift
    )

    def over_tp(v_z, v_x):
        v_x = tie(v_x, small_ff)
        return v_z, v_x, swap(jnp.stack([v_z, v_x]), "tp", 4, 1)

    weights = gather_halves(mix_out_shard, fsdp, f, 1, small_ff)
    n1, xhat_all, g, trig, kt, vt, qt, dot = project(
        at, inputs, cotangent, over_tp(far_z, far_x), over_tp(others_z, others_x), trig, weights,
        query_key_value_bias, first_scale, first_shift,
    )
    def over_core(keep, send, *earlier):
        v = keep.astype(F32) + tie(swap(send, "tp", 4, 1), *earlier).astype(F32)
        return v.reshape(2, 2, quarter, width)

    def over_x(v, *earlier):
        return v[:, 0] + tie(swap(v[:, 1].astype(BF16), "tp", 4, 2), *earlier).astype(F32)

    per_head = []
    for h in range(heads):
        after = ()
        if h == 1:
            early = over_core(keep_e, send_e, per_head[0][0])
            ff_rest = small_ff
            if split:
                ff_rest = tie(swap(ff_second, "fsdp", 2, 1), per_head[0][0])
                ff_rest = ff_first + ff_rest.astype(F32)
            after = (early, ff_rest)
        if h == heads - 1:
            early = over_x(early, per_head[h - 1][0])
            after = (early,)
        per_head.append(attention(h, after, qt, dot, kt, vt, trig))
    o, dq, dk, dv = zip(*per_head)
    ff_quarter = quarter_sum(ff_rest, c, o[-1]) if split else small_ff
    keep_b, send_b, out_part = branch(o, g, ff, weights)
    keep_o, send_o, mix_other, small_other = back(
        False, split, at, (dk, dv), n1, xhat_all, weights, tie(first_scale, keep_b), ()
    )
    half_b = over_core(keep_b, send_b)
    keep_w, send_w, late_first, late_second = back(
        True, split, at, (dq, dk, dv), n1, xhat_all, weights,
        tie(first_scale, ff_quarter, half_b), (a2, small_ff, small_other, mix_other, out_part),
    )
    half_o = over_core(keep_o, send_o)
    half_w = over_core(keep_w, send_w)
    ff_pair = pair_up(ff_quarter, half_w) if split else half_w

    def over_ctx(v, distance, *earlier):
        return tie(swap(v.astype(BF16), "ctx", 4, distance), *earlier).astype(F32)

    def gather_tp(ours):
        pair = jnp.stack([ours, swap(ours, "tp", 4, 2)])
        core = swap(pair, "tp", 4, 1)
        pieces = by_xor((pair[0], core[0], pair[1], core[1]), t)
        pieces = jnp.concatenate(pieces, axis=1)
        return jnp.stack([jnp.where(s == 0, pieces[0], pieces[1]),
                          jnp.where(s == 0, pieces[1], pieces[0])]).astype(F32)

    sums_b = over_x(half_b, half_w)
    branches = jnp.stack([sums_b[0], over_ctx(sums_b[1], 2) + early[0]]).astype(BF16)
    block_out = gather_tp(branches)
    block_out = (
        inputs.astype(F32) + block_out + (attention_output_bias + down_projection_bias)
    )

    sums_o = over_x(half_o, ff_pair)
    sums_w = over_x(half_w)
    sums_w = sums_w + over_ctx(sums_o, 1)
    a = jnp.stack([sums_w[0], over_ctx(sums_w[1], 2, branches) + early[1]])
    xhat, inv = xhat_of(jnp.concatenate([x_mine, x_theirs], axis=0).astype(F32))
    norm_grad = inv * (
        a
        - jnp.mean(a, axis=-1, keepdims=True)
        - xhat * jnp.mean(a * xhat, axis=-1, keepdims=True)
    )
    norm_grad = norm_grad.astype(BF16)
    inputs_grad = cotangent.astype(F32) + gather_tp(norm_grad)

    if split:
        q = double(ff_pair, c, norm_grad)
        up_total = jnp.concatenate(q[:2], axis=0).astype(F32)
        down_total = jnp.concatenate(q[2:], axis=0).astype(F32)
        down_total = jnp.concatenate(
            [down_total[:, : width // 2], down_total[:, width // 2 :]], axis=0
        )
        late = late_first + tie(swap(late_second, "fsdp", 2, 1), sums_o).astype(F32)
        late = double(pair_up(quarter_sum(late, c, sums_w), norm_grad), c)
        late = jnp.concatenate(late, axis=0).astype(F32)
        small = jnp.concatenate([late[4 * local : 4 * local + 8], late[4 * local + 8 :][:8]], axis=1)
    else:
        q = sum_over_ctx(scatter_any(ff_first, 0), c)
        up_total = jnp.concatenate(q, axis=0).astype(F32)
        q = sum_over_ctx(scatter_any(ff_second, 1), c)
        down_total = jnp.concatenate(q, axis=0).astype(F32)
        q = sum_over_ctx(scatter_any(late_first, 1), c)
        late = jnp.concatenate(q, axis=0).astype(F32)
        small = butterfly(butterfly(late_second, "fsdp", fsdp), "ctx", 4)
    mix_total = late[: 3 * local].reshape(3, local, -1).transpose(2, 0, 1)
    out_total = late[3 * local : 4 * local]
    norm_small = butterfly(small, "tp", 4)
    bias_total = norm_small[5] * 0.25
    return (
        block_out,
        inputs_grad,
        mix_total,
        small[6, : 3 * local].reshape(3, local),
        out_total,
        bias_total,
        up_total,
        small[4, :hidden],
        down_total,
        bias_total,
        norm_small[0],
        norm_small[1],
        norm_small[2],
        norm_small[3],
    )


def solution(mesh):
    in_specs = (
        P("fsdp", "ctx", None),
        P("fsdp", None),
        P("fsdp", None, "tp"),
        P(None, "tp"),
        P("tp", "fsdp"),
        P(),
        P("fsdp", "tp"),
        P("tp"),
        P("tp", "fsdp"),
        P(),
        P(),
        P(),
        P(),
        P(),
        P("fsdp", "ctx", None),
    )
    out_specs = (
        P("fsdp", "ctx", None),
        P("fsdp", "ctx", None),
        P("fsdp", None, "tp"),
        P(None, "tp"),
        P("tp", "fsdp"),
        P(),
        P("fsdp", "tp"),
        P("tp"),
        P("tp", "fsdp"),
        P(),
        P(),
        P(),
        P(),
        P(),
    )
    body = functools.partial(shards, dict(mesh.shape))
    return jax.shard_map(body, mesh=mesh, in_specs=in_specs, out_specs=out_specs, check_vma=False)
```

```python
import functools

import jax
import jax.numpy as jnp
from jax import lax
from jax.experimental import pallas as pl
from jax.experimental.pallas import tpu as pltpu
from jax.sharding import PartitionSpec as P

HEAD = 64
ROT = 16
HALF = ROT // 2
EPS = 1e-5
NEG = -1e30
STEP = 256
F32 = jnp.float32
BF16 = jnp.bfloat16
MIB = 1024 * 1024


def mm(a, b, ca=1, cb=0):
    return lax.dot_general(a, b, (((ca,), (cb,)), ((), ())), preferred_element_type=F32)


def params(mib):
    return pltpu.CompilerParams(vmem_limit_bytes=mib * MIB)


def cost(flops, moved, exps=0):
    return pl.CostEstimate(flops=int(flops), bytes_accessed=int(moved), transcendentals=int(exps))


def xhat_of(x):
    width = x.shape[-1]
    centred = x - jnp.sum(x, axis=-1, keepdims=True) * (1.0 / width)
    spread = jnp.sum(centred * centred, axis=-1, keepdims=True) * (1.0 / width)
    inv = lax.rsqrt(spread + EPS)
    return centred * inv, inv


def row_of(ref):
    return ref[...].reshape(1, -1)


def shape(*dims):
    return jax.ShapeDtypeStruct(dims, F32)


def low_shape(*dims):
    return jax.ShapeDtypeStruct(dims, BF16)


def two_quarters(width, seq_of):
    def piece(high):
        return pl.BlockSpec(
            (1, STEP // 2, width), lambda i, at: (seq_of(i, at), at[2] ^ (i % 2 + high), 0)
        )

    return [piece(0), piece(2)]


def project_kernel(at, xa, xb, ga, gb, fz, fx, fc, nz, nx, nc, ta, tb, w_ref, b_ref, s1, b1,
                   n1_ref, xhat_ref, g_ref, trig_ref, k_ref, v_ref, q_ref, do_ref, x, bias):
    i = pl.program_id(0)
    wide = k_ref.shape[0]
    q = STEP // 2
    b = jnp.maximum(i // 2 - 2, 0)

    @pl.when(i == 0)
    def _():
        for j in range(3):
            line = jnp.broadcast_to(b_ref[j : j + 1, :], (8, wide))
            bias[j * wide : (j + 1) * wide, :] = line.T[:, 0:1]

    @pl.when(i < 2)
    def _():
        x[:q, :] = xa[0]
        x[q:, :] = xb[0]
        g_ref[:q, :] = ga[0]
        g_ref[q:, :] = gb[0]

    @pl.when(i == 2)
    def _():
        x[:q, :] = fz[0]
        x[q:, :] = fx[0]
        g_ref[:q, :] = fz[1]
        g_ref[q:, :] = fx[1]

    @pl.when(i == 3)
    def _():
        x[:q, :] = fc[0, 0]
        x[q:, :] = fc[1, 0]
        g_ref[:q, :] = fc[0, 1]
        g_ref[q:, :] = fc[1, 1]

    @pl.when((i >= 4) & (i % 2 == 0))
    def _():
        x[:q, :] = nz[b]
        x[q:, :] = nx[b]

    @pl.when((i >= 4) & (i % 2 == 1))
    def _():
        x[:q, :] = nc[0, b]
        x[q:, :] = nc[1, b]

    trig_ref[:, :q] = ta[0]
    trig_ref[:, q:] = tb[0]
    trig = trig_ref[...]
    cosine, sine = trig[:HALF], trig[HALF:ROT]
    xhat, _ = xhat_of(x[...].astype(F32))
    xhat_ref[...] = xhat.astype(BF16)
    n1 = (xhat * row_of(s1) + row_of(b1)).astype(BF16)
    n1_ref[...] = n1

    def rotated(ref, mixed, factor):
        for h in range(0, wide, HEAD):
            a, b = mixed[h : h + HALF], mixed[h + HALF : h + ROT]
            turned = jnp.concatenate([a * cosine - b * sine, b * cosine + a * sine], axis=0)
            ref[h : h + ROT, :] = turned.astype(BF16) * factor
            ref[h + ROT : h + HEAD, :] = mixed[h + ROT : h + HEAD].astype(BF16) * factor

    mixed = mm(w_ref[wide : 3 * wide, :], n1, 1, 1) + bias[wide:, :]
    rotated(k_ref, mixed[:wide], BF16(1.0))
    v_ref[...] = mixed[wide:].astype(BF16)

    @pl.when(i < 4)
    def _():
        rotated(q_ref, mm(w_ref[:wide, :], n1, 1, 1) + bias[:wide, :], BF16(HEAD**-0.5))
        do_ref[...] = mm(w_ref[3 * wide :, :], g_ref[...], 1, 1).astype(BF16)


def project(at, x, g, far, others, trig, weights, bias, scale, offset):
    width = x.shape[2]
    rows = 8 * STEP
    wide = bias.shape[1]
    tall = trig.shape[1]

    def pick(high):
        def place(i, at):
            b = i // 2
            block = at[1] ^ (b % 2 * 2 + b // 2)
            return (at[0], 0, block * 4 + (at[2] ^ (i % 2 + high)))

        return pl.BlockSpec((1, tall, STEP // 2), place)

    def whole(v):
        return pl.BlockSpec(v.shape, lambda i, at: (0,) * v.ndim)

    def piece(high):
        return pl.BlockSpec(
            (1, STEP // 2, width), lambda i, at: (at[0], at[2] ^ (jnp.minimum(i, 1) + high), 0)
        )

    pieces = [piece(0), piece(2)]
    row = pl.BlockSpec((STEP, width), lambda i, at: (i, 0))
    own_row = pl.BlockSpec((STEP, width), lambda i, at: (jnp.minimum(i, 3), 0))
    col = pl.BlockSpec((wide, STEP), lambda i, at: (0, i))
    own_col = pl.BlockSpec((wide, STEP), lambda i, at: (0, jnp.minimum(i, 3)))
    received = (*far, *others)
    fixed = (weights, bias, scale, offset)
    return pl.pallas_call(
        project_kernel,
        grid_spec=pltpu.PrefetchScalarGridSpec(
            num_scalar_prefetch=1,
            grid=(8,),
            in_specs=pieces * 2 + [whole(v) for v in received] + [pick(0), pick(2)]
            + [whole(v) for v in fixed],
            out_specs=[row, row, own_row, pl.BlockSpec((tall, STEP), lambda i, at: (0, i)),
                       col, col, own_col, own_col],
            scratch_shapes=[pltpu.VMEM((STEP, width), BF16), pltpu.VMEM((3 * wide, 1), F32)],
        ),
        out_shape=[low_shape(rows, width)] * 2
        + [low_shape(rows // 2, width), shape(tall, rows)]
        + [low_shape(wide, rows)] * 2 + [low_shape(wide, rows // 2)] * 2,
        compiler_params=params(20),
        cost_estimate=cost(6 * rows * width * wide, 8 * rows * width),
    )(at, x, x, g, g, *received, trig, trig, *fixed)


def attention_kernel(count, *refs):
    (q_ref, do_ref, k_ref, v_ref, tq_ref, tk_ref,
     o_ref, dq_ref, dk_ref, dv_ref, kn, vn, kp, dk, dv, es, dps) = refs[count:]
    i = pl.program_id(0)
    length = k_ref.shape[1]
    chunk = STEP
    steps = length // chunk

    @pl.when(i == 0)
    def _():
        kn[...] = k_ref[...].T
        vn[...] = v_ref[...].T
        kp[...] = tk_ref[ROT:, :].T[:, 0:1]
        dk[...] = jnp.zeros_like(dk)
        dv[...] = jnp.zeros_like(dv)

    qt = q_ref[...]
    dot = do_ref[...]
    qn = qt.T
    don = dot.T
    qpos = tq_ref[ROT : ROT + 1, :]
    lanes = qt.shape[1]
    fold = (chunk // 8, 8, lanes)

    top = jnp.full((8, lanes), NEG, F32)
    for j in range(steps):
        here = slice(j * chunk, (j + 1) * chunk)
        s = mm(kn[here, :], qt)
        s = jnp.where(kp[here, :] <= qpos, s, NEG)
        es[here, :] = s
        top = jnp.maximum(top, jnp.max(s.reshape(fold), axis=0))
    top = jnp.max(top, axis=0, keepdims=True)

    total = jnp.zeros((8, lanes), F32)
    inner = jnp.zeros((8, lanes), F32)
    for j in range(steps):
        here = slice(j * chunk, (j + 1) * chunk)
        e = jnp.exp(es[here, :] - top)
        dp = mm(vn[here, :], dot)
        es[here, :] = e
        dps[here, :] = dp
        total = total + jnp.sum(e.reshape(fold), axis=0)
        inner = inner + jnp.sum((e * dp).reshape(fold), axis=0)
    share = 1.0 / jnp.sum(total, axis=0, keepdims=True)
    inner = jnp.sum(inner, axis=0, keepdims=True) * share

    ot = jnp.zeros((HEAD, lanes), F32)
    dqt = jnp.zeros((HEAD, lanes), F32)
    for j in range(steps):
        here = slice(j * chunk, (j + 1) * chunk)
        p = es[here, :] * share
        ds = (p * (dps[here, :] - inner)).astype(BF16)
        p = p.astype(BF16)
        dv[here, :] += mm(p, don)
        dk[here, :] += mm(ds, qn)
        ot = ot + mm(v_ref[:, here], p)
        dqt = dqt + mm(k_ref[:, here], ds)
    o_ref[...] = ot.astype(BF16)

    def unrotated(grad, trig):
        cosine, sine = trig[:HALF], trig[HALF:ROT]
        a, b = grad[:HALF], grad[HALF:ROT]
        turned = jnp.concatenate([a * cosine + b * sine, b * cosine - a * sine], axis=0)
        return turned.astype(BF16), grad[ROT:].astype(BF16)

    dq_ref[:ROT, :], dq_ref[ROT:, :] = unrotated(dqt * (HEAD**-0.5), tq_ref[...])

    @pl.when(i == pl.num_programs(0) - 1)
    def _():
        dk_ref[:ROT, :], dk_ref[ROT:, :] = unrotated(dk[...].T, tk_ref[...])
        dv_ref[...] = dv[...].T.astype(BF16)


def attention(h, after, qt, dot, kt, vt, trig):
    rows, length = qt.shape[1], kt.shape[1]
    lanes = STEP
    tall = trig.shape[0]
    q_spec = pl.BlockSpec((HEAD, lanes), lambda i: (h, i))
    k_spec = pl.BlockSpec((HEAD, length), lambda i: (h, 0))
    return pl.pallas_call(
        functools.partial(attention_kernel, len(after)),
        grid=(rows // lanes,),
        in_specs=[pl.BlockSpec(memory_space=pl.ANY)] * len(after)
        + [q_spec, q_spec, k_spec, k_spec, pl.BlockSpec((tall, lanes), lambda i: (0, i)),
           pl.BlockSpec((tall, length), lambda i: (0, 0))],
        out_specs=[pl.BlockSpec((HEAD, lanes), lambda i: (0, i))] * 2
        + [pl.BlockSpec((HEAD, length), lambda i: (0, 0))] * 2,
        out_shape=[low_shape(HEAD, rows)] * 2 + [low_shape(HEAD, length)] * 2,
        scratch_shapes=[
            pltpu.VMEM((length, HEAD), BF16),
            pltpu.VMEM((length, HEAD), BF16),
            pltpu.VMEM((length, 1), F32),
            pltpu.VMEM((length, HEAD), F32),
            pltpu.VMEM((length, HEAD), F32),
            pltpu.VMEM((length, lanes), F32),
            pltpu.VMEM((length, lanes), F32),
        ],
        compiler_params=params(16),
        cost_estimate=cost(40 * rows * length * HEAD, 16 * HEAD * length, rows * length),
    )(*after, qt, dot, kt, vt, trig, trig)


def forward_kernel(split, at, xa, xb, ga, gb, up_ref, bias_ref, down_ref, s2_ref, b2_ref,
                   ff_ref, a_ref, keep_ref, send_ref, small_ref, first_ref, second_ref, *scratch):
    i = pl.program_id(0)
    up_part, down_part = scratch if split else (first_ref, second_ref)

    @pl.when(i == 0)
    def _():
        up_part[...] = jnp.zeros_like(up_part)
        down_part[...] = jnp.zeros_like(down_part)
        small_ref[...] = jnp.zeros_like(small_ref)

    xhat, _ = xhat_of(jnp.concatenate([xa[0], xb[0]], axis=0).astype(F32))
    g = jnp.concatenate([ga[0], gb[0]], axis=0)
    scale = row_of(s2_ref)
    n2 = (xhat * scale + row_of(b2_ref)).astype(BF16)
    up = mm(n2, up_ref[...]) + row_of(bias_ref)
    cdf = 0.5 + 0.5 * lax.erf(up * (0.5**0.5))
    act = (up * cdf).astype(BF16)
    slope = cdf + up * (jnp.exp(up * up * -0.5) * 0.3989422804014327)
    up_grad = (mm(g, down_ref[...], 1, 1) * slope).astype(BF16)
    ff = mm(act, down_ref[...]).astype(BF16)
    second = mm(up_grad, up_ref[...], 1, 1)
    a = (second * scale).astype(BF16)

    @pl.when(i < 2)
    def _():
        ff_ref[...] = ff
        a_ref[...] = a

    @pl.when(i == 2)
    def _():
        keep_ref[0] = ff
        keep_ref[1] = a

    @pl.when(i == 3)
    def _():
        send_ref[0] = ff
        send_ref[1] = a

    up_part[...] += mm(n2, up_grad, 0, 0)
    down_part[...] += mm(act, g, 0, 0)
    small_ref[0:1, :] += jnp.sum(up_grad.astype(F32), axis=0, keepdims=True)
    small_ref[1:2, :] += jnp.sum(g.astype(F32), axis=0, keepdims=True)
    small_ref[2:3, :] += jnp.sum(second * xhat, axis=0, keepdims=True)
    small_ref[3:4, :] += jnp.sum(second, axis=0, keepdims=True)

    if split:
        half = up_part.shape[0] // 2

        @pl.when(i == pl.num_programs(0) - 1)
        def _():
            for ref, f in ((first_ref, at[3]), (second_ref, 1 - at[3])):
                piece = pl.ds(pl.multiple_of(f * half, 128), half)
                ref[:half, :] = up_part[piece, :].astype(ref.dtype)
                ref[half:, :half] = down_part[:half, piece].astype(ref.dtype)
                ref[half:, half:] = down_part[half:, piece].astype(ref.dtype)


def feed_forward(split, at, x, g, up, bias, down, scale, offset):
    width = x.shape[2]
    hidden = up.shape[1]
    pieces = two_quarters(width, lambda i, at: at[0] ^ (i // 2))
    own_row = pl.BlockSpec((STEP, width), lambda i, at: (jnp.minimum(i, 1), 0))

    def whole(*dims):
        return pl.BlockSpec(dims, lambda i, at: (0,) * len(dims))

    if split:
        assert width == hidden
        parts = [shape(width, hidden), low_shape(width, hidden)]
    else:
        parts = [shape(width, hidden), shape(hidden, width)]
    slots = whole(2, STEP, width)
    return pl.pallas_call(
        functools.partial(forward_kernel, split),
        grid_spec=pltpu.PrefetchScalarGridSpec(
            num_scalar_prefetch=1,
            grid=(4,),
            in_specs=pieces * 2 + [whole(width, hidden), whole(hidden), whole(hidden, width),
                                   whole(width), whole(width)],
            out_specs=[own_row, own_row, slots, slots, whole(8, width)]
            + [whole(*p.shape) for p in parts],
            scratch_shapes=[pltpu.VMEM((width, hidden), F32), pltpu.VMEM((hidden, width), F32)]
            if split
            else [],
        ),
        out_shape=[low_shape(2 * STEP, width)] * 2 + [low_shape(2, STEP, width)] * 2
        + [shape(8, width)] + parts,
        compiler_params=params(28),
        cost_estimate=cost(48 * STEP * width * hidden, 16 * MIB, 8 * STEP * hidden),
    )(at, x, x, g, g, up, bias, down, scale, offset)


def emit(keep_ref, send_ref, v, own_ref=None):
    i = pl.program_id(0)
    if own_ref is not None:
        v = jnp.where(i < 2, v + own_ref[...].astype(F32), v)

    @pl.when(i % 2 == 0)
    def _():
        keep_ref[0] = v.astype(BF16)

    @pl.when(i % 2 == 1)
    def _():
        send_ref[0] = v.astype(BF16)


def branch_kernel(heads, *refs):
    o = refs[:heads]
    g_ref, ff_ref, w_ref, keep_ref, send_ref, out = refs[heads:]
    wide = heads * HEAD

    @pl.when(pl.program_id(0) == 0)
    def _():
        out[...] = jnp.zeros_like(out)

    ot = jnp.concatenate([r[...] for r in o], axis=0)
    emit(keep_ref, send_ref, mm(ot, w_ref[...], 0, 0), ff_ref)
    out[...] += mm(ot, g_ref[...])


def branch(o, g, ff, weights):
    rows, width = g.shape
    heads = len(o)
    wide = heads * HEAD
    row = pl.BlockSpec((STEP, width), lambda i: (i, 0))
    slots = pl.BlockSpec((1, STEP, width), lambda i: (i // 2, 0, 0))
    return pl.pallas_call(
        functools.partial(branch_kernel, heads),
        grid=(rows // STEP,),
        in_specs=[pl.BlockSpec((HEAD, STEP), lambda i: (0, i))] * heads
        + [row, pl.BlockSpec((STEP, width), lambda i: (jnp.minimum(i, 1), 0)),
           pl.BlockSpec((wide, width), lambda i: (3, 0))],
        out_specs=[slots, slots, pl.BlockSpec((wide, width), lambda i: (0, 0))],
        out_shape=[low_shape(2, STEP, width)] * 2 + [shape(wide, width)],
        compiler_params=params(12),
        cost_estimate=cost(4 * rows * width * wide, 8 * MIB),
    )(*o, g, ff, weights)


def back_kernel(own, split, heads, at, *refs):
    count = 3 if own else 2
    grads, refs = refs[: count * heads], refs[count * heads :]
    n1_ref, xhat_ref, w_ref, s1_ref, *refs = refs
    if own:
        (a2_ref, small_ff, small_other, mix_other, out_part,
         keep_ref, send_ref, first_ref, second_ref, mix, small) = refs
    else:
        keep_ref, send_ref, mix, small = refs
    i = pl.program_id(0)
    wide = heads * HEAD
    tall = mix.shape[0]

    @pl.when(i == 0)
    def _():
        if own:
            mix[:wide, :] = jnp.zeros((wide, mix.shape[1]), F32)
            mix[wide:, :] = mix_other[...]
            small[...] = small_other[...]
        else:
            mix[...] = jnp.zeros_like(mix)
            small[...] = jnp.zeros_like(small)

    grad = jnp.concatenate([r[...] for r in grads], axis=0)
    first = mm(grad, w_ref[3 * wide - tall : 3 * wide, :], 0, 0)
    a = first * row_of(s1_ref)
    emit(keep_ref, send_ref, a, a2_ref if own else None)
    mix[...] += mm(grad, n1_ref[...])
    small[0:1, :] += jnp.sum(first * xhat_ref[...].astype(F32), axis=0, keepdims=True)
    small[1:2, :] += jnp.sum(first, axis=0, keepdims=True)
    ones = jnp.ones((8, grad.shape[1]), BF16)
    small[6:7, 3 * wide - tall : 3 * wide] += mm(ones, grad, 1, 1)[0:1]

    if own:
        @pl.when(i == pl.num_programs(0) - 1)
        def _():
            small[2:4, :] = small_ff[2:4, :]
            small[4:6, :] = small_ff[0:2, :]
            if split:
                half = mix.shape[1] // 2
                vectors = small[...].astype(BF16)
                for ref, f in ((first_ref, at[3]), (second_ref, 1 - at[3])):
                    piece = pl.ds(pl.multiple_of(f * half, 128), half)
                    ref[: 3 * wide, :] = mix[:, piece].astype(ref.dtype)
                    ref[3 * wide : 4 * wide, :] = out_part[:, piece].astype(ref.dtype)
                    both = jnp.concatenate([vectors[:, :half], vectors[:, half:]], axis=0)
                    ref[4 * wide : 4 * wide + 16, :] = both.astype(ref.dtype)
                    ref[4 * wide + 16 :, :] = jnp.zeros((48, half), ref.dtype)
            else:
                first_ref[: 3 * wide, :] = mix[...]
                first_ref[3 * wide :, :] = out_part[...]
                second_ref[...] = small[...]


def back(own, split, at, grads, n1, xhat, weights, scale, extra):
    rows, width = n1.shape[0] // 2, n1.shape[1]
    heads = len(grads[0])
    wide = heads * HEAD
    tall = 3 * wide if own else 2 * wide
    offset = 0 if own else rows // STEP
    row = pl.BlockSpec((STEP, width), lambda i, at: (i + offset, 0))
    col = pl.BlockSpec((HEAD, STEP), lambda i, at: (0, i + offset))
    slots = pl.BlockSpec((1, STEP, width), lambda i, at: (i // 2, 0, 0))

    def whole(*dims):
        return pl.BlockSpec(dims, lambda i, at: (0,) * len(dims))

    half = width // 2
    specs = [col] * (len(grads) * heads) + [row, row, whole(4 * wide, width), whole(width)]
    if not own:
        parts = [shape(tall, width), shape(8, width)]
        scratch = []
    else:
        specs += [pl.BlockSpec((STEP, width), lambda i, at: (jnp.minimum(i, 1), 0)),
                  whole(8, width), whole(8, width), whole(2 * wide, width),
                  whole(wide, width)]
        scratch = [pltpu.VMEM((tall, width), F32), pltpu.VMEM((8, width), F32)]
        if split:
            parts = [shape(4 * wide + 64, half), low_shape(4 * wide + 64, half)]
        else:
            parts = [shape(4 * wide, width), shape(8, width)]
    return pl.pallas_call(
        functools.partial(back_kernel, own, split, heads),
        grid_spec=pltpu.PrefetchScalarGridSpec(
            num_scalar_prefetch=1,
            grid=(rows // STEP,),
            in_specs=specs,
            out_specs=[slots, slots] + [whole(*p.shape) for p in parts],
            scratch_shapes=scratch,
        ),
        out_shape=[low_shape(2, STEP, width)] * 2 + parts,
        compiler_params=params(20),
        cost_estimate=cost(4 * rows * width * tall, 10 * MIB),
    )(at, *[v for vs in grads for v in vs], n1, xhat, weights, scale, *extra)


def swap(v, axis, size, distance):
    return lax.ppermute(v, axis, [(i, i ^ distance) for i in range(size)])


def by_xor(pieces, index):
    low, high = (index & 1) == 1, (index & 2) == 2
    a, b, c, d = pieces
    a, b, c, d = (jnp.where(low, b, a), jnp.where(low, a, b),
                  jnp.where(low, d, c), jnp.where(low, c, d))
    return (jnp.where(high, c, a), jnp.where(high, d, b),
            jnp.where(high, a, c), jnp.where(high, b, d))


def tie(v, *earlier):
    return lax.optimization_barrier((v, *earlier))[0]


def gather_halves(shard, size, mine, dim, *earlier):
    if size != 2:
        return lax.all_gather(shard, "fsdp", axis=dim, tiled=True)
    other = swap(shard, "fsdp", 2, 1)
    if earlier:
        other = tie(other, *earlier)
    first = mine == 0
    return jnp.concatenate(
        [jnp.where(first, shard, other), jnp.where(first, other, shard)], axis=dim
    )


def scatter_any(part, dim):
    return lax.psum_scatter(
        part.astype(BF16), "fsdp", scatter_dimension=dim, tiled=True
    ).astype(F32)


def quarter_sum(v, c, *earlier):
    rows = v.shape[0] // 4
    mine = 2 * (c % 2) + c // 2

    def part(j):
        return lax.dynamic_slice_in_dim(v, (mine ^ j) * rows, rows, 0)

    total = part(0)
    for distance, j in ((3, 3), (2, 1), (1, 2)):
        sent = swap(part(j).astype(BF16), "ctx", 4, distance)
        total = total + tie(sent, *earlier).astype(F32)
    return total


def halve(v, distance, bit, *earlier):
    rows = v.shape[0] // 2
    keep = lax.dynamic_slice_in_dim(v, bit * rows, rows, 0)
    send = lax.dynamic_slice_in_dim(v, (1 - bit) * rows, rows, 0).astype(BF16)
    return keep + tie(swap(send, "ctx", 4, distance), *earlier).astype(F32)


def pair_up(v, *earlier):
    v = v.astype(BF16)
    return jnp.stack([v, tie(swap(v, "ctx", 4, 2), *earlier)])


def double(pair, c, *earlier):
    others = tie(swap(pair, "ctx", 4, 1), *earlier)
    return by_xor([pair[0], pair[1], others[0], others[1]], 2 * (c % 2) + c // 2)


def sum_over_ctx(v, c):
    return double(pair_up(quarter_sum(v, c)), c)


def butterfly(v, axis_name, size):
    distance = 1
    while distance < size:
        v = v + swap(v, axis_name, size, distance)
        distance *= 2
    return v


def shards(
    sizes,
    inputs,
    positions,
    query_key_value_weight,
    query_key_value_bias,
    attention_output_weight,
    attention_output_bias,
    up_projection_weight,
    up_projection_bias,
    down_projection_weight,
    down_projection_bias,
    first_scale,
    first_shift,
    second_scale,
    second_shift,
    cotangent,
):
    fsdp = sizes["fsdp"]
    split = fsdp == 2
    seq_count, block, width = inputs.shape
    assert seq_count == 2 and sizes["ctx"] == 4 and sizes["tp"] == 4 and block == 2 * STEP
    length = positions.shape[1]
    local = query_key_value_weight.shape[2]
    heads = local // HEAD
    hidden = up_projection_weight.shape[1]
    quarter = block // 4
    f = lax.axis_index("fsdp")
    c = lax.axis_index("ctx")
    t = lax.axis_index("tp")
    s = c // 2
    at = jnp.stack([s, c, t, f]).astype(jnp.int32)

    def my_quarter(v, seq):
        return lax.dynamic_slice(v, (seq, t * quarter, 0), (1, quarter, width))

    x_mine, x_theirs = my_quarter(inputs, s), my_quarter(inputs, 1 - s)
    g_theirs = my_quarter(cotangent, 1 - s)
    far_z = swap(jnp.concatenate([x_theirs, g_theirs], axis=0), "ctx", 4, 2)
    cross = swap(x_theirs, "ctx", 4, 3)
    near = swap(x_mine, "ctx", 4, 1)

    others_z = jnp.concatenate([near, cross], axis=0)
    others_x = swap(others_z, "tp", 4, 2)
    far_x = swap(far_z, "tp", 4, 2)

    wup = gather_halves(up_projection_weight, fsdp, f, 0)
    wdown = gather_halves(down_projection_weight, fsdp, f, 1)
    mix_shard = query_key_value_weight.transpose(1, 2, 0).reshape(3 * local, -1)
    mix_out_shard = jnp.concatenate([mix_shard, attention_output_weight], axis=0)

    inverse = 10000.0 ** (-2.0 * jnp.arange(HALF, dtype=F32) / ROT)
    places = positions.astype(F32)[:, None, :]
    angles = inverse[None, :, None] * places
    trig = jnp.concatenate(
        [jnp.cos(angles), jnp.sin(angles), jnp.broadcast_to(places, angles.shape)], axis=1
    )

    ff, a2, keep_e, send_e, small_ff, ff_first, ff_second = feed_forward(
        split, at, inputs, cotangent, wup, up_projection_bias, wdown, second_scale, second_shift
    )

    def over_tp(v_z, v_x):
        v_x = tie(v_x, small_ff)
        return v_z, v_x, swap(jnp.stack([v_z, v_x]), "tp", 4, 1)

    weights = gather_halves(mix_out_shard, fsdp, f, 1, small_ff)
    n1, xhat_all, g, trig, kt, vt, qt, dot = project(
        at, inputs, cotangent, over_tp(far_z, far_x), over_tp(others_z, others_x), trig, weights,
        query_key_value_bias, first_scale, first_shift,
    )
    def over_core(keep, send, *earlier):
        v = keep.astype(F32) + tie(swap(send, "tp", 4, 1), *earlier).astype(F32)
        return v.reshape(2, 2, quarter, width)

    def over_x(v, *earlier):
        return v[:, 0] + tie(swap(v[:, 1].astype(BF16), "tp", 4, 2), *earlier).astype(F32)

    per_head = []
    for h in range(heads):
        after = ()
        if h == 1:
            early = over_core(keep_e, send_e, per_head[0][0])
            ff_rest = small_ff
            if split:
                ff_rest = tie(swap(ff_second, "fsdp", 2, 1), per_head[0][0])
                ff_rest = ff_first + ff_rest.astype(F32)
            after = (early, ff_rest)
        if h == heads - 1:
            early = over_x(early, per_head[h - 1][0])
            ff_half = halve(ff_rest, 1, c % 2, per_head[h - 1][0]) if split else small_ff
            after = (early, ff_half)
        per_head.append(attention(h, after, qt, dot, kt, vt, trig))
    o, dq, dk, dv = zip(*per_head)
    ff_quarter = halve(ff_half, 2, c // 2, o[-1]) if split else small_ff
    keep_b, send_b, out_part = branch(o, g, tie(ff, ff_quarter), weights)
    keep_o, send_o, mix_other, small_other = back(
        False, split, at, (dk, dv), n1, xhat_all, weights, tie(first_scale, keep_b), ()
    )
    half_b = over_core(keep_b, send_b)
    keep_w, send_w, late_first, late_second = back(
        True, split, at, (dq, dk, dv), n1, xhat_all, weights,
        tie(first_scale, half_b), (a2, small_ff, small_other, mix_other, out_part),
    )
    half_o = over_core(keep_o, send_o)
    half_w = over_core(keep_w, send_w)
    ff_pair = pair_up(ff_quarter, half_w) if split else half_w

    def over_ctx(v, distance, *earlier):
        return tie(swap(v.astype(BF16), "ctx", 4, distance), *earlier).astype(F32)

    def gather_tp(ours):
        pair = jnp.stack([ours, swap(ours, "tp", 4, 2)])
        core = swap(pair, "tp", 4, 1)
        pieces = by_xor((pair[0], core[0], pair[1], core[1]), t)
        pieces = jnp.concatenate(pieces, axis=1)
        return jnp.stack([jnp.where(s == 0, pieces[0], pieces[1]),
                          jnp.where(s == 0, pieces[1], pieces[0])]).astype(F32)

    sums_b = over_x(half_b, half_w)
    branches = jnp.stack([sums_b[0], over_ctx(sums_b[1], 2) + early[0]]).astype(BF16)
    block_out = gather_tp(branches)
    block_out = (
        inputs.astype(F32) + block_out + (attention_output_bias + down_projection_bias)
    )

    sums_o = over_x(half_o, ff_pair)
    sums_w = over_x(half_w)
    sums_w = sums_w + over_ctx(sums_o, 1)
    a = jnp.stack([sums_w[0], over_ctx(sums_w[1], 2, branches) + early[1]])
    xhat, inv = xhat_of(jnp.concatenate([x_mine, x_theirs], axis=0).astype(F32))
    norm_grad = inv * (
        a
        - jnp.mean(a, axis=-1, keepdims=True)
        - xhat * jnp.mean(a * xhat, axis=-1, keepdims=True)
    )
    norm_grad = norm_grad.astype(BF16)
    inputs_grad = cotangent.astype(F32) + gather_tp(norm_grad)

    if split:
        q = double(ff_pair, c, norm_grad)
        up_total = jnp.concatenate(q[:2], axis=0).astype(F32)
        down_total = jnp.concatenate(q[2:], axis=0).astype(F32)
        down_total = jnp.concatenate(
            [down_total[:, : width // 2], down_total[:, width // 2 :]], axis=0
        )
        late = late_first + tie(swap(late_second, "fsdp", 2, 1), sums_o).astype(F32)
        late = double(pair_up(quarter_sum(late, c, sums_w), norm_grad), c)
        late = jnp.concatenate(late, axis=0).astype(F32)
        small = jnp.concatenate([late[4 * local : 4 * local + 8], late[4 * local + 8 :][:8]], axis=1)
    else:
        q = sum_over_ctx(scatter_any(ff_first, 0), c)
        up_total = jnp.concatenate(q, axis=0).astype(F32)
        q = sum_over_ctx(scatter_any(ff_second, 1), c)
        down_total = jnp.concatenate(q, axis=0).astype(F32)
        q = sum_over_ctx(scatter_any(late_first, 1), c)
        late = jnp.concatenate(q, axis=0).astype(F32)
        small = butterfly(butterfly(late_second, "fsdp", fsdp), "ctx", 4)
    mix_total = late[: 3 * local].reshape(3, local, -1).transpose(2, 0, 1)
    out_total = late[3 * local : 4 * local]
    norm_small = butterfly(small, "tp", 4)
    bias_total = norm_small[5] * 0.25
    return (
        block_out,
        inputs_grad,
        mix_total,
        small[6, : 3 * local].reshape(3, local),
        out_total,
        bias_total,
        up_total,
        small[4, :hidden],
        down_total,
        bias_total,
        norm_small[0],
        norm_small[1],
        norm_small[2],
        norm_small[3],
    )


def solution(mesh):
    in_specs = (
        P("fsdp", "ctx", None),
        P("fsdp", None),
        P("fsdp", None, "tp"),
        P(None, "tp"),
        P("tp", "fsdp"),
        P(),
        P("fsdp", "tp"),
        P("tp"),
        P("tp", "fsdp"),
        P(),
        P(),
        P(),
        P(),
        P(),
        P("fsdp", "ctx", None),
    )
    out_specs = (
        P("fsdp", "ctx", None),
        P("fsdp", "ctx", None),
        P("fsdp", None, "tp"),
        P(None, "tp"),
        P("tp", "fsdp"),
        P(),
        P("fsdp", "tp"),
        P("tp"),
        P("tp", "fsdp"),
        P(),
        P(),
        P(),
        P(),
        P(),
    )
    body = functools.partial(shards, dict(mesh.shape))
    return jax.shard_map(body, mesh=mesh, in_specs=in_specs, out_specs=out_specs, check_vma=False)
```

```python
import functools

import jax
import jax.numpy as jnp
from jax import lax
from jax.experimental import pallas as pl
from jax.experimental.pallas import tpu as pltpu
from jax.sharding import PartitionSpec as P

HEAD = 64
ROT = 16
HALF = ROT // 2
EPS = 1e-5
NEG = -1e30
STEP = 256
F32 = jnp.float32
BF16 = jnp.bfloat16
MIB = 1024 * 1024


def mm(a, b, ca=1, cb=0):
    return lax.dot_general(a, b, (((ca,), (cb,)), ((), ())), preferred_element_type=F32)


def params(mib):
    return pltpu.CompilerParams(vmem_limit_bytes=mib * MIB)


def cost(flops, moved, exps=0):
    return pl.CostEstimate(flops=int(flops), bytes_accessed=int(moved), transcendentals=int(exps))


def xhat_of(x):
    width = x.shape[-1]
    centred = x - jnp.sum(x, axis=-1, keepdims=True) * (1.0 / width)
    spread = jnp.sum(centred * centred, axis=-1, keepdims=True) * (1.0 / width)
    inv = lax.rsqrt(spread + EPS)
    return centred * inv, inv


def row_of(ref):
    return ref[...].reshape(1, -1)


def shape(*dims):
    return jax.ShapeDtypeStruct(dims, F32)


def low_shape(*dims):
    return jax.ShapeDtypeStruct(dims, BF16)


def norm_own_kernel(at, xa, xb, ga, gb, fz, fx, fc, ta, tb, s1, b1, s2, b2,
                    n1_ref, n2_ref, g_ref, trig_ref, x):
    i = pl.program_id(0)
    q = xa.shape[1]

    @pl.when(i < 2)
    def _():
        x[:q, :] = xa[0]
        x[q:, :] = xb[0]
        g_ref[:q, :] = ga[0]
        g_ref[q:, :] = gb[0]

    @pl.when(i == 2)
    def _():
        x[:q, :] = fz[0]
        x[q:, :] = fx[0]
        g_ref[:q, :] = fz[1]
        g_ref[q:, :] = fx[1]

    @pl.when(i == 3)
    def _():
        x[:q, :] = fc[0, 0]
        x[q:, :] = fc[1, 0]
        g_ref[:q, :] = fc[0, 1]
        g_ref[q:, :] = fc[1, 1]

    trig_ref[:, :q] = ta[0]
    trig_ref[:, q:] = tb[0]
    xhat, _ = xhat_of(x[...].astype(F32))
    n1_ref[...] = (xhat * row_of(s1) + row_of(b1)).astype(BF16)
    n2_ref[...] = (xhat * row_of(s2) + row_of(b2)).astype(BF16)


def norm_other_kernel(at, nz, nx, nc, ta, tb, s1, b1, n1_ref, trig_ref, x):
    i = pl.program_id(0)
    q = nz.shape[1]
    b = i // 2

    @pl.when(i % 2 == 0)
    def _():
        x[:q, :] = nz[b]
        x[q:, :] = nx[b]

    @pl.when(i % 2 == 1)
    def _():
        x[:q, :] = nc[0, b]
        x[q:, :] = nc[1, b]

    trig_ref[:, :q] = ta[0]
    trig_ref[:, q:] = tb[0]
    xhat, _ = xhat_of(x[...].astype(F32))
    n1_ref[...] = (xhat * row_of(s1) + row_of(b1)).astype(BF16)


def norms(at, own, arrays, trig, vectors):
    width = vectors[0].shape[0]
    rows, q = 4 * STEP, STEP // 2
    tall = trig.shape[1]
    first = 0 if own else 1

    def pick(high):
        def place(i, at):
            block = at[1] ^ (first + 2 * (i // 2))
            return (at[0], 0, block * 4 + (at[2] ^ (i % 2 + high)))

        return pl.BlockSpec((1, tall, q), place)

    def piece(high):
        return pl.BlockSpec(
            (1, q, width), lambda i, at: (at[0], at[2] ^ (jnp.minimum(i, 1) + high), 0)
        )

    def whole(v):
        return pl.BlockSpec(v.shape, lambda i, at: (0,) * v.ndim)

    row = pl.BlockSpec((STEP, width), lambda i, at: (i, 0))
    out_trig = pl.BlockSpec((tall, STEP), lambda i, at: (0, i))
    if own:
        x, g, received = arrays[0], arrays[1], arrays[2:]
        specs = [piece(0), piece(2), piece(0), piece(2)]
        operands = [x, x, g, g]
        kernel, count = norm_own_kernel, 3
    else:
        received, specs, operands = arrays, [], []
        kernel, count = norm_other_kernel, 1
    specs += [whole(v) for v in received] + [pick(0), pick(2)] + [whole(v) for v in vectors]
    operands += [*received, trig, trig, *vectors]
    return pl.pallas_call(
        kernel,
        grid_spec=pltpu.PrefetchScalarGridSpec(
            num_scalar_prefetch=1,
            grid=(rows // STEP,),
            in_specs=specs,
            out_specs=[row] * count + [out_trig],
            scratch_shapes=[pltpu.VMEM((STEP, width), BF16)],
        ),
        out_shape=[low_shape(rows, width)] * count + [shape(tall, rows)],
        compiler_params=params(24),
        cost_estimate=cost(0, 6 * rows * width),
    )(at, *operands)


def project_kernel(n1o, n1x, to, tx, g_ref, w_ref, b_ref, k_ref, v_ref, q_ref, do_ref, bias):
    i = pl.program_id(0)
    wide = k_ref.shape[0]

    @pl.when(i == 0)
    def _():
        for j in range(3):
            line = jnp.broadcast_to(b_ref[j : j + 1, :], (8, wide))
            bias[j * wide : (j + 1) * wide, :] = line.T[:, 0:1]

    def rotated(ref, mixed, trig, factor):
        cosine, sine = trig[:HALF], trig[HALF:ROT]
        for h in range(0, wide, HEAD):
            a, b = mixed[h : h + HALF], mixed[h + HALF : h + ROT]
            turned = jnp.concatenate([a * cosine - b * sine, b * cosine + a * sine], axis=0)
            ref[h : h + ROT, :] = turned.astype(BF16) * factor
            ref[h + ROT : h + HEAD, :] = mixed[h + ROT : h + HEAD].astype(BF16) * factor

    def keys_values(mixed, trig):
        rotated(k_ref, mixed[:wide], trig, BF16(1.0))
        v_ref[...] = mixed[wide:].astype(BF16)

    @pl.when(i < 4)
    def _():
        trig = to[...]
        mixed = mm(w_ref[: 3 * wide, :], n1o[...], 1, 1) + bias[...]
        rotated(q_ref, mixed[:wide], trig, BF16(HEAD**-0.5))
        keys_values(mixed[wide:], trig)
        do_ref[...] = mm(w_ref[3 * wide :, :], g_ref[...], 1, 1).astype(BF16)

    @pl.when(i >= 4)
    def _():
        mixed = mm(w_ref[wide : 3 * wide, :], n1x[...], 1, 1) + bias[wide:, :]
        keys_values(mixed, tx[...])


def project(n1_own, n1_other, trig_own, trig_other, g, weights, bias):
    rows, width = n1_own.shape
    wide = bias.shape[1]
    tall = trig_own.shape[0]

    def own(i):
        return jnp.minimum(i, 3)

    def other(i):
        return jnp.maximum(i - 4, 0)

    col = pl.BlockSpec((wide, STEP), lambda i: (0, i))
    own_col = pl.BlockSpec((wide, STEP), lambda i: (0, own(i)))
    return pl.pallas_call(
        project_kernel,
        grid=(8,),
        in_specs=[
            pl.BlockSpec((STEP, width), lambda i: (own(i), 0)),
            pl.BlockSpec((STEP, width), lambda i: (other(i), 0)),
            pl.BlockSpec((tall, STEP), lambda i: (0, own(i))),
            pl.BlockSpec((tall, STEP), lambda i: (0, other(i))),
            pl.BlockSpec((STEP, width), lambda i: (own(i), 0)),
            pl.BlockSpec((4 * wide, width), lambda i: (0, 0)),
            pl.BlockSpec((3, wide), lambda i: (0, 0)),
        ],
        out_specs=[col, col, own_col, own_col],
        out_shape=[low_shape(wide, 2 * rows)] * 2 + [low_shape(wide, rows)] * 2,
        scratch_shapes=[pltpu.VMEM((3 * wide, 1), F32)],
        compiler_params=params(24),
        cost_estimate=cost(12 * rows * width * wide, 12 * rows * width),
    )(n1_own, n1_other, trig_own, trig_other, g, weights, bias)


def attention_kernel(after, q_ref, do_ref, k_ref, v_ref, tq_ref, to_ref, tx_ref,
                     o_ref, dq_ref, dk_ref, dv_ref, kn, vn, kp, dk, dv, es, dps):
    i = pl.program_id(0)
    length = k_ref.shape[1]
    half = length // 2
    chunk = STEP
    steps = length // chunk

    @pl.when(i == 0)
    def _():
        kn[...] = k_ref[...].T
        vn[...] = v_ref[...].T
        kp[:half, :] = to_ref[ROT:, :].T[:, 0:1]
        kp[half:, :] = tx_ref[ROT:, :].T[:, 0:1]
        dk[...] = jnp.zeros_like(dk)
        dv[...] = jnp.zeros_like(dv)

    qt = q_ref[...]
    dot = do_ref[...]
    qn = qt.T
    don = dot.T
    qpos = tq_ref[ROT : ROT + 1, :]
    lanes = qt.shape[1]
    fold = (chunk // 8, 8, lanes)

    top = jnp.full((8, lanes), NEG, F32)
    for j in range(steps):
        here = slice(j * chunk, (j + 1) * chunk)
        s = mm(kn[here, :], qt)
        s = jnp.where(kp[here, :] <= qpos, s, NEG)
        es[here, :] = s
        top = jnp.maximum(top, jnp.max(s.reshape(fold), axis=0))
    top = jnp.max(top, axis=0, keepdims=True)

    total = jnp.zeros((8, lanes), F32)
    inner = jnp.zeros((8, lanes), F32)
    for j in range(steps):
        here = slice(j * chunk, (j + 1) * chunk)
        e = jnp.exp(es[here, :] - top)
        dp = mm(vn[here, :], dot)
        es[here, :] = e
        dps[here, :] = dp
        total = total + jnp.sum(e.reshape(fold), axis=0)
        inner = inner + jnp.sum((e * dp).reshape(fold), axis=0)
    share = 1.0 / jnp.sum(total, axis=0, keepdims=True)
    inner = jnp.sum(inner, axis=0, keepdims=True) * share

    ot = jnp.zeros((HEAD, lanes), F32)
    dqt = jnp.zeros((HEAD, lanes), F32)
    for j in range(steps):
        here = slice(j * chunk, (j + 1) * chunk)
        p = es[here, :] * share
        ds = (p * (dps[here, :] - inner)).astype(BF16)
        p = p.astype(BF16)
        dv[here, :] += mm(p, don)
        dk[here, :] += mm(ds, qn)
        ot = ot + mm(v_ref[:, here], p)
        dqt = dqt + mm(k_ref[:, here], ds)
    o_ref[...] = ot.astype(BF16)

    def unrotated(grad, trig):
        cosine, sine = trig[:HALF], trig[HALF:ROT]
        a, b = grad[:HALF], grad[HALF:ROT]
        turned = jnp.concatenate([a * cosine + b * sine, b * cosine - a * sine], axis=0)
        return turned.astype(BF16), grad[ROT:].astype(BF16)

    dq_ref[:ROT, :], dq_ref[ROT:, :] = unrotated(dqt * (HEAD**-0.5), tq_ref[...])

    @pl.when(i == pl.num_programs(0) - 1)
    def _():
        grad = dk[...].T
        dk_ref[:ROT, :half], dk_ref[ROT:, :half] = unrotated(grad[:, :half], to_ref[...])
        dk_ref[:ROT, half:], dk_ref[ROT:, half:] = unrotated(grad[:, half:], tx_ref[...])
        dv_ref[...] = dv[...].T.astype(BF16)


def attention(h, after, qt, dot, kt, vt, trig_own, trig_other):
    rows, length = qt.shape[1], kt.shape[1]
    lanes = STEP
    tall = trig_own.shape[0]
    q_spec = pl.BlockSpec((HEAD, lanes), lambda i: (h, i))
    k_spec = pl.BlockSpec((HEAD, length), lambda i: (h, 0))
    trig_spec = pl.BlockSpec((tall, rows), lambda i: (0, 0))
    return pl.pallas_call(
        attention_kernel,
        grid=(rows // lanes,),
        in_specs=[pl.BlockSpec(memory_space=pl.ANY), q_spec, q_spec, k_spec, k_spec,
                  pl.BlockSpec((tall, lanes), lambda i: (0, i)), trig_spec, trig_spec],
        out_specs=[pl.BlockSpec((HEAD, lanes), lambda i: (0, i))] * 2
        + [pl.BlockSpec((HEAD, length), lambda i: (0, 0))] * 2,
        out_shape=[low_shape(HEAD, rows)] * 2 + [low_shape(HEAD, length)] * 2,
        scratch_shapes=[
            pltpu.VMEM((length, HEAD), BF16),
            pltpu.VMEM((length, HEAD), BF16),
            pltpu.VMEM((length, 1), F32),
            pltpu.VMEM((length, HEAD), F32),
            pltpu.VMEM((length, HEAD), F32),
            pltpu.VMEM((length, lanes), F32),
            pltpu.VMEM((length, lanes), F32),
        ],
        compiler_params=params(32),
        cost_estimate=cost(40 * rows * length * HEAD, 16 * HEAD * length, rows * length),
    )(after, qt, dot, kt, vt, trig_own, trig_own, trig_other)


def forward_kernel(split, at, n2_ref, g_ref, up_ref, bias_ref, down_ref, s2_ref, b2_ref,
                   ff_ref, a_ref, small_ref, first_ref, second_ref, *scratch):
    i = pl.program_id(0)
    up_part, down_part = scratch if split else (first_ref, second_ref)

    @pl.when(i == 0)
    def _():
        up_part[...] = jnp.zeros_like(up_part)
        down_part[...] = jnp.zeros_like(down_part)
        small_ref[...] = jnp.zeros_like(small_ref)

    n2, g = n2_ref[...], g_ref[...]
    up = mm(n2, up_ref[...]) + row_of(bias_ref)
    cdf = 0.5 + 0.5 * lax.erf(up * (0.5**0.5))
    act = (up * cdf).astype(BF16)
    slope = cdf + up * (jnp.exp(up * up * -0.5) * 0.3989422804014327)
    up_grad = (mm(g, down_ref[...], 1, 1) * slope).astype(BF16)
    ff_ref[...] = mm(act, down_ref[...]).astype(BF16)
    second = mm(up_grad, up_ref[...], 1, 1)
    up_part[...] += mm(n2, up_grad, 0, 0)
    down_part[...] += mm(act, g, 0, 0)
    a_ref[...] = (second * row_of(s2_ref)).astype(BF16)
    small_ref[0:1, :] += jnp.sum(up_grad.astype(F32), axis=0, keepdims=True)
    small_ref[1:2, :] += jnp.sum(g.astype(F32), axis=0, keepdims=True)
    small_ref[2:3, :] += jnp.sum(second * n2.astype(F32), axis=0, keepdims=True)
    small_ref[3:4, :] += jnp.sum(second, axis=0, keepdims=True)

    @pl.when(i == pl.num_programs(0) - 1)
    def _():
        rest = small_ref[2:3, :] - row_of(b2_ref) * small_ref[3:4, :]
        small_ref[2:3, :] = rest / row_of(s2_ref)

    if split:
        half = up_part.shape[0] // 2

        @pl.when(i == pl.num_programs(0) - 1)
        def _():
            for ref, f in ((first_ref, at[3]), (second_ref, 1 - at[3])):
                piece = pl.ds(pl.multiple_of(f * half, 128), half)
                ref[:half, :] = up_part[piece, :].astype(ref.dtype)
                ref[half:, :half] = down_part[:half, piece].astype(ref.dtype)
                ref[half:, half:] = down_part[half:, piece].astype(ref.dtype)


def feed_forward(split, at, n2, g, up, bias, down, scale, offset):
    rows, width = n2.shape
    hidden = up.shape[1]
    row = pl.BlockSpec((STEP, width), lambda i, at: (i, 0))

    def whole(*dims):
        return pl.BlockSpec(dims, lambda i, at: (0,) * len(dims))

    if split:
        assert width == hidden
        parts = [shape(width, hidden), low_shape(width, hidden)]
    else:
        parts = [shape(width, hidden), shape(hidden, width)]
    return pl.pallas_call(
        functools.partial(forward_kernel, split),
        grid_spec=pltpu.PrefetchScalarGridSpec(
            num_scalar_prefetch=1,
            grid=(rows // STEP,),
            in_specs=[row, row, whole(width, hidden), whole(hidden), whole(hidden, width),
                      whole(width), whole(width)],
            out_specs=[row, row, whole(8, width)] + [whole(*p.shape) for p in parts],
            scratch_shapes=[pltpu.VMEM((width, hidden), F32), pltpu.VMEM((hidden, width), F32)]
            if split
            else [],
        ),
        out_shape=[low_shape(rows, width)] * 2 + [shape(8, width)] + parts,
        compiler_params=params(40),
        cost_estimate=cost(12 * rows * width * hidden, 16 * MIB, 2 * rows * hidden),
    )(at, n2, g, up, bias, down, scale, offset)


def emit(keep_ref, send_ref, v):
    i = pl.program_id(0)

    @pl.when(i % 2 == 0)
    def _():
        keep_ref[0] = v.astype(BF16)

    @pl.when(i % 2 == 1)
    def _():
        send_ref[0] = v.astype(BF16)


def branch_kernel(heads, *refs):
    o = refs[:heads]
    g_ref, ff_ref, w_ref, keep_ref, send_ref, out = refs[heads:]
    wide = heads * HEAD

    @pl.when(pl.program_id(0) == 0)
    def _():
        out[...] = jnp.zeros_like(out)

    ot = jnp.concatenate([r[...] for r in o], axis=0)
    emit(keep_ref, send_ref, mm(ot, w_ref[...], 0, 0) + ff_ref[...].astype(F32))
    out[...] += mm(ot, g_ref[...])


def branch(o, g, ff, weights):
    rows, width = g.shape
    heads = len(o)
    wide = heads * HEAD
    row = pl.BlockSpec((STEP, width), lambda i: (i, 0))
    slots = pl.BlockSpec((1, STEP, width), lambda i: (i // 2, 0, 0))
    return pl.pallas_call(
        functools.partial(branch_kernel, heads),
        grid=(rows // STEP,),
        in_specs=[pl.BlockSpec((HEAD, STEP), lambda i: (0, i))] * heads
        + [row, row, pl.BlockSpec((wide, width), lambda i: (3, 0))],
        out_specs=[slots, slots, pl.BlockSpec((wide, width), lambda i: (0, 0))],
        out_shape=[low_shape(2, STEP, width)] * 2 + [shape(wide, width)],
        compiler_params=params(24),
        cost_estimate=cost(4 * rows * width * wide, 8 * MIB),
    )(*o, g, ff, weights)


def back_kernel(own, split, heads, at, *refs):
    count = 3 if own else 2
    grads, refs = refs[: count * heads], refs[count * heads :]
    n1_ref, w_ref, s1_ref, *refs = refs
    if own:
        (a2_ref, b1_ref, small_ff, small_other, mix_other, out_part,
         keep_ref, send_ref, first_ref, second_ref, mix, small) = refs
    else:
        keep_ref, send_ref, mix, small = refs
    i = pl.program_id(0)
    wide = heads * HEAD
    tall = mix.shape[0]

    @pl.when(i == 0)
    def _():
        if own:
            mix[:wide, :] = jnp.zeros((wide, mix.shape[1]), F32)
            mix[wide:, :] = mix_other[...]
            small[...] = small_other[...]
        else:
            mix[...] = jnp.zeros_like(mix)
            small[...] = jnp.zeros_like(small)

    grad = jnp.concatenate([r[...] for r in grads], axis=0)
    first = mm(grad, w_ref[3 * wide - tall : 3 * wide, :], 0, 0)
    a = first * row_of(s1_ref)
    emit(keep_ref, send_ref, a + a2_ref[...].astype(F32) if own else a)
    mix[...] += mm(grad, n1_ref[...])
    small[0:1, :] += jnp.sum(first * n1_ref[...].astype(F32), axis=0, keepdims=True)
    small[1:2, :] += jnp.sum(first, axis=0, keepdims=True)
    ones = jnp.ones((8, grad.shape[1]), BF16)
    small[6:7, 3 * wide - tall : 3 * wide] += mm(ones, grad, 1, 1)[0:1]

    if own:
        @pl.when(i == pl.num_programs(0) - 1)
        def _():
            rest = small[0:1, :] - row_of(b1_ref) * small[1:2, :]
            small[0:1, :] = rest / row_of(s1_ref)
            small[2:4, :] = small_ff[2:4, :]
            small[4:6, :] = small_ff[0:2, :]
            if split:
                half = mix.shape[1] // 2
                vectors = small[...].astype(BF16)
                for ref, f in ((first_ref, at[3]), (second_ref, 1 - at[3])):
                    piece = pl.ds(pl.multiple_of(f * half, 128), half)
                    ref[: 3 * wide, :] = mix[:, piece].astype(ref.dtype)
                    ref[3 * wide : 4 * wide, :] = out_part[:, piece].astype(ref.dtype)
                    both = jnp.concatenate([vectors[:, :half], vectors[:, half:]], axis=0)
                    ref[4 * wide : 4 * wide + 16, :] = both.astype(ref.dtype)
                    ref[4 * wide + 16 :, :] = jnp.zeros((48, half), ref.dtype)
            else:
                first_ref[: 3 * wide, :] = mix[...]
                first_ref[3 * wide :, :] = out_part[...]
                second_ref[...] = small[...]


def back(own, split, at, grads, n1, weights, scale, extra):
    rows, width = n1.shape
    heads = len(grads[0])
    wide = heads * HEAD
    tall = 3 * wide if own else 2 * wide
    offset = 0 if own else rows // STEP
    row = pl.BlockSpec((STEP, width), lambda i, at: (i, 0))
    col = pl.BlockSpec((HEAD, STEP), lambda i, at: (0, i + offset))
    slots = pl.BlockSpec((1, STEP, width), lambda i, at: (i // 2, 0, 0))

    def whole(*dims):
        return pl.BlockSpec(dims, lambda i, at: (0,) * len(dims))

    half = width // 2
    specs = [col] * (len(grads) * heads) + [row, whole(4 * wide, width), whole(width)]
    if not own:
        parts = [shape(tall, width), shape(8, width)]
        scratch = []
    else:
        specs += [row, whole(width), whole(8, width), whole(8, width), whole(2 * wide, width),
                  whole(wide, width)]
        scratch = [pltpu.VMEM((tall, width), F32), pltpu.VMEM((8, width), F32)]
        if split:
            parts = [shape(4 * wide + 64, half), low_shape(4 * wide + 64, half)]
        else:
            parts = [shape(4 * wide, width), shape(8, width)]
    return pl.pallas_call(
        functools.partial(back_kernel, own, split, heads),
        grid_spec=pltpu.PrefetchScalarGridSpec(
            num_scalar_prefetch=1,
            grid=(rows // STEP,),
            in_specs=specs,
            out_specs=[slots, slots] + [whole(*p.shape) for p in parts],
            scratch_shapes=scratch,
        ),
        out_shape=[low_shape(2, STEP, width)] * 2 + parts,
        compiler_params=params(32),
        cost_estimate=cost(4 * rows * width * tall, 10 * MIB),
    )(at, *[v for vs in grads for v in vs], n1, weights, scale, *extra)


def swap(v, axis, size, distance):
    return lax.ppermute(v, axis, [(i, i ^ distance) for i in range(size)])


def by_xor(pieces, index):
    low, high = (index & 1) == 1, (index & 2) == 2
    a, b, c, d = pieces
    a, b, c, d = (jnp.where(low, b, a), jnp.where(low, a, b),
                  jnp.where(low, d, c), jnp.where(low, c, d))
    return (jnp.where(high, c, a), jnp.where(high, d, b),
            jnp.where(high, a, c), jnp.where(high, b, d))


def tie(v, *earlier):
    return lax.optimization_barrier((v, *earlier))[0]


def gather_halves(shard, size, mine, dim, *earlier):
    if size != 2:
        return lax.all_gather(shard, "fsdp", axis=dim, tiled=True)
    other = swap(shard, "fsdp", 2, 1)
    if earlier:
        other = tie(other, *earlier)
    first = mine == 0
    return jnp.concatenate(
        [jnp.where(first, shard, other), jnp.where(first, other, shard)], axis=dim
    )


def scatter_any(part, dim):
    return lax.psum_scatter(
        part.astype(BF16), "fsdp", scatter_dimension=dim, tiled=True
    ).astype(F32)


def halve(v, distance, bit, *earlier):
    rows = v.shape[0] // 2
    keep = lax.dynamic_slice_in_dim(v, bit * rows, rows, 0)
    send = lax.dynamic_slice_in_dim(v, (1 - bit) * rows, rows, 0).astype(BF16)
    return keep + tie(swap(send, "ctx", 4, distance), *earlier).astype(F32)


def quarter_sum(v, c, *earlier):
    rows = v.shape[0] // 4
    mine = 2 * (c % 2) + c // 2

    def part(j):
        return lax.dynamic_slice_in_dim(v, (mine ^ j) * rows, rows, 0)

    total = part(0)
    for distance, j in ((3, 3), (2, 1), (1, 2)):
        sent = swap(part(j).astype(BF16), "ctx", 4, distance)
        total = total + tie(sent, *earlier).astype(F32)
    return total


def pair_up(v, *earlier):
    v = v.astype(BF16)
    return jnp.stack([v, tie(swap(v, "ctx", 4, 2), *earlier)])


def double(pair, c, *earlier):
    others = tie(swap(pair, "ctx", 4, 1), *earlier)
    return by_xor([pair[0], pair[1], others[0], others[1]], 2 * (c % 2) + c // 2)


def sum_over_ctx(v, c):
    return double(pair_up(quarter_sum(v, c)), c)


def butterfly(v, axis_name, size):
    distance = 1
    while distance < size:
        v = v + swap(v, axis_name, size, distance)
        distance *= 2
    return v


def shards(
    sizes,
    inputs,
    positions,
    query_key_value_weight,
    query_key_value_bias,
    attention_output_weight,
    attention_output_bias,
    up_projection_weight,
    up_projection_bias,
    down_projection_weight,
    down_projection_bias,
    first_scale,
    first_shift,
    second_scale,
    second_shift,
    cotangent,
):
    fsdp = sizes["fsdp"]
    split = fsdp == 2
    seq_count, block, width = inputs.shape
    assert seq_count == 2 and sizes["ctx"] == 4 and sizes["tp"] == 4 and block == 2 * STEP
    length = positions.shape[1]
    local = query_key_value_weight.shape[2]
    heads = local // HEAD
    hidden = up_projection_weight.shape[1]
    quarter = block // 4
    f = lax.axis_index("fsdp")
    c = lax.axis_index("ctx")
    t = lax.axis_index("tp")
    s = c // 2
    at = jnp.stack([s, c, t, f]).astype(jnp.int32)

    def my_quarter(v, seq):
        return lax.dynamic_slice(v, (seq, t * quarter, 0), (1, quarter, width))

    x_mine, x_theirs = my_quarter(inputs, s), my_quarter(inputs, 1 - s)
    g_theirs = my_quarter(cotangent, 1 - s)
    far_z = swap(jnp.concatenate([x_theirs, g_theirs], axis=0), "ctx", 4, 2)
    cross = swap(tie(x_theirs, far_z), "ctx", 4, 3)
    near = swap(x_mine, "ctx", 4, 1)
    far_x = swap(far_z, "tp", 4, 2)
    far = (far_z, far_x, swap(jnp.stack([far_z, far_x]), "tp", 4, 1))

    wup = gather_halves(up_projection_weight, fsdp, f, 0)
    wdown = gather_halves(down_projection_weight, fsdp, f, 1)
    mix_shard = query_key_value_weight.transpose(1, 2, 0).reshape(3 * local, -1)
    mix_out_shard = jnp.concatenate([mix_shard, attention_output_weight], axis=0)

    inverse = 10000.0 ** (-2.0 * jnp.arange(HALF, dtype=F32) / ROT)
    places = positions.astype(F32)[:, None, :]
    angles = inverse[None, :, None] * places
    trig = jnp.concatenate(
        [jnp.cos(angles), jnp.sin(angles), jnp.broadcast_to(places, angles.shape)], axis=1
    )

    n1_own, n2, g, trig_own = norms(
        at, True, (inputs, cotangent, *far), trig,
        (first_scale, first_shift, second_scale, second_shift),
    )
    others_z = jnp.concatenate([tie(near, n2), tie(cross, n2)], axis=0)
    others_x = swap(others_z, "tp", 4, 2)
    ff, a2, small_ff, ff_first, ff_second = feed_forward(
        split, at, n2, g, wup, up_projection_bias, wdown, second_scale, second_shift
    )
    weights = gather_halves(mix_out_shard, fsdp, f, 1, small_ff)
    others_x = tie(others_x, small_ff)
    others = (others_z, others_x, swap(jnp.stack([others_z, others_x]), "tp", 4, 1))
    n1_other, trig_other = norms(at, False, others, trig, (first_scale, first_shift))
    kt, vt, qt, dot = project(
        n1_own, n1_other, trig_own, trig_other, g, weights, query_key_value_bias
    )
    per_head = []
    after = small_ff
    for h in range(heads):
        if split and h == heads - 1:
            after = tie(swap(ff_second, "fsdp", 2, 1), per_head[h - 1][0])
            after = ff_first + after.astype(F32)
        per_head.append(attention(h, after, qt, dot, kt, vt, trig_own, trig_other))
    o, dq, dk, dv = zip(*per_head)
    ff_half = halve(after, 1, c % 2, o[-1]) if split else after

    def over_core(keep, send, *earlier):
        v = keep.astype(F32) + tie(swap(send, "tp", 4, 1), *earlier).astype(F32)
        return v.reshape(2, 2, quarter, width)

    def over_x(v, *earlier):
        return v[:, 0] + tie(swap(v[:, 1].astype(BF16), "tp", 4, 2), *earlier).astype(F32)

    keep_b, send_b, out_part = branch(o, g, ff, weights)
    keep_o, send_o, mix_other, small_other = back(
        False, split, at, (dk, dv), n1_other, weights, tie(first_scale, keep_b, ff_half), ()
    )
    half_b = over_core(keep_b, send_b)
    keep_w, send_w, late_first, late_second = back(
        True, split, at, (dq, dk, dv), n1_own, weights, tie(first_scale, half_b),
        (a2, first_shift, small_ff, small_other, mix_other, out_part),
    )
    half_o = over_core(keep_o, send_o)
    half_w = over_core(keep_w, send_w)
    if split:
        ff_pair = pair_up(halve(ff_half, 2, c // 2, keep_w), half_w)
    else:
        ff_pair = half_w

    def over_ctx(v, distance, *earlier):
        return tie(swap(v.astype(BF16), "ctx", 4, distance), *earlier).astype(F32)

    def gather_tp(ours):
        pair = jnp.stack([ours, swap(ours, "tp", 4, 2)])
        core = swap(pair, "tp", 4, 1)
        pieces = by_xor((pair[0], core[0], pair[1], core[1]), t)
        pieces = jnp.concatenate(pieces, axis=1)
        return jnp.stack([jnp.where(s == 0, pieces[0], pieces[1]),
                          jnp.where(s == 0, pieces[1], pieces[0])]).astype(F32)

    sums_b = over_x(half_b, half_w)
    branches = jnp.stack([sums_b[0], over_ctx(sums_b[1], 2)]).astype(BF16)
    block_out = gather_tp(branches)
    block_out = (
        inputs.astype(F32) + block_out + (attention_output_bias + down_projection_bias)
    )

    sums_o = over_x(half_o, ff_pair)
    sums_w = over_x(half_w)
    sums_w = sums_w + over_ctx(sums_o, 1)
    a = jnp.stack([sums_w[0], over_ctx(sums_w[1], 2, branches)])
    xhat, inv = xhat_of(jnp.concatenate([x_mine, x_theirs], axis=0).astype(F32))
    norm_grad = inv * (
        a
        - jnp.mean(a, axis=-1, keepdims=True)
        - xhat * jnp.mean(a * xhat, axis=-1, keepdims=True)
    )
    norm_grad = norm_grad.astype(BF16)
    inputs_grad = cotangent.astype(F32) + gather_tp(norm_grad)

    if split:
        q = double(ff_pair, c, norm_grad)
        up_total = jnp.concatenate(q[:2], axis=0).astype(F32)
        down_total = jnp.concatenate(q[2:], axis=0).astype(F32)
        down_total = jnp.concatenate(
            [down_total[:, : width // 2], down_total[:, width // 2 :]], axis=0
        )
        late = late_first + tie(swap(late_second, "fsdp", 2, 1), sums_o).astype(F32)
        late = double(pair_up(quarter_sum(late, c, sums_w), norm_grad), c)
        late = jnp.concatenate(late, axis=0).astype(F32)
        small = jnp.concatenate([late[4 * local : 4 * local + 8], late[4 * local + 8 :][:8]], axis=1)
    else:
        q = sum_over_ctx(scatter_any(ff_first, 0), c)
        up_total = jnp.concatenate(q, axis=0).astype(F32)
        q = sum_over_ctx(scatter_any(ff_second, 1), c)
        down_total = jnp.concatenate(q, axis=0).astype(F32)
        q = sum_over_ctx(scatter_any(late_first, 1), c)
        late = jnp.concatenate(q, axis=0).astype(F32)
        small = butterfly(butterfly(late_second, "fsdp", fsdp), "ctx", 4)
    mix_total = late[: 3 * local].reshape(3, local, -1).transpose(2, 0, 1)
    out_total = late[3 * local : 4 * local]
    norm_small = butterfly(small, "tp", 4)
    bias_total = norm_small[5] * 0.25
    return (
        block_out,
        inputs_grad,
        mix_total,
        small[6, : 3 * local].reshape(3, local),
        out_total,
        bias_total,
        up_total,
        small[4, :hidden],
        down_total,
        bias_total,
        norm_small[0],
        norm_small[1],
        norm_small[2],
        norm_small[3],
    )


def solution(mesh):
    in_specs = (
        P("fsdp", "ctx", None),
        P("fsdp", None),
        P("fsdp", None, "tp"),
        P(None, "tp"),
        P("tp", "fsdp"),
        P(),
        P("fsdp", "tp"),
        P("tp"),
        P("tp", "fsdp"),
        P(),
        P(),
        P(),
        P(),
        P(),
        P("fsdp", "ctx", None),
    )
    out_specs = (
        P("fsdp", "ctx", None),
        P("fsdp", "ctx", None),
        P("fsdp", None, "tp"),
        P(None, "tp"),
        P("tp", "fsdp"),
        P(),
        P("fsdp", "tp"),
        P("tp"),
        P("tp", "fsdp"),
        P(),
        P(),
        P(),
        P(),
        P(),
    )
    body = functools.partial(shards, dict(mesh.shape))
    return jax.shard_map(body, mesh=mesh, in_specs=in_specs, out_specs=out_specs, check_vma=False)
```

```python
import functools

import jax
import jax.numpy as jnp
from jax import lax
from jax.experimental import pallas as pl
from jax.experimental.pallas import tpu as pltpu
from jax.sharding import PartitionSpec as P

HEAD = 64
ROT = 16
HALF = ROT // 2
EPS = 1e-5
NEG = -1e30
STEP = 256
F32 = jnp.float32
BF16 = jnp.bfloat16
MIB = 1024 * 1024


def mm(a, b, ca=1, cb=0):
    return lax.dot_general(a, b, (((ca,), (cb,)), ((), ())), preferred_element_type=F32)


def params(mib):
    return pltpu.CompilerParams(vmem_limit_bytes=mib * MIB)


def cost(flops, moved, exps=0):
    return pl.CostEstimate(flops=int(flops), bytes_accessed=int(moved), transcendentals=int(exps))


def xhat_of(x):
    width = x.shape[-1]
    centred = x - jnp.sum(x, axis=-1, keepdims=True) * (1.0 / width)
    spread = jnp.sum(centred * centred, axis=-1, keepdims=True) * (1.0 / width)
    inv = lax.rsqrt(spread + EPS)
    return centred * inv, inv


def row_of(ref):
    return ref[...].reshape(1, -1)


def shape(*dims):
    return jax.ShapeDtypeStruct(dims, F32)


def low_shape(*dims):
    return jax.ShapeDtypeStruct(dims, BF16)


def norm_own_kernel(at, xa, xb, ga, gb, fz, fx, fc, ta, tb, s1, b1, s2, b2,
                    n1_ref, n2_ref, g_ref, trig_ref, x):
    i = pl.program_id(0)
    q = xa.shape[1]

    @pl.when(i < 2)
    def _():
        x[:q, :] = xa[0]
        x[q:, :] = xb[0]
        g_ref[:q, :] = ga[0]
        g_ref[q:, :] = gb[0]

    @pl.when(i == 2)
    def _():
        x[:q, :] = fz[0]
        x[q:, :] = fx[0]
        g_ref[:q, :] = fz[1]
        g_ref[q:, :] = fx[1]

    @pl.when(i == 3)
    def _():
        x[:q, :] = fc[0, 0]
        x[q:, :] = fc[1, 0]
        g_ref[:q, :] = fc[0, 1]
        g_ref[q:, :] = fc[1, 1]

    trig_ref[:, :q] = ta[0]
    trig_ref[:, q:] = tb[0]
    xhat, _ = xhat_of(x[...].astype(F32))
    n1_ref[...] = (xhat * row_of(s1) + row_of(b1)).astype(BF16)
    n2_ref[...] = (xhat * row_of(s2) + row_of(b2)).astype(BF16)


def norm_other_kernel(at, nz, nx, nc, ta, tb, s1, b1, n1_ref, trig_ref, x):
    i = pl.program_id(0)
    q = nz.shape[1]
    b = i // 2

    @pl.when(i % 2 == 0)
    def _():
        x[:q, :] = nz[b]
        x[q:, :] = nx[b]

    @pl.when(i % 2 == 1)
    def _():
        x[:q, :] = nc[0, b]
        x[q:, :] = nc[1, b]

    trig_ref[:, :q] = ta[0]
    trig_ref[:, q:] = tb[0]
    xhat, _ = xhat_of(x[...].astype(F32))
    n1_ref[...] = (xhat * row_of(s1) + row_of(b1)).astype(BF16)


def norms(at, own, arrays, trig, vectors):
    width = vectors[0].shape[0]
    rows, q = 4 * STEP, STEP // 2
    tall = trig.shape[1]
    first = 0 if own else 1

    def pick(high):
        def place(i, at):
            block = at[1] ^ (first + 2 * (i // 2))
            return (at[0], 0, block * 4 + (at[2] ^ (i % 2 + high)))

        return pl.BlockSpec((1, tall, q), place)

    def piece(high):
        return pl.BlockSpec(
            (1, q, width), lambda i, at: (at[0], at[2] ^ (jnp.minimum(i, 1) + high), 0)
        )

    def whole(v):
        return pl.BlockSpec(v.shape, lambda i, at: (0,) * v.ndim)

    row = pl.BlockSpec((STEP, width), lambda i, at: (i, 0))
    out_trig = pl.BlockSpec((tall, STEP), lambda i, at: (0, i))
    if own:
        x, g, received = arrays[0], arrays[1], arrays[2:]
        specs = [piece(0), piece(2), piece(0), piece(2)]
        operands = [x, x, g, g]
        kernel, count = norm_own_kernel, 3
    else:
        received, specs, operands = arrays, [], []
        kernel, count = norm_other_kernel, 1
    specs += [whole(v) for v in received] + [pick(0), pick(2)] + [whole(v) for v in vectors]
    operands += [*received, trig, trig, *vectors]
    return pl.pallas_call(
        kernel,
        grid_spec=pltpu.PrefetchScalarGridSpec(
            num_scalar_prefetch=1,
            grid=(rows // STEP,),
            in_specs=specs,
            out_specs=[row] * count + [out_trig],
            scratch_shapes=[pltpu.VMEM((STEP, width), BF16)],
        ),
        out_shape=[low_shape(rows, width)] * count + [shape(tall, rows)],
        compiler_params=params(24),
        cost_estimate=cost(0, 6 * rows * width),
    )(at, *operands)


def project_kernel(n1o, n1x, to, tx, g_ref, w_ref, b_ref, k_ref, v_ref, q_ref, do_ref, bias):
    i = pl.program_id(0)
    wide = k_ref.shape[0]

    @pl.when(i == 0)
    def _():
        for j in range(3):
            line = jnp.broadcast_to(b_ref[j : j + 1, :], (8, wide))
            bias[j * wide : (j + 1) * wide, :] = line.T[:, 0:1]

    def rotated(ref, mixed, trig, factor):
        cosine, sine = trig[:HALF], trig[HALF:ROT]
        for h in range(0, wide, HEAD):
            a, b = mixed[h : h + HALF], mixed[h + HALF : h + ROT]
            turned = jnp.concatenate([a * cosine - b * sine, b * cosine + a * sine], axis=0)
            ref[h : h + ROT, :] = turned.astype(BF16) * factor
            ref[h + ROT : h + HEAD, :] = mixed[h + ROT : h + HEAD].astype(BF16) * factor

    def keys_values(mixed, trig):
        rotated(k_ref, mixed[:wide], trig, BF16(1.0))
        v_ref[...] = mixed[wide:].astype(BF16)

    @pl.when(i < 4)
    def _():
        trig = to[...]
        mixed = mm(w_ref[: 3 * wide, :], n1o[...], 1, 1) + bias[...]
        rotated(q_ref, mixed[:wide], trig, BF16(HEAD**-0.5))
        keys_values(mixed[wide:], trig)
        do_ref[...] = mm(w_ref[3 * wide :, :], g_ref[...], 1, 1).astype(BF16)

    @pl.when(i >= 4)
    def _():
        mixed = mm(w_ref[wide : 3 * wide, :], n1x[...], 1, 1) + bias[wide:, :]
        keys_values(mixed, tx[...])


def project(n1_own, n1_other, trig_own, trig_other, g, weights, bias):
    rows, width = n1_own.shape
    wide = bias.shape[1]
    tall = trig_own.shape[0]

    def own(i):
        return jnp.minimum(i, 3)

    def other(i):
        return jnp.maximum(i - 4, 0)

    col = pl.BlockSpec((wide, STEP), lambda i: (0, i))
    own_col = pl.BlockSpec((wide, STEP), lambda i: (0, own(i)))
    return pl.pallas_call(
        project_kernel,
        grid=(8,),
        in_specs=[
            pl.BlockSpec((STEP, width), lambda i: (own(i), 0)),
            pl.BlockSpec((STEP, width), lambda i: (other(i), 0)),
            pl.BlockSpec((tall, STEP), lambda i: (0, own(i))),
            pl.BlockSpec((tall, STEP), lambda i: (0, other(i))),
            pl.BlockSpec((STEP, width), lambda i: (own(i), 0)),
            pl.BlockSpec((4 * wide, width), lambda i: (0, 0)),
            pl.BlockSpec((3, wide), lambda i: (0, 0)),
        ],
        out_specs=[col, col, own_col, own_col],
        out_shape=[low_shape(wide, 2 * rows)] * 2 + [low_shape(wide, rows)] * 2,
        scratch_shapes=[pltpu.VMEM((3 * wide, 1), F32)],
        compiler_params=params(24),
        cost_estimate=cost(12 * rows * width * wide, 12 * rows * width),
    )(n1_own, n1_other, trig_own, trig_other, g, weights, bias)


def attention_kernel(after, q_ref, do_ref, k_ref, v_ref, tq_ref, to_ref, tx_ref,
                     o_ref, dq_ref, dk_ref, dv_ref, kn, vn, kp, dk, dv, es, dps):
    i = pl.program_id(0)
    length = k_ref.shape[1]
    half = length // 2
    chunk = STEP
    steps = length // chunk

    @pl.when(i == 0)
    def _():
        kn[...] = k_ref[...].T
        vn[...] = v_ref[...].T
        kp[:half, :] = to_ref[ROT:, :].T[:, 0:1]
        kp[half:, :] = tx_ref[ROT:, :].T[:, 0:1]
        dk[...] = jnp.zeros_like(dk)
        dv[...] = jnp.zeros_like(dv)

    qt = q_ref[...]
    dot = do_ref[...]
    qn = qt.T
    don = dot.T
    qpos = tq_ref[ROT : ROT + 1, :]
    lanes = qt.shape[1]
    fold = (chunk // 8, 8, lanes)

    top = jnp.full((8, lanes), NEG, F32)
    for j in range(steps):
        here = slice(j * chunk, (j + 1) * chunk)
        s = mm(kn[here, :], qt)
        s = jnp.where(kp[here, :] <= qpos, s, NEG)
        es[here, :] = s
        top = jnp.maximum(top, jnp.max(s.reshape(fold), axis=0))
    top = jnp.max(top, axis=0, keepdims=True)

    total = jnp.zeros((8, lanes), F32)
    inner = jnp.zeros((8, lanes), F32)
    for j in range(steps):
        here = slice(j * chunk, (j + 1) * chunk)
        e = jnp.exp(es[here, :] - top)
        dp = mm(vn[here, :], dot)
        es[here, :] = e
        dps[here, :] = dp
        total = total + jnp.sum(e.reshape(fold), axis=0)
        inner = inner + jnp.sum((e * dp).reshape(fold), axis=0)
    share = 1.0 / jnp.sum(total, axis=0, keepdims=True)
    inner = jnp.sum(inner, axis=0, keepdims=True) * share

    ot = jnp.zeros((HEAD, lanes), F32)
    dqt = jnp.zeros((HEAD, lanes), F32)
    for j in range(steps):
        here = slice(j * chunk, (j + 1) * chunk)
        p = es[here, :] * share
        ds = (p * (dps[here, :] - inner)).astype(BF16)
        p = p.astype(BF16)
        dv[here, :] += mm(p, don)
        dk[here, :] += mm(ds, qn)
        ot = ot + mm(v_ref[:, here], p)
        dqt = dqt + mm(k_ref[:, here], ds)
    o_ref[...] = ot.astype(BF16)

    def unrotated(grad, trig):
        cosine, sine = trig[:HALF], trig[HALF:ROT]
        a, b = grad[:HALF], grad[HALF:ROT]
        turned = jnp.concatenate([a * cosine + b * sine, b * cosine - a * sine], axis=0)
        return turned.astype(BF16), grad[ROT:].astype(BF16)

    dq_ref[:ROT, :], dq_ref[ROT:, :] = unrotated(dqt * (HEAD**-0.5), tq_ref[...])

    @pl.when(i == pl.num_programs(0) - 1)
    def _():
        grad = dk[...].T
        dk_ref[:ROT, :half], dk_ref[ROT:, :half] = unrotated(grad[:, :half], to_ref[...])
        dk_ref[:ROT, half:], dk_ref[ROT:, half:] = unrotated(grad[:, half:], tx_ref[...])
        dv_ref[...] = dv[...].T.astype(BF16)


def attention(h, after, qt, dot, kt, vt, trig_own, trig_other):
    rows, length = qt.shape[1], kt.shape[1]
    lanes = STEP
    tall = trig_own.shape[0]
    q_spec = pl.BlockSpec((HEAD, lanes), lambda i: (h, i))
    k_spec = pl.BlockSpec((HEAD, length), lambda i: (h, 0))
    trig_spec = pl.BlockSpec((tall, rows), lambda i: (0, 0))
    return pl.pallas_call(
        attention_kernel,
        grid=(rows // lanes,),
        in_specs=[pl.BlockSpec(memory_space=pl.ANY), q_spec, q_spec, k_spec, k_spec,
                  pl.BlockSpec((tall, lanes), lambda i: (0, i)), trig_spec, trig_spec],
        out_specs=[pl.BlockSpec((HEAD, lanes), lambda i: (0, i))] * 2
        + [pl.BlockSpec((HEAD, length), lambda i: (0, 0))] * 2,
        out_shape=[low_shape(HEAD, rows)] * 2 + [low_shape(HEAD, length)] * 2,
        scratch_shapes=[
            pltpu.VMEM((length, HEAD), BF16),
            pltpu.VMEM((length, HEAD), BF16),
            pltpu.VMEM((length, 1), F32),
            pltpu.VMEM((length, HEAD), F32),
            pltpu.VMEM((length, HEAD), F32),
            pltpu.VMEM((length, lanes), F32),
            pltpu.VMEM((length, lanes), F32),
        ],
        compiler_params=params(32),
        cost_estimate=cost(40 * rows * length * HEAD, 16 * HEAD * length, rows * length),
    )(after, qt, dot, kt, vt, trig_own, trig_own, trig_other)


def forward_kernel(split, at, n2_ref, g_ref, up_ref, bias_ref, down_ref, s2_ref, b2_ref,
                   ff_ref, a_ref, small_ref, first_ref, second_ref, *scratch):
    i = pl.program_id(0)
    up_part, down_part = scratch if split else (first_ref, second_ref)

    @pl.when(i == 0)
    def _():
        up_part[...] = jnp.zeros_like(up_part)
        down_part[...] = jnp.zeros_like(down_part)
        small_ref[...] = jnp.zeros_like(small_ref)

    n2, g = n2_ref[...], g_ref[...]
    up = mm(n2, up_ref[...]) + row_of(bias_ref)
    cdf = 0.5 + 0.5 * lax.erf(up * (0.5**0.5))
    act = (up * cdf).astype(BF16)
    slope = cdf + up * (jnp.exp(up * up * -0.5) * 0.3989422804014327)
    up_grad = (mm(g, down_ref[...], 1, 1) * slope).astype(BF16)
    ff_ref[...] = mm(act, down_ref[...]).astype(BF16)
    second = mm(up_grad, up_ref[...], 1, 1)
    up_part[...] += mm(n2, up_grad, 0, 0)
    down_part[...] += mm(act, g, 0, 0)
    a_ref[...] = (second * row_of(s2_ref)).astype(BF16)
    small_ref[0:1, :] += jnp.sum(up_grad.astype(F32), axis=0, keepdims=True)
    small_ref[1:2, :] += jnp.sum(g.astype(F32), axis=0, keepdims=True)
    small_ref[2:3, :] += jnp.sum(second * n2.astype(F32), axis=0, keepdims=True)
    small_ref[3:4, :] += jnp.sum(second, axis=0, keepdims=True)

    @pl.when(i == pl.num_programs(0) - 1)
    def _():
        rest = small_ref[2:3, :] - row_of(b2_ref) * small_ref[3:4, :]
        small_ref[2:3, :] = rest / row_of(s2_ref)

    if split:
        half = up_part.shape[0] // 2

        @pl.when(i == pl.num_programs(0) - 1)
        def _():
            for ref, f in ((first_ref, at[3]), (second_ref, 1 - at[3])):
                piece = pl.ds(pl.multiple_of(f * half, 128), half)
                ref[:half, :] = up_part[piece, :].astype(ref.dtype)
                ref[half:, :half] = down_part[:half, piece].astype(ref.dtype)
                ref[half:, half:] = down_part[half:, piece].astype(ref.dtype)


def feed_forward(split, at, n2, g, up, bias, down, scale, offset):
    rows, width = n2.shape
    hidden = up.shape[1]
    row = pl.BlockSpec((STEP, width), lambda i, at: (i, 0))

    def whole(*dims):
        return pl.BlockSpec(dims, lambda i, at: (0,) * len(dims))

    if split:
        assert width == hidden
        parts = [shape(width, hidden), low_shape(width, hidden)]
    else:
        parts = [shape(width, hidden), shape(hidden, width)]
    return pl.pallas_call(
        functools.partial(forward_kernel, split),
        grid_spec=pltpu.PrefetchScalarGridSpec(
            num_scalar_prefetch=1,
            grid=(rows // STEP,),
            in_specs=[row, row, whole(width, hidden), whole(hidden), whole(hidden, width),
                      whole(width), whole(width)],
            out_specs=[row, row, whole(8, width)] + [whole(*p.shape) for p in parts],
            scratch_shapes=[pltpu.VMEM((width, hidden), F32), pltpu.VMEM((hidden, width), F32)]
            if split
            else [],
        ),
        out_shape=[low_shape(rows, width)] * 2 + [shape(8, width)] + parts,
        compiler_params=params(40),
        cost_estimate=cost(12 * rows * width * hidden, 16 * MIB, 2 * rows * hidden),
    )(at, n2, g, up, bias, down, scale, offset)


def emit(keep_ref, send_ref, v):
    i = pl.program_id(0)

    @pl.when(i % 2 == 0)
    def _():
        keep_ref[0] = v.astype(BF16)

    @pl.when(i % 2 == 1)
    def _():
        send_ref[0] = v.astype(BF16)


def branch_kernel(heads, *refs):
    o = refs[:heads]
    g_ref, ff_ref, w_ref, keep_ref, send_ref, out = refs[heads:]
    wide = heads * HEAD

    @pl.when(pl.program_id(0) == 0)
    def _():
        out[...] = jnp.zeros_like(out)

    ot = jnp.concatenate([r[...] for r in o], axis=0)
    emit(keep_ref, send_ref, mm(ot, w_ref[...], 0, 0) + ff_ref[...].astype(F32))
    out[...] += mm(ot, g_ref[...])


def branch(o, g, ff, weights):
    rows, width = g.shape
    heads = len(o)
    wide = heads * HEAD
    row = pl.BlockSpec((STEP, width), lambda i: (i, 0))
    slots = pl.BlockSpec((1, STEP, width), lambda i: (i // 2, 0, 0))
    return pl.pallas_call(
        functools.partial(branch_kernel, heads),
        grid=(rows // STEP,),
        in_specs=[pl.BlockSpec((HEAD, STEP), lambda i: (0, i))] * heads
        + [row, row, pl.BlockSpec((wide, width), lambda i: (3, 0))],
        out_specs=[slots, slots, pl.BlockSpec((wide, width), lambda i: (0, 0))],
        out_shape=[low_shape(2, STEP, width)] * 2 + [shape(wide, width)],
        compiler_params=params(24),
        cost_estimate=cost(4 * rows * width * wide, 8 * MIB),
    )(*o, g, ff, weights)


def back_kernel(own, split, heads, at, *refs):
    count = 3 if own else 2
    grads, refs = refs[: count * heads], refs[count * heads :]
    n1_ref, w_ref, s1_ref, *refs = refs
    if own:
        (half_b, a2_ref, b1_ref, small_ff, small_other, mix_other, out_part,
         keep_ref, send_ref, first_ref, second_ref, mix, small) = refs
    else:
        keep_b, ff_half, keep_ref, send_ref, mix, small = refs
    i = pl.program_id(0)
    wide = heads * HEAD
    tall = mix.shape[0]

    @pl.when(i == 0)
    def _():
        if own:
            mix[:wide, :] = jnp.zeros((wide, mix.shape[1]), F32)
            mix[wide:, :] = mix_other[...]
            small[...] = small_other[...]
        else:
            mix[...] = jnp.zeros_like(mix)
            small[...] = jnp.zeros_like(small)

    grad = jnp.concatenate([r[...] for r in grads], axis=0)
    first = mm(grad, w_ref[3 * wide - tall : 3 * wide, :], 0, 0)
    a = first * row_of(s1_ref)
    emit(keep_ref, send_ref, a + a2_ref[...].astype(F32) if own else a)
    mix[...] += mm(grad, n1_ref[...])
    small[0:1, :] += jnp.sum(first * n1_ref[...].astype(F32), axis=0, keepdims=True)
    small[1:2, :] += jnp.sum(first, axis=0, keepdims=True)
    ones = jnp.ones((8, grad.shape[1]), BF16)
    small[6:7, 3 * wide - tall : 3 * wide] += mm(ones, grad, 1, 1)[0:1]

    if own:
        @pl.when(i == pl.num_programs(0) - 1)
        def _():
            rest = small[0:1, :] - row_of(b1_ref) * small[1:2, :]
            small[0:1, :] = rest / row_of(s1_ref)
            small[2:4, :] = small_ff[2:4, :]
            small[4:6, :] = small_ff[0:2, :]
            if split:
                half = mix.shape[1] // 2
                vectors = small[...].astype(BF16)
                for ref, f in ((first_ref, at[3]), (second_ref, 1 - at[3])):
                    piece = pl.ds(pl.multiple_of(f * half, 128), half)
                    ref[: 3 * wide, :] = mix[:, piece].astype(ref.dtype)
                    ref[3 * wide : 4 * wide, :] = out_part[:, piece].astype(ref.dtype)
                    both = jnp.concatenate([vectors[:, :half], vectors[:, half:]], axis=0)
                    ref[4 * wide : 4 * wide + 16, :] = both.astype(ref.dtype)
                    ref[4 * wide + 16 :, :] = jnp.zeros((48, half), ref.dtype)
            else:
                first_ref[: 3 * wide, :] = mix[...]
                first_ref[3 * wide :, :] = out_part[...]
                second_ref[...] = small[...]


def back(own, split, at, grads, n1, weights, scale, extra):
    rows, width = n1.shape
    heads = len(grads[0])
    wide = heads * HEAD
    tall = 3 * wide if own else 2 * wide
    offset = 0 if own else rows // STEP
    row = pl.BlockSpec((STEP, width), lambda i, at: (i, 0))
    col = pl.BlockSpec((HEAD, STEP), lambda i, at: (0, i + offset))
    slots = pl.BlockSpec((1, STEP, width), lambda i, at: (i // 2, 0, 0))

    def whole(*dims):
        return pl.BlockSpec(dims, lambda i, at: (0,) * len(dims))

    half = width // 2
    specs = [col] * (len(grads) * heads) + [row, whole(4 * wide, width), whole(width)]
    earlier = pl.BlockSpec(memory_space=pl.ANY)
    if not own:
        specs += [earlier, earlier]
        parts = [shape(tall, width), shape(8, width)]
        scratch = []
    else:
        specs += [earlier, row, whole(width), whole(8, width), whole(8, width), whole(2 * wide, width),
                  whole(wide, width)]
        scratch = [pltpu.VMEM((tall, width), F32), pltpu.VMEM((8, width), F32)]
        if split:
            parts = [shape(4 * wide + 64, half), low_shape(4 * wide + 64, half)]
        else:
            parts = [shape(4 * wide, width), shape(8, width)]
    return pl.pallas_call(
        functools.partial(back_kernel, own, split, heads),
        grid_spec=pltpu.PrefetchScalarGridSpec(
            num_scalar_prefetch=1,
            grid=(rows // STEP,),
            in_specs=specs,
            out_specs=[slots, slots] + [whole(*p.shape) for p in parts],
            scratch_shapes=scratch,
        ),
        out_shape=[low_shape(2, STEP, width)] * 2 + parts,
        compiler_params=params(32),
        cost_estimate=cost(4 * rows * width * tall, 10 * MIB),
    )(at, *[v for vs in grads for v in vs], n1, weights, scale, *extra)


def swap(v, axis, size, distance):
    return lax.ppermute(v, axis, [(i, i ^ distance) for i in range(size)])


def by_xor(pieces, index):
    low, high = (index & 1) == 1, (index & 2) == 2
    a, b, c, d = pieces
    a, b, c, d = (jnp.where(low, b, a), jnp.where(low, a, b),
                  jnp.where(low, d, c), jnp.where(low, c, d))
    return (jnp.where(high, c, a), jnp.where(high, d, b),
            jnp.where(high, a, c), jnp.where(high, b, d))


def tie(v, *earlier):
    return lax.optimization_barrier((v, *earlier))[0]


def gather_halves(shard, size, mine, dim, *earlier):
    if size != 2:
        return lax.all_gather(shard, "fsdp", axis=dim, tiled=True)
    other = swap(shard, "fsdp", 2, 1)
    if earlier:
        other = tie(other, *earlier)
    first = mine == 0
    return jnp.concatenate(
        [jnp.where(first, shard, other), jnp.where(first, other, shard)], axis=dim
    )


def scatter_any(part, dim):
    return lax.psum_scatter(
        part.astype(BF16), "fsdp", scatter_dimension=dim, tiled=True
    ).astype(F32)


def halve(v, distance, bit, *earlier):
    rows = v.shape[0] // 2
    keep = lax.dynamic_slice_in_dim(v, bit * rows, rows, 0)
    send = lax.dynamic_slice_in_dim(v, (1 - bit) * rows, rows, 0).astype(BF16)
    return keep + tie(swap(send, "ctx", 4, distance), *earlier).astype(F32)


def quarter_sum(v, c, *earlier):
    rows = v.shape[0] // 4
    mine = 2 * (c % 2) + c // 2

    def part(j):
        return lax.dynamic_slice_in_dim(v, (mine ^ j) * rows, rows, 0)

    total = part(0)
    for distance, j in ((3, 3), (2, 1), (1, 2)):
        sent = swap(part(j).astype(BF16), "ctx", 4, distance)
        total = total + tie(sent, *earlier).astype(F32)
    return total


def pair_up(v, *earlier):
    v = v.astype(BF16)
    return jnp.stack([v, tie(swap(v, "ctx", 4, 2), *earlier)])


def double(pair, c, *earlier):
    others = tie(swap(pair, "ctx", 4, 1), *earlier)
    return by_xor([pair[0], pair[1], others[0], others[1]], 2 * (c % 2) + c // 2)


def sum_over_ctx(v, c):
    return double(pair_up(quarter_sum(v, c)), c)


def butterfly(v, axis_name, size):
    distance = 1
    while distance < size:
        v = v + swap(v, axis_name, size, distance)
        distance *= 2
    return v


def shards(
    sizes,
    inputs,
    positions,
    query_key_value_weight,
    query_key_value_bias,
    attention_output_weight,
    attention_output_bias,
    up_projection_weight,
    up_projection_bias,
    down_projection_weight,
    down_projection_bias,
    first_scale,
    first_shift,
    second_scale,
    second_shift,
    cotangent,
):
    fsdp = sizes["fsdp"]
    split = fsdp == 2
    seq_count, block, width = inputs.shape
    assert seq_count == 2 and sizes["ctx"] == 4 and sizes["tp"] == 4 and block == 2 * STEP
    length = positions.shape[1]
    local = query_key_value_weight.shape[2]
    heads = local // HEAD
    hidden = up_projection_weight.shape[1]
    quarter = block // 4
    f = lax.axis_index("fsdp")
    c = lax.axis_index("ctx")
    t = lax.axis_index("tp")
    s = c // 2
    at = jnp.stack([s, c, t, f]).astype(jnp.int32)

    def my_quarter(v, seq):
        return lax.dynamic_slice(v, (seq, t * quarter, 0), (1, quarter, width))

    x_mine, x_theirs = my_quarter(inputs, s), my_quarter(inputs, 1 - s)
    g_theirs = my_quarter(cotangent, 1 - s)
    far_z = swap(jnp.concatenate([x_theirs, g_theirs], axis=0), "ctx", 4, 2)
    cross = swap(x_theirs, "ctx", 4, 3)
    near = swap(x_mine, "ctx", 4, 1)

    def over_tp(v):
        v_x = swap(v, "tp", 4, 2)
        return v, v_x, swap(jnp.stack([v, v_x]), "tp", 4, 1)

    far = over_tp(far_z)
    others = over_tp(jnp.concatenate([near, cross], axis=0))

    wup = gather_halves(up_projection_weight, fsdp, f, 0)
    wdown = gather_halves(down_projection_weight, fsdp, f, 1)
    mix_shard = query_key_value_weight.transpose(1, 2, 0).reshape(3 * local, -1)
    mix_out_shard = jnp.concatenate([mix_shard, attention_output_weight], axis=0)

    inverse = 10000.0 ** (-2.0 * jnp.arange(HALF, dtype=F32) / ROT)
    places = positions.astype(F32)[:, None, :]
    angles = inverse[None, :, None] * places
    trig = jnp.concatenate(
        [jnp.cos(angles), jnp.sin(angles), jnp.broadcast_to(places, angles.shape)], axis=1
    )

    n1_own, n2, g, trig_own = norms(
        at, True, (inputs, cotangent, *far), trig,
        (first_scale, first_shift, second_scale, second_shift),
    )
    ff, a2, small_ff, ff_first, ff_second = feed_forward(
        split, at, n2, g, wup, up_projection_bias, wdown, second_scale, second_shift
    )
    weights = gather_halves(mix_out_shard, fsdp, f, 1, small_ff)
    n1_other, trig_other = norms(
        at, False, (others[0], others[1], tie(others[2], small_ff)), trig,
        (first_scale, first_shift),
    )
    kt, vt, qt, dot = project(
        n1_own, n1_other, trig_own, trig_other, g, weights, query_key_value_bias
    )
    per_head = []
    after = small_ff
    for h in range(heads):
        if split and h == heads - 1:
            after = ff_first + swap(ff_second, "fsdp", 2, 1).astype(F32)
        per_head.append(attention(h, after, qt, dot, kt, vt, trig_own, trig_other))
    o, dq, dk, dv = zip(*per_head)
    ff_half = halve(after, 1, c % 2) if split else after

    def over_core(keep, send, *earlier):
        v = keep.astype(F32) + tie(swap(send, "tp", 4, 1), *earlier).astype(F32)
        return v.reshape(2, 2, quarter, width)

    def over_x(v, *earlier):
        return v[:, 0] + tie(swap(v[:, 1].astype(BF16), "tp", 4, 2), *earlier).astype(F32)

    keep_b, send_b, out_part = branch(o, g, ff, weights)
    keep_o, send_o, mix_other, small_other = back(
        False, split, at, (dk, dv), n1_other, weights, first_scale, (keep_b, ff_half)
    )
    half_b = over_core(keep_b, send_b)
    keep_w, send_w, late_first, late_second = back(
        True, split, at, (dq, dk, dv), n1_own, weights, first_scale,
        (half_b, a2, first_shift, small_ff, small_other, mix_other, out_part),
    )
    half_o = over_core(keep_o, send_o)
    half_w = over_core(keep_w, send_w)

    def over_ctx(v, distance, *earlier):
        return tie(swap(v.astype(BF16), "ctx", 4, distance), *earlier).astype(F32)

    def gather_tp(ours):
        pair = jnp.stack([ours, swap(ours, "tp", 4, 2)])
        core = swap(pair, "tp", 4, 1)
        pieces = by_xor((pair[0], core[0], pair[1], core[1]), t)
        pieces = jnp.concatenate(pieces, axis=1)
        return jnp.stack([jnp.where(s == 0, pieces[0], pieces[1]),
                          jnp.where(s == 0, pieces[1], pieces[0])]).astype(F32)

    sums_b = over_x(half_b, half_w)
    branches = jnp.stack([sums_b[0], over_ctx(sums_b[1], 2)]).astype(BF16)
    block_out = gather_tp(branches)
    block_out = (
        inputs.astype(F32) + block_out + (attention_output_bias + down_projection_bias)
    )

    sums_o = over_x(half_o, half_w)
    sums_w = over_x(half_w)
    sums_w = sums_w + over_ctx(sums_o, 1)
    a = jnp.stack([sums_w[0], over_ctx(sums_w[1], 2, branches)])
    xhat, inv = xhat_of(jnp.concatenate([x_mine, x_theirs], axis=0).astype(F32))
    norm_grad = inv * (
        a
        - jnp.mean(a, axis=-1, keepdims=True)
        - xhat * jnp.mean(a * xhat, axis=-1, keepdims=True)
    )
    norm_grad = norm_grad.astype(BF16)
    inputs_grad = cotangent.astype(F32) + gather_tp(norm_grad)

    if split:
        q = double(pair_up(halve(ff_half, 2, c // 2), sums_o), c, norm_grad)
        up_total = jnp.concatenate(q[:2], axis=0).astype(F32)
        down_total = jnp.concatenate(q[2:], axis=0).astype(F32)
        down_total = jnp.concatenate(
            [down_total[:, : width // 2], down_total[:, width // 2 :]], axis=0
        )
        late = late_first + tie(swap(late_second, "fsdp", 2, 1), sums_o).astype(F32)
        late = double(pair_up(quarter_sum(late, c, sums_w), norm_grad), c)
        late = jnp.concatenate(late, axis=0).astype(F32)
        small = jnp.concatenate([late[4 * local : 4 * local + 8], late[4 * local + 8 :][:8]], axis=1)
    else:
        q = sum_over_ctx(scatter_any(ff_first, 0), c)
        up_total = jnp.concatenate(q, axis=0).astype(F32)
        q = sum_over_ctx(scatter_any(ff_second, 1), c)
        down_total = jnp.concatenate(q, axis=0).astype(F32)
        q = sum_over_ctx(scatter_any(late_first, 1), c)
        late = jnp.concatenate(q, axis=0).astype(F32)
        small = butterfly(butterfly(late_second, "fsdp", fsdp), "ctx", 4)
    mix_total = late[: 3 * local].reshape(3, local, -1).transpose(2, 0, 1)
    out_total = late[3 * local : 4 * local]
    norm_small = butterfly(small, "tp", 4)
    bias_total = norm_small[5] * 0.25
    return (
        block_out,
        inputs_grad,
        mix_total,
        small[6, : 3 * local].reshape(3, local),
        out_total,
        bias_total,
        up_total,
        small[4, :hidden],
        down_total,
        bias_total,
        norm_small[0],
        norm_small[1],
        norm_small[2],
        norm_small[3],
    )


def solution(mesh):
    in_specs = (
        P("fsdp", "ctx", None),
        P("fsdp", None),
        P("fsdp", None, "tp"),
        P(None, "tp"),
        P("tp", "fsdp"),
        P(),
        P("fsdp", "tp"),
        P("tp"),
        P("tp", "fsdp"),
        P(),
        P(),
        P(),
        P(),
        P(),
        P("fsdp", "ctx", None),
    )
    out_specs = (
        P("fsdp", "ctx", None),
        P("fsdp", "ctx", None),
        P("fsdp", None, "tp"),
        P(None, "tp"),
        P("tp", "fsdp"),
        P(),
        P("fsdp", "tp"),
        P("tp"),
        P("tp", "fsdp"),
        P(),
        P(),
        P(),
        P(),
        P(),
    )
    body = functools.partial(shards, dict(mesh.shape))
    return jax.shard_map(body, mesh=mesh, in_specs=in_specs, out_specs=out_specs, check_vma=False)
```

```python
import functools

import jax
import jax.numpy as jnp
from jax import lax
from jax.experimental import pallas as pl
from jax.experimental.pallas import tpu as pltpu
from jax.sharding import PartitionSpec as P

HEAD = 64
ROT = 16
HALF = ROT // 2
EPS = 1e-5
NEG = -1e30
STEP = 256
F32 = jnp.float32
BF16 = jnp.bfloat16
MIB = 1024 * 1024


def mm(a, b, ca=1, cb=0):
    return lax.dot_general(a, b, (((ca,), (cb,)), ((), ())), preferred_element_type=F32)


def params(mib):
    return pltpu.CompilerParams(vmem_limit_bytes=mib * MIB)


def cost(flops, moved, exps=0):
    return pl.CostEstimate(flops=int(flops), bytes_accessed=int(moved), transcendentals=int(exps))


def xhat_of(x):
    width = x.shape[-1]
    centred = x - jnp.sum(x, axis=-1, keepdims=True) * (1.0 / width)
    spread = jnp.sum(centred * centred, axis=-1, keepdims=True) * (1.0 / width)
    inv = lax.rsqrt(spread + EPS)
    return centred * inv, inv


def row_of(ref):
    return ref[...].reshape(1, -1)


def shape(*dims):
    return jax.ShapeDtypeStruct(dims, F32)


def low_shape(*dims):
    return jax.ShapeDtypeStruct(dims, BF16)


def norm_own_kernel(at, xa, xb, ga, gb, fz, fx, fc, ta, tb, s1, b1, s2, b2,
                    n1_ref, n2_ref, g_ref, trig_ref, x):
    i = pl.program_id(0)
    q = xa.shape[1]

    @pl.when(i < 2)
    def _():
        x[:q, :] = xa[0]
        x[q:, :] = xb[0]
        g_ref[:q, :] = ga[0]
        g_ref[q:, :] = gb[0]

    @pl.when(i == 2)
    def _():
        x[:q, :] = fz[0]
        x[q:, :] = fx[0]
        g_ref[:q, :] = fz[1]
        g_ref[q:, :] = fx[1]

    @pl.when(i == 3)
    def _():
        x[:q, :] = fc[0, 0]
        x[q:, :] = fc[1, 0]
        g_ref[:q, :] = fc[0, 1]
        g_ref[q:, :] = fc[1, 1]

    trig_ref[:, :q] = ta[0]
    trig_ref[:, q:] = tb[0]
    xhat, _ = xhat_of(x[...].astype(F32))
    n1_ref[...] = (xhat * row_of(s1) + row_of(b1)).astype(BF16)
    n2_ref[...] = (xhat * row_of(s2) + row_of(b2)).astype(BF16)


def norm_other_kernel(at, nz, nx, nc, ta, tb, s1, b1, n1_ref, trig_ref, x):
    i = pl.program_id(0)
    q = nz.shape[1]
    b = i // 2

    @pl.when(i % 2 == 0)
    def _():
        x[:q, :] = nz[b]
        x[q:, :] = nx[b]

    @pl.when(i % 2 == 1)
    def _():
        x[:q, :] = nc[0, b]
        x[q:, :] = nc[1, b]

    trig_ref[:, :q] = ta[0]
    trig_ref[:, q:] = tb[0]
    xhat, _ = xhat_of(x[...].astype(F32))
    n1_ref[...] = (xhat * row_of(s1) + row_of(b1)).astype(BF16)


def norms(at, own, arrays, trig, vectors):
    width = vectors[0].shape[0]
    rows, q = 4 * STEP, STEP // 2
    tall = trig.shape[1]
    first = 0 if own else 1

    def pick(high):
        def place(i, at):
            block = at[1] ^ (first + 2 * (i // 2))
            return (at[0], 0, block * 4 + (at[2] ^ (i % 2 + high)))

        return pl.BlockSpec((1, tall, q), place)

    def piece(high):
        return pl.BlockSpec(
            (1, q, width), lambda i, at: (at[0], at[2] ^ (jnp.minimum(i, 1) + high), 0)
        )

    def whole(v):
        return pl.BlockSpec(v.shape, lambda i, at: (0,) * v.ndim)

    row = pl.BlockSpec((STEP, width), lambda i, at: (i, 0))
    out_trig = pl.BlockSpec((tall, STEP), lambda i, at: (0, i))
    if own:
        x, g, received = arrays[0], arrays[1], arrays[2:]
        specs = [piece(0), piece(2), piece(0), piece(2)]
        operands = [x, x, g, g]
        kernel, count = norm_own_kernel, 3
    else:
        received, specs, operands = arrays, [], []
        kernel, count = norm_other_kernel, 1
    specs += [whole(v) for v in received] + [pick(0), pick(2)] + [whole(v) for v in vectors]
    operands += [*received, trig, trig, *vectors]
    return pl.pallas_call(
        kernel,
        grid_spec=pltpu.PrefetchScalarGridSpec(
            num_scalar_prefetch=1,
            grid=(rows // STEP,),
            in_specs=specs,
            out_specs=[row] * count + [out_trig],
            scratch_shapes=[pltpu.VMEM((STEP, width), BF16)],
        ),
        out_shape=[low_shape(rows, width)] * count + [shape(tall, rows)],
        compiler_params=params(24),
        cost_estimate=cost(0, 6 * rows * width),
    )(at, *operands)


def project_kernel(n1o, n1x, to, tx, g_ref, w_ref, b_ref, k_ref, v_ref, q_ref, do_ref, bias):
    i = pl.program_id(0)
    wide = k_ref.shape[0]

    @pl.when(i == 0)
    def _():
        for j in range(3):
            line = jnp.broadcast_to(b_ref[j : j + 1, :], (8, wide))
            bias[j * wide : (j + 1) * wide, :] = line.T[:, 0:1]

    def rotated(ref, mixed, trig, factor):
        cosine, sine = trig[:HALF], trig[HALF:ROT]
        for h in range(0, wide, HEAD):
            a, b = mixed[h : h + HALF], mixed[h + HALF : h + ROT]
            turned = jnp.concatenate([a * cosine - b * sine, b * cosine + a * sine], axis=0)
            ref[h : h + ROT, :] = turned.astype(BF16) * factor
            ref[h + ROT : h + HEAD, :] = mixed[h + ROT : h + HEAD].astype(BF16) * factor

    def keys_values(mixed, trig):
        rotated(k_ref, mixed[:wide], trig, BF16(1.0))
        v_ref[...] = mixed[wide:].astype(BF16)

    @pl.when(i < 4)
    def _():
        trig = to[...]
        mixed = mm(w_ref[: 3 * wide, :], n1o[...], 1, 1) + bias[...]
        rotated(q_ref, mixed[:wide], trig, BF16(HEAD**-0.5))
        keys_values(mixed[wide:], trig)
        do_ref[...] = mm(w_ref[3 * wide :, :], g_ref[...], 1, 1).astype(BF16)

    @pl.when(i >= 4)
    def _():
        mixed = mm(w_ref[wide : 3 * wide, :], n1x[...], 1, 1) + bias[wide:, :]
        keys_values(mixed, tx[...])


def project(n1_own, n1_other, trig_own, trig_other, g, weights, bias):
    rows, width = n1_own.shape
    wide = bias.shape[1]
    tall = trig_own.shape[0]

    def own(i):
        return jnp.minimum(i, 3)

    def other(i):
        return jnp.maximum(i - 4, 0)

    col = pl.BlockSpec((wide, STEP), lambda i: (0, i))
    own_col = pl.BlockSpec((wide, STEP), lambda i: (0, own(i)))
    return pl.pallas_call(
        project_kernel,
        grid=(8,),
        in_specs=[
            pl.BlockSpec((STEP, width), lambda i: (own(i), 0)),
            pl.BlockSpec((STEP, width), lambda i: (other(i), 0)),
            pl.BlockSpec((tall, STEP), lambda i: (0, own(i))),
            pl.BlockSpec((tall, STEP), lambda i: (0, other(i))),
            pl.BlockSpec((STEP, width), lambda i: (own(i), 0)),
            pl.BlockSpec((4 * wide, width), lambda i: (0, 0)),
            pl.BlockSpec((3, wide), lambda i: (0, 0)),
        ],
        out_specs=[col, col, own_col, own_col],
        out_shape=[low_shape(wide, 2 * rows)] * 2 + [low_shape(wide, rows)] * 2,
        scratch_shapes=[pltpu.VMEM((3 * wide, 1), F32)],
        compiler_params=params(24),
        cost_estimate=cost(12 * rows * width * wide, 12 * rows * width),
    )(n1_own, n1_other, trig_own, trig_other, g, weights, bias)


def attention_kernel(after, q_ref, do_ref, k_ref, v_ref, tq_ref, to_ref, tx_ref,
                     o_ref, dq_ref, dk_ref, dv_ref, kn, vn, kp, dk, dv, es, dps):
    i = pl.program_id(0)
    length = k_ref.shape[1]
    half = length // 2
    chunk = STEP
    steps = length // chunk

    @pl.when(i == 0)
    def _():
        kn[...] = k_ref[...].T
        vn[...] = v_ref[...].T
        kp[:half, :] = to_ref[ROT:, :].T[:, 0:1]
        kp[half:, :] = tx_ref[ROT:, :].T[:, 0:1]
        dk[...] = jnp.zeros_like(dk)
        dv[...] = jnp.zeros_like(dv)

    qt = q_ref[...]
    dot = do_ref[...]
    qn = qt.T
    don = dot.T
    qpos = tq_ref[ROT : ROT + 1, :]
    lanes = qt.shape[1]
    fold = (chunk // 8, 8, lanes)

    top = jnp.full((8, lanes), NEG, F32)
    for j in range(steps):
        here = slice(j * chunk, (j + 1) * chunk)
        s = mm(kn[here, :], qt)
        s = jnp.where(kp[here, :] <= qpos, s, NEG)
        es[here, :] = s
        top = jnp.maximum(top, jnp.max(s.reshape(fold), axis=0))
    top = jnp.max(top, axis=0, keepdims=True)

    total = jnp.zeros((8, lanes), F32)
    inner = jnp.zeros((8, lanes), F32)
    for j in range(steps):
        here = slice(j * chunk, (j + 1) * chunk)
        e = jnp.exp(es[here, :] - top)
        dp = mm(vn[here, :], dot)
        es[here, :] = e
        dps[here, :] = dp
        total = total + jnp.sum(e.reshape(fold), axis=0)
        inner = inner + jnp.sum((e * dp).reshape(fold), axis=0)
    share = 1.0 / jnp.sum(total, axis=0, keepdims=True)
    inner = jnp.sum(inner, axis=0, keepdims=True) * share

    ot = jnp.zeros((HEAD, lanes), F32)
    dqt = jnp.zeros((HEAD, lanes), F32)
    for j in range(steps):
        here = slice(j * chunk, (j + 1) * chunk)
        p = es[here, :] * share
        ds = (p * (dps[here, :] - inner)).astype(BF16)
        p = p.astype(BF16)
        dv[here, :] += mm(p, don)
        dk[here, :] += mm(ds, qn)
        ot = ot + mm(v_ref[:, here], p)
        dqt = dqt + mm(k_ref[:, here], ds)
    o_ref[...] = ot.astype(BF16)

    def unrotated(grad, trig):
        cosine, sine = trig[:HALF], trig[HALF:ROT]
        a, b = grad[:HALF], grad[HALF:ROT]
        turned = jnp.concatenate([a * cosine + b * sine, b * cosine - a * sine], axis=0)
        return turned.astype(BF16), grad[ROT:].astype(BF16)

    dq_ref[:ROT, :], dq_ref[ROT:, :] = unrotated(dqt * (HEAD**-0.5), tq_ref[...])

    @pl.when(i == pl.num_programs(0) - 1)
    def _():
        grad = dk[...].T
        dk_ref[:ROT, :half], dk_ref[ROT:, :half] = unrotated(grad[:, :half], to_ref[...])
        dk_ref[:ROT, half:], dk_ref[ROT:, half:] = unrotated(grad[:, half:], tx_ref[...])
        dv_ref[...] = dv[...].T.astype(BF16)


def attention(h, after, qt, dot, kt, vt, trig_own, trig_other):
    rows, length = qt.shape[1], kt.shape[1]
    lanes = STEP
    tall = trig_own.shape[0]
    q_spec = pl.BlockSpec((HEAD, lanes), lambda i: (h, i))
    k_spec = pl.BlockSpec((HEAD, length), lambda i: (h, 0))
    trig_spec = pl.BlockSpec((tall, rows), lambda i: (0, 0))
    return pl.pallas_call(
        attention_kernel,
        grid=(rows // lanes,),
        in_specs=[pl.BlockSpec(memory_space=pl.ANY), q_spec, q_spec, k_spec, k_spec,
                  pl.BlockSpec((tall, lanes), lambda i: (0, i)), trig_spec, trig_spec],
        out_specs=[pl.BlockSpec((HEAD, lanes), lambda i: (0, i))] * 2
        + [pl.BlockSpec((HEAD, length), lambda i: (0, 0))] * 2,
        out_shape=[low_shape(HEAD, rows)] * 2 + [low_shape(HEAD, length)] * 2,
        scratch_shapes=[
            pltpu.VMEM((length, HEAD), BF16),
            pltpu.VMEM((length, HEAD), BF16),
            pltpu.VMEM((length, 1), F32),
            pltpu.VMEM((length, HEAD), F32),
            pltpu.VMEM((length, HEAD), F32),
            pltpu.VMEM((length, lanes), F32),
            pltpu.VMEM((length, lanes), F32),
        ],
        compiler_params=params(32),
        cost_estimate=cost(40 * rows * length * HEAD, 16 * HEAD * length, rows * length),
    )(after, qt, dot, kt, vt, trig_own, trig_own, trig_other)


def forward_kernel(split, at, n2_ref, g_ref, up_ref, bias_ref, down_ref, s2_ref, b2_ref,
                   ff_ref, a_ref, small_ref, first_ref, second_ref, *scratch):
    i = pl.program_id(0)
    up_part, down_part = scratch if split else (first_ref, second_ref)

    @pl.when(i == 0)
    def _():
        up_part[...] = jnp.zeros_like(up_part)
        down_part[...] = jnp.zeros_like(down_part)
        small_ref[...] = jnp.zeros_like(small_ref)

    n2, g = n2_ref[...], g_ref[...]
    up = mm(n2, up_ref[...]) + row_of(bias_ref)
    cdf = 0.5 + 0.5 * lax.erf(up * (0.5**0.5))
    act = (up * cdf).astype(BF16)
    slope = cdf + up * (jnp.exp(up * up * -0.5) * 0.3989422804014327)
    up_grad = (mm(g, down_ref[...], 1, 1) * slope).astype(BF16)
    ff_ref[...] = mm(act, down_ref[...]).astype(BF16)
    second = mm(up_grad, up_ref[...], 1, 1)
    up_part[...] += mm(n2, up_grad, 0, 0)
    down_part[...] += mm(act, g, 0, 0)
    a_ref[...] = (second * row_of(s2_ref)).astype(BF16)
    small_ref[0:1, :] += jnp.sum(up_grad.astype(F32), axis=0, keepdims=True)
    small_ref[1:2, :] += jnp.sum(g.astype(F32), axis=0, keepdims=True)
    small_ref[2:3, :] += jnp.sum(second * n2.astype(F32), axis=0, keepdims=True)
    small_ref[3:4, :] += jnp.sum(second, axis=0, keepdims=True)

    @pl.when(i == pl.num_programs(0) - 1)
    def _():
        rest = small_ref[2:3, :] - row_of(b2_ref) * small_ref[3:4, :]
        small_ref[2:3, :] = rest / row_of(s2_ref)

    if split:
        half = up_part.shape[0] // 2

        @pl.when(i == pl.num_programs(0) - 1)
        def _():
            for ref, f in ((first_ref, at[3]), (second_ref, 1 - at[3])):
                piece = pl.ds(pl.multiple_of(f * half, 128), half)
                ref[:half, :] = up_part[piece, :].astype(ref.dtype)
                ref[half:, :half] = down_part[:half, piece].astype(ref.dtype)
                ref[half:, half:] = down_part[half:, piece].astype(ref.dtype)


def feed_forward(split, at, n2, g, up, bias, down, scale, offset):
    rows, width = n2.shape
    hidden = up.shape[1]
    row = pl.BlockSpec((STEP, width), lambda i, at: (i, 0))

    def whole(*dims):
        return pl.BlockSpec(dims, lambda i, at: (0,) * len(dims))

    if split:
        assert width == hidden
        parts = [shape(width, hidden), low_shape(width, hidden)]
    else:
        parts = [shape(width, hidden), shape(hidden, width)]
    return pl.pallas_call(
        functools.partial(forward_kernel, split),
        grid_spec=pltpu.PrefetchScalarGridSpec(
            num_scalar_prefetch=1,
            grid=(rows // STEP,),
            in_specs=[row, row, whole(width, hidden), whole(hidden), whole(hidden, width),
                      whole(width), whole(width)],
            out_specs=[row, row, whole(8, width)] + [whole(*p.shape) for p in parts],
            scratch_shapes=[pltpu.VMEM((width, hidden), F32), pltpu.VMEM((hidden, width), F32)]
            if split
            else [],
        ),
        out_shape=[low_shape(rows, width)] * 2 + [shape(8, width)] + parts,
        compiler_params=params(40),
        cost_estimate=cost(12 * rows * width * hidden, 16 * MIB, 2 * rows * hidden),
    )(at, n2, g, up, bias, down, scale, offset)


def emit(keep_ref, send_ref, v):
    i = pl.program_id(0)

    @pl.when(i % 2 == 0)
    def _():
        keep_ref[0] = v.astype(BF16)

    @pl.when(i % 2 == 1)
    def _():
        send_ref[0] = v.astype(BF16)


def branch_kernel(heads, *refs):
    o = refs[:heads]
    g_ref, ff_ref, w_ref, keep_ref, send_ref, out = refs[heads:]
    wide = heads * HEAD

    @pl.when(pl.program_id(0) == 0)
    def _():
        out[...] = jnp.zeros_like(out)

    ot = jnp.concatenate([r[...] for r in o], axis=0)
    emit(keep_ref, send_ref, mm(ot, w_ref[...], 0, 0) + ff_ref[...].astype(F32))
    out[...] += mm(ot, g_ref[...])


def branch(o, g, ff, weights):
    rows, width = g.shape
    heads = len(o)
    wide = heads * HEAD
    row = pl.BlockSpec((STEP, width), lambda i: (i, 0))
    slots = pl.BlockSpec((1, STEP, width), lambda i: (i // 2, 0, 0))
    return pl.pallas_call(
        functools.partial(branch_kernel, heads),
        grid=(rows // STEP,),
        in_specs=[pl.BlockSpec((HEAD, STEP), lambda i: (0, i))] * heads
        + [row, row, pl.BlockSpec((wide, width), lambda i: (3, 0))],
        out_specs=[slots, slots, pl.BlockSpec((wide, width), lambda i: (0, 0))],
        out_shape=[low_shape(2, STEP, width)] * 2 + [shape(wide, width)],
        compiler_params=params(24),
        cost_estimate=cost(4 * rows * width * wide, 8 * MIB),
    )(*o, g, ff, weights)


def back_kernel(own, split, heads, at, *refs):
    count = 3 if own else 2
    grads, refs = refs[: count * heads], refs[count * heads :]
    n1_ref, w_ref, s1_ref, *refs = refs
    if own:
        (half_b, a2_ref, b1_ref, small_ff, small_other, mix_other, out_part,
         keep_ref, send_ref, small, first_ref, *refs) = refs
        *second, mix = refs
    else:
        keep_b, ff_half, keep_ref, send_ref, mix, small = refs
    i = pl.program_id(0)
    wide = heads * HEAD
    tall = mix.shape[0]

    @pl.when(i == 0)
    def _():
        if own:
            mix[:wide, :] = jnp.zeros((wide, mix.shape[1]), F32)
            mix[wide:, :] = mix_other[...]
            small[...] = small_other[...]
        else:
            mix[...] = jnp.zeros_like(mix)
            small[...] = jnp.zeros_like(small)

    grad = jnp.concatenate([r[...] for r in grads], axis=0)
    first = mm(grad, w_ref[3 * wide - tall : 3 * wide, :], 0, 0)
    a = first * row_of(s1_ref)
    emit(keep_ref, send_ref, a + a2_ref[...].astype(F32) if own else a)
    mix[...] += mm(grad, n1_ref[...])
    small[0:1, :] += jnp.sum(first * n1_ref[...].astype(F32), axis=0, keepdims=True)
    small[1:2, :] += jnp.sum(first, axis=0, keepdims=True)
    ones = jnp.ones((8, grad.shape[1]), BF16)
    small[6:7, 3 * wide - tall : 3 * wide] += mm(ones, grad, 1, 1)[0:1]

    if own:
        @pl.when(i == pl.num_programs(0) - 1)
        def _():
            rest = small[0:1, :] - row_of(b1_ref) * small[1:2, :]
            small[0:1, :] = rest / row_of(s1_ref)
            small[2:4, :] = small_ff[2:4, :]
            small[4:6, :] = small_ff[0:2, :]
            if split:
                half = mix.shape[1] // 2
                for ref, f in ((first_ref, at[3]), (second[0], 1 - at[3])):
                    piece = pl.ds(pl.multiple_of(f * half, 128), half)
                    ref[: 3 * wide, :] = mix[:, piece].astype(ref.dtype)
                    ref[3 * wide :, :] = out_part[:, piece].astype(ref.dtype)
            else:
                first_ref[: 3 * wide, :] = mix[...]
                first_ref[3 * wide :, :] = out_part[...]


def back(own, split, at, grads, n1, weights, scale, extra):
    rows, width = n1.shape
    heads = len(grads[0])
    wide = heads * HEAD
    tall = 3 * wide if own else 2 * wide
    offset = 0 if own else rows // STEP
    row = pl.BlockSpec((STEP, width), lambda i, at: (i, 0))
    col = pl.BlockSpec((HEAD, STEP), lambda i, at: (0, i + offset))
    slots = pl.BlockSpec((1, STEP, width), lambda i, at: (i // 2, 0, 0))

    def whole(*dims):
        return pl.BlockSpec(dims, lambda i, at: (0,) * len(dims))

    half = width // 2
    specs = [col] * (len(grads) * heads) + [row, whole(4 * wide, width), whole(width)]
    earlier = pl.BlockSpec(memory_space=pl.ANY)
    if not own:
        specs += [earlier, earlier]
        parts = [shape(tall, width), shape(8, width)]
        scratch = []
    else:
        specs += [earlier, row, whole(width), whole(8, width), whole(8, width), whole(2 * wide, width),
                  whole(wide, width)]
        scratch = [pltpu.VMEM((tall, width), F32)]
        parts = [shape(8, width)]
        if split:
            parts += [shape(4 * wide, half), low_shape(4 * wide, half)]
        else:
            parts += [shape(4 * wide, width)]
    return pl.pallas_call(
        functools.partial(back_kernel, own, split, heads),
        grid_spec=pltpu.PrefetchScalarGridSpec(
            num_scalar_prefetch=1,
            grid=(rows // STEP,),
            in_specs=specs,
            out_specs=[slots, slots] + [whole(*p.shape) for p in parts],
            scratch_shapes=scratch,
        ),
        out_shape=[low_shape(2, STEP, width)] * 2 + parts,
        compiler_params=params(32),
        cost_estimate=cost(4 * rows * width * tall, 10 * MIB),
    )(at, *[v for vs in grads for v in vs], n1, weights, scale, *extra)


def swap(v, axis, size, distance):
    return lax.ppermute(v, axis, [(i, i ^ distance) for i in range(size)])


def by_xor(pieces, index):
    low, high = (index & 1) == 1, (index & 2) == 2
    a, b, c, d = pieces
    a, b, c, d = (jnp.where(low, b, a), jnp.where(low, a, b),
                  jnp.where(low, d, c), jnp.where(low, c, d))
    return (jnp.where(high, c, a), jnp.where(high, d, b),
            jnp.where(high, a, c), jnp.where(high, b, d))


def tie(v, *earlier):
    return lax.optimization_barrier((v, *earlier))[0]


def gather_halves(shard, size, mine, dim, *earlier):
    if size != 2:
        return lax.all_gather(shard, "fsdp", axis=dim, tiled=True)
    other = swap(shard, "fsdp", 2, 1)
    if earlier:
        other = tie(other, *earlier)
    first = mine == 0
    return jnp.concatenate(
        [jnp.where(first, shard, other), jnp.where(first, other, shard)], axis=dim
    )


def scatter_any(part, dim):
    return lax.psum_scatter(
        part.astype(BF16), "fsdp", scatter_dimension=dim, tiled=True
    ).astype(F32)


def halve(v, distance, bit, *earlier):
    rows = v.shape[0] // 2
    keep = lax.dynamic_slice_in_dim(v, bit * rows, rows, 0)
    send = lax.dynamic_slice_in_dim(v, (1 - bit) * rows, rows, 0).astype(BF16)
    return keep + tie(swap(send, "ctx", 4, distance), *earlier).astype(F32)


def quarter_sum(v, c, *earlier):
    rows = v.shape[0] // 4
    mine = 2 * (c % 2) + c // 2

    def part(j):
        return lax.dynamic_slice_in_dim(v, (mine ^ j) * rows, rows, 0)

    total = part(0)
    for distance, j in ((3, 3), (2, 1), (1, 2)):
        sent = swap(part(j).astype(BF16), "ctx", 4, distance)
        total = total + tie(sent, *earlier).astype(F32)
    return total


def pair_up(v, *earlier):
    v = v.astype(BF16)
    return jnp.stack([v, tie(swap(v, "ctx", 4, 2), *earlier)])


def double(pair, c, *earlier):
    others = tie(swap(pair, "ctx", 4, 1), *earlier)
    return by_xor([pair[0], pair[1], others[0], others[1]], 2 * (c % 2) + c // 2)


def sum_over_ctx(v, c):
    return double(pair_up(quarter_sum(v, c)), c)


def butterfly(v, axis_name, size):
    distance = 1
    while distance < size:
        v = v + swap(v, axis_name, size, distance)
        distance *= 2
    return v


def shards(
    sizes,
    inputs,
    positions,
    query_key_value_weight,
    query_key_value_bias,
    attention_output_weight,
    attention_output_bias,
    up_projection_weight,
    up_projection_bias,
    down_projection_weight,
    down_projection_bias,
    first_scale,
    first_shift,
    second_scale,
    second_shift,
    cotangent,
):
    fsdp = sizes["fsdp"]
    split = fsdp == 2
    seq_count, block, width = inputs.shape
    assert seq_count == 2 and sizes["ctx"] == 4 and sizes["tp"] == 4 and block == 2 * STEP
    length = positions.shape[1]
    local = query_key_value_weight.shape[2]
    heads = local // HEAD
    hidden = up_projection_weight.shape[1]
    quarter = block // 4
    f = lax.axis_index("fsdp")
    c = lax.axis_index("ctx")
    t = lax.axis_index("tp")
    s = c // 2
    at = jnp.stack([s, c, t, f]).astype(jnp.int32)

    def my_quarter(v, seq):
        return lax.dynamic_slice(v, (seq, t * quarter, 0), (1, quarter, width))

    x_mine, x_theirs = my_quarter(inputs, s), my_quarter(inputs, 1 - s)
    g_theirs = my_quarter(cotangent, 1 - s)
    far_z = swap(jnp.concatenate([x_theirs, g_theirs], axis=0), "ctx", 4, 2)
    cross = swap(x_theirs, "ctx", 4, 3)
    near = swap(x_mine, "ctx", 4, 1)

    def over_tp(v):
        v_x = swap(v, "tp", 4, 2)
        return v, v_x, swap(jnp.stack([v, v_x]), "tp", 4, 1)

    far = over_tp(far_z)
    others = over_tp(jnp.concatenate([near, cross], axis=0))

    wup = gather_halves(up_projection_weight, fsdp, f, 0)
    wdown = gather_halves(down_projection_weight, fsdp, f, 1)
    mix_shard = query_key_value_weight.transpose(1, 2, 0).reshape(3 * local, -1)
    mix_out_shard = jnp.concatenate([mix_shard, attention_output_weight], axis=0)

    inverse = 10000.0 ** (-2.0 * jnp.arange(HALF, dtype=F32) / ROT)
    places = positions.astype(F32)[:, None, :]
    angles = inverse[None, :, None] * places
    trig = jnp.concatenate(
        [jnp.cos(angles), jnp.sin(angles), jnp.broadcast_to(places, angles.shape)], axis=1
    )

    n1_own, n2, g, trig_own = norms(
        at, True, (inputs, cotangent, *far), trig,
        (first_scale, first_shift, second_scale, second_shift),
    )
    ff, a2, small_ff, ff_first, ff_second = feed_forward(
        split, at, n2, g, wup, up_projection_bias, wdown, second_scale, second_shift
    )
    weights = gather_halves(mix_out_shard, fsdp, f, 1, small_ff)
    n1_other, trig_other = norms(
        at, False, (others[0], others[1], tie(others[2], small_ff)), trig,
        (first_scale, first_shift),
    )
    kt, vt, qt, dot = project(
        n1_own, n1_other, trig_own, trig_other, g, weights, query_key_value_bias
    )
    per_head = []
    after = small_ff
    for h in range(heads):
        if split and h == heads - 1:
            after = ff_first + swap(ff_second, "fsdp", 2, 1).astype(F32)
        per_head.append(attention(h, after, qt, dot, kt, vt, trig_own, trig_other))
    o, dq, dk, dv = zip(*per_head)
    ff_half = halve(after, 1, c % 2) if split else after

    def over_core(keep, send, *earlier):
        v = keep.astype(F32) + tie(swap(send, "tp", 4, 1), *earlier).astype(F32)
        return v.reshape(2, 2, quarter, width)

    def over_x(v, *earlier):
        return v[:, 0] + tie(swap(v[:, 1].astype(BF16), "tp", 4, 2), *earlier).astype(F32)

    keep_b, send_b, out_part = branch(o, g, ff, weights)
    keep_o, send_o, mix_other, small_other = back(
        False, split, at, (dk, dv), n1_other, weights, first_scale, (keep_b, ff_half)
    )
    half_b = over_core(keep_b, send_b)
    keep_w, send_w, small, *late_parts = back(
        True, split, at, (dq, dk, dv), n1_own, weights, first_scale,
        (half_b, a2, first_shift, small_ff, small_other, mix_other, out_part),
    )
    half_o = over_core(keep_o, send_o)
    half_w = over_core(keep_w, send_w)

    def over_ctx(v, distance, *earlier):
        return tie(swap(v.astype(BF16), "ctx", 4, distance), *earlier).astype(F32)

    def gather_tp(ours, *earlier):
        pair = jnp.stack([ours, tie(swap(ours, "tp", 4, 2), *earlier)])
        core = swap(pair, "tp", 4, 1)
        pieces = by_xor((pair[0], core[0], pair[1], core[1]), t)
        pieces = jnp.concatenate(pieces, axis=1)
        return jnp.stack([jnp.where(s == 0, pieces[0], pieces[1]),
                          jnp.where(s == 0, pieces[1], pieces[0])]).astype(F32)

    sums_b = over_x(half_b, half_w)
    branches = jnp.stack([sums_b[0], over_ctx(sums_b[1], 2)]).astype(BF16)
    sums_o = over_x(half_o, half_w)
    sums_w = over_x(half_w)
    sums_w = sums_w + over_ctx(sums_o, 1)
    a = jnp.stack([sums_w[0], over_ctx(sums_w[1], 2, branches)])
    xhat, inv = xhat_of(jnp.concatenate([x_mine, x_theirs], axis=0).astype(F32))
    norm_grad = inv * (
        a
        - jnp.mean(a, axis=-1, keepdims=True)
        - xhat * jnp.mean(a * xhat, axis=-1, keepdims=True)
    )
    norm_grad = norm_grad.astype(BF16)
    block_out = gather_tp(branches, a)
    block_out = (
        inputs.astype(F32) + block_out + (attention_output_bias + down_projection_bias)
    )
    inputs_grad = cotangent.astype(F32) + gather_tp(norm_grad)

    if split:
        q = double(pair_up(halve(ff_half, 2, c // 2), norm_grad), c)
        up_total = jnp.concatenate(q[:2], axis=0).astype(F32)
        down_total = jnp.concatenate(q[2:], axis=0).astype(F32)
        down_total = jnp.concatenate(
            [down_total[:, : width // 2], down_total[:, width // 2 :]], axis=0
        )
        late = late_parts[0] + tie(swap(late_parts[1], "fsdp", 2, 1), sums_o).astype(F32)
        late = double(pair_up(quarter_sum(late, c, a), norm_grad), c)
    else:
        q = sum_over_ctx(scatter_any(ff_first, 0), c)
        up_total = jnp.concatenate(q, axis=0).astype(F32)
        q = sum_over_ctx(scatter_any(ff_second, 1), c)
        down_total = jnp.concatenate(q, axis=0).astype(F32)
        q = sum_over_ctx(scatter_any(late_parts[0], 1), c)
        late = q
    mix_total = jnp.stack(late[:3]).astype(F32).transpose(2, 0, 1)
    out_total = late[3].astype(F32)
    small = butterfly(butterfly(tie(small, norm_grad), "fsdp", fsdp), "ctx", 4)
    norm_small = butterfly(small, "tp", 4)
    bias_total = norm_small[5] * 0.25
    return (
        block_out,
        inputs_grad,
        mix_total,
        small[6, : 3 * local].reshape(3, local),
        out_total,
        bias_total,
        up_total,
        small[4, :hidden],
        down_total,
        bias_total,
        norm_small[0],
        norm_small[1],
        norm_small[2],
        norm_small[3],
    )


def solution(mesh):
    in_specs = (
        P("fsdp", "ctx", None),
        P("fsdp", None),
        P("fsdp", None, "tp"),
        P(None, "tp"),
        P("tp", "fsdp"),
        P(),
        P("fsdp", "tp"),
        P("tp"),
        P("tp", "fsdp"),
        P(),
        P(),
        P(),
        P(),
        P(),
        P("fsdp", "ctx", None),
    )
    out_specs = (
        P("fsdp", "ctx", None),
        P("fsdp", "ctx", None),
        P("fsdp", None, "tp"),
        P(None, "tp"),
        P("tp", "fsdp"),
        P(),
        P("fsdp", "tp"),
        P("tp"),
        P("tp", "fsdp"),
        P(),
        P(),
        P(),
        P(),
        P(),
    )
    body = functools.partial(shards, dict(mesh.shape))
    return jax.shard_map(body, mesh=mesh, in_specs=in_specs, out_specs=out_specs, check_vma=False)
```

```python
import functools

import jax
import jax.numpy as jnp
from jax import lax
from jax.experimental import pallas as pl
from jax.experimental.pallas import tpu as pltpu
from jax.sharding import PartitionSpec as P

HEAD = 64
ROT = 16
HALF = ROT // 2
EPS = 1e-5
NEG = -1e30
STEP = 256
F32 = jnp.float32
BF16 = jnp.bfloat16
MIB = 1024 * 1024


def mm(a, b, ca=1, cb=0):
    return lax.dot_general(a, b, (((ca,), (cb,)), ((), ())), preferred_element_type=F32)


def params(mib):
    return pltpu.CompilerParams(vmem_limit_bytes=mib * MIB)


def cost(flops, moved, exps=0):
    return pl.CostEstimate(flops=int(flops), bytes_accessed=int(moved), transcendentals=int(exps))


def xhat_of(x):
    width = x.shape[-1]
    centred = x - jnp.sum(x, axis=-1, keepdims=True) * (1.0 / width)
    spread = jnp.sum(centred * centred, axis=-1, keepdims=True) * (1.0 / width)
    inv = lax.rsqrt(spread + EPS)
    return centred * inv, inv


def row_of(ref):
    return ref[...].reshape(1, -1)


def shape(*dims):
    return jax.ShapeDtypeStruct(dims, F32)


def low_shape(*dims):
    return jax.ShapeDtypeStruct(dims, BF16)


def norm_own_kernel(at, xa, xb, ga, gb, fz, fx, fc, ta, tb, s1, b1, s2, b2,
                    n1_ref, n2_ref, g_ref, trig_ref, x):
    i = pl.program_id(0)
    q = xa.shape[1]

    @pl.when(i < 2)
    def _():
        x[:q, :] = xa[0]
        x[q:, :] = xb[0]
        g_ref[:q, :] = ga[0]
        g_ref[q:, :] = gb[0]

    @pl.when(i == 2)
    def _():
        x[:q, :] = fz[0]
        x[q:, :] = fx[0]
        g_ref[:q, :] = fz[1]
        g_ref[q:, :] = fx[1]

    @pl.when(i == 3)
    def _():
        x[:q, :] = fc[0, 0]
        x[q:, :] = fc[1, 0]
        g_ref[:q, :] = fc[0, 1]
        g_ref[q:, :] = fc[1, 1]

    trig_ref[:, :q] = ta[0]
    trig_ref[:, q:] = tb[0]
    xhat, _ = xhat_of(x[...].astype(F32))
    n1_ref[...] = (xhat * row_of(s1) + row_of(b1)).astype(BF16)
    n2_ref[...] = (xhat * row_of(s2) + row_of(b2)).astype(BF16)


def norm_other_kernel(at, nz, nx, nc, ta, tb, s1, b1, n1_ref, trig_ref, x):
    i = pl.program_id(0)
    q = nz.shape[1]
    b = i // 2

    @pl.when(i % 2 == 0)
    def _():
        x[:q, :] = nz[b]
        x[q:, :] = nx[b]

    @pl.when(i % 2 == 1)
    def _():
        x[:q, :] = nc[0, b]
        x[q:, :] = nc[1, b]

    trig_ref[:, :q] = ta[0]
    trig_ref[:, q:] = tb[0]
    xhat, _ = xhat_of(x[...].astype(F32))
    n1_ref[...] = (xhat * row_of(s1) + row_of(b1)).astype(BF16)


def norms(at, own, arrays, trig, vectors):
    width = vectors[0].shape[0]
    rows, q = 4 * STEP, STEP // 2
    tall = trig.shape[1]
    first = 0 if own else 1

    def pick(high):
        def place(i, at):
            block = at[1] ^ (first + 2 * (i // 2))
            return (at[0], 0, block * 4 + (at[2] ^ (i % 2 + high)))

        return pl.BlockSpec((1, tall, q), place)

    def piece(high):
        return pl.BlockSpec(
            (1, q, width), lambda i, at: (at[0], at[2] ^ (jnp.minimum(i, 1) + high), 0)
        )

    def whole(v):
        return pl.BlockSpec(v.shape, lambda i, at: (0,) * v.ndim)

    row = pl.BlockSpec((STEP, width), lambda i, at: (i, 0))
    out_trig = pl.BlockSpec((tall, STEP), lambda i, at: (0, i))
    if own:
        x, g, received = arrays[0], arrays[1], arrays[2:]
        specs = [piece(0), piece(2), piece(0), piece(2)]
        operands = [x, x, g, g]
        kernel, count = norm_own_kernel, 3
    else:
        received, specs, operands = arrays, [], []
        kernel, count = norm_other_kernel, 1
    specs += [whole(v) for v in received] + [pick(0), pick(2)] + [whole(v) for v in vectors]
    operands += [*received, trig, trig, *vectors]
    return pl.pallas_call(
        kernel,
        grid_spec=pltpu.PrefetchScalarGridSpec(
            num_scalar_prefetch=1,
            grid=(rows // STEP,),
            in_specs=specs,
            out_specs=[row] * count + [out_trig],
            scratch_shapes=[pltpu.VMEM((STEP, width), BF16)],
        ),
        out_shape=[low_shape(rows, width)] * count + [shape(tall, rows)],
        compiler_params=params(24),
        cost_estimate=cost(0, 6 * rows * width),
    )(at, *operands)


def project_kernel(n1o, n1x, to, tx, g_ref, w_ref, b_ref, k_ref, v_ref, q_ref, do_ref, bias):
    i = pl.program_id(0)
    wide = k_ref.shape[0]

    @pl.when(i == 0)
    def _():
        for j in range(3):
            line = jnp.broadcast_to(b_ref[j : j + 1, :], (8, wide))
            bias[j * wide : (j + 1) * wide, :] = line.T[:, 0:1]

    def rotated(ref, mixed, trig, factor):
        cosine, sine = trig[:HALF], trig[HALF:ROT]
        for h in range(0, wide, HEAD):
            a, b = mixed[h : h + HALF], mixed[h + HALF : h + ROT]
            turned = jnp.concatenate([a * cosine - b * sine, b * cosine + a * sine], axis=0)
            ref[h : h + ROT, :] = turned.astype(BF16) * factor
            ref[h + ROT : h + HEAD, :] = mixed[h + ROT : h + HEAD].astype(BF16) * factor

    def keys_values(mixed, trig):
        rotated(k_ref, mixed[:wide], trig, BF16(1.0))
        v_ref[...] = mixed[wide:].astype(BF16)

    @pl.when(i < 4)
    def _():
        trig = to[...]
        mixed = mm(w_ref[: 3 * wide, :], n1o[...], 1, 1) + bias[...]
        rotated(q_ref, mixed[:wide], trig, BF16(HEAD**-0.5))
        keys_values(mixed[wide:], trig)
        do_ref[...] = mm(w_ref[3 * wide :, :], g_ref[...], 1, 1).astype(BF16)

    @pl.when(i >= 4)
    def _():
        mixed = mm(w_ref[wide : 3 * wide, :], n1x[...], 1, 1) + bias[wide:, :]
        keys_values(mixed, tx[...])


def project(n1_own, n1_other, trig_own, trig_other, g, weights, bias):
    rows, width = n1_own.shape
    wide = bias.shape[1]
    tall = trig_own.shape[0]

    def own(i):
        return jnp.minimum(i, 3)

    def other(i):
        return jnp.maximum(i - 4, 0)

    col = pl.BlockSpec((wide, STEP), lambda i: (0, i))
    own_col = pl.BlockSpec((wide, STEP), lambda i: (0, own(i)))
    return pl.pallas_call(
        project_kernel,
        grid=(8,),
        in_specs=[
            pl.BlockSpec((STEP, width), lambda i: (own(i), 0)),
            pl.BlockSpec((STEP, width), lambda i: (other(i), 0)),
            pl.BlockSpec((tall, STEP), lambda i: (0, own(i))),
            pl.BlockSpec((tall, STEP), lambda i: (0, other(i))),
            pl.BlockSpec((STEP, width), lambda i: (own(i), 0)),
            pl.BlockSpec((4 * wide, width), lambda i: (0, 0)),
            pl.BlockSpec((3, wide), lambda i: (0, 0)),
        ],
        out_specs=[col, col, own_col, own_col],
        out_shape=[low_shape(wide, 2 * rows)] * 2 + [low_shape(wide, rows)] * 2,
        scratch_shapes=[pltpu.VMEM((3 * wide, 1), F32)],
        compiler_params=params(24),
        cost_estimate=cost(12 * rows * width * wide, 12 * rows * width),
    )(n1_own, n1_other, trig_own, trig_other, g, weights, bias)


def attention_kernel(after, q_ref, do_ref, k_ref, v_ref, tq_ref, to_ref, tx_ref,
                     o_ref, dq_ref, dk_ref, dv_ref, kn, vn, kp, dk, dv, es, dps):
    i = pl.program_id(0)
    length = k_ref.shape[1]
    half = length // 2
    chunk = STEP
    steps = length // chunk

    @pl.when(i == 0)
    def _():
        kn[...] = k_ref[...].T
        vn[...] = v_ref[...].T
        kp[:half, :] = to_ref[ROT:, :].T[:, 0:1]
        kp[half:, :] = tx_ref[ROT:, :].T[:, 0:1]
        dk[...] = jnp.zeros_like(dk)
        dv[...] = jnp.zeros_like(dv)

    qt = q_ref[...]
    dot = do_ref[...]
    qn = qt.T
    don = dot.T
    qpos = tq_ref[ROT : ROT + 1, :]
    lanes = qt.shape[1]
    fold = (chunk // 8, 8, lanes)

    top = jnp.full((8, lanes), NEG, F32)
    for j in range(steps):
        here = slice(j * chunk, (j + 1) * chunk)
        s = mm(kn[here, :], qt)
        s = jnp.where(kp[here, :] <= qpos, s, NEG)
        es[here, :] = s
        top = jnp.maximum(top, jnp.max(s.reshape(fold), axis=0))
    top = jnp.max(top, axis=0, keepdims=True)

    total = jnp.zeros((8, lanes), F32)
    inner = jnp.zeros((8, lanes), F32)
    for j in range(steps):
        here = slice(j * chunk, (j + 1) * chunk)
        e = jnp.exp(es[here, :] - top)
        dp = mm(vn[here, :], dot)
        es[here, :] = e
        dps[here, :] = dp
        total = total + jnp.sum(e.reshape(fold), axis=0)
        inner = inner + jnp.sum((e * dp).reshape(fold), axis=0)
    share = 1.0 / jnp.sum(total, axis=0, keepdims=True)
    inner = jnp.sum(inner, axis=0, keepdims=True) * share

    ot = jnp.zeros((HEAD, lanes), F32)
    dqt = jnp.zeros((HEAD, lanes), F32)
    for j in range(steps):
        here = slice(j * chunk, (j + 1) * chunk)
        p = es[here, :] * share
        ds = (p * (dps[here, :] - inner)).astype(BF16)
        p = p.astype(BF16)
        dv[here, :] += mm(p, don)
        dk[here, :] += mm(ds, qn)
        ot = ot + mm(v_ref[:, here], p)
        dqt = dqt + mm(k_ref[:, here], ds)
    o_ref[...] = ot.astype(BF16)

    def unrotated(grad, trig):
        cosine, sine = trig[:HALF], trig[HALF:ROT]
        a, b = grad[:HALF], grad[HALF:ROT]
        turned = jnp.concatenate([a * cosine + b * sine, b * cosine - a * sine], axis=0)
        return turned.astype(BF16), grad[ROT:].astype(BF16)

    dq_ref[:ROT, :], dq_ref[ROT:, :] = unrotated(dqt * (HEAD**-0.5), tq_ref[...])

    @pl.when(i == pl.num_programs(0) - 1)
    def _():
        grad = dk[...].T
        dk_ref[:ROT, :half], dk_ref[ROT:, :half] = unrotated(grad[:, :half], to_ref[...])
        dk_ref[:ROT, half:], dk_ref[ROT:, half:] = unrotated(grad[:, half:], tx_ref[...])
        dv_ref[...] = dv[...].T.astype(BF16)


def attention(h, after, qt, dot, kt, vt, trig_own, trig_other):
    rows, length = qt.shape[1], kt.shape[1]
    lanes = STEP
    tall = trig_own.shape[0]
    q_spec = pl.BlockSpec((HEAD, lanes), lambda i: (h, i))
    k_spec = pl.BlockSpec((HEAD, length), lambda i: (h, 0))
    trig_spec = pl.BlockSpec((tall, rows), lambda i: (0, 0))
    return pl.pallas_call(
        attention_kernel,
        grid=(rows // lanes,),
        in_specs=[pl.BlockSpec(memory_space=pl.ANY), q_spec, q_spec, k_spec, k_spec,
                  pl.BlockSpec((tall, lanes), lambda i: (0, i)), trig_spec, trig_spec],
        out_specs=[pl.BlockSpec((HEAD, lanes), lambda i: (0, i))] * 2
        + [pl.BlockSpec((HEAD, length), lambda i: (0, 0))] * 2,
        out_shape=[low_shape(HEAD, rows)] * 2 + [low_shape(HEAD, length)] * 2,
        scratch_shapes=[
            pltpu.VMEM((length, HEAD), BF16),
            pltpu.VMEM((length, HEAD), BF16),
            pltpu.VMEM((length, 1), F32),
            pltpu.VMEM((length, HEAD), F32),
            pltpu.VMEM((length, HEAD), F32),
            pltpu.VMEM((length, lanes), F32),
            pltpu.VMEM((length, lanes), F32),
        ],
        compiler_params=params(32),
        cost_estimate=cost(40 * rows * length * HEAD, 16 * HEAD * length, rows * length),
    )(after, qt, dot, kt, vt, trig_own, trig_own, trig_other)


def forward_kernel(split, at, n2_ref, g_ref, up_ref, bias_ref, down_ref, s2_ref, b2_ref,
                   ff_ref, a_ref, small_ref, first_ref, second_ref, *scratch):
    i = pl.program_id(0)
    up_part, down_part = scratch if split else (first_ref, second_ref)

    @pl.when(i == 0)
    def _():
        up_part[...] = jnp.zeros_like(up_part)
        down_part[...] = jnp.zeros_like(down_part)
        small_ref[...] = jnp.zeros_like(small_ref)

    n2, g = n2_ref[...], g_ref[...]
    up = mm(n2, up_ref[...]) + row_of(bias_ref)
    cdf = 0.5 + 0.5 * lax.erf(up * (0.5**0.5))
    act = (up * cdf).astype(BF16)
    slope = cdf + up * (jnp.exp(up * up * -0.5) * 0.3989422804014327)
    up_grad = (mm(g, down_ref[...], 1, 1) * slope).astype(BF16)
    ff_ref[...] = mm(act, down_ref[...]).astype(BF16)
    second = mm(up_grad, up_ref[...], 1, 1)
    up_part[...] += mm(n2, up_grad, 0, 0)
    down_part[...] += mm(act, g, 0, 0)
    a_ref[...] = (second * row_of(s2_ref)).astype(BF16)
    small_ref[0:1, :] += jnp.sum(up_grad.astype(F32), axis=0, keepdims=True)
    small_ref[1:2, :] += jnp.sum(g.astype(F32), axis=0, keepdims=True)
    small_ref[2:3, :] += jnp.sum(second * n2.astype(F32), axis=0, keepdims=True)
    small_ref[3:4, :] += jnp.sum(second, axis=0, keepdims=True)

    @pl.when(i == pl.num_programs(0) - 1)
    def _():
        rest = small_ref[2:3, :] - row_of(b2_ref) * small_ref[3:4, :]
        small_ref[2:3, :] = rest / row_of(s2_ref)

    if split:
        half = up_part.shape[0] // 2

        @pl.when(i == pl.num_programs(0) - 1)
        def _():
            for ref, f in ((first_ref, at[3]), (second_ref, 1 - at[3])):
                piece = pl.ds(pl.multiple_of(f * half, 128), half)
                ref[:half, :] = up_part[piece, :].astype(ref.dtype)
                ref[half:, :half] = down_part[:half, piece].astype(ref.dtype)
                ref[half:, half:] = down_part[half:, piece].astype(ref.dtype)


def feed_forward(split, at, n2, g, up, bias, down, scale, offset):
    rows, width = n2.shape
    hidden = up.shape[1]
    row = pl.BlockSpec((STEP, width), lambda i, at: (i, 0))

    def whole(*dims):
        return pl.BlockSpec(dims, lambda i, at: (0,) * len(dims))

    if split:
        assert width == hidden
        parts = [shape(width, hidden), low_shape(width, hidden)]
    else:
        parts = [shape(width, hidden), shape(hidden, width)]
    return pl.pallas_call(
        functools.partial(forward_kernel, split),
        grid_spec=pltpu.PrefetchScalarGridSpec(
            num_scalar_prefetch=1,
            grid=(rows // STEP,),
            in_specs=[row, row, whole(width, hidden), whole(hidden), whole(hidden, width),
                      whole(width), whole(width)],
            out_specs=[row, row, whole(8, width)] + [whole(*p.shape) for p in parts],
            scratch_shapes=[pltpu.VMEM((width, hidden), F32), pltpu.VMEM((hidden, width), F32)]
            if split
            else [],
        ),
        out_shape=[low_shape(rows, width)] * 2 + [shape(8, width)] + parts,
        compiler_params=params(40),
        cost_estimate=cost(12 * rows * width * hidden, 16 * MIB, 2 * rows * hidden),
    )(at, n2, g, up, bias, down, scale, offset)


def emit(keep_ref, send_ref, v):
    i = pl.program_id(0)

    @pl.when(i % 2 == 0)
    def _():
        keep_ref[0] = v.astype(BF16)

    @pl.when(i % 2 == 1)
    def _():
        send_ref[0] = v.astype(BF16)


def branch_kernel(heads, *refs):
    o = refs[:heads]
    g_ref, ff_ref, w_ref, keep_ref, send_ref, out = refs[heads:]
    wide = heads * HEAD

    @pl.when(pl.program_id(0) == 0)
    def _():
        out[...] = jnp.zeros_like(out)

    ot = jnp.concatenate([r[...] for r in o], axis=0)
    emit(keep_ref, send_ref, mm(ot, w_ref[...], 0, 0) + ff_ref[...].astype(F32))
    out[...] += mm(ot, g_ref[...])


def branch(o, g, ff, weights):
    rows, width = g.shape
    heads = len(o)
    wide = heads * HEAD
    row = pl.BlockSpec((STEP, width), lambda i: (i, 0))
    slots = pl.BlockSpec((1, STEP, width), lambda i: (i // 2, 0, 0))
    return pl.pallas_call(
        functools.partial(branch_kernel, heads),
        grid=(rows // STEP,),
        in_specs=[pl.BlockSpec((HEAD, STEP), lambda i: (0, i))] * heads
        + [row, row, pl.BlockSpec((wide, width), lambda i: (3, 0))],
        out_specs=[slots, slots, pl.BlockSpec((wide, width), lambda i: (0, 0))],
        out_shape=[low_shape(2, STEP, width)] * 2 + [shape(wide, width)],
        compiler_params=params(24),
        cost_estimate=cost(4 * rows * width * wide, 8 * MIB),
    )(*o, g, ff, weights)


def back_kernel(own, split, heads, at, *refs):
    count = 3 if own else 2
    grads, refs = refs[: count * heads], refs[count * heads :]
    n1_ref, w_ref, s1_ref, *refs = refs
    if own:
        (half_b, a2_ref, b1_ref, small_ff, small_other, mix_other, out_part,
         keep_ref, send_ref, first_ref, second_ref, mix, small) = refs
    else:
        keep_b, ff_half, keep_ref, send_ref, mix, small = refs
    i = pl.program_id(0)
    wide = heads * HEAD
    tall = mix.shape[0]

    @pl.when(i == 0)
    def _():
        if own:
            mix[:wide, :] = jnp.zeros((wide, mix.shape[1]), F32)
            mix[wide:, :] = mix_other[...]
            small[...] = small_other[...]
        else:
            mix[...] = jnp.zeros_like(mix)
            small[...] = jnp.zeros_like(small)

    grad = jnp.concatenate([r[...] for r in grads], axis=0)
    first = mm(grad, w_ref[3 * wide - tall : 3 * wide, :], 0, 0)
    a = first * row_of(s1_ref)
    emit(keep_ref, send_ref, a + a2_ref[...].astype(F32) if own else a)
    mix[...] += mm(grad, n1_ref[...])
    small[0:1, :] += jnp.sum(first * n1_ref[...].astype(F32), axis=0, keepdims=True)
    small[1:2, :] += jnp.sum(first, axis=0, keepdims=True)
    ones = jnp.ones((8, grad.shape[1]), BF16)
    small[6:7, 3 * wide - tall : 3 * wide] += mm(ones, grad, 1, 1)[0:1]

    if own:
        @pl.when(i == pl.num_programs(0) - 1)
        def _():
            rest = small[0:1, :] - row_of(b1_ref) * small[1:2, :]
            small[0:1, :] = rest / row_of(s1_ref)
            small[2:4, :] = small_ff[2:4, :]
            small[4:6, :] = small_ff[0:2, :]
            if split:
                half = mix.shape[1] // 2
                vectors = small[...].astype(BF16)
                for ref, f in ((first_ref, at[3]), (second_ref, 1 - at[3])):
                    piece = pl.ds(pl.multiple_of(f * half, 128), half)
                    ref[: 3 * wide, :] = mix[:, piece].astype(ref.dtype)
                    ref[3 * wide : 4 * wide, :] = out_part[:, piece].astype(ref.dtype)
                    both = jnp.concatenate([vectors[:, :half], vectors[:, half:]], axis=0)
                    ref[4 * wide : 4 * wide + 16, :] = both.astype(ref.dtype)
                    ref[4 * wide + 16 :, :] = jnp.zeros((48, half), ref.dtype)
            else:
                first_ref[: 3 * wide, :] = mix[...]
                first_ref[3 * wide :, :] = out_part[...]
                second_ref[...] = small[...]


def back(own, split, at, grads, n1, weights, scale, extra):
    rows, width = n1.shape
    heads = len(grads[0])
    wide = heads * HEAD
    tall = 3 * wide if own else 2 * wide
    offset = 0 if own else rows // STEP
    row = pl.BlockSpec((STEP, width), lambda i, at: (i, 0))
    col = pl.BlockSpec((HEAD, STEP), lambda i, at: (0, i + offset))
    slots = pl.BlockSpec((1, STEP, width), lambda i, at: (i // 2, 0, 0))

    def whole(*dims):
        return pl.BlockSpec(dims, lambda i, at: (0,) * len(dims))

    half = width // 2
    specs = [col] * (len(grads) * heads) + [row, whole(4 * wide, width), whole(width)]
    earlier = pl.BlockSpec(memory_space=pl.ANY)
    if not own:
        specs += [earlier, earlier]
        parts = [shape(tall, width), shape(8, width)]
        scratch = []
    else:
        specs += [earlier, row, whole(width), whole(8, width), whole(8, width), whole(2 * wide, width),
                  whole(wide, width)]
        scratch = [pltpu.VMEM((tall, width), F32), pltpu.VMEM((8, width), F32)]
        if split:
            parts = [shape(4 * wide + 64, half), low_shape(4 * wide + 64, half)]
        else:
            parts = [shape(4 * wide, width), shape(8, width)]
    return pl.pallas_call(
        functools.partial(back_kernel, own, split, heads),
        grid_spec=pltpu.PrefetchScalarGridSpec(
            num_scalar_prefetch=1,
            grid=(rows // STEP,),
            in_specs=specs,
            out_specs=[slots, slots] + [whole(*p.shape) for p in parts],
            scratch_shapes=scratch,
        ),
        out_shape=[low_shape(2, STEP, width)] * 2 + parts,
        compiler_params=params(32),
        cost_estimate=cost(4 * rows * width * tall, 10 * MIB),
    )(at, *[v for vs in grads for v in vs], n1, weights, scale, *extra)


def swap(v, axis, size, distance):
    return lax.ppermute(v, axis, [(i, i ^ distance) for i in range(size)])


def by_xor(pieces, index):
    low, high = (index & 1) == 1, (index & 2) == 2
    a, b, c, d = pieces
    a, b, c, d = (jnp.where(low, b, a), jnp.where(low, a, b),
                  jnp.where(low, d, c), jnp.where(low, c, d))
    return (jnp.where(high, c, a), jnp.where(high, d, b),
            jnp.where(high, a, c), jnp.where(high, b, d))


def tie(v, *earlier):
    return lax.optimization_barrier((v, *earlier))[0]


def gather_halves(shard, size, mine, dim, *earlier):
    if size != 2:
        return lax.all_gather(shard, "fsdp", axis=dim, tiled=True)
    other = swap(shard, "fsdp", 2, 1)
    if earlier:
        other = tie(other, *earlier)
    first = mine == 0
    return jnp.concatenate(
        [jnp.where(first, shard, other), jnp.where(first, other, shard)], axis=dim
    )


def scatter_any(part, dim):
    return lax.psum_scatter(
        part.astype(BF16), "fsdp", scatter_dimension=dim, tiled=True
    ).astype(F32)


def halve(v, distance, bit, *earlier):
    rows = v.shape[0] // 2
    keep = lax.dynamic_slice_in_dim(v, bit * rows, rows, 0)
    send = lax.dynamic_slice_in_dim(v, (1 - bit) * rows, rows, 0).astype(BF16)
    return keep + tie(swap(send, "ctx", 4, distance), *earlier).astype(F32)


def quarter_sum(v, c, *earlier):
    rows = v.shape[0] // 4
    mine = 2 * (c % 2) + c // 2

    def part(j):
        return lax.dynamic_slice_in_dim(v, (mine ^ j) * rows, rows, 0)

    total = part(0)
    for distance, j in ((3, 3), (2, 1), (1, 2)):
        sent = swap(part(j).astype(BF16), "ctx", 4, distance)
        total = total + tie(sent, *earlier).astype(F32)
    return total


def pair_up(v, *earlier):
    v = v.astype(BF16)
    return jnp.stack([v, tie(swap(v, "ctx", 4, 2), *earlier)])


def double(pair, c, *earlier):
    others = tie(swap(pair, "ctx", 4, 1), *earlier)
    return by_xor([pair[0], pair[1], others[0], others[1]], 2 * (c % 2) + c // 2)


def sum_over_ctx(v, c):
    return double(pair_up(quarter_sum(v, c)), c)


def butterfly(v, axis_name, size):
    distance = 1
    while distance < size:
        v = v + swap(v, axis_name, size, distance)
        distance *= 2
    return v


def shards(
    sizes,
    inputs,
    positions,
    query_key_value_weight,
    query_key_value_bias,
    attention_output_weight,
    attention_output_bias,
    up_projection_weight,
    up_projection_bias,
    down_projection_weight,
    down_projection_bias,
    first_scale,
    first_shift,
    second_scale,
    second_shift,
    cotangent,
):
    fsdp = sizes["fsdp"]
    split = fsdp == 2
    seq_count, block, width = inputs.shape
    assert seq_count == 2 and sizes["ctx"] == 4 and sizes["tp"] == 4 and block == 2 * STEP
    length = positions.shape[1]
    local = query_key_value_weight.shape[2]
    heads = local // HEAD
    hidden = up_projection_weight.shape[1]
    quarter = block // 4
    f = lax.axis_index("fsdp")
    c = lax.axis_index("ctx")
    t = lax.axis_index("tp")
    s = c // 2
    at = jnp.stack([s, c, t, f]).astype(jnp.int32)

    def my_quarter(v, seq):
        return lax.dynamic_slice(v, (seq, t * quarter, 0), (1, quarter, width))

    x_mine, x_theirs = my_quarter(inputs, s), my_quarter(inputs, 1 - s)
    g_theirs = my_quarter(cotangent, 1 - s)
    far_z = swap(jnp.concatenate([x_theirs, g_theirs], axis=0), "ctx", 4, 2)
    cross = swap(x_theirs, "ctx", 4, 3)
    near = swap(x_mine, "ctx", 4, 1)

    def over_tp(v):
        v_x = swap(v, "tp", 4, 2)
        return v, v_x, swap(jnp.stack([v, v_x]), "tp", 4, 1)

    far = over_tp(far_z)
    others = over_tp(jnp.concatenate([near, cross], axis=0))

    wup = gather_halves(up_projection_weight, fsdp, f, 0)
    wdown = gather_halves(down_projection_weight, fsdp, f, 1)
    mix_shard = query_key_value_weight.transpose(1, 2, 0).reshape(3 * local, -1)
    mix_out_shard = jnp.concatenate([mix_shard, attention_output_weight], axis=0)

    inverse = 10000.0 ** (-2.0 * jnp.arange(HALF, dtype=F32) / ROT)
    places = positions.astype(F32)[:, None, :]
    angles = inverse[None, :, None] * places
    trig = jnp.concatenate(
        [jnp.cos(angles), jnp.sin(angles), jnp.broadcast_to(places, angles.shape)], axis=1
    )

    n1_own, n2, g, trig_own = norms(
        at, True, (inputs, cotangent, *far), trig,
        (first_scale, first_shift, second_scale, second_shift),
    )
    ff, a2, small_ff, ff_first, ff_second = feed_forward(
        split, at, n2, g, wup, up_projection_bias, wdown, second_scale, second_shift
    )
    weights = gather_halves(mix_out_shard, fsdp, f, 1, small_ff)
    n1_other, trig_other = norms(
        at, False, (others[0], others[1], tie(others[2], small_ff)), trig,
        (first_scale, first_shift),
    )
    kt, vt, qt, dot = project(
        n1_own, n1_other, trig_own, trig_other, g, weights, query_key_value_bias
    )
    per_head = []
    after = small_ff
    for h in range(heads):
        if split and h == heads - 1:
            after = ff_first + swap(ff_second, "fsdp", 2, 1).astype(F32)
        per_head.append(attention(h, after, qt, dot, kt, vt, trig_own, trig_other))
    o, dq, dk, dv = zip(*per_head)
    ff_half = halve(after, 1, c % 2) if split else after

    def over_core(keep, send, *earlier):
        v = keep.astype(F32) + tie(swap(send, "tp", 4, 1), *earlier).astype(F32)
        return v.reshape(2, 2, quarter, width)

    def over_x(v, *earlier):
        return v[:, 0] + tie(swap(v[:, 1].astype(BF16), "tp", 4, 2), *earlier).astype(F32)

    keep_b, send_b, out_part = branch(o, g, ff, weights)
    keep_o, send_o, mix_other, small_other = back(
        False, split, at, (dk, dv), n1_other, weights, first_scale, (keep_b, ff_half)
    )
    half_b = over_core(keep_b, send_b)
    keep_w, send_w, late_first, late_second = back(
        True, split, at, (dq, dk, dv), n1_own, weights, first_scale,
        (half_b, a2, first_shift, small_ff, small_other, mix_other, out_part),
    )
    half_o = over_core(keep_o, send_o)
    half_w = over_core(keep_w, send_w)

    def over_ctx(v, distance, *earlier):
        return tie(swap(v.astype(BF16), "ctx", 4, distance), *earlier).astype(F32)

    def gather_tp(ours, *earlier):
        pair = jnp.stack([ours, tie(swap(ours, "tp", 4, 2), *earlier)])
        core = swap(pair, "tp", 4, 1)
        pieces = by_xor((pair[0], core[0], pair[1], core[1]), t)
        pieces = jnp.concatenate(pieces, axis=1)
        return jnp.stack([jnp.where(s == 0, pieces[0], pieces[1]),
                          jnp.where(s == 0, pieces[1], pieces[0])]).astype(F32)

    sums_b = over_x(half_b, half_w)
    branches = jnp.stack([sums_b[0], over_ctx(sums_b[1], 2)]).astype(BF16)
    sums_o = over_x(half_o, half_w)
    sums_w = over_x(half_w)
    sums_w = sums_w + over_ctx(sums_o, 1)
    a = jnp.stack([sums_w[0], over_ctx(sums_w[1], 2, branches)])
    xhat, inv = xhat_of(jnp.concatenate([x_mine, x_theirs], axis=0).astype(F32))
    norm_grad = inv * (
        a
        - jnp.mean(a, axis=-1, keepdims=True)
        - xhat * jnp.mean(a * xhat, axis=-1, keepdims=True)
    )
    norm_grad = norm_grad.astype(BF16)
    block_out = gather_tp(branches, a)
    block_out = (
        inputs.astype(F32) + block_out + (attention_output_bias + down_projection_bias)
    )
    inputs_grad = cotangent.astype(F32) + gather_tp(norm_grad)

    if split:
        q = double(pair_up(halve(ff_half, 2, c // 2), sums_o), c, norm_grad)
        up_total = jnp.concatenate(q[:2], axis=0).astype(F32)
        down_total = jnp.concatenate(q[2:], axis=0).astype(F32)
        down_total = jnp.concatenate(
            [down_total[:, : width // 2], down_total[:, width // 2 :]], axis=0
        )
        late = late_first + tie(swap(late_second, "fsdp", 2, 1), sums_w).astype(F32)
        late = double(pair_up(quarter_sum(late, c, a), norm_grad), c)
        late = jnp.concatenate(late, axis=0).astype(F32)
        small = jnp.concatenate([late[4 * local : 4 * local + 8], late[4 * local + 8 :][:8]], axis=1)
    else:
        q = sum_over_ctx(scatter_any(ff_first, 0), c)
        up_total = jnp.concatenate(q, axis=0).astype(F32)
        q = sum_over_ctx(scatter_any(ff_second, 1), c)
        down_total = jnp.concatenate(q, axis=0).astype(F32)
        q = sum_over_ctx(scatter_any(late_first, 1), c)
        late = jnp.concatenate(q, axis=0).astype(F32)
        small = butterfly(butterfly(late_second, "fsdp", fsdp), "ctx", 4)
    mix_total = late[: 3 * local].reshape(3, local, -1).transpose(2, 0, 1)
    out_total = late[3 * local : 4 * local]
    norm_small = butterfly(small, "tp", 4)
    bias_total = norm_small[5] * 0.25
    return (
        block_out,
        inputs_grad,
        mix_total,
        small[6, : 3 * local].reshape(3, local),
        out_total,
        bias_total,
        up_total,
        small[4, :hidden],
        down_total,
        bias_total,
        norm_small[0],
        norm_small[1],
        norm_small[2],
        norm_small[3],
    )


def solution(mesh):
    in_specs = (
        P("fsdp", "ctx", None),
        P("fsdp", None),
        P("fsdp", None, "tp"),
        P(None, "tp"),
        P("tp", "fsdp"),
        P(),
        P("fsdp", "tp"),
        P("tp"),
        P("tp", "fsdp"),
        P(),
        P(),
        P(),
        P(),
        P(),
        P("fsdp", "ctx", None),
    )
    out_specs = (
        P("fsdp", "ctx", None),
        P("fsdp", "ctx", None),
        P("fsdp", None, "tp"),
        P(None, "tp"),
        P("tp", "fsdp"),
        P(),
        P("fsdp", "tp"),
        P("tp"),
        P("tp", "fsdp"),
        P(),
        P(),
        P(),
        P(),
        P(),
    )
    body = functools.partial(shards, dict(mesh.shape))
    return jax.shard_map(body, mesh=mesh, in_specs=in_specs, out_specs=out_specs, check_vma=False)
```

```python
import functools

import jax
import jax.numpy as jnp
from jax import lax
from jax.experimental import pallas as pl
from jax.experimental.pallas import tpu as pltpu
from jax.sharding import PartitionSpec as P

HEAD = 64
ROT = 16
HALF = ROT // 2
EPS = 1e-5
NEG = -1e30
STEP = 256
F32 = jnp.float32
BF16 = jnp.bfloat16
MIB = 1024 * 1024


def mm(a, b, ca=1, cb=0):
    return lax.dot_general(a, b, (((ca,), (cb,)), ((), ())), preferred_element_type=F32)


def params(mib):
    return pltpu.CompilerParams(vmem_limit_bytes=mib * MIB)


def cost(flops, moved, exps=0):
    return pl.CostEstimate(flops=int(flops), bytes_accessed=int(moved), transcendentals=int(exps))


def xhat_of(x):
    width = x.shape[-1]
    centred = x - jnp.sum(x, axis=-1, keepdims=True) * (1.0 / width)
    spread = jnp.sum(centred * centred, axis=-1, keepdims=True) * (1.0 / width)
    inv = lax.rsqrt(spread + EPS)
    return centred * inv, inv


def row_of(ref):
    return ref[...].reshape(1, -1)


def shape(*dims):
    return jax.ShapeDtypeStruct(dims, F32)


def low_shape(*dims):
    return jax.ShapeDtypeStruct(dims, BF16)


def norm_own_kernel(at, xa, xb, ga, gb, fz, fx, fc, ta, tb, s1, b1, s2, b2,
                    n1_ref, n2_ref, g_ref, trig_ref, x):
    i = pl.program_id(0)
    q = xa.shape[1]

    @pl.when(i < 2)
    def _():
        x[:q, :] = xa[0]
        x[q:, :] = xb[0]
        g_ref[:q, :] = ga[0]
        g_ref[q:, :] = gb[0]

    @pl.when(i == 2)
    def _():
        x[:q, :] = fz[0]
        x[q:, :] = fx[0]
        g_ref[:q, :] = fz[1]
        g_ref[q:, :] = fx[1]

    @pl.when(i == 3)
    def _():
        x[:q, :] = fc[0, 0]
        x[q:, :] = fc[1, 0]
        g_ref[:q, :] = fc[0, 1]
        g_ref[q:, :] = fc[1, 1]

    trig_ref[:, :q] = ta[0]
    trig_ref[:, q:] = tb[0]
    xhat, _ = xhat_of(x[...].astype(F32))
    n1_ref[...] = (xhat * row_of(s1) + row_of(b1)).astype(BF16)
    n2_ref[...] = (xhat * row_of(s2) + row_of(b2)).astype(BF16)


def norm_other_kernel(at, nz, nx, nc, ta, tb, s1, b1, n1_ref, trig_ref, x):
    i = pl.program_id(0)
    q = nz.shape[1]
    b = i // 2

    @pl.when(i % 2 == 0)
    def _():
        x[:q, :] = nz[b]
        x[q:, :] = nx[b]

    @pl.when(i % 2 == 1)
    def _():
        x[:q, :] = nc[0, b]
        x[q:, :] = nc[1, b]

    trig_ref[:, :q] = ta[0]
    trig_ref[:, q:] = tb[0]
    xhat, _ = xhat_of(x[...].astype(F32))
    n1_ref[...] = (xhat * row_of(s1) + row_of(b1)).astype(BF16)


def norms(at, own, arrays, trig, vectors):
    width = vectors[0].shape[0]
    rows, q = 4 * STEP, STEP // 2
    tall = trig.shape[1]
    first = 0 if own else 1

    def pick(high):
        def place(i, at):
            block = at[1] ^ (first + 2 * (i // 2))
            return (at[0], 0, block * 4 + (at[2] ^ (i % 2 + high)))

        return pl.BlockSpec((1, tall, q), place)

    def piece(high):
        return pl.BlockSpec(
            (1, q, width), lambda i, at: (at[0], at[2] ^ (jnp.minimum(i, 1) + high), 0)
        )

    def whole(v):
        return pl.BlockSpec(v.shape, lambda i, at: (0,) * v.ndim)

    row = pl.BlockSpec((STEP, width), lambda i, at: (i, 0))
    out_trig = pl.BlockSpec((tall, STEP), lambda i, at: (0, i))
    if own:
        x, g, received = arrays[0], arrays[1], arrays[2:]
        specs = [piece(0), piece(2), piece(0), piece(2)]
        operands = [x, x, g, g]
        kernel, count = norm_own_kernel, 3
    else:
        received, specs, operands = arrays, [], []
        kernel, count = norm_other_kernel, 1
    specs += [whole(v) for v in received] + [pick(0), pick(2)] + [whole(v) for v in vectors]
    operands += [*received, trig, trig, *vectors]
    return pl.pallas_call(
        kernel,
        grid_spec=pltpu.PrefetchScalarGridSpec(
            num_scalar_prefetch=1,
            grid=(rows // STEP,),
            in_specs=specs,
            out_specs=[row] * count + [out_trig],
            scratch_shapes=[pltpu.VMEM((STEP, width), BF16)],
        ),
        out_shape=[low_shape(rows, width)] * count + [shape(tall, rows)],
        compiler_params=params(24),
        cost_estimate=cost(0, 6 * rows * width),
    )(at, *operands)


def project_kernel(n1o, n1x, to, tx, g_ref, w_ref, b_ref, k_ref, v_ref, q_ref, do_ref, bias):
    i = pl.program_id(0)
    wide = k_ref.shape[0]

    @pl.when(i == 0)
    def _():
        for j in range(3):
            line = jnp.broadcast_to(b_ref[j : j + 1, :], (8, wide))
            bias[j * wide : (j + 1) * wide, :] = line.T[:, 0:1]

    def rotated(ref, mixed, trig, factor):
        cosine, sine = trig[:HALF], trig[HALF:ROT]
        for h in range(0, wide, HEAD):
            a, b = mixed[h : h + HALF], mixed[h + HALF : h + ROT]
            turned = jnp.concatenate([a * cosine - b * sine, b * cosine + a * sine], axis=0)
            ref[h : h + ROT, :] = turned.astype(BF16) * factor
            ref[h + ROT : h + HEAD, :] = mixed[h + ROT : h + HEAD].astype(BF16) * factor

    def keys_values(mixed, trig):
        rotated(k_ref, mixed[:wide], trig, BF16(1.0))
        v_ref[...] = mixed[wide:].astype(BF16)

    @pl.when(i < 4)
    def _():
        trig = to[...]
        mixed = mm(w_ref[: 3 * wide, :], n1o[...], 1, 1) + bias[...]
        rotated(q_ref, mixed[:wide], trig, BF16(HEAD**-0.5))
        keys_values(mixed[wide:], trig)
        do_ref[...] = mm(w_ref[3 * wide :, :], g_ref[...], 1, 1).astype(BF16)

    @pl.when(i >= 4)
    def _():
        mixed = mm(w_ref[wide : 3 * wide, :], n1x[...], 1, 1) + bias[wide:, :]
        keys_values(mixed, tx[...])


def project(n1_own, n1_other, trig_own, trig_other, g, weights, bias):
    rows, width = n1_own.shape
    wide = bias.shape[1]
    tall = trig_own.shape[0]

    def own(i):
        return jnp.minimum(i, 3)

    def other(i):
        return jnp.maximum(i - 4, 0)

    col = pl.BlockSpec((wide, STEP), lambda i: (0, i))
    own_col = pl.BlockSpec((wide, STEP), lambda i: (0, own(i)))
    return pl.pallas_call(
        project_kernel,
        grid=(8,),
        in_specs=[
            pl.BlockSpec((STEP, width), lambda i: (own(i), 0)),
            pl.BlockSpec((STEP, width), lambda i: (other(i), 0)),
            pl.BlockSpec((tall, STEP), lambda i: (0, own(i))),
            pl.BlockSpec((tall, STEP), lambda i: (0, other(i))),
            pl.BlockSpec((STEP, width), lambda i: (own(i), 0)),
            pl.BlockSpec((4 * wide, width), lambda i: (0, 0)),
            pl.BlockSpec((3, wide), lambda i: (0, 0)),
        ],
        out_specs=[col, col, own_col, own_col],
        out_shape=[low_shape(wide, 2 * rows)] * 2 + [low_shape(wide, rows)] * 2,
        scratch_shapes=[pltpu.VMEM((3 * wide, 1), F32)],
        compiler_params=params(24),
        cost_estimate=cost(12 * rows * width * wide, 12 * rows * width),
    )(n1_own, n1_other, trig_own, trig_other, g, weights, bias)


def attention_kernel(after, q_ref, do_ref, k_ref, v_ref, tq_ref, to_ref, tx_ref,
                     o_ref, dq_ref, dk_ref, dv_ref, kn, vn, kp, dk, dv, es, dps):
    i = pl.program_id(0)
    length = k_ref.shape[1]
    half = length // 2
    chunk = STEP
    steps = length // chunk

    @pl.when(i == 0)
    def _():
        kn[...] = k_ref[...].T
        vn[...] = v_ref[...].T
        kp[:half, :] = to_ref[ROT:, :].T[:, 0:1]
        kp[half:, :] = tx_ref[ROT:, :].T[:, 0:1]
        dk[...] = jnp.zeros_like(dk)
        dv[...] = jnp.zeros_like(dv)

    qt = q_ref[...]
    dot = do_ref[...]
    qn = qt.T
    don = dot.T
    qpos = tq_ref[ROT : ROT + 1, :]
    lanes = qt.shape[1]
    fold = (chunk // 8, 8, lanes)

    top = jnp.full((8, lanes), NEG, F32)
    for j in range(steps):
        here = slice(j * chunk, (j + 1) * chunk)
        s = mm(kn[here, :], qt)
        s = jnp.where(kp[here, :] <= qpos, s, NEG)
        es[here, :] = s
        top = jnp.maximum(top, jnp.max(s.reshape(fold), axis=0))
    top = jnp.max(top, axis=0, keepdims=True)

    total = jnp.zeros((8, lanes), F32)
    inner = jnp.zeros((8, lanes), F32)
    for j in range(steps):
        here = slice(j * chunk, (j + 1) * chunk)
        e = jnp.exp(es[here, :] - top)
        dp = mm(vn[here, :], dot)
        es[here, :] = e
        dps[here, :] = dp
        total = total + jnp.sum(e.reshape(fold), axis=0)
        inner = inner + jnp.sum((e * dp).reshape(fold), axis=0)
    share = 1.0 / jnp.sum(total, axis=0, keepdims=True)
    inner = jnp.sum(inner, axis=0, keepdims=True) * share

    ot = jnp.zeros((HEAD, lanes), F32)
    dqt = jnp.zeros((HEAD, lanes), F32)
    for j in range(steps):
        here = slice(j * chunk, (j + 1) * chunk)
        p = es[here, :] * share
        ds = (p * (dps[here, :] - inner)).astype(BF16)
        p = p.astype(BF16)
        dv[here, :] += mm(p, don)
        dk[here, :] += mm(ds, qn)
        ot = ot + mm(v_ref[:, here], p)
        dqt = dqt + mm(k_ref[:, here], ds)
    o_ref[...] = ot.astype(BF16)

    def unrotated(grad, trig):
        cosine, sine = trig[:HALF], trig[HALF:ROT]
        a, b = grad[:HALF], grad[HALF:ROT]
        turned = jnp.concatenate([a * cosine + b * sine, b * cosine - a * sine], axis=0)
        return turned.astype(BF16), grad[ROT:].astype(BF16)

    dq_ref[:ROT, :], dq_ref[ROT:, :] = unrotated(dqt * (HEAD**-0.5), tq_ref[...])

    @pl.when(i == pl.num_programs(0) - 1)
    def _():
        grad = dk[...].T
        dk_ref[:ROT, :half], dk_ref[ROT:, :half] = unrotated(grad[:, :half], to_ref[...])
        dk_ref[:ROT, half:], dk_ref[ROT:, half:] = unrotated(grad[:, half:], tx_ref[...])
        dv_ref[...] = dv[...].T.astype(BF16)


def attention(h, after, qt, dot, kt, vt, trig_own, trig_other):
    rows, length = qt.shape[1], kt.shape[1]
    lanes = STEP
    tall = trig_own.shape[0]
    q_spec = pl.BlockSpec((HEAD, lanes), lambda i: (h, i))
    k_spec = pl.BlockSpec((HEAD, length), lambda i: (h, 0))
    trig_spec = pl.BlockSpec((tall, rows), lambda i: (0, 0))
    return pl.pallas_call(
        attention_kernel,
        grid=(rows // lanes,),
        in_specs=[pl.BlockSpec(memory_space=pl.ANY), q_spec, q_spec, k_spec, k_spec,
                  pl.BlockSpec((tall, lanes), lambda i: (0, i)), trig_spec, trig_spec],
        out_specs=[pl.BlockSpec((HEAD, lanes), lambda i: (0, i))] * 2
        + [pl.BlockSpec((HEAD, length), lambda i: (0, 0))] * 2,
        out_shape=[low_shape(HEAD, rows)] * 2 + [low_shape(HEAD, length)] * 2,
        scratch_shapes=[
            pltpu.VMEM((length, HEAD), BF16),
            pltpu.VMEM((length, HEAD), BF16),
            pltpu.VMEM((length, 1), F32),
            pltpu.VMEM((length, HEAD), F32),
            pltpu.VMEM((length, HEAD), F32),
            pltpu.VMEM((length, lanes), F32),
            pltpu.VMEM((length, lanes), F32),
        ],
        compiler_params=params(32),
        cost_estimate=cost(40 * rows * length * HEAD, 16 * HEAD * length, rows * length),
    )(after, qt, dot, kt, vt, trig_own, trig_own, trig_other)


def forward_kernel(split, at, n2_ref, g_ref, up_ref, bias_ref, down_ref, s2_ref, b2_ref,
                   ff_ref, a_ref, small_ref, first_ref, second_ref, *scratch):
    i = pl.program_id(0)
    up_part, down_part = scratch if split else (first_ref, second_ref)

    @pl.when(i == 0)
    def _():
        up_part[...] = jnp.zeros_like(up_part)
        down_part[...] = jnp.zeros_like(down_part)
        small_ref[...] = jnp.zeros_like(small_ref)

    n2, g = n2_ref[...], g_ref[...]
    up = mm(n2, up_ref[...]) + row_of(bias_ref)
    cdf = 0.5 + 0.5 * lax.erf(up * (0.5**0.5))
    act = (up * cdf).astype(BF16)
    slope = cdf + up * (jnp.exp(up * up * -0.5) * 0.3989422804014327)
    up_grad = (mm(g, down_ref[...], 1, 1) * slope).astype(BF16)
    ff_ref[...] = mm(act, down_ref[...]).astype(BF16)
    second = mm(up_grad, up_ref[...], 1, 1)
    up_part[...] += mm(n2, up_grad, 0, 0)
    down_part[...] += mm(act, g, 0, 0)
    a_ref[...] = (second * row_of(s2_ref)).astype(BF16)
    small_ref[0:1, :] += jnp.sum(up_grad.astype(F32), axis=0, keepdims=True)
    small_ref[1:2, :] += jnp.sum(g.astype(F32), axis=0, keepdims=True)
    small_ref[2:3, :] += jnp.sum(second * n2.astype(F32), axis=0, keepdims=True)
    small_ref[3:4, :] += jnp.sum(second, axis=0, keepdims=True)

    @pl.when(i == pl.num_programs(0) - 1)
    def _():
        rest = small_ref[2:3, :] - row_of(b2_ref) * small_ref[3:4, :]
        small_ref[2:3, :] = rest / row_of(s2_ref)

    if split:
        half = up_part.shape[0] // 2

        @pl.when(i == pl.num_programs(0) - 1)
        def _():
            for ref, f in ((first_ref, at[3]), (second_ref, 1 - at[3])):
                piece = pl.ds(pl.multiple_of(f * half, 128), half)
                ref[:half, :] = up_part[piece, :].astype(ref.dtype)
                ref[half:, :half] = down_part[:half, piece].astype(ref.dtype)
                ref[half:, half:] = down_part[half:, piece].astype(ref.dtype)


def feed_forward(split, at, n2, g, up, bias, down, scale, offset):
    rows, width = n2.shape
    hidden = up.shape[1]
    row = pl.BlockSpec((STEP, width), lambda i, at: (i, 0))

    def whole(*dims):
        return pl.BlockSpec(dims, lambda i, at: (0,) * len(dims))

    if split:
        assert width == hidden
        parts = [shape(width, hidden), low_shape(width, hidden)]
    else:
        parts = [shape(width, hidden), shape(hidden, width)]
    return pl.pallas_call(
        functools.partial(forward_kernel, split),
        grid_spec=pltpu.PrefetchScalarGridSpec(
            num_scalar_prefetch=1,
            grid=(rows // STEP,),
            in_specs=[row, row, whole(width, hidden), whole(hidden), whole(hidden, width),
                      whole(width), whole(width)],
            out_specs=[row, row, whole(8, width)] + [whole(*p.shape) for p in parts],
            scratch_shapes=[pltpu.VMEM((width, hidden), F32), pltpu.VMEM((hidden, width), F32)]
            if split
            else [],
        ),
        out_shape=[low_shape(rows, width)] * 2 + [shape(8, width)] + parts,
        compiler_params=params(40),
        cost_estimate=cost(12 * rows * width * hidden, 16 * MIB, 2 * rows * hidden),
    )(at, n2, g, up, bias, down, scale, offset)


def emit(keep_ref, send_ref, v):
    i = pl.program_id(0)

    @pl.when(i % 2 == 0)
    def _():
        keep_ref[0] = v.astype(BF16)

    @pl.when(i % 2 == 1)
    def _():
        send_ref[0] = v.astype(BF16)


def branch_kernel(heads, *refs):
    o = refs[:heads]
    g_ref, ff_ref, w_ref, keep_ref, send_ref, out = refs[heads:]
    wide = heads * HEAD

    @pl.when(pl.program_id(0) == 0)
    def _():
        out[...] = jnp.zeros_like(out)

    ot = jnp.concatenate([r[...] for r in o], axis=0)
    emit(keep_ref, send_ref, mm(ot, w_ref[...], 0, 0) + ff_ref[...].astype(F32))
    out[...] += mm(ot, g_ref[...])


def branch(o, g, ff, weights):
    rows, width = g.shape
    heads = len(o)
    wide = heads * HEAD
    row = pl.BlockSpec((STEP, width), lambda i: (i, 0))
    slots = pl.BlockSpec((1, STEP, width), lambda i: (i // 2, 0, 0))
    return pl.pallas_call(
        functools.partial(branch_kernel, heads),
        grid=(rows // STEP,),
        in_specs=[pl.BlockSpec((HEAD, STEP), lambda i: (0, i))] * heads
        + [row, row, pl.BlockSpec((wide, width), lambda i: (3, 0))],
        out_specs=[slots, slots, pl.BlockSpec((wide, width), lambda i: (0, 0))],
        out_shape=[low_shape(2, STEP, width)] * 2 + [shape(wide, width)],
        compiler_params=params(24),
        cost_estimate=cost(4 * rows * width * wide, 8 * MIB),
    )(*o, g, ff, weights)


def back_kernel(own, split, heads, at, *refs):
    count = 3 if own else 2
    grads, refs = refs[: count * heads], refs[count * heads :]
    n1_ref, w_ref, s1_ref, *refs = refs
    if own:
        (half_b, a2_ref, b1_ref, small_ff, small_other, mix_other, out_part,
         keep_ref, send_ref, first_ref, second_ref, mix, small) = refs
    else:
        keep_b, ff_half, keep_ref, send_ref, mix, small = refs
    i = pl.program_id(0)
    wide = heads * HEAD
    tall = mix.shape[0]

    @pl.when(i == 0)
    def _():
        if own:
            mix[:wide, :] = jnp.zeros((wide, mix.shape[1]), F32)
            mix[wide:, :] = mix_other[...]
            small[...] = small_other[...]
        else:
            mix[...] = jnp.zeros_like(mix)
            small[...] = jnp.zeros_like(small)

    grad = jnp.concatenate([r[...] for r in grads], axis=0)
    first = mm(grad, w_ref[3 * wide - tall : 3 * wide, :], 0, 0)
    a = first * row_of(s1_ref)
    emit(keep_ref, send_ref, a + a2_ref[...].astype(F32) if own else a)
    mix[...] += mm(grad, n1_ref[...])
    small[0:1, :] += jnp.sum(first * n1_ref[...].astype(F32), axis=0, keepdims=True)
    small[1:2, :] += jnp.sum(first, axis=0, keepdims=True)
    ones = jnp.ones((8, grad.shape[1]), BF16)
    small[6:7, 3 * wide - tall : 3 * wide] += mm(ones, grad, 1, 1)[0:1]

    if own:
        @pl.when(i == pl.num_programs(0) - 1)
        def _():
            rest = small[0:1, :] - row_of(b1_ref) * small[1:2, :]
            small[0:1, :] = rest / row_of(s1_ref)
            small[2:4, :] = small_ff[2:4, :]
            small[4:6, :] = small_ff[0:2, :]
            if split:
                half = mix.shape[1] // 2
                vectors = small[...].astype(BF16)
                for ref, f in ((first_ref, at[3]), (second_ref, 1 - at[3])):
                    piece = pl.ds(pl.multiple_of(f * half, 128), half)
                    ref[: 3 * wide, :] = mix[:, piece].astype(ref.dtype)
                    ref[3 * wide : 4 * wide, :] = out_part[:, piece].astype(ref.dtype)
                    both = jnp.concatenate([vectors[:, :half], vectors[:, half:]], axis=0)
                    ref[4 * wide : 4 * wide + 16, :] = both.astype(ref.dtype)
                    ref[4 * wide + 16 :, :] = jnp.zeros((48, half), ref.dtype)
            else:
                first_ref[: 3 * wide, :] = mix[...]
                first_ref[3 * wide :, :] = out_part[...]
                second_ref[...] = small[...]


def back(own, split, at, grads, n1, weights, scale, extra):
    rows, width = n1.shape
    heads = len(grads[0])
    wide = heads * HEAD
    tall = 3 * wide if own else 2 * wide
    offset = 0 if own else rows // STEP
    row = pl.BlockSpec((STEP, width), lambda i, at: (i, 0))
    col = pl.BlockSpec((HEAD, STEP), lambda i, at: (0, i + offset))
    slots = pl.BlockSpec((1, STEP, width), lambda i, at: (i // 2, 0, 0))

    def whole(*dims):
        return pl.BlockSpec(dims, lambda i, at: (0,) * len(dims))

    half = width // 2
    specs = [col] * (len(grads) * heads) + [row, whole(4 * wide, width), whole(width)]
    earlier = pl.BlockSpec(memory_space=pl.ANY)
    if not own:
        specs += [earlier, earlier]
        parts = [shape(tall, width), shape(8, width)]
        scratch = []
    else:
        specs += [earlier, row, whole(width), whole(8, width), whole(8, width), whole(2 * wide, width),
                  whole(wide, width)]
        scratch = [pltpu.VMEM((tall, width), F32), pltpu.VMEM((8, width), F32)]
        if split:
            parts = [shape(4 * wide + 64, half), low_shape(4 * wide + 64, half)]
        else:
            parts = [shape(4 * wide, width), shape(8, width)]
    return pl.pallas_call(
        functools.partial(back_kernel, own, split, heads),
        grid_spec=pltpu.PrefetchScalarGridSpec(
            num_scalar_prefetch=1,
            grid=(rows // STEP,),
            in_specs=specs,
            out_specs=[slots, slots] + [whole(*p.shape) for p in parts],
            scratch_shapes=scratch,
        ),
        out_shape=[low_shape(2, STEP, width)] * 2 + parts,
        compiler_params=params(32),
        cost_estimate=cost(4 * rows * width * tall, 10 * MIB),
    )(at, *[v for vs in grads for v in vs], n1, weights, scale, *extra)


def swap(v, axis, size, distance):
    return lax.ppermute(v, axis, [(i, i ^ distance) for i in range(size)])


def by_xor(pieces, index):
    low, high = (index & 1) == 1, (index & 2) == 2
    a, b, c, d = pieces
    a, b, c, d = (jnp.where(low, b, a), jnp.where(low, a, b),
                  jnp.where(low, d, c), jnp.where(low, c, d))
    return (jnp.where(high, c, a), jnp.where(high, d, b),
            jnp.where(high, a, c), jnp.where(high, b, d))


def tie(v, *earlier):
    return lax.optimization_barrier((v, *earlier))[0]


def gather_halves(shard, size, mine, dim, *earlier):
    if size != 2:
        return lax.all_gather(shard, "fsdp", axis=dim, tiled=True)
    other = swap(shard, "fsdp", 2, 1)
    if earlier:
        other = tie(other, *earlier)
    first = mine == 0
    return jnp.concatenate(
        [jnp.where(first, shard, other), jnp.where(first, other, shard)], axis=dim
    )


def scatter_any(part, dim):
    return lax.psum_scatter(
        part.astype(BF16), "fsdp", scatter_dimension=dim, tiled=True
    ).astype(F32)


def halve(v, distance, bit, *earlier):
    rows = v.shape[0] // 2
    keep = lax.dynamic_slice_in_dim(v, bit * rows, rows, 0)
    send = lax.dynamic_slice_in_dim(v, (1 - bit) * rows, rows, 0).astype(BF16)
    return keep + tie(swap(send, "ctx", 4, distance), *earlier).astype(F32)


def quarter_sum(v, c, *earlier):
    rows = v.shape[0] // 4
    mine = 2 * (c % 2) + c // 2

    def part(j):
        return lax.dynamic_slice_in_dim(v, (mine ^ j) * rows, rows, 0)

    total = part(0)
    for distance, j in ((3, 3), (2, 1), (1, 2)):
        sent = swap(part(j).astype(BF16), "ctx", 4, distance)
        total = total + tie(sent, *earlier).astype(F32)
    return total


def pair_up(v, *earlier):
    v = v.astype(BF16)
    return jnp.stack([v, tie(swap(v, "ctx", 4, 2), *earlier)])


def double(pair, c, *earlier):
    others = tie(swap(pair, "ctx", 4, 1), *earlier)
    return by_xor([pair[0], pair[1], others[0], others[1]], 2 * (c % 2) + c // 2)


def sum_over_ctx(v, c):
    return double(pair_up(quarter_sum(v, c)), c)


def butterfly(v, axis_name, size):
    distance = 1
    while distance < size:
        v = v + swap(v, axis_name, size, distance)
        distance *= 2
    return v


def shards(
    sizes,
    inputs,
    positions,
    query_key_value_weight,
    query_key_value_bias,
    attention_output_weight,
    attention_output_bias,
    up_projection_weight,
    up_projection_bias,
    down_projection_weight,
    down_projection_bias,
    first_scale,
    first_shift,
    second_scale,
    second_shift,
    cotangent,
):
    fsdp = sizes["fsdp"]
    split = fsdp == 2
    seq_count, block, width = inputs.shape
    assert seq_count == 2 and sizes["ctx"] == 4 and sizes["tp"] == 4 and block == 2 * STEP
    length = positions.shape[1]
    local = query_key_value_weight.shape[2]
    heads = local // HEAD
    hidden = up_projection_weight.shape[1]
    quarter = block // 4
    f = lax.axis_index("fsdp")
    c = lax.axis_index("ctx")
    t = lax.axis_index("tp")
    s = c // 2
    at = jnp.stack([s, c, t, f]).astype(jnp.int32)

    def my_quarter(v, seq):
        return lax.dynamic_slice(v, (seq, t * quarter, 0), (1, quarter, width))

    x_mine, x_theirs = my_quarter(inputs, s), my_quarter(inputs, 1 - s)
    g_theirs = my_quarter(cotangent, 1 - s)
    far_z = swap(jnp.concatenate([x_theirs, g_theirs], axis=0), "ctx", 4, 2)
    cross = swap(x_theirs, "ctx", 4, 3)
    near = swap(x_mine, "ctx", 4, 1)

    def over_tp(v):
        v_x = swap(v, "tp", 4, 2)
        return v, v_x, swap(jnp.stack([v, v_x]), "tp", 4, 1)

    far = over_tp(far_z)
    others = over_tp(jnp.concatenate([near, cross], axis=0))

    wup = gather_halves(up_projection_weight, fsdp, f, 0)
    wdown = gather_halves(down_projection_weight, fsdp, f, 1)
    mix_shard = query_key_value_weight.transpose(1, 2, 0).reshape(3 * local, -1)
    mix_out_shard = jnp.concatenate([mix_shard, attention_output_weight], axis=0)

    inverse = 10000.0 ** (-2.0 * jnp.arange(HALF, dtype=F32) / ROT)
    places = positions.astype(F32)[:, None, :]
    angles = inverse[None, :, None] * places
    trig = jnp.concatenate(
        [jnp.cos(angles), jnp.sin(angles), jnp.broadcast_to(places, angles.shape)], axis=1
    )

    n1_own, n2, g, trig_own = norms(
        at, True, (inputs, cotangent, *far), trig,
        (first_scale, first_shift, second_scale, second_shift),
    )
    ff, a2, small_ff, ff_first, ff_second = feed_forward(
        split, at, n2, g, wup, up_projection_bias, wdown, second_scale, second_shift
    )
    weights = gather_halves(mix_out_shard, fsdp, f, 1, small_ff)
    n1_other, trig_other = norms(
        at, False, (others[0], others[1], tie(others[2], small_ff)), trig,
        (first_scale, first_shift),
    )
    kt, vt, qt, dot = project(
        n1_own, n1_other, trig_own, trig_other, g, weights, query_key_value_bias
    )
    per_head = []
    after = small_ff
    for h in range(heads):
        if split and h == heads - 1:
            after = ff_first + swap(ff_second, "fsdp", 2, 1).astype(F32)
        per_head.append(attention(h, after, qt, dot, kt, vt, trig_own, trig_other))
    o, dq, dk, dv = zip(*per_head)
    ff_half = halve(after, 1, c % 2) if split else after

    def over_core(keep, send, *earlier):
        v = keep.astype(F32) + tie(swap(send, "tp", 4, 1), *earlier).astype(F32)
        return v.reshape(2, 2, quarter, width)

    def over_x(v, *earlier):
        return v[:, 0] + tie(swap(v[:, 1].astype(BF16), "tp", 4, 2), *earlier).astype(F32)

    keep_b, send_b, out_part = branch(o, g, ff, weights)
    keep_o, send_o, mix_other, small_other = back(
        False, split, at, (dk, dv), n1_other, weights, first_scale, (keep_b, ff_half)
    )
    half_b = over_core(keep_b, send_b)
    keep_w, send_w, late_first, late_second = back(
        True, split, at, (dq, dk, dv), n1_own, weights, first_scale,
        (half_b, a2, first_shift, small_ff, small_other, mix_other, out_part),
    )
    half_o = over_core(keep_o, send_o)
    half_w = over_core(keep_w, send_w)

    def over_ctx(v, distance, *earlier):
        return tie(swap(v.astype(BF16), "ctx", 4, distance), *earlier).astype(F32)

    def gather_tp(ours, *earlier):
        pair = jnp.stack([ours, tie(swap(ours, "tp", 4, 2), *earlier)])
        core = swap(pair, "tp", 4, 1)
        pieces = by_xor((pair[0], core[0], pair[1], core[1]), t)
        pieces = jnp.concatenate(pieces, axis=1)
        return jnp.stack([jnp.where(s == 0, pieces[0], pieces[1]),
                          jnp.where(s == 0, pieces[1], pieces[0])]).astype(F32)

    sums_b = over_x(half_b, half_w)
    branches = jnp.stack([sums_b[0], over_ctx(sums_b[1], 2)]).astype(BF16)
    sums_o = over_x(half_o, half_w)
    sums_w = over_x(half_w)
    sums_w = sums_w + over_ctx(sums_o, 1)
    a = jnp.stack([sums_w[0], over_ctx(sums_w[1], 2, branches)])
    xhat, inv = xhat_of(jnp.concatenate([x_mine, x_theirs], axis=0).astype(F32))
    norm_grad = inv * (
        a
        - jnp.mean(a, axis=-1, keepdims=True)
        - xhat * jnp.mean(a * xhat, axis=-1, keepdims=True)
    )
    norm_grad = norm_grad.astype(BF16)
    block_out = gather_tp(branches, a)
    block_out = (
        inputs.astype(F32) + block_out + (attention_output_bias + down_projection_bias)
    )
    inputs_grad = cotangent.astype(F32) + gather_tp(norm_grad)

    if split:
        q = double(pair_up(halve(ff_half, 2, c // 2), sums_o), c, norm_grad)
        up_total = jnp.concatenate(q[:2], axis=0).astype(F32)
        down_total = jnp.concatenate(q[2:], axis=0).astype(F32)
        down_total = jnp.concatenate(
            [down_total[:, : width // 2], down_total[:, width // 2 :]], axis=0
        )
        late = late_first + tie(swap(late_second, "fsdp", 2, 1), a).astype(F32)
        late = double(pair_up(quarter_sum(late, c, norm_grad)), c, block_out)
        late = jnp.concatenate(late, axis=0).astype(F32)
        small = jnp.concatenate([late[4 * local : 4 * local + 8], late[4 * local + 8 :][:8]], axis=1)
    else:
        q = sum_over_ctx(scatter_any(ff_first, 0), c)
        up_total = jnp.concatenate(q, axis=0).astype(F32)
        q = sum_over_ctx(scatter_any(ff_second, 1), c)
        down_total = jnp.concatenate(q, axis=0).astype(F32)
        q = sum_over_ctx(scatter_any(late_first, 1), c)
        late = jnp.concatenate(q, axis=0).astype(F32)
        small = butterfly(butterfly(late_second, "fsdp", fsdp), "ctx", 4)
    mix_total = late[: 3 * local].reshape(3, local, -1).transpose(2, 0, 1)
    out_total = late[3 * local : 4 * local]
    norm_small = butterfly(small, "tp", 4)
    bias_total = norm_small[5] * 0.25
    return (
        block_out,
        inputs_grad,
        mix_total,
        small[6, : 3 * local].reshape(3, local),
        out_total,
        bias_total,
        up_total,
        small[4, :hidden],
        down_total,
        bias_total,
        norm_small[0],
        norm_small[1],
        norm_small[2],
        norm_small[3],
    )


def solution(mesh):
    in_specs = (
        P("fsdp", "ctx", None),
        P("fsdp", None),
        P("fsdp", None, "tp"),
        P(None, "tp"),
        P("tp", "fsdp"),
        P(),
        P("fsdp", "tp"),
        P("tp"),
        P("tp", "fsdp"),
        P(),
        P(),
        P(),
        P(),
        P(),
        P("fsdp", "ctx", None),
    )
    out_specs = (
        P("fsdp", "ctx", None),
        P("fsdp", "ctx", None),
        P("fsdp", None, "tp"),
        P(None, "tp"),
        P("tp", "fsdp"),
        P(),
        P("fsdp", "tp"),
        P("tp"),
        P("tp", "fsdp"),
        P(),
        P(),
        P(),
        P(),
        P(),
    )
    body = functools.partial(shards, dict(mesh.shape))
    return jax.shard_map(body, mesh=mesh, in_specs=in_specs, out_specs=out_specs, check_vma=False)
```
